32 devices in a mesh: seq: 8 (over z, x), ctx: 4 (over y, core).
Axes of the slice: x: 2, y: 2, z: 4, core: 2. Of those that a mesh axis runs over, the one named last changes fastest.
Arguments:
- inputs: bfloat16 [2, 8, 4, 128, 2048], P(None, 'seq', None, 'ctx'), may hold values from -6 to 6
- doc_ids: int32 [2, 8, 4, 128], P(None, 'seq', None, 'ctx'), may hold values from 0 to 8, as said below
- cotangent: bfloat16 [2, 8, 4, 128, 2048], P(None, 'seq', None, 'ctx'), may hold values from -11 to 11
- weight_qkv: float32 [2048, 3, 2048], P('seq', None, 'ctx'), may hold values from -0.110485435 to 0.110485435
- moment_qkv: float32 [2048, 3, 2048], P('seq', None, 'ctx'), may hold values from -2.8076172e-05 to 2.8076172e-05
- second_qkv: float32 [2048, 3, 2048], P('seq', None, 'ctx'), may hold values from 1.9520521e-10 to 7.852912e-10
- weight_out: float32 [2048, 2048], P('seq', 'ctx'), may hold values from -0.5 to 0.5
- moment_out: float32 [2048, 2048], P('seq', 'ctx'), may hold values from -5.493164e-05 to 5.493164e-05
- second_out: float32 [2048, 2048], P('seq', 'ctx'), may hold values from 7.838011e-10 to 3.1381845e-09
- weight_mlp: float32 [2048, 2, 8192], P('seq', None, 'ctx'), may hold values from -0.176776695 to 0.176776695
- moment_mlp: float32 [2048, 2, 8192], P('seq', None, 'ctx'), may hold values from -5.493164e-05 to 5.493164e-05
- second_mlp: float32 [2048, 2, 8192], P('seq', None, 'ctx'), may hold values from 7.838011e-10 to 3.1381845e-09
- weight_down: float32 [2048, 8192], P('seq', 'ctx'), may hold values from -0.0625 to 0.0625
- moment_down: float32 [2048, 8192], P('seq', 'ctx'), may hold values from -5.493164e-05 to 5.493164e-05
- second_down: float32 [2048, 8192], P('seq', 'ctx'), may hold values from 7.838011e-10 to 3.1381845e-09
- norm_gains: float32 [2, 2048], replicated, may hold values from 0.4 to 2.5
- moment_gains: float32 [2, 2048], replicated, may hold values from -0.00021972656 to 0.00021972656
- second_gains: float32 [2, 2048], replicated, may hold values from 1.2546778e-08 to 5.021691e-08
- gate_logit: float32 [16], replicated, may hold values from -2 to 2
- moment_gate: float32 [16], replicated, may hold values from -0.0004394531 to 0.0004394531
- second_gate: float32 [16], replicated, may hold values from 5.00679e-08 to 2.0116568e-07
Outputs:
- block_out: bfloat16 [2, 8, 4, 128, 2048], P(None, 'seq', None, 'ctx')
- input_grad: bfloat16 [2, 8, 4, 128, 2048], P(None, 'seq', None, 'ctx')
- grad_norm: float32 [], replicated
- qkv_moment: float32 [2048, 3, 2048], P('seq', None, 'ctx')
- qkv_second: float32 [2048, 3, 2048], P('seq', None, 'ctx')
- qkv_weight: float32 [2048, 3, 2048], P('seq', None, 'ctx')
- out_moment: float32 [2048, 2048], P('seq', 'ctx')
- out_second: float32 [2048, 2048], P('seq', 'ctx')
- out_weight: float32 [2048, 2048], P('seq', 'ctx')
- mlp_moment: float32 [2048, 2, 8192], P('seq', None, 'ctx')
- mlp_second: float32 [2048, 2, 8192], P('seq', None, 'ctx')
- mlp_weight: float32 [2048, 2, 8192], P('seq', None, 'ctx')
- down_moment: float32 [2048, 8192], P('seq', 'ctx')
- down_second: float32 [2048, 8192], P('seq', 'ctx')
- down_weight: float32 [2048, 8192], P('seq', 'ctx')
- gains_moment: float32 [2, 2048], replicated
- gains_second: float32 [2, 2048], replicated
- gains_weight: float32 [2, 2048], replicated
- gate_moment: float32 [16], replicated
- gate_second: float32 [16], replicated
- gate_weight: float32 [16], replicated
The draws below stay inside these ranges and needn't reach their ends.
Inputs may be any that keep to these rules, and one draw needn't show every extreme that they name: `doc_ids`: within each sequence (512 tokens) the ids are 0 at its first token and rise by 0 or 1 from token to token, ending at 8 in every sequence; in every sequence some whole segment after the first belongs to the document of the token just before it.
All inputs are finite; a program needn't handle non-finite values.
Results may differ from the reference program's by a relative error of at most 0.025.
Values may be sent and summed in bfloat16 or wider, within the bound.
No kernel may reach another device: no remote copies, remote signals or barrier semaphores. Data moves between devices by JAX's collectives and lax.ppermute only.
A program may use at most 320 MiB of HBM per device.

```python
import math
import jax
import jax.numpy as jnp
from jax import lax

D = 2048
HEADS = 16
HEAD_DIM = 128
FF = 8192
SEGS = 4
MICRO = 2
STEP_COUNT = 10
SEG = 128
SEQS = 8


def rising(count, low_end, high_end):
    return low_end + (high_end - low_end) * jnp.arange(count, dtype=jnp.float32) / max(count - 1, 1)


def base_draw(key, array_shape, spread):
    return jnp.clip(jax.random.normal(key, array_shape, jnp.float32), -4.0, 4.0) * spread


def moment_scale(factor):
    return factor * (D * (4 * HEADS * HEAD_DIM + 3 * FF)) ** (-0.5)


def first_draw(key, array_shape, factor):
    return base_draw(key, array_shape, 0.1 / 0.9 * moment_scale(factor))


def second_draw(key, array_shape, factor):
    spread = jnp.exp(jax.random.uniform(key, array_shape, jnp.float32, minval=0.0, maxval=math.log(4.0)))
    return spread * (0.05 / 0.95) * moment_scale(factor) ** 2


def draw_doc_ids(key, part):
    key = jax.random.fold_in(key, 1)
    first_key, second_key = jax.random.split(key)
    seq_count = MICRO * SEQS
    total_len = SEGS * SEG
    start_count = 2 * SEGS
    row_keys = jax.random.split(first_key, seq_count)
    scores = jax.vmap(lambda k: jax.random.permutation(k, total_len))(row_keys).astype(jnp.int32)
    held = jax.random.randint(second_key, (seq_count, 1), 1, SEGS)
    position = jnp.arange(total_len, dtype=jnp.int32)[None, :]
    inside = (position >= held * SEG) & (position < (held + 1) * SEG)
    barred = inside | (position == 0)
    scores = jnp.where(barred, total_len + position, scores)
    order = jnp.argsort(scores, axis=1, stable=True)
    ranks = jnp.argsort(order, axis=1, stable=True)
    starts = (ranks < start_count).astype(jnp.int32)
    numbers = jnp.cumsum(starts, axis=1).astype(jnp.int32)
    return numbers.reshape(MICRO, SEQS, SEGS, SEG)


def draw_cotangent(key, part):
    key = jax.random.fold_in(key, 2)
    array_shape = (MICRO, SEQS, SEGS, SEG, D)
    return (jnp.clip(jax.random.normal(key, array_shape, jnp.float32), -6.0, 6.0) * rising(D, 0.6, 1.8)).astype(jnp.bfloat16)


def draw_weight_qkv(key, part):
    key = jax.random.fold_in(key, 3)
    array_shape = (D, 3, HEADS * HEAD_DIM)
    ramp = rising(HEADS * HEAD_DIM, 0.6, 1.4)
    return base_draw(key, array_shape, 0.8 * D ** (-0.5)) * ramp


def draw_weight_mlp(key, part):
    key = jax.random.fold_in(key, 4)
    array_shape = (D, 2, FF)
    return base_draw(key, array_shape, D ** (-0.5)) * rising(FF, 0.6, 1.8)


def draw_norm_gains(key, part):
    key = jax.random.fold_in(key, 5)
    return (1.0 + base_draw(key, (2, D), 0.05)) * rising(D, 0.6, 1.5)


def draw_moment_qkv(key, part):
    key = jax.random.fold_in(key, 6)
    return first_draw(key, (D, 3, HEADS * HEAD_DIM), 0.5)


def draw_second_qkv(key, part):
    key = jax.random.fold_in(key, 7)
    return second_draw(key, (D, 3, HEADS * HEAD_DIM), 0.5)


def draw_moment_out(key, part):
    key = jax.random.fold_in(key, 8)
    return first_draw(key, (D, HEADS * HEAD_DIM), 1.0)


def draw_second_out(key, part):
    key = jax.random.fold_in(key, 9)
    return second_draw(key, (D, HEADS * HEAD_DIM), 1.0)


def draw_moment_mlp(key, part):
    key = jax.random.fold_in(key, 10)
    return first_draw(key, (D, 2, FF), 1.0)


def draw_second_mlp(key, part):
    key = jax.random.fold_in(key, 11)
    return second_draw(key, (D, 2, FF), 1.0)


def draw_moment_down(key, part):
    key = jax.random.fold_in(key, 12)
    return first_draw(key, (D, FF), 1.0)


def draw_second_down(key, part):
    key = jax.random.fold_in(key, 13)
    return second_draw(key, (D, FF), 1.0)


def draw_moment_gains(key, part):
    key = jax.random.fold_in(key, 14)
    return first_draw(key, (2, D), 4.0)


def draw_second_gains(key, part):
    key = jax.random.fold_in(key, 15)
    return second_draw(key, (2, D), 4.0)


def draw_moment_gate(key, part):
    key = jax.random.fold_in(key, 16)
    return first_draw(key, (HEADS,), 8.0)


def draw_second_gate(key, part):
    key = jax.random.fold_in(key, 17)
    return second_draw(key, (HEADS,), 8.0)


def levels(stream_key, shape, cuts, least, high):
    gain, own = 1.0, jax.random.fold_in(stream_key, 6)
    for dim, parts in cuts:
        heights = jnp.exp(jax.random.uniform(jax.random.fold_in(own, dim), (parts,), jnp.float32, least / len(cuts), high / len(cuts)))
        gain = gain * jnp.repeat(heights, shape[dim] // parts).reshape([-1 if axis == dim else 1 for axis in range(len(shape))])
    return gain


def gaussian(stream_key, dims, scale, reach, cuts=(), held_as=jnp.bfloat16):
    entries = jax.random.normal(stream_key, dims, jnp.float32) * scale
    if len(cuts) > 0:
        entries = levels(stream_key, dims, cuts, -0.22, 0.18) * entries
    return jnp.clip(entries, min=-reach, max=reach).astype(held_as)


def setup_inputs(seed: int = 0) -> dict:
    splits = jax.random.split(jax.random.key(seed), 22)
    inputs = gaussian(splits[0], (MICRO, SEQS, SEGS, SEG, D), 1.0, 6.0, ((1, 8), (3, 4)))
    doc_ids = draw_doc_ids(jax.random.fold_in(splits[21], 71), 0)
    cotangent = draw_cotangent(jax.random.fold_in(splits[21], 71), 0)
    weight_qkv = draw_weight_qkv(jax.random.fold_in(splits[21], 71), 0)
    moment_qkv = draw_moment_qkv(jax.random.fold_in(splits[21], 71), 0)
    second_qkv = draw_second_qkv(jax.random.fold_in(splits[21], 71), 0)
    weight_out = gaussian(splits[6], (D, HEADS * HEAD_DIM), (HEADS * HEAD_DIM // 16) ** -0.5, 0.5, ((0, 8), (1, 4)), jnp.float32)
    moment_out = draw_moment_out(jax.random.fold_in(splits[21], 71), 0)
    second_out = draw_second_out(jax.random.fold_in(splits[21], 71), 0)
    weight_mlp = draw_weight_mlp(jax.random.fold_in(splits[21], 71), 0)
    moment_mlp = draw_moment_mlp(jax.random.fold_in(splits[21], 71), 0)
    second_mlp = draw_second_mlp(jax.random.fold_in(splits[21], 71), 0)
    weight_down = gaussian(splits[12], (D, FF), FF ** -0.5, 0.0625, ((0, 8), (1, 4)), jnp.float32)
    moment_down = draw_moment_down(jax.random.fold_in(splits[21], 71), 0)
    second_down = draw_second_down(jax.random.fold_in(splits[21], 71), 0)
    norm_gains = draw_norm_gains(jax.random.fold_in(splits[21], 71), 0)
    moment_gains = draw_moment_gains(jax.random.fold_in(splits[21], 71), 0)
    second_gains = draw_second_gains(jax.random.fold_in(splits[21], 71), 0)
    gate_logit = jnp.clip(jax.random.uniform(splits[18], (HEADS,), jnp.float32, -2.0, 2.0), -2.0, 2.0)
    moment_gate = draw_moment_gate(jax.random.fold_in(splits[21], 71), 0)
    second_gate = draw_second_gate(jax.random.fold_in(splits[21], 71), 0)
    return dict(inputs=inputs, doc_ids=doc_ids, cotangent=cotangent, weight_qkv=weight_qkv, moment_qkv=moment_qkv, second_qkv=second_qkv, weight_out=weight_out, moment_out=moment_out, second_out=second_out, weight_mlp=weight_mlp, moment_mlp=moment_mlp, second_mlp=second_mlp, weight_down=weight_down, moment_down=moment_down, second_down=second_down, norm_gains=norm_gains, moment_gains=moment_gains, second_gains=second_gains, gate_logit=gate_logit, moment_gate=moment_gate, second_gate=second_gate)


@jax.custom_vjp
def low(v):
    return lax.optimization_barrier(v.astype(jnp.bfloat16)).astype(jnp.float32)

@jax.custom_vjp
def low_back(v):
    return v

def low_keep(v):
    return (low(v), None)

def low_pass(kept, grad):
    return (grad,)

def back_keep(v):
    return (v, None)

def back_low(kept, grad):
    return (low(grad),)
low.defvjp(low_keep, low_pass)
low_back.defvjp(back_keep, back_low)
EPS = 1e-06
NEG = -1e+30
CLIP = 1.0
BETA1 = 0.9
BETA2 = 0.95
ADAM_EPS = 1e-08
DECAY = 0.1
HIGH = lax.Precision.HIGHEST

def elu_one(tensor):
    return jnp.where(tensor > 0, tensor + 1.0, jnp.exp(jnp.minimum(tensor, 0.0)))

def rms_norm(tensor, scaling):
    return tensor * lax.rsqrt(lax.optimization_barrier(jnp.mean(tensor * tensor, axis=-1, keepdims=True)) + EPS) * scaling

def memory_read(queries, keys_in, values_in, doc_rows):
    head_count = queries.shape[2]
    feat_width = queries.shape[3]

    def advance(state_in, segment):
        memory, normer, previous = state_in
        query_seg, key_seg, value_seg, doc_seg = segment
        query_pos = elu_one(query_seg)
        key_pos = elu_one(key_seg)
        reading = (doc_seg == previous).astype(jnp.float32)[:, None, None]
        numerator = jnp.einsum('lhe,hef->lhf', query_pos, memory, precision=HIGH)
        denominator = 1.0 + jnp.einsum('lhe,he->lh', query_pos, normer, precision=HIGH)
        recalled = reading * numerator / denominator[:, :, None]
        last_id = doc_seg[-1]
        keeping = (last_id == previous).astype(jnp.float32)
        base_memory = keeping * memory
        base_norm = keeping * normer
        key_denom = 1.0 + jnp.einsum('lhe,he->lh', key_pos, base_norm, precision=HIGH)
        before = jnp.einsum('lhe,hef->lhf', key_pos, base_memory, precision=HIGH)
        change = value_seg - before / key_denom[:, :, None]
        writing = key_pos * (doc_seg == last_id).astype(jnp.float32)[:, None, None]
        memory = base_memory + jnp.einsum('lhe,lhf->hef', writing, change, precision=HIGH)
        normer = base_norm + lax.optimization_barrier(jnp.sum(writing, axis=0))
        return ((memory, normer, last_id), recalled)
    initial = (jnp.zeros((head_count, feat_width, feat_width), jnp.float32), jnp.zeros((head_count, feat_width), jnp.float32), jnp.array(-1, jnp.int32))
    ignored, recalled = lax.scan(jax.checkpoint(advance), initial, (queries, keys_in, values_in, doc_rows))
    return recalled

def layer_apply(token_rows, doc_rows, weight_qkv, weight_out, weight_mlp, weight_down, norm_gains, gate_logit):
    seg_count = token_rows.shape[0]
    seg_len = token_rows.shape[1]
    head_count = gate_logit.shape[0]
    head_size = weight_qkv.shape[2] // head_count
    normed_att = low(rms_norm(token_rows, norm_gains[0]))
    projected = jnp.einsum('rld,dcj->rlcj', normed_att, low(weight_qkv), precision=HIGH)
    projected = low_back(low(projected))
    shaped = projected.reshape(seg_count, seg_len, 3, head_count, head_size)
    queries = shaped[:, :, 0]
    keys_in = shaped[:, :, 1]
    values_in = shaped[:, :, 2]
    scaling = head_size ** (-0.5)
    scores = low_back(jnp.einsum('rlhe,rmhe->rhlm', queries, keys_in, precision=HIGH) * scaling)
    position = jnp.arange(seg_len)
    allowed = (position[:, None] >= position[None, :])[None] & (doc_rows[:, :, None] == doc_rows[:, None, :])
    scores = jnp.where(allowed[:, None], scores, NEG)
    row_peak = lax.optimization_barrier(jnp.max(scores, axis=-1, keepdims=True))
    exponent = jnp.exp(scores - row_peak)
    prob_low = low(exponent / lax.optimization_barrier(jnp.sum(exponent, axis=-1, keepdims=True)))
    local_out = low_back(jnp.einsum('rhlm,rmhe->rlhe', prob_low, values_in, precision=HIGH))
    recalled = memory_read(queries, keys_in, values_in, doc_rows)
    mixing = jax.nn.sigmoid(gate_logit)[:, None]
    combined = low((mixing * recalled + (1.0 - mixing) * local_out).reshape(seg_count, seg_len, head_count * head_size))
    attended = low_back(jnp.einsum('rlj,dj->rld', combined, low(weight_out), precision=HIGH))
    hidden = token_rows + attended
    normed_mlp = low(rms_norm(hidden, norm_gains[1]))
    gate_up = low_back(jnp.einsum('rld,dcf->rlcf', normed_mlp, low(weight_mlp), precision=HIGH))
    active = low(jax.nn.gelu(gate_up[:, :, 0]) * gate_up[:, :, 1])
    mlp_out = low_back(jnp.einsum('rlf,df->rld', active, low(weight_down), precision=HIGH))
    return hidden + mlp_out

def adam_update(weight, moment, second, gradient, factor, step_rate, decay):
    clipped = gradient * factor
    moment = BETA1 * moment + (1.0 - BETA1) * clipped
    second = BETA2 * second + (1.0 - BETA2) * clipped * clipped
    fixed_first = moment / (1.0 - BETA1 ** STEP_COUNT)
    fixed_second = second / (1.0 - BETA2 ** STEP_COUNT)
    updated = weight - step_rate * (fixed_first / (jnp.sqrt(fixed_second) + ADAM_EPS) + decay * weight)
    return (moment, second, updated)

def reference(inputs, doc_ids, cotangent, weight_qkv, moment_qkv, second_qkv, weight_out, moment_out, second_out, weight_mlp, moment_mlp, second_mlp, weight_down, moment_down, second_down, norm_gains, moment_gains, second_gains, gate_logit, moment_gate, second_gate):
    seq_count = MICRO * SEQS
    rows_all = inputs.astype(jnp.float32).reshape(seq_count, SEGS, SEG, D)
    ids_all = doc_ids.reshape(seq_count, SEGS, SEG)
    back_all = cotangent.astype(jnp.float32).reshape(seq_count, SEGS, SEG, D)
    params = (weight_qkv, weight_out, weight_mlp, weight_down, norm_gains, gate_logit)

    def per_sequence(totals, segment):
        token_rows, doc_rows, back_rows = segment

        def apply_one(rows_in, w_a, w_b, w_c, w_d, w_e, w_f):
            return layer_apply(rows_in, doc_rows, w_a, w_b, w_c, w_d, w_e, w_f)
        result, pullback = jax.vjp(apply_one, token_rows, weight_qkv, weight_out, weight_mlp, weight_down, norm_gains, gate_logit)
        grad_list = pullback(back_rows)
        totals = tuple((t + g for t, g in zip(totals, grad_list[1:])))
        return (totals, (result.astype(jnp.bfloat16), grad_list[0].astype(jnp.bfloat16)))
    zeros_init = tuple((jnp.zeros_like(p) for p in params))
    totals, outputs = lax.scan(per_sequence, zeros_init, (rows_all, ids_all, back_all))
    block_out = outputs[0].reshape(MICRO, SEQS, SEGS, SEG, D)
    input_grad = outputs[1].reshape(MICRO, SEQS, SEGS, SEG, D)
    squares = jnp.float32(0.0)
    for gradient in totals:
        squares = squares + jnp.sum(gradient * gradient)
    grad_norm = jnp.sqrt(squares)
    factor = jnp.minimum(1.0, CLIP / (grad_norm + 1e-06))
    rates = (D ** (-0.5), 4.0 * (HEADS * HEAD_DIM) ** (-0.5), D ** (-0.5), FF ** (-0.5), 0.5, 1.0)
    decays = (DECAY, DECAY, DECAY, DECAY, 0.0, 0.0)
    moments = (moment_qkv, moment_out, moment_mlp, moment_down, moment_gains, moment_gate)
    seconds = (second_qkv, second_out, second_mlp, second_down, second_gains, second_gate)
    results = []
    for number in range(6):
        results.extend(adam_update(params[number], moments[number], seconds[number], totals[number], factor, rates[number], decays[number]))
    return (block_out, input_grad, grad_norm, results[0], results[1], results[2], results[3], results[4], results[5], results[6], results[7], results[8], results[9], results[10], results[11], results[12], results[13], results[14], results[15], results[16], results[17])
```

```python
import functools

import jax
import jax.numpy as jnp
from jax import lax
from jax.experimental import pallas as pl
from jax.experimental.pallas import tpu as pltpu
from jax.sharding import Mesh
from jax.sharding import PartitionSpec as P

D = 2048
HEADS = 16
HEAD_DIM = 128
FF = 8192
STEP_COUNT = 10
CHUNKS = 2

EPS = 1e-06
NEG = -1e30
CLIP = 1.0
BETA1 = 0.9
BETA2 = 0.95
ADAM_EPS = 1e-08
DECAY = 0.1
BF = jnp.bfloat16
F32 = jnp.float32
SCALING = HEAD_DIM ** (-0.5)
VMEM_LIMIT = 48 * 1024 * 1024


def rms_norm(tensor, scaling):
    return tensor * lax.rsqrt(jnp.mean(tensor * tensor, axis=-1, keepdims=True) + EPS) * scaling


def adam_update(weight, moment, second, gradient, factor, step_rate, decay):
    clipped = gradient * factor
    moment = BETA1 * moment + (1.0 - BETA1) * clipped
    second = BETA2 * second + (1.0 - BETA2) * clipped * clipped
    fixed_first = moment / (1.0 - BETA1**STEP_COUNT)
    fixed_second = second / (1.0 - BETA2**STEP_COUNT)
    updated = weight - step_rate * (
        fixed_first / (jnp.sqrt(fixed_second) + ADAM_EPS) + decay * weight
    )
    return (moment, second, updated)


def swap(tensor, axis):
    return lax.ppermute(tensor, axis, [(0, 1), (1, 0)])


def gather_tokens(own, outer, inner):
    by_inner = swap(own, inner)
    by_outer = swap(own, outer)
    by_both = swap(by_inner, outer)
    pieces = [own, by_inner, by_outer, by_both]
    pieces = pieces + [swap(p, "c") for p in pieces]
    return jnp.concatenate([p[None] for p in pieces], axis=0)


def scatter_tokens(partial, outer, inner):
    half = partial[:4].astype(F32) + swap(partial[4:], "c").astype(F32)
    low = half.astype(BF)
    half = half[:2] + swap(low[2:], outer).astype(F32)
    low = half.astype(BF)
    return half[0] + swap(low[1], inner).astype(F32)


def mm(a, b, dims):
    return lax.dot_general(a, b, (dims, ((), ())), preferred_element_type=F32)


NN = ((1,), (0,))
NT = ((1,), (1,))
TN = ((0,), (0,))


def mm_mem(a, b, dims):
    return mm(a.astype(BF), b.astype(BF), dims)


def elu_one(tensor):
    return jnp.where(tensor > 0, tensor + 1.0, jnp.exp(jnp.minimum(tensor, 0.0)))


def elu_slope(tensor):
    low = jnp.where(tensor == 0, 0.5, jnp.exp(jnp.minimum(tensor, 0.0)))
    return jnp.where(tensor > 0, 1.0, low)


def segment_of(ref, r, part):
    block = ref[:, :, r, :, part * HEAD_DIM : (part + 1) * HEAD_DIM]
    return block.reshape(-1, HEAD_DIM)


def memory_forward(qs, ks, vs, cols):
    seg_count = len(qs)
    saved = []
    memory = normer = None
    for r in range(seg_count):
        reading, writing, keep = cols[r]
        sq = elu_one(qs[r].astype(F32))
        sk = elu_one(ks[r].astype(F32))
        value = vs[r].astype(F32)
        rows = sq.shape[0]
        item = dict(sq=sq, sk=sk)
        if r == 0:
            item["recalled"] = jnp.zeros_like(sq)
            change = value
        else:
            both = mm_mem(jnp.concatenate([sq, sk], axis=0), memory, NN)
            num = both[:rows]
            den = 1.0 + jnp.sum(sq * normer, axis=-1, keepdims=True)
            item["recalled"] = reading * num / den
            before = keep * both[rows:]
            kden = 1.0 + keep * jnp.sum(sk * normer, axis=-1, keepdims=True)
            change = value - before / kden
            item.update(num=num, den=den, before=before, kden=kden, memory=memory, normer=normer)
        item["change"] = change
        if r < seg_count - 1:
            write = sk * writing
            fresh = mm_mem(write, change, TN)
            fresh_norm = jnp.sum(write, axis=0, keepdims=True)
            memory = fresh if r == 0 else keep * memory + fresh
            normer = fresh_norm if r == 0 else keep[:1] * normer + fresh_norm
        saved.append(item)
    return saved


def local_probs(query, key, allowed):
    scores = jnp.where(allowed > 0, mm(query, key, NT) * SCALING, NEG)
    exponent = jnp.exp(scores - jnp.max(scores, axis=-1, keepdims=True))
    return exponent / jnp.sum(exponent, axis=-1, keepdims=True)


def columns_of(cols_ref, r):
    cols = cols_ref[r]
    return cols[:, 0:1], cols[:, 1:2], cols[:, 2:3]


def attention_fwd_kernel(heads, proj_ref, mask_ref, cols_ref, gate_ref, out_ref):
    seg_count = mask_ref.shape[0]
    cols = [columns_of(cols_ref, r) for r in range(seg_count)]
    for h in range(heads):
        qs = [segment_of(proj_ref, r, h) for r in range(seg_count)]
        ks = [segment_of(proj_ref, r, heads + h) for r in range(seg_count)]
        vs = [segment_of(proj_ref, r, 2 * heads + h) for r in range(seg_count)]
        saved = memory_forward(qs, ks, vs, cols)
        mixing = gate_ref[h : h + 1]
        for r in range(seg_count):
            prob_low = local_probs(qs[r], ks[r], mask_ref[r]).astype(BF)
            local_out = mm(prob_low, vs[r], NN)
            combined = mixing * saved[r]["recalled"] + (1.0 - mixing) * local_out
            out_ref[:, :, r, :, h * HEAD_DIM : (h + 1) * HEAD_DIM] = combined.astype(BF).reshape(
                out_ref.shape[0], out_ref.shape[1], out_ref.shape[3], HEAD_DIM
            )


def attention_bwd_kernel(
    heads, proj_ref, grad_ref, mask_ref, cols_ref, gate_ref, out_ref, gate_out_ref
):
    seg_count = mask_ref.shape[0]
    cols = [columns_of(cols_ref, r) for r in range(seg_count)]

    def put(r, part, value):
        out_ref[:, :, r, :, part * HEAD_DIM : (part + 1) * HEAD_DIM] = value.astype(BF).reshape(
            out_ref.shape[0], out_ref.shape[1], out_ref.shape[3], HEAD_DIM
        )

    for h in range(heads):
        qs = [segment_of(proj_ref, r, h) for r in range(seg_count)]
        ks = [segment_of(proj_ref, r, heads + h) for r in range(seg_count)]
        vs = [segment_of(proj_ref, r, 2 * heads + h) for r in range(seg_count)]
        saved = memory_forward(qs, ks, vs, cols)
        mixing = gate_ref[h : h + 1]
        gate_sum = jnp.zeros((1, HEAD_DIM), F32)
        d_memory = d_normer = None
        for r in reversed(range(seg_count)):
            reading, writing, keep = cols[r]
            item = saved[r]
            sq, sk = item["sq"], item["sk"]
            rows = sq.shape[0]
            d_combined = segment_of(grad_ref, r, h).astype(F32)
            d_recalled = mixing * d_combined
            d_local = ((1.0 - mixing) * d_combined).astype(BF)
            probs = local_probs(qs[r], ks[r], mask_ref[r])
            prob_low = probs.astype(BF)
            local_out = mm(prob_low, vs[r], NN)
            gate_sum = gate_sum + jnp.sum(
                d_combined * (item["recalled"] - local_out), axis=0, keepdims=True
            )
            d_prob = mm(d_local, vs[r], NT)
            d_value = mm(prob_low, d_local, TN)
            d_scores = (
                probs * (d_prob - jnp.sum(d_prob * probs, axis=-1, keepdims=True))
            ).astype(BF)
            d_query = mm(d_scores, ks[r], NN) * SCALING
            d_key = mm(d_scores, qs[r], TN) * SCALING
            d_sk = None
            d_before = d_kden = None
            if r < seg_count - 1:
                d_change = writing * mm_mem(sk, d_memory, NN)
                d_sk = writing * (mm_mem(item["change"], d_memory, NT) + d_normer)
                d_value = d_value + d_change
                if r > 0:
                    d_before = keep * (-d_change / item["kden"])
                    d_kden = keep * (
                        jnp.sum(d_change * item["before"], axis=-1, keepdims=True)
                        / (item["kden"] * item["kden"])
                    )
            if r > 0:
                d_num = reading * d_recalled / item["den"]
                d_den = -reading * (
                    jnp.sum(d_recalled * item["num"], axis=-1, keepdims=True)
                    / (item["den"] * item["den"])
                )
                if d_before is None:
                    d_sq = mm_mem(d_num, item["memory"], NT) + d_den * item["normer"]
                    new_memory = mm_mem(sq, d_num, TN)
                    new_normer = jnp.sum(sq * d_den, axis=0, keepdims=True)
                else:
                    stacked = jnp.concatenate([d_num, d_before], axis=0)
                    both = mm_mem(stacked, item["memory"], NT)
                    d_sq = both[:rows] + d_den * item["normer"]
                    d_sk = d_sk + both[rows:] + d_kden * item["normer"]
                    new_memory = keep * d_memory + mm_mem(
                        jnp.concatenate([sq, sk], axis=0), stacked, TN
                    )
                    new_normer = keep[:1] * d_normer + jnp.sum(
                        sq * d_den + sk * d_kden, axis=0, keepdims=True
                    )
                d_memory, d_normer = new_memory, new_normer
                d_query = d_query + d_sq * elu_slope(qs[r].astype(F32))
            if d_sk is not None:
                d_key = d_key + d_sk * elu_slope(ks[r].astype(F32))
            put(r, h, d_query)
            put(r, heads + h, d_key)
            put(r, 2 * heads + h, d_value)
        gate_out_ref[h : h + 1] = gate_sum


def block_spec(shape, where):
    dims = list(shape)
    dims[where] = None

    def index(s):
        place = [0] * len(dims)
        place[where] = s
        return tuple(place)

    return pl.BlockSpec(tuple(dims), index)


def attention_fwd(projected, mask, cols, gate_rows, where):
    heads = gate_rows.shape[0]
    out_shape = projected.shape[:-1] + (heads * HEAD_DIM,)
    return pl.pallas_call(
        functools.partial(attention_fwd_kernel, heads),
        grid=(projected.shape[where],),
        in_specs=[
            block_spec(projected.shape, where),
            pl.BlockSpec((None,) + mask.shape[1:], lambda s: (s, 0, 0, 0)),
            pl.BlockSpec((None,) + cols.shape[1:], lambda s: (s, 0, 0, 0)),
            pl.BlockSpec(gate_rows.shape, lambda s: (0, 0)),
        ],
        out_specs=block_spec(out_shape, where),
        out_shape=jax.ShapeDtypeStruct(out_shape, BF),
        compiler_params=pltpu.CompilerParams(vmem_limit_bytes=VMEM_LIMIT),
        cost_estimate=pl.CostEstimate(
            flops=400_000_000 * 50, bytes_accessed=6_000_000, transcendentals=0
        ),
        name="attention_forward",
    )(projected, mask, cols, gate_rows)


def attention_bwd(projected, d_combined, mask, cols, gate_rows, where):
    heads = gate_rows.shape[0]
    seqs = projected.shape[where]
    return pl.pallas_call(
        functools.partial(attention_bwd_kernel, heads),
        grid=(seqs,),
        in_specs=[
            block_spec(projected.shape, where),
            block_spec(d_combined.shape, where),
            pl.BlockSpec((None,) + mask.shape[1:], lambda s: (s, 0, 0, 0)),
            pl.BlockSpec((None,) + cols.shape[1:], lambda s: (s, 0, 0, 0)),
            pl.BlockSpec(gate_rows.shape, lambda s: (0, 0)),
        ],
        out_specs=[
            block_spec(projected.shape, where),
            pl.BlockSpec((None, heads, HEAD_DIM), lambda s: (s, 0, 0)),
        ],
        out_shape=[
            jax.ShapeDtypeStruct(projected.shape, BF),
            jax.ShapeDtypeStruct((seqs, heads, HEAD_DIM), F32),
        ],
        compiler_params=pltpu.CompilerParams(vmem_limit_bytes=VMEM_LIMIT),
        cost_estimate=pl.CostEstimate(
            flops=1_000_000_000 * 50, bytes_accessed=10_000_000, transcendentals=0
        ),
        name="attention_backward",
    )(projected, d_combined, mask, cols, gate_rows)


GELU_A = 0.7978845608028654
GELU_B = 0.044715


def ff_kernel(width, x_ref, g_ref, w_ref, act_ref, grad_ref):
    weights = w_ref[...]
    gate_up = mm(x_ref[...], weights[:, : 2 * width], NN)
    d_active = mm(g_ref[...], weights[:, 2 * width :], NN)
    gate = gate_up[:, :width]
    up = gate_up[:, width:]
    square = gate * gate
    tanh = jnp.tanh(GELU_A * gate * (1.0 + GELU_B * square))
    half = 0.5 * (1.0 + tanh)
    gelu = gate * half
    slope = half + 0.5 * gate * (1.0 - tanh * tanh) * GELU_A * (1.0 + 3.0 * GELU_B * square)
    act_ref[...] = (gelu * up).astype(BF)
    grad_ref[:, :width] = (d_active * up * slope).astype(BF)
    grad_ref[:, width:] = (d_active * gelu).astype(BF)


def feed_forward(rows, grads, weights):
    tokens = rows.shape[0]
    width = weights.shape[1] // 3
    tile = 256
    return pl.pallas_call(
        functools.partial(ff_kernel, width),
        grid=(tokens // tile,),
        in_specs=[
            pl.BlockSpec((tile, D), lambda i: (i, 0)),
            pl.BlockSpec((tile, D), lambda i: (i, 0)),
            pl.BlockSpec(weights.shape, lambda i: (0, 0)),
        ],
        out_specs=[
            pl.BlockSpec((tile, width), lambda i: (i, 0)),
            pl.BlockSpec((tile, 2 * width), lambda i: (i, 0)),
        ],
        out_shape=[
            jax.ShapeDtypeStruct((tokens, width), BF),
            jax.ShapeDtypeStruct((tokens, 2 * width), BF),
        ],
        compiler_params=pltpu.CompilerParams(vmem_limit_bytes=VMEM_LIMIT),
        cost_estimate=pl.CostEstimate(
            flops=2 * tokens * D * 3 * width,
            bytes_accessed=2 * (2 * tokens * D + 3 * D * width + 3 * tokens * width),
            transcendentals=tokens * width,
        ),
        name="feed_forward",
    )(rows, grads, weights)


def on_device(
    inputs,
    doc_ids,
    cotangent,
    weight_qkv,
    moment_qkv,
    second_qkv,
    weight_out,
    moment_out,
    second_out,
    weight_mlp,
    moment_mlp,
    second_mlp,
    weight_down,
    moment_down,
    second_down,
    norm_gains,
    moment_gains,
    second_gains,
    gate_logit,
    moment_gate,
    second_gate,
):
    micro_count, _, seg_count, own_len, _ = inputs.shape
    own_tokens = seg_count * own_len
    x_place = lax.axis_index("x")
    y_place = lax.axis_index("y")
    c_place = lax.axis_index("c")
    is_low = x_place == 0
    orders = [("x", "y") if m % 2 == 0 else ("y", "x") for m in range(micro_count)]

    def half_columns(weight, which):
        width = weight.shape[-1] // 2
        return lax.dynamic_slice_in_dim(weight, which * width, width, axis=weight.ndim - 1)

    def by_place(own, other, axis):
        return jnp.where(
            is_low,
            jnp.concatenate([own, other], axis=axis),
            jnp.concatenate([other, own], axis=axis),
        )

    def exchange_weight(weight):
        low = weight.astype(BF)
        mine = half_columns(low, x_place)
        theirs = swap(half_columns(low, 1 - x_place), "x")
        return by_place(mine, theirs, 0)

    def fetch(block):
        return lax.all_gather(block, "z", axis=0, tiled=True)

    shard_qkv = exchange_weight(weight_qkv)
    heads = shard_qkv.shape[2] // HEAD_DIM
    width_att = shard_qkv.shape[2]
    full_qkv = fetch(shard_qkv.reshape(-1, 3 * width_att))
    full_out = fetch(exchange_weight(weight_out))
    shard_mlp = exchange_weight(weight_mlp)
    shard_down = exchange_weight(weight_down)
    width_ff = shard_down.shape[1]
    width = width_ff // CHUNKS
    full_ff = []
    for k in range(CHUNKS):
        part = slice(k * width, (k + 1) * width)
        full_ff.append(
            fetch(
                jnp.concatenate(
                    [shard_mlp[:, 0, part], shard_mlp[:, 1, part], shard_down[:, part]], axis=1
                )
            )
        )

    head_start = (y_place * 2 + c_place) * (2 * heads) + x_place * heads
    gate_local = lax.dynamic_slice_in_dim(gate_logit, head_start, heads)
    mixing = jax.nn.sigmoid(gate_local)
    gate_rows = jnp.broadcast_to(mixing[:, None], (heads, HEAD_DIM))

    token_rows = [
        inputs[m, 0].reshape(own_tokens, D).astype(F32) for m in range(micro_count)
    ]
    back_low = [cotangent[m, 0].reshape(own_tokens, D) for m in range(micro_count)]

    normed_att = [rms_norm(t, norm_gains[0]).astype(BF) for t in token_rows]
    att_rows = [
        gather_tokens(normed_att[m], *orders[m]).reshape(8 * own_tokens, D)
        for m in range(micro_count)
    ]
    gathered_ids = [gather_tokens(doc_ids[m, 0], *orders[m]) for m in range(micro_count)]
    all_back = jnp.concatenate(
        [gather_tokens(back_low[m], *orders[m]).reshape(8 * own_tokens, D) for m in range(micro_count)],
        axis=0,
    )

    rel_c = jnp.arange(2)[:, None, None] ^ c_place
    rel_y = jnp.arange(2)[None, :, None] ^ y_place
    places = ((rel_y * 2 + rel_c) * own_len + jnp.arange(own_len)).reshape(-1)
    causal = places[:, None] >= places[None, :]
    masks = []
    columns = []
    for m in range(micro_count):
        ids = gathered_ids[m].reshape(2, 2, 2, seg_count, own_len)
        where = 1 if orders[m][0] == "x" else 2
        ids = jnp.moveaxis(ids, where, 0)
        ids = jnp.moveaxis(ids, 3, 1).reshape(2, seg_count, -1)
        same = ids[:, :, :, None] == ids[:, :, None, :]
        masks.append((same & causal).astype(F32))
        last = jnp.max(ids, axis=2)
        previous = jnp.concatenate([jnp.full((2, 1), -1, last.dtype), last[:, :-1]], axis=1)
        reading = ids == previous[:, :, None]
        writing = ids == last[:, :, None]
        keep = jnp.broadcast_to((last == previous)[:, :, None], ids.shape)
        columns.append(jnp.stack([reading, writing, keep], axis=-1).astype(F32))

    slots = (2, 2, 2, seg_count, own_len)
    projected = []
    combined = []
    hidden = []
    normed_mlp = []
    for m in range(micro_count):
        where = 1 if orders[m][0] == "x" else 2
        proj = mm(att_rows[m], full_qkv, NN).astype(BF)
        projected.append(proj.reshape(slots + (3 * width_att,)))
        comb = attention_fwd(projected[m], masks[m], columns[m], gate_rows, where)
        combined.append(comb.reshape(8 * own_tokens, width_att))
        partial = mm(combined[m], full_out, NT).astype(BF)
        attended = scatter_tokens(partial.reshape(8, own_tokens, D), *orders[m])
        hidden.append(token_rows[m] + attended)
        normed_mlp.append(rms_norm(hidden[m], norm_gains[1]).astype(BF))
    mlp_rows = jnp.concatenate(
        [
            gather_tokens(normed_mlp[m], *orders[m]).reshape(8 * own_tokens, D)
            for m in range(micro_count)
        ],
        axis=0,
    )

    def reduce_rows(partial):
        return lax.psum_scatter(partial, "z", scatter_dimension=0, tiled=True)

    active = []
    d_gate_up = []
    own_ff = []
    for k in range(CHUNKS):
        act, grad = feed_forward(mlp_rows, all_back, full_ff[k])
        active.append(act)
        d_gate_up.append(grad)
        grad_ff = jnp.concatenate(
            [mm(mlp_rows, grad, TN).astype(BF), mm(all_back, act, TN).astype(BF)], axis=1
        )
        own_ff.append(reduce_rows(grad_ff))
    d_partial = sum(mm(d_gate_up[k], full_ff[k][:, : 2 * width], NT) for k in range(CHUNKS)).astype(BF)
    out_partial = sum(mm(active[k], full_ff[k][:, 2 * width :], NT) for k in range(CHUNKS)).astype(BF)
    d_partial = d_partial.reshape(micro_count, 8, own_tokens, D)
    out_partial = out_partial.reshape(micro_count, 8, own_tokens, D)

    gain_grad_att = jnp.zeros((D,), F32)
    gain_grad_mlp = jnp.zeros((D,), F32)
    d_hidden = []
    for m in range(micro_count):
        d_normed = scatter_tokens(d_partial[m], *orders[m])
        ignored, norm_back = jax.vjp(rms_norm, hidden[m], norm_gains[1])
        d_norm, d_gain = norm_back(d_normed)
        gain_grad_mlp = gain_grad_mlp + d_gain
        d_hidden.append(back_low[m].astype(F32) + d_norm)

    gate_sum = jnp.zeros((heads,), F32)
    grad_qkv = jnp.zeros((D, 3 * width_att), F32)
    grad_out = jnp.zeros((D, width_att), F32)
    grad_rows = []
    for m in range(micro_count):
        where = 1 if orders[m][0] == "x" else 2
        att_grads = gather_tokens(d_hidden[m].astype(BF), *orders[m]).reshape(8 * own_tokens, D)
        d_combined = mm(att_grads, full_out, NN)
        grad_out = grad_out + mm(att_grads, combined[m], TN)
        d_proj, gate_part = attention_bwd(
            projected[m],
            d_combined.reshape(slots + (width_att,)),
            masks[m],
            columns[m],
            gate_rows,
            where,
        )
        gate_sum = gate_sum + jnp.sum(gate_part, axis=(0, 2))
        d_proj = d_proj.reshape(8 * own_tokens, 3 * width_att)
        grad_qkv = grad_qkv + mm(att_rows[m], d_proj, TN)
        partial = mm(d_proj, full_qkv, NT).astype(BF).reshape(8, own_tokens, D)
        d_normed = scatter_tokens(partial, *orders[m])
        ignored, norm_first = jax.vjp(rms_norm, token_rows[m], norm_gains[0])
        d_norm, d_gain = norm_first(d_normed)
        gain_grad_att = gain_grad_att + d_gain
        grad_rows.append((d_hidden[m] + d_norm).astype(BF))
    own_out = reduce_rows(grad_out.astype(BF))
    own_qkv = reduce_rows(grad_qkv.astype(BF))

    block_out = []
    for m in range(micro_count):
        mlp_out = scatter_tokens(out_partial[m], *orders[m])
        block_out.append((hidden[m] + mlp_out).astype(BF))

    def exchange_grad(grad):
        rows = grad.shape[0] // 2
        mine = lax.dynamic_slice_in_dim(grad, x_place * rows, rows, axis=0)
        theirs = swap(lax.dynamic_slice_in_dim(grad, (1 - x_place) * rows, rows, axis=0), "x")
        return mine, theirs

    def join(mine, theirs):
        return by_place(mine, theirs, mine.ndim - 1).astype(F32)

    parts = [exchange_grad(g) for g in own_ff]
    rows = weight_qkv.shape[0]
    sides = []
    for side in range(2):
        stacked = jnp.stack([p[side].reshape(rows, 3, width) for p in parts], axis=2)
        sides.append(stacked.reshape(rows, 3, width_ff))
    ff_grad = join(*sides)
    own_mlp, own_down = ff_grad[:, :2], ff_grad[:, 2]
    own_out = join(*exchange_grad(own_out))
    mine, theirs = exchange_grad(own_qkv)
    own_qkv = join(mine.reshape(rows, 3, width_att), theirs.reshape(rows, 3, width_att))

    gate_grad = gate_sum * mixing * (1.0 - mixing)
    gate_padded = lax.dynamic_update_slice(
        jnp.zeros(gate_logit.shape, F32), gate_grad, (head_start,)
    )
    owned = (
        jnp.sum(own_qkv * own_qkv)
        + jnp.sum(own_out * own_out)
        + jnp.sum(own_mlp * own_mlp)
        + jnp.sum(own_down * own_down)
    )
    everywhere = ("z", "x", "y", "c")
    gain_grad = jnp.stack([gain_grad_att, gain_grad_mlp], axis=0)
    gains_total, gate_total, owned_total = lax.psum((gain_grad, gate_padded, owned), everywhere)
    squares = owned_total + jnp.sum(gains_total * gains_total) + jnp.sum(gate_total * gate_total)
    grad_norm = jnp.sqrt(squares)
    factor = jnp.minimum(1.0, CLIP / (grad_norm + 1e-06))
    qkv_new = adam_update(weight_qkv, moment_qkv, second_qkv, own_qkv, factor, D ** (-0.5), DECAY)
    out_new = adam_update(
        weight_out, moment_out, second_out, own_out, factor, 4.0 * (HEADS * HEAD_DIM) ** (-0.5), DECAY
    )
    mlp_new = adam_update(weight_mlp, moment_mlp, second_mlp, own_mlp, factor, D ** (-0.5), DECAY)
    down_new = adam_update(
        weight_down, moment_down, second_down, own_down, factor, FF ** (-0.5), DECAY
    )
    gains_new = adam_update(norm_gains, moment_gains, second_gains, gains_total, factor, 0.5, 0.0)
    gate_new = adam_update(gate_logit, moment_gate, second_gate, gate_total, factor, 1.0, 0.0)
    shape = (micro_count, 1, seg_count, own_len, D)
    return (
        jnp.stack(block_out, axis=0).reshape(shape),
        jnp.stack(grad_rows, axis=0).reshape(shape),
        grad_norm,
        *qkv_new,
        *out_new,
        *mlp_new,
        *down_new,
        *gains_new,
        *gate_new,
    )


def solution(mesh):
    seq_count, ctx_count = mesh.devices.shape
    inner = Mesh(
        mesh.devices.reshape(seq_count // 2, 2, ctx_count // 2, 2), ("z", "x", "y", "c")
    )
    seq, ctx = ("z", "x"), ("y", "c")
    rows = P(None, seq, None, ctx, None)
    wide = P(seq, None, ctx)
    flat = P(seq, ctx)
    weights = (wide,) * 3 + (flat,) * 3 + (wide,) * 3 + (flat,) * 3 + (P(),) * 6
    return jax.shard_map(
        on_device,
        mesh=inner,
        in_specs=(rows, P(None, seq, None, ctx), rows) + weights,
        out_specs=(rows, rows, P()) + weights,
        check_vma=False,
    )
```

```python
import functools

import jax
import jax.numpy as jnp
from jax import lax
from jax.experimental import pallas as pl
from jax.experimental.pallas import tpu as pltpu
from jax.sharding import Mesh
from jax.sharding import PartitionSpec as P

D = 2048
HEADS = 16
HEAD_DIM = 128
FF = 8192
STEP_COUNT = 10
CHUNKS = 2

EPS = 1e-06
NEG = -1e30
CLIP = 1.0
BETA1 = 0.9
BETA2 = 0.95
ADAM_EPS = 1e-08
DECAY = 0.1
BF = jnp.bfloat16
F32 = jnp.float32
SCALING = HEAD_DIM ** (-0.5)
VMEM_LIMIT = 48 * 1024 * 1024


def rms_norm(tensor, scaling):
    return tensor * lax.rsqrt(jnp.mean(tensor * tensor, axis=-1, keepdims=True) + EPS) * scaling


def adam_update(weight, moment, second, gradient, factor, step_rate, decay):
    clipped = gradient * factor
    moment = BETA1 * moment + (1.0 - BETA1) * clipped
    second = BETA2 * second + (1.0 - BETA2) * clipped * clipped
    fixed_first = moment / (1.0 - BETA1**STEP_COUNT)
    fixed_second = second / (1.0 - BETA2**STEP_COUNT)
    updated = weight - step_rate * (
        fixed_first / (jnp.sqrt(fixed_second) + ADAM_EPS) + decay * weight
    )
    return (moment, second, updated)


def swap(tensor, axis):
    return lax.ppermute(tensor, axis, [(0, 1), (1, 0)])


def tie(tensor, *earlier):
    return lax.optimization_barrier((tensor,) + earlier)[0]


def gather_tokens(own, outer, inner):
    by_inner = swap(own, inner)
    by_outer = swap(own, outer)
    by_both = swap(by_inner, outer)
    mine = jnp.concatenate([own, by_inner, by_outer, by_both], axis=0)
    return mine, swap(mine, "c")


def scatter_tokens(partial, outer, inner, *earlier):
    half = partial[:4].astype(F32) + swap(partial[4:], "c").astype(F32)
    low = half.astype(BF)
    half = half[:2] + swap(low[2:], outer).astype(F32)
    low = tie(half[1].astype(BF), *earlier)
    return half[0] + swap(low, inner).astype(F32)


def sum_everywhere(tensor, z_count, beside):
    reach = 1
    while reach < z_count:
        tensor = tensor + lax.ppermute(tensor, "z", [(i, i ^ reach) for i in range(z_count)])
        reach *= 2
    tensor = tie(tensor + swap(tensor, "c"), beside)
    for axis in ("y", "x"):
        tensor = tensor + swap(tensor, axis)
    return tensor


def mm(a, b, dims):
    return lax.dot_general(a, b, (dims, ((), ())), preferred_element_type=F32)


NN = ((1,), (0,))
NT = ((1,), (1,))
TN = ((0,), (0,))


def mm_mem(a, b, dims):
    return mm(a.astype(BF), b.astype(BF), dims)


def elu_one(tensor):
    return jnp.where(tensor > 0, tensor + 1.0, jnp.exp(jnp.minimum(tensor, 0.0)))


def elu_slope(tensor):
    low = jnp.where(tensor == 0, 0.5, jnp.exp(jnp.minimum(tensor, 0.0)))
    return jnp.where(tensor > 0, 1.0, low)


def segment_of(ref, r, part):
    block = ref[:, :, r, :, part * HEAD_DIM : (part + 1) * HEAD_DIM]
    return block.reshape(-1, HEAD_DIM)


def memory_forward(qs, ks, vs, cols):
    seg_count = len(qs)
    saved = []
    memory = normer = None
    for r in range(seg_count):
        reading, writing, keep = cols[r]
        sq = elu_one(qs[r].astype(F32))
        sk = elu_one(ks[r].astype(F32))
        value = vs[r].astype(F32)
        rows = sq.shape[0]
        item = dict(sq=sq, sk=sk)
        if r == 0:
            item["recalled"] = jnp.zeros_like(sq)
            change = value
        else:
            both = mm_mem(jnp.concatenate([sq, sk], axis=0), memory, NN)
            num = both[:rows]
            den = 1.0 + jnp.sum(sq * normer, axis=-1, keepdims=True)
            item["recalled"] = reading * num / den
            before = keep * both[rows:]
            kden = 1.0 + keep * jnp.sum(sk * normer, axis=-1, keepdims=True)
            change = value - before / kden
            item.update(num=num, den=den, before=before, kden=kden, memory=memory, normer=normer)
        item["change"] = change
        if r < seg_count - 1:
            write = sk * writing
            fresh = mm_mem(write, change, TN)
            fresh_norm = jnp.sum(write, axis=0, keepdims=True)
            memory = fresh if r == 0 else keep * memory + fresh
            normer = fresh_norm if r == 0 else keep[:1] * normer + fresh_norm
        saved.append(item)
    return saved


def local_probs(query, key, allowed):
    scores = jnp.where(allowed > 0, mm(query, key, NT) * SCALING, NEG)
    exponent = jnp.exp(scores - jnp.max(scores, axis=-1, keepdims=True))
    return exponent / jnp.sum(exponent, axis=-1, keepdims=True)


def columns_of(cols_ref, r):
    cols = cols_ref[r]
    return cols[:, 0:1], cols[:, 1:2], cols[:, 2:3]


def attention_fwd_kernel(heads, proj_ref, mask_ref, cols_ref, gate_ref, out_ref):
    seg_count = mask_ref.shape[0]
    cols = [columns_of(cols_ref, r) for r in range(seg_count)]
    for h in range(heads):
        qs = [segment_of(proj_ref, r, h) for r in range(seg_count)]
        ks = [segment_of(proj_ref, r, heads + h) for r in range(seg_count)]
        vs = [segment_of(proj_ref, r, 2 * heads + h) for r in range(seg_count)]
        saved = memory_forward(qs, ks, vs, cols)
        mixing = gate_ref[h : h + 1]
        for r in range(seg_count):
            prob_low = local_probs(qs[r], ks[r], mask_ref[r]).astype(BF)
            local_out = mm(prob_low, vs[r], NN)
            combined = mixing * saved[r]["recalled"] + (1.0 - mixing) * local_out
            out_ref[:, :, r, :, h * HEAD_DIM : (h + 1) * HEAD_DIM] = combined.astype(BF).reshape(
                out_ref.shape[0], out_ref.shape[1], out_ref.shape[3], HEAD_DIM
            )


def attention_bwd_kernel(
    heads, proj_ref, grad_ref, mask_ref, cols_ref, gate_ref, out_ref, gate_out_ref
):
    seg_count = mask_ref.shape[0]
    cols = [columns_of(cols_ref, r) for r in range(seg_count)]

    def put(r, part, value):
        out_ref[:, :, r, :, part * HEAD_DIM : (part + 1) * HEAD_DIM] = value.astype(BF).reshape(
            out_ref.shape[0], out_ref.shape[1], out_ref.shape[3], HEAD_DIM
        )

    for h in range(heads):
        qs = [segment_of(proj_ref, r, h) for r in range(seg_count)]
        ks = [segment_of(proj_ref, r, heads + h) for r in range(seg_count)]
        vs = [segment_of(proj_ref, r, 2 * heads + h) for r in range(seg_count)]
        saved = memory_forward(qs, ks, vs, cols)
        mixing = gate_ref[h : h + 1]
        gate_sum = jnp.zeros((1, HEAD_DIM), F32)
        d_memory = d_normer = None
        for r in reversed(range(seg_count)):
            reading, writing, keep = cols[r]
            item = saved[r]
            sq, sk = item["sq"], item["sk"]
            rows = sq.shape[0]
            d_combined = segment_of(grad_ref, r, h).astype(F32)
            d_recalled = mixing * d_combined
            d_local = ((1.0 - mixing) * d_combined).astype(BF)
            probs = local_probs(qs[r], ks[r], mask_ref[r])
            prob_low = probs.astype(BF)
            local_out = mm(prob_low, vs[r], NN)
            gate_sum = gate_sum + jnp.sum(
                d_combined * (item["recalled"] - local_out), axis=0, keepdims=True
            )
            d_prob = mm(d_local, vs[r], NT)
            d_value = mm(prob_low, d_local, TN)
            d_scores = (
                probs * (d_prob - jnp.sum(d_prob * probs, axis=-1, keepdims=True))
            ).astype(BF)
            d_query = mm(d_scores, ks[r], NN) * SCALING
            d_key = mm(d_scores, qs[r], TN) * SCALING
            d_sk = None
            d_before = d_kden = None
            if r < seg_count - 1:
                d_change = writing * mm_mem(sk, d_memory, NN)
                d_sk = writing * (mm_mem(item["change"], d_memory, NT) + d_normer)
                d_value = d_value + d_change
                if r > 0:
                    d_before = keep * (-d_change / item["kden"])
                    d_kden = keep * (
                        jnp.sum(d_change * item["before"], axis=-1, keepdims=True)
                        / (item["kden"] * item["kden"])
                    )
            if r > 0:
                d_num = reading * d_recalled / item["den"]
                d_den = -reading * (
                    jnp.sum(d_recalled * item["num"], axis=-1, keepdims=True)
                    / (item["den"] * item["den"])
                )
                if d_before is None:
                    d_sq = mm_mem(d_num, item["memory"], NT) + d_den * item["normer"]
                    new_memory = mm_mem(sq, d_num, TN)
                    new_normer = jnp.sum(sq * d_den, axis=0, keepdims=True)
                else:
                    stacked = jnp.concatenate([d_num, d_before], axis=0)
                    both = mm_mem(stacked, item["memory"], NT)
                    d_sq = both[:rows] + d_den * item["normer"]
                    d_sk = d_sk + both[rows:] + d_kden * item["normer"]
                    new_memory = keep * d_memory + mm_mem(
                        jnp.concatenate([sq, sk], axis=0), stacked, TN
                    )
                    new_normer = keep[:1] * d_normer + jnp.sum(
                        sq * d_den + sk * d_kden, axis=0, keepdims=True
                    )
                d_memory, d_normer = new_memory, new_normer
                d_query = d_query + d_sq * elu_slope(qs[r].astype(F32))
            if d_sk is not None:
                d_key = d_key + d_sk * elu_slope(ks[r].astype(F32))
            put(r, h, d_query)
            put(r, heads + h, d_key)
            put(r, 2 * heads + h, d_value)
        gate_out_ref[h : h + 1] = gate_sum


def block_spec(shape, where):
    dims = list(shape)
    dims[where] = None

    def index(s):
        place = [0] * len(dims)
        place[where] = s
        return tuple(place)

    return pl.BlockSpec(tuple(dims), index)


def attention_fwd(projected, mask, cols, gate_rows, where):
    heads = gate_rows.shape[0]
    out_shape = projected.shape[:-1] + (heads * HEAD_DIM,)
    return pl.pallas_call(
        functools.partial(attention_fwd_kernel, heads),
        grid=(projected.shape[where],),
        in_specs=[
            block_spec(projected.shape, where),
            pl.BlockSpec((None,) + mask.shape[1:], lambda s: (s, 0, 0, 0)),
            pl.BlockSpec((None,) + cols.shape[1:], lambda s: (s, 0, 0, 0)),
            pl.BlockSpec(gate_rows.shape, lambda s: (0, 0)),
        ],
        out_specs=block_spec(out_shape, where),
        out_shape=jax.ShapeDtypeStruct(out_shape, BF),
        compiler_params=pltpu.CompilerParams(vmem_limit_bytes=VMEM_LIMIT),
        cost_estimate=pl.CostEstimate(
            flops=400_000_000, bytes_accessed=3_000_000, transcendentals=0
        ),
        name="attention_forward",
    )(projected, mask, cols, gate_rows)


def attention_bwd(projected, d_combined, mask, cols, gate_rows, where):
    heads = gate_rows.shape[0]
    seqs = projected.shape[where]
    return pl.pallas_call(
        functools.partial(attention_bwd_kernel, heads),
        grid=(seqs,),
        in_specs=[
            block_spec(projected.shape, where),
            block_spec(d_combined.shape, where),
            pl.BlockSpec((None,) + mask.shape[1:], lambda s: (s, 0, 0, 0)),
            pl.BlockSpec((None,) + cols.shape[1:], lambda s: (s, 0, 0, 0)),
            pl.BlockSpec(gate_rows.shape, lambda s: (0, 0)),
        ],
        out_specs=[
            block_spec(projected.shape, where),
            pl.BlockSpec((None, heads, HEAD_DIM), lambda s: (s, 0, 0)),
        ],
        out_shape=[
            jax.ShapeDtypeStruct(projected.shape, BF),
            jax.ShapeDtypeStruct((seqs, heads, HEAD_DIM), F32),
        ],
        compiler_params=pltpu.CompilerParams(vmem_limit_bytes=VMEM_LIMIT),
        cost_estimate=pl.CostEstimate(
            flops=1_000_000_000, bytes_accessed=5_000_000, transcendentals=0
        ),
        name="attention_backward",
    )(projected, d_combined, mask, cols, gate_rows)


GELU_A = 0.7978845608028654
GELU_B = 0.044715


def ff_kernel(width, half, mine_ref, other_ref, g_ref, w_ref, act_ref, grad_ref):
    step = pl.program_id(0)

    @pl.when(step < half)
    def first():
        ff_tile(width, mine_ref, g_ref, w_ref, act_ref, grad_ref)

    @pl.when(step >= half)
    def second():
        ff_tile(width, other_ref, g_ref, w_ref, act_ref, grad_ref)


def ff_tile(width, x_ref, g_ref, w_ref, act_ref, grad_ref):
    weights = w_ref[...]
    gate_up = mm(x_ref[...], weights[:, : 2 * width], NN)
    d_active = mm(g_ref[...], weights[:, 2 * width :], NN)
    gate = gate_up[:, :width]
    up = gate_up[:, width:]
    square = gate * gate
    tanh = jnp.tanh(GELU_A * gate * (1.0 + GELU_B * square))
    half = 0.5 * (1.0 + tanh)
    gelu = gate * half
    slope = half + 0.5 * gate * (1.0 - tanh * tanh) * GELU_A * (1.0 + 3.0 * GELU_B * square)
    act_ref[...] = (gelu * up).astype(BF)
    grad_ref[:, :width] = (d_active * up * slope).astype(BF)
    grad_ref[:, width:] = (d_active * gelu).astype(BF)


def feed_forward(rows, grads, weights):
    tokens = grads.shape[0]
    width = weights.shape[1] // 3
    tile = 256
    half = tokens // (2 * tile)
    return pl.pallas_call(
        functools.partial(ff_kernel, width, half),
        grid=(tokens // tile,),
        in_specs=[
            pl.BlockSpec((tile, D), lambda i: (jnp.minimum(i, half - 1), 0)),
            pl.BlockSpec((tile, D), lambda i: (jnp.maximum(i - half, 0), 0)),
            pl.BlockSpec((tile, D), lambda i: (i, 0)),
            pl.BlockSpec(weights.shape, lambda i: (0, 0), pipeline_mode=pl.Buffered(1)),
        ],
        out_specs=[
            pl.BlockSpec((tile, width), lambda i: (i, 0)),
            pl.BlockSpec((tile, 2 * width), lambda i: (i, 0)),
        ],
        out_shape=[
            jax.ShapeDtypeStruct((tokens, width), BF),
            jax.ShapeDtypeStruct((tokens, 2 * width), BF),
        ],
        compiler_params=pltpu.CompilerParams(vmem_limit_bytes=VMEM_LIMIT),
        cost_estimate=pl.CostEstimate(
            flops=tokens * D * width, bytes_accessed=tokens * D, transcendentals=0
        ),
        name="feed_forward",
    )(*rows, grads, weights)


def grads_kernel(count, *refs):
    rows, grads, by_rows, by_grads = (refs[k * count : (k + 1) * count] for k in range(4))
    out_ref = refs[4 * count]
    split = by_rows[0].shape[1]

    def total(left, right):
        acc = None
        for a, b in zip(left, right):
            term = mm(a[...], b[...], TN)
            acc = term if acc is None else acc + term
        return acc

    out_ref[:, :split] = total(rows, by_rows).astype(BF)
    out_ref[:, split:] = total(grads, by_grads).astype(BF)


def weight_grads(rows, grads, by_rows, by_grads):
    def halves(arrays):
        parts = []
        for a in arrays:
            parts += [(a[0], 0), (a[1], 0)] if isinstance(a, tuple) else [(a, 0), (a, 1)]
        return parts

    groups = [halves(a) for a in (rows, grads, by_rows, by_grads)]
    count = len(groups[0])
    tokens = by_rows[0].shape[0] // 2
    first, second = by_rows[0].shape[1], by_grads[0].shape[1]
    tile = 512

    def tall(half):
        return pl.BlockSpec((tokens, tile), lambda i: (half, i))

    def whole(width, half):
        return pl.BlockSpec((tokens, width), lambda i: (half, 0), pipeline_mode=pl.Buffered(1))

    return pl.pallas_call(
        functools.partial(grads_kernel, count),
        grid=(D // tile,),
        in_specs=[tall(half) for _, half in groups[0] + groups[1]]
        + [whole(first, half) for _, half in groups[2]]
        + [whole(second, half) for _, half in groups[3]],
        out_specs=pl.BlockSpec((tile, first + second), lambda i: (i, 0)),
        out_shape=jax.ShapeDtypeStruct((D, first + second), BF),
        compiler_params=pltpu.CompilerParams(vmem_limit_bytes=VMEM_LIMIT),
        cost_estimate=pl.CostEstimate(
            flops=tokens * D * (first + second), bytes_accessed=tokens * D, transcendentals=0
        ),
        name="weight_grads",
    )(*[a for group in groups for a, _ in group])


RATE_QKV = D ** (-0.5)
RATE_OUT = 4.0 * (HEADS * HEAD_DIM) ** (-0.5)
RATE_DOWN = FF ** (-0.5)


def clip_factor(small):
    row = lax.broadcasted_iota(jnp.int32, small.shape, 0)
    lane = lax.broadcasted_iota(jnp.int32, small.shape, 1)
    summed = (row == small.shape[0] - 1) & (lane >= HEADS)
    squares = jnp.sum(jnp.where(summed, small, small * small), axis=(0, 1), keepdims=True)
    grad_norm = jnp.sqrt(squares)
    return grad_norm, jnp.minimum(1.0, CLIP / (grad_norm + 1e-06))


def adam_kernel(place_ref, small_ref, *refs):
    ins, grads, outs = refs[:12], refs[12:16], refs[16:]
    factor = clip_factor(small_ref[...])[1]
    is_low = place_ref[0] == 0

    def put(number, place, gradient, rate):
        weight, moment, second = (r[place] for r in ins[3 * number : 3 * number + 3])
        new = adam_update(weight, moment, second, gradient.astype(F32), factor, rate, DECAY)
        for ref, value in zip(outs[3 * number : 3 * number + 3], new):
            ref[place] = value

    mine, theirs = grads[0][...], grads[1][...]
    sides = (jnp.where(is_low, mine, theirs), jnp.where(is_low, theirs, mine))
    width = mine.shape[1] // 4
    everything = slice(None)
    for s, side in enumerate(sides):
        cols = slice(s * width, (s + 1) * width)
        for part in range(3):
            put(0, (part, everything, cols), side[:, part * width : (part + 1) * width], RATE_QKV)
        put(1, (everything, cols), side[:, 3 * width :], RATE_OUT)
    put(2, (everything, everything), grads[2][...], RATE_QKV)
    put(2 + 1, (everything, everything), grads[3][...], RATE_DOWN)


def mlp_view(t):
    rows, _, width_ff = t.shape
    return t.reshape(rows, 2, width_ff // 128, 128).transpose(0, 2, 1, 3).reshape(-1, 128)


def adam_all(small, x_place, arrays, att_mine, att_theirs, grad_mlp, grad_down):
    rows, _, width_ff = arrays[6].shape
    lanes = width_ff // 128

    def qkv_view(t):
        return jnp.transpose(t, (1, 0, 2))

    def mlp_back(t):
        return t.reshape(rows, lanes, 2, 128).transpose(0, 2, 1, 3).reshape(rows, 2, width_ff)

    views = [qkv_view(t) for t in arrays[:3]] + list(arrays[3:6])
    views += [mlp_view(t) for t in arrays[6:9]] + list(arrays[9:])
    grads = [att_mine, att_theirs, grad_mlp, grad_down]
    steps = 8

    def spec(t):
        axis = t.ndim - 2
        block = list(t.shape)
        block[axis] //= steps
        return pl.BlockSpec(tuple(block), lambda i: (0,) * axis + (i, 0))

    new = pl.pallas_call(
        adam_kernel,
        grid=(steps,),
        in_specs=[
            pl.BlockSpec(memory_space=pltpu.SMEM),
            pl.BlockSpec(small.shape, lambda i: (0, 0)),
        ]
        + [spec(t) for t in views + grads],
        out_specs=[spec(t) for t in views],
        out_shape=[jax.ShapeDtypeStruct(t.shape, F32) for t in views],
        compiler_params=pltpu.CompilerParams(vmem_limit_bytes=VMEM_LIMIT),
        cost_estimate=pl.CostEstimate(
            flops=20 * sum(t.size for t in views) // 3,
            bytes_accessed=8 * sum(t.size for t in views),
            transcendentals=0,
        ),
        name="adam",
    )(x_place[None], small, *views, *grads)
    new = list(new)
    return (
        [qkv_view(t) for t in new[:3]] + new[3:6] + [mlp_back(t) for t in new[6:9]] + new[9:]
    )


def on_device(
    inputs,
    doc_ids,
    cotangent,
    weight_qkv,
    moment_qkv,
    second_qkv,
    weight_out,
    moment_out,
    second_out,
    weight_mlp,
    moment_mlp,
    second_mlp,
    weight_down,
    moment_down,
    second_down,
    norm_gains,
    moment_gains,
    second_gains,
    gate_logit,
    moment_gate,
    second_gate,
):
    micro_count, _, seg_count, own_len, _ = inputs.shape
    own_tokens = seg_count * own_len
    x_place = lax.axis_index("x")
    y_place = lax.axis_index("y")
    c_place = lax.axis_index("c")
    is_low = x_place == 0
    orders = [("x", "y") if m % 2 == 0 else ("y", "x") for m in range(micro_count)]

    z_count = D // (2 * weight_qkv.shape[0])

    def half_columns(weight, which):
        width = weight.shape[-1] // 2
        return lax.dynamic_slice_in_dim(weight, which * width, width, axis=weight.ndim - 1)

    def by_place(own, other, axis):
        return jnp.where(
            is_low,
            jnp.concatenate([own, other], axis=axis),
            jnp.concatenate([other, own], axis=axis),
        )

    def exchange_rows(columns_for, *earlier):
        theirs = swap(tie(columns_for(1 - x_place), *earlier), "x")
        mine = columns_for(x_place)
        both = jnp.zeros((2 * rows, mine.shape[1]), BF)
        both = lax.dynamic_update_slice_in_dim(both, mine, x_place * rows, axis=0)
        return lax.dynamic_update_slice_in_dim(both, theirs, (1 - x_place) * rows, axis=0)

    def fetch(block):
        return lax.all_gather(block, "z", axis=0, tiled=True)

    rows = weight_qkv.shape[0]
    heads = weight_qkv.shape[2] // (2 * HEAD_DIM)
    width_att = heads * HEAD_DIM
    width_ff = weight_down.shape[1] // 2
    width = width_ff // CHUNKS

    def att_columns(which):
        qkv = half_columns(weight_qkv, which).astype(BF).reshape(rows, -1)
        return jnp.concatenate([qkv, half_columns(weight_out, which).astype(BF)], axis=1)

    def ff_columns(k, which):
        start = which * width_ff + k * width
        mlp = lax.dynamic_slice_in_dim(weight_mlp, start, width, axis=2).astype(BF)
        down = lax.dynamic_slice_in_dim(weight_down, start, width, axis=1).astype(BF)
        return jnp.concatenate([mlp[:, 0], mlp[:, 1], down], axis=1)

    shard_att = exchange_rows(att_columns)
    full_att = fetch(shard_att)
    full_qkv = full_att[:, : 3 * width_att]
    full_out = full_att[:, 3 * width_att :]

    head_start = (y_place * 2 + c_place) * (2 * heads) + x_place * heads
    gate_local = lax.dynamic_slice_in_dim(gate_logit, head_start, heads)
    mixing = jax.nn.sigmoid(gate_local)
    gate_rows = jnp.broadcast_to(mixing[:, None], (heads, HEAD_DIM))

    micros = range(micro_count)
    tokens = 8 * own_tokens
    token_rows = [inputs[m, 0].reshape(own_tokens, D).astype(F32) for m in micros]
    back_low = [cotangent[m, 0].reshape(own_tokens, D) for m in micros]
    normed_att = [rms_norm(t, norm_gains[0]).astype(BF) for t in token_rows]
    att_pairs = [gather_tokens(normed_att[m], *orders[m]) for m in micros]
    att_rows = [jnp.concatenate(pair, axis=0) for pair in att_pairs]
    all_ids = doc_ids[:, 0]
    for axis in ("y", "x", "c"):
        all_ids = jnp.stack([all_ids, swap(all_ids, axis)], axis=0)

    shard_ff = [exchange_rows(functools.partial(ff_columns, 0), *att_rows)]
    full_ff = [fetch(shard_ff[0])]
    back_rows = [
        jnp.concatenate(gather_tokens(tie(back_low[m], *att_rows), *orders[m]), axis=0)
        for m in micros
    ]
    for k in range(1, CHUNKS):
        shard = exchange_rows(functools.partial(ff_columns, k), shard_ff[-1])
        shard_ff.append(shard)
        full_ff.append(fetch(shard))

    rel_c = jnp.arange(2)[:, None, None] ^ c_place
    rel_y = jnp.arange(2)[None, :, None] ^ y_place
    places = ((rel_y * 2 + rel_c) * own_len + jnp.arange(own_len)).reshape(-1)
    causal = places[:, None] >= places[None, :]
    masks = []
    columns = []
    for m in micros:
        ids = jnp.transpose(all_ids[:, :, :, m], (1, 3, 0, 2, 4)).reshape(2, seg_count, -1)
        same = ids[:, :, :, None] == ids[:, :, None, :]
        masks.append((same & causal).astype(F32))
        last = jnp.max(ids, axis=2)
        previous = jnp.concatenate([jnp.full((2, 1), -1, last.dtype), last[:, :-1]], axis=1)
        reading = ids == previous[:, :, None]
        writing = ids == last[:, :, None]
        keep = jnp.broadcast_to((last == previous)[:, :, None], ids.shape)
        columns.append(jnp.stack([reading, writing, keep], axis=-1).astype(F32))

    slots = (2, 2, 2, seg_count, own_len)
    wheres = [1 if orders[m][0] == "x" else 2 for m in micros]
    projected = []
    combined = []
    hidden = []
    mlp_rows = []
    for m in micros:
        rows_in = att_rows[m] if m == 0 else tie(att_rows[m], *back_rows, *shard_ff)
        proj = mm(rows_in, full_qkv, NN).astype(BF)
        projected.append(proj.reshape(slots + (3 * width_att,)))
        comb = attention_fwd(projected[m], masks[m], columns[m], gate_rows, wheres[m])
        combined.append(comb.reshape(tokens, width_att))
        partial = mm(combined[m], full_out, NT).astype(BF)
        attended = scatter_tokens(partial.reshape(8, own_tokens, D), *orders[m])
        hidden.append(token_rows[m] + attended)
        normed_mlp = rms_norm(hidden[m], norm_gains[1]).astype(BF)
        mlp_rows.append(gather_tokens(normed_mlp, *orders[m]))

    def reduce_rows(partial):
        return lax.psum_scatter(partial, "z", scatter_dimension=0, tiled=True)

    active = []
    d_gate_up = []
    own_ff = []
    d_total = [None] * micro_count
    out_total = [None] * micro_count
    for k in range(CHUNKS):
        active.append([])
        d_gate_up.append([])
        for m in micros:
            rows_in = mlp_rows[m]
            if k == CHUNKS - 1 and m > 0:
                rows_in = (tie(rows_in[0], d_total[m - 1]), rows_in[1])
            act, grad = feed_forward(rows_in, back_rows[m], full_ff[k])
            active[k].append(act)
            d_gate_up[k].append(grad)
            d_term = mm(grad, full_ff[k][:, : 2 * width], NT)
            d_total[m] = d_term if k == 0 else d_total[m] + d_term
            if k < CHUNKS - 1:
                out_term = mm(act, full_ff[k][:, 2 * width :], NT)
                out_total[m] = out_term if k == 0 else out_total[m] + out_term
            else:
                d_total[m] = d_total[m].astype(BF)
        if k < CHUNKS - 1:
            grad_ff = weight_grads(mlp_rows, back_rows, d_gate_up[k], active[k])
            own_ff.append(reduce_rows(grad_ff))
            full_ff[k + 1] = tie(full_ff[k + 1], grad_ff, *d_total, *out_total)
    d_partial = [t.reshape(8, own_tokens, D) for t in d_total]

    gain_grad_att = jnp.zeros((D,), F32)
    gain_grad_mlp = jnp.zeros((D,), F32)
    d_hidden = []
    att_grads = []
    last_active = [tie(active[-1][m], *d_partial) for m in micros]
    grad_ff = weight_grads(mlp_rows, back_rows, d_gate_up[-1], last_active)
    for m in micros:
        d_normed = scatter_tokens(d_partial[m], *orders[m], grad_ff)
        ignored, norm_back = jax.vjp(rms_norm, hidden[m], norm_gains[1])
        d_norm, d_gain = norm_back(d_normed)
        gain_grad_mlp = gain_grad_mlp + d_gain
        d_hidden.append(back_low[m].astype(F32) + d_norm)
        d_hidden_low = d_hidden[m].astype(BF)
        att_grads.append(gather_tokens(d_hidden_low, *orders[m]))

    own_ff.append(reduce_rows(grad_ff))
    for m in micros:
        act = tie(last_active[m], d_hidden[m])
        out_total[m] = out_total[m] + mm(act, full_ff[-1][:, 2 * width :], NT)

    gate_sum = jnp.zeros((heads,), F32)
    d_projs = []
    for m in micros:
        other = att_grads[m][1] if m > 0 else tie(att_grads[m][1], own_ff[0])
        d_combined = jnp.concatenate(
            [mm(att_grads[m][0], full_out, NN), mm(other, full_out, NN)], axis=0
        )
        d_proj, gate_part = attention_bwd(
            projected[m],
            d_combined.reshape(slots + (width_att,)),
            masks[m],
            columns[m],
            gate_rows,
            wheres[m],
        )
        gate_sum = gate_sum + jnp.sum(gate_part, axis=(0, 2))
        d_projs.append(d_proj.reshape(tokens, 3 * width_att))
    grad_att = weight_grads(att_rows, att_grads, d_projs, combined)
    own_att = reduce_rows(grad_att)

    grad_rows = []
    for m in micros:
        partial = mm(tie(d_projs[m], grad_att), full_qkv, NT).astype(BF)
        d_normed = scatter_tokens(partial.reshape(8, own_tokens, D), *orders[m], own_ff[-1])
        ignored, norm_first = jax.vjp(rms_norm, token_rows[m], norm_gains[0])
        d_norm, d_gain = norm_first(d_normed)
        gain_grad_att = gain_grad_att + d_gain
        grad_rows.append((d_hidden[m] + d_norm).astype(BF))

    block_out = []
    for m in micros:
        partial = tie(out_total[m].astype(BF), *[pair[1] for pair in att_grads])
        mlp_out = scatter_tokens(partial.reshape(8, own_tokens, D), *orders[m])
        block_out.append((hidden[m] + mlp_out).astype(BF))

    def exchange_grad(grad):
        mine = lax.dynamic_slice_in_dim(grad, x_place * rows, rows, axis=0)
        theirs = swap(lax.dynamic_slice_in_dim(grad, (1 - x_place) * rows, rows, axis=0), "x")
        return mine, theirs

    def squares_of(grad):
        wide = grad.astype(F32)
        return jnp.sum(wide * wide)

    pairs = [exchange_grad(g) for g in own_ff]

    def ff_part(start, stop):
        low = jnp.concatenate([p[0][:, start * width : stop * width] for p in pairs], axis=1)
        high = jnp.concatenate([p[1][:, start * width : stop * width] for p in pairs], axis=1)
        return by_place(low, high, 1)

    grad_mlp = mlp_view(jnp.stack([ff_part(0, 1), ff_part(1, 2)], axis=1))
    grad_down = ff_part(2, 3)
    att_mine, att_theirs = exchange_grad(own_att)

    gate_grad = gate_sum * mixing * (1.0 - mixing)
    gate_padded = lax.dynamic_update_slice(
        jnp.zeros(gate_logit.shape, F32), gate_grad, (head_start,)
    )
    ff_owned = tie(sum(squares_of(g) for g in own_ff), grad_mlp, grad_down)
    owned = squares_of(own_att) + ff_owned
    small = jnp.concatenate(
        [gain_grad_att, gain_grad_mlp, gate_padded, owned[None], jnp.zeros((111,), F32)]
    ).reshape(-1, 128)
    small = sum_everywhere(small, z_count, att_theirs)
    grad_norm, factor = (t.reshape(()) for t in clip_factor(small))
    flat = small.reshape(-1)
    gains_total = flat[: 2 * D].reshape(2, D)
    gate_total = flat[2 * D : 2 * D + HEADS]
    arrays = [
        weight_qkv,
        moment_qkv,
        second_qkv,
        weight_out,
        moment_out,
        second_out,
        weight_mlp,
        moment_mlp,
        second_mlp,
        weight_down,
        moment_down,
        second_down,
    ]
    new = adam_all(small, x_place, arrays, att_mine, att_theirs, grad_mlp, grad_down)
    gains_new = adam_update(norm_gains, moment_gains, second_gains, gains_total, factor, 0.5, 0.0)
    gate_new = adam_update(gate_logit, moment_gate, second_gate, gate_total, factor, 1.0, 0.0)
    shape = (micro_count, 1, seg_count, own_len, D)
    return (
        jnp.stack(block_out, axis=0).reshape(shape),
        jnp.stack(grad_rows, axis=0).reshape(shape),
        grad_norm,
        *new,
        *gains_new,
        *gate_new,
    )


def solution(mesh):
    seq_count, ctx_count = mesh.devices.shape
    inner = Mesh(
        mesh.devices.reshape(seq_count // 2, 2, ctx_count // 2, 2), ("z", "x", "y", "c")
    )
    seq, ctx = ("z", "x"), ("y", "c")
    rows = P(None, seq, None, ctx, None)
    wide = P(seq, None, ctx)
    flat = P(seq, ctx)
    weights = (wide,) * 3 + (flat,) * 3 + (wide,) * 3 + (flat,) * 3 + (P(),) * 6
    return jax.shard_map(
        on_device,
        mesh=inner,
        in_specs=(rows, P(None, seq, None, ctx), rows) + weights,
        out_specs=(rows, rows, P()) + weights,
        check_vma=False,
    )
```

```python
import functools

import jax
import jax.numpy as jnp
from jax import lax
from jax.experimental import pallas as pl
from jax.experimental.pallas import tpu as pltpu
from jax.sharding import Mesh
from jax.sharding import PartitionSpec as P

D = 2048
HEADS = 16
HEAD_DIM = 128
FF = 8192
STEP_COUNT = 10
CHUNKS = 2

EPS = 1e-06
NEG = -1e30
CLIP = 1.0
BETA1 = 0.9
BETA2 = 0.95
ADAM_EPS = 1e-08
DECAY = 0.1
BF = jnp.bfloat16
F32 = jnp.float32
SCALING = HEAD_DIM ** (-0.5)
VMEM_LIMIT = 48 * 1024 * 1024


def rms_norm(tensor, scaling):
    return tensor * lax.rsqrt(jnp.mean(tensor * tensor, axis=-1, keepdims=True) + EPS) * scaling


def adam_update(weight, moment, second, gradient, factor, step_rate, decay):
    clipped = gradient * factor
    moment = BETA1 * moment + (1.0 - BETA1) * clipped
    second = BETA2 * second + (1.0 - BETA2) * clipped * clipped
    fixed_first = moment / (1.0 - BETA1**STEP_COUNT)
    fixed_second = second / (1.0 - BETA2**STEP_COUNT)
    updated = weight - step_rate * (
        fixed_first / (jnp.sqrt(fixed_second) + ADAM_EPS) + decay * weight
    )
    return (moment, second, updated)


def swap(tensor, axis):
    return lax.ppermute(tensor, axis, [(0, 1), (1, 0)])


def tie(tensor, *earlier):
    return lax.optimization_barrier((tensor,) + earlier)[0]


def gather_start(own, outer, inner, *before_x):
    start = {"x": tie(own, *before_x), "y": own}
    return own, swap(start[inner], inner), swap(start[outer], outer)


def gather_across(state, outer):
    return state + (swap(state[1], outer),)


def gather_core(state):
    mine = jnp.concatenate(state, axis=0)
    return mine, swap(mine, "c")


def gather_tokens(own, outer, inner, *before_x):
    return gather_core(gather_across(gather_start(own, outer, inner, *before_x), outer))


def scatter_core(mine, other, units):
    came = swap(other, "c").reshape(4, units, -1)
    mine = mine.reshape(4, units, -1)
    send = (mine[2:].astype(F32) + came[2:].astype(F32)).astype(BF)
    return mine[:2].astype(F32) + came[:2].astype(F32), send


def scatter_outer(state, outer):
    keep, send = state
    came = swap(send, outer)
    send = (keep[1] + came[1].astype(F32)).astype(BF)
    return keep[0] + came[0].astype(F32), send


def scatter_inner(state, inner):
    keep, send = state
    return keep + swap(send, inner).astype(F32)


def tie_send(state, *earlier):
    return state[0], tie(state[1], *earlier)


def sum_everywhere(tensor, z_count, beside):
    reach = 1
    while reach < z_count:
        tensor = tensor + lax.ppermute(tensor, "z", [(i, i ^ reach) for i in range(z_count)])
        reach *= 2
    tensor = tie(tensor + swap(tensor, "c"), beside)
    for axis in ("y", "x"):
        tensor = tensor + swap(tensor, axis)
    return tensor


def mm(a, b, dims):
    return lax.dot_general(a, b, (dims, ((), ())), preferred_element_type=F32)


NN = ((1,), (0,))
NT = ((1,), (1,))
TN = ((0,), (0,))


def mm_mem(a, b, dims):
    return mm(a.astype(BF), b.astype(BF), dims)


def elu_one(tensor):
    return jnp.where(tensor > 0, tensor + 1.0, jnp.exp(jnp.minimum(tensor, 0.0)))


def elu_slope(tensor):
    low = jnp.where(tensor == 0, 0.5, jnp.exp(jnp.minimum(tensor, 0.0)))
    return jnp.where(tensor > 0, 1.0, low)


def segment_of(ref, r, part):
    block = ref[:, :, r, :, part * HEAD_DIM : (part + 1) * HEAD_DIM]
    return block.reshape(-1, HEAD_DIM)


def memory_forward(qs, ks, vs, cols):
    seg_count = len(qs)
    saved = []
    memory = normer = None
    for r in range(seg_count):
        reading, writing, keep = cols[r]
        sq = elu_one(qs[r].astype(F32))
        sk = elu_one(ks[r].astype(F32))
        value = vs[r].astype(F32)
        rows = sq.shape[0]
        item = dict(sq=sq, sk=sk)
        if r == 0:
            item["recalled"] = jnp.zeros_like(sq)
            change = value
        else:
            both = mm_mem(jnp.concatenate([sq, sk], axis=0), memory, NN)
            num = both[:rows]
            den = 1.0 + jnp.sum(sq * normer, axis=-1, keepdims=True)
            item["recalled"] = reading * num / den
            before = keep * both[rows:]
            kden = 1.0 + keep * jnp.sum(sk * normer, axis=-1, keepdims=True)
            change = value - before / kden
            item.update(num=num, den=den, before=before, kden=kden, memory=memory, normer=normer)
        item["change"] = change
        if r < seg_count - 1:
            write = sk * writing
            fresh = mm_mem(write, change, TN)
            fresh_norm = jnp.sum(write, axis=0, keepdims=True)
            memory = fresh if r == 0 else keep * memory + fresh
            normer = fresh_norm if r == 0 else keep[:1] * normer + fresh_norm
        saved.append(item)
    return saved


def local_probs(query, key, allowed):
    scores = jnp.where(allowed > 0, mm(query, key, NT) * SCALING, NEG)
    exponent = jnp.exp(scores - jnp.max(scores, axis=-1, keepdims=True))
    return exponent / jnp.sum(exponent, axis=-1, keepdims=True)


def columns_of(cols_ref, r):
    cols = cols_ref[r]
    return cols[:, 0:1], cols[:, 1:2], cols[:, 2:3]


def attention_fwd_kernel(heads, proj_ref, mask_ref, cols_ref, gate_ref, out_ref):
    seg_count = mask_ref.shape[0]
    cols = [columns_of(cols_ref, r) for r in range(seg_count)]
    for h in range(heads):
        qs = [segment_of(proj_ref, r, h) for r in range(seg_count)]
        ks = [segment_of(proj_ref, r, heads + h) for r in range(seg_count)]
        vs = [segment_of(proj_ref, r, 2 * heads + h) for r in range(seg_count)]
        saved = memory_forward(qs, ks, vs, cols)
        mixing = gate_ref[h : h + 1]
        for r in range(seg_count):
            prob_low = local_probs(qs[r], ks[r], mask_ref[r]).astype(BF)
            local_out = mm(prob_low, vs[r], NN)
            combined = mixing * saved[r]["recalled"] + (1.0 - mixing) * local_out
            out_ref[:, :, r, :, h * HEAD_DIM : (h + 1) * HEAD_DIM] = combined.astype(BF).reshape(
                out_ref.shape[0], out_ref.shape[1], out_ref.shape[3], HEAD_DIM
            )


def attention_bwd_kernel(
    heads, proj_ref, grad_ref, mask_ref, cols_ref, gate_ref, out_ref, gate_out_ref
):
    seg_count = mask_ref.shape[0]
    cols = [columns_of(cols_ref, r) for r in range(seg_count)]

    def put(r, part, value):
        out_ref[:, :, r, :, part * HEAD_DIM : (part + 1) * HEAD_DIM] = value.astype(BF).reshape(
            out_ref.shape[0], out_ref.shape[1], out_ref.shape[3], HEAD_DIM
        )

    for h in range(heads):
        qs = [segment_of(proj_ref, r, h) for r in range(seg_count)]
        ks = [segment_of(proj_ref, r, heads + h) for r in range(seg_count)]
        vs = [segment_of(proj_ref, r, 2 * heads + h) for r in range(seg_count)]
        saved = memory_forward(qs, ks, vs, cols)
        mixing = gate_ref[h : h + 1]
        gate_sum = jnp.zeros((1, HEAD_DIM), F32)
        d_memory = d_normer = None
        for r in reversed(range(seg_count)):
            reading, writing, keep = cols[r]
            item = saved[r]
            sq, sk = item["sq"], item["sk"]
            rows = sq.shape[0]
            d_combined = segment_of(grad_ref, r, h).astype(F32)
            d_recalled = mixing * d_combined
            d_local = ((1.0 - mixing) * d_combined).astype(BF)
            probs = local_probs(qs[r], ks[r], mask_ref[r])
            prob_low = probs.astype(BF)
            local_out = mm(prob_low, vs[r], NN)
            gate_sum = gate_sum + jnp.sum(
                d_combined * (item["recalled"] - local_out), axis=0, keepdims=True
            )
            d_prob = mm(d_local, vs[r], NT)
            d_value = mm(prob_low, d_local, TN)
            d_scores = (
                probs * (d_prob - jnp.sum(d_prob * probs, axis=-1, keepdims=True))
            ).astype(BF)
            d_query = mm(d_scores, ks[r], NN) * SCALING
            d_key = mm(d_scores, qs[r], TN) * SCALING
            d_sk = None
            d_before = d_kden = None
            if r < seg_count - 1:
                d_change = writing * mm_mem(sk, d_memory, NN)
                d_sk = writing * (mm_mem(item["change"], d_memory, NT) + d_normer)
                d_value = d_value + d_change
                if r > 0:
                    d_before = keep * (-d_change / item["kden"])
                    d_kden = keep * (
                        jnp.sum(d_change * item["before"], axis=-1, keepdims=True)
                        / (item["kden"] * item["kden"])
                    )
            if r > 0:
                d_num = reading * d_recalled / item["den"]
                d_den = -reading * (
                    jnp.sum(d_recalled * item["num"], axis=-1, keepdims=True)
                    / (item["den"] * item["den"])
                )
                if d_before is None:
                    d_sq = mm_mem(d_num, item["memory"], NT) + d_den * item["normer"]
                    new_memory = mm_mem(sq, d_num, TN)
                    new_normer = jnp.sum(sq * d_den, axis=0, keepdims=True)
                else:
                    stacked = jnp.concatenate([d_num, d_before], axis=0)
                    both = mm_mem(stacked, item["memory"], NT)
                    d_sq = both[:rows] + d_den * item["normer"]
                    d_sk = d_sk + both[rows:] + d_kden * item["normer"]
                    new_memory = keep * d_memory + mm_mem(
                        jnp.concatenate([sq, sk], axis=0), stacked, TN
                    )
                    new_normer = keep[:1] * d_normer + jnp.sum(
                        sq * d_den + sk * d_kden, axis=0, keepdims=True
                    )
                d_memory, d_normer = new_memory, new_normer
                d_query = d_query + d_sq * elu_slope(qs[r].astype(F32))
            if d_sk is not None:
                d_key = d_key + d_sk * elu_slope(ks[r].astype(F32))
            put(r, h, d_query)
            put(r, heads + h, d_key)
            put(r, 2 * heads + h, d_value)
        gate_out_ref[h : h + 1] = gate_sum


def block_spec(shape, where):
    dims = list(shape)
    dims[where] = None

    def index(s):
        place = [0] * len(dims)
        place[where] = s
        return tuple(place)

    return pl.BlockSpec(tuple(dims), index)


def attention_fwd(projected, mask, cols, gate_rows, where):
    heads = gate_rows.shape[0]
    out_shape = projected.shape[:-1] + (heads * HEAD_DIM,)
    return pl.pallas_call(
        functools.partial(attention_fwd_kernel, heads),
        grid=(projected.shape[where],),
        in_specs=[
            block_spec(projected.shape, where),
            pl.BlockSpec((None,) + mask.shape[1:], lambda s: (s, 0, 0, 0)),
            pl.BlockSpec((None,) + cols.shape[1:], lambda s: (s, 0, 0, 0)),
            pl.BlockSpec(gate_rows.shape, lambda s: (0, 0)),
        ],
        out_specs=block_spec(out_shape, where),
        out_shape=jax.ShapeDtypeStruct(out_shape, BF),
        compiler_params=pltpu.CompilerParams(vmem_limit_bytes=VMEM_LIMIT),
        cost_estimate=pl.CostEstimate(
            flops=400_000_000, bytes_accessed=3_000_000, transcendentals=0
        ),
        name="attention_forward",
    )(projected, mask, cols, gate_rows)


def attention_bwd(projected, d_combined, mask, cols, gate_rows, where):
    heads = gate_rows.shape[0]
    seqs = projected.shape[where]
    return pl.pallas_call(
        functools.partial(attention_bwd_kernel, heads),
        grid=(seqs,),
        in_specs=[
            block_spec(projected.shape, where),
            block_spec(d_combined.shape, where),
            pl.BlockSpec((None,) + mask.shape[1:], lambda s: (s, 0, 0, 0)),
            pl.BlockSpec((None,) + cols.shape[1:], lambda s: (s, 0, 0, 0)),
            pl.BlockSpec(gate_rows.shape, lambda s: (0, 0)),
        ],
        out_specs=[
            block_spec(projected.shape, where),
            pl.BlockSpec((None, heads, HEAD_DIM), lambda s: (s, 0, 0)),
        ],
        out_shape=[
            jax.ShapeDtypeStruct(projected.shape, BF),
            jax.ShapeDtypeStruct((seqs, heads, HEAD_DIM), F32),
        ],
        compiler_params=pltpu.CompilerParams(vmem_limit_bytes=VMEM_LIMIT),
        cost_estimate=pl.CostEstimate(
            flops=1_000_000_000, bytes_accessed=5_000_000, transcendentals=0
        ),
        name="attention_backward",
    )(projected, d_combined, mask, cols, gate_rows)


GELU_A = 0.7978845608028654
GELU_B = 0.044715


def ff_kernel(width, half, x_mine, x_other, g_mine, g_other, w_ref, *outs):
    step = pl.program_id(0)

    @pl.when(step < half)
    def first():
        ff_tile(width, x_mine, g_mine, w_ref, outs[0], outs[2])

    @pl.when(step >= half)
    def second():
        ff_tile(width, x_other, g_other, w_ref, outs[1], outs[3])


def ff_tile(width, x_ref, g_ref, w_ref, act_ref, grad_ref):
    weights = w_ref[...]
    gate_up = mm(x_ref[...], weights[:, : 2 * width], NN)
    d_active = mm(g_ref[...], weights[:, 2 * width :], NN)
    gate = gate_up[:, :width]
    up = gate_up[:, width:]
    square = gate * gate
    tanh = jnp.tanh(GELU_A * gate * (1.0 + GELU_B * square))
    half = 0.5 * (1.0 + tanh)
    gelu = gate * half
    slope = half + 0.5 * gate * (1.0 - tanh * tanh) * GELU_A * (1.0 + 3.0 * GELU_B * square)
    act_ref[...] = (gelu * up).astype(BF)
    grad_ref[:, :width] = (d_active * up * slope).astype(BF)
    grad_ref[:, width:] = (d_active * gelu).astype(BF)


def feed_forward(rows, grads, weights):
    tokens = rows[0].shape[0]
    width = weights.shape[1] // 3
    tile = 256
    half = tokens // tile

    def first(columns):
        return pl.BlockSpec((tile, columns), lambda i: (jnp.minimum(i, half - 1), 0))

    def second(columns):
        return pl.BlockSpec((tile, columns), lambda i: (jnp.maximum(i - half, 0), 0))

    whole = pl.BlockSpec(weights.shape, lambda i: (0, 0), pipeline_mode=pl.Buffered(1))
    act = jax.ShapeDtypeStruct((tokens, width), BF)
    grad = jax.ShapeDtypeStruct((tokens, 2 * width), BF)
    out = pl.pallas_call(
        functools.partial(ff_kernel, width, half),
        grid=(2 * half,),
        in_specs=[first(D), second(D), first(D), second(D), whole],
        out_specs=[first(width), second(width), first(2 * width), second(2 * width)],
        out_shape=[act, act, grad, grad],
        compiler_params=pltpu.CompilerParams(vmem_limit_bytes=VMEM_LIMIT),
        cost_estimate=pl.CostEstimate(
            flops=tokens * D * width, bytes_accessed=tokens * D, transcendentals=0
        ),
        name="feed_forward",
    )(*rows, *grads, weights)
    return (out[0], out[1]), (out[2], out[3])


def grads_kernel(count, *refs):
    rows, grads, by_rows, by_grads = (refs[k * count : (k + 1) * count] for k in range(4))
    out_ref = refs[4 * count]
    split = by_rows[0].shape[1]

    def total(left, right):
        acc = None
        for a, b in zip(left, right):
            term = mm(a[...], b[...], TN)
            acc = term if acc is None else acc + term
        return acc

    out_ref[:, :split] = total(rows, by_rows).astype(BF)
    out_ref[:, split:] = total(grads, by_grads).astype(BF)


def weight_grads(rows, grads, by_rows, by_grads):
    def halves(arrays):
        parts = []
        for a in arrays:
            parts += [(a[0], 0), (a[1], 0)] if isinstance(a, tuple) else [(a, 0), (a, 1)]
        return parts

    groups = [halves(a) for a in (rows, grads, by_rows, by_grads)]
    count = len(groups[0])
    tokens = groups[0][0][0].shape[0] // (1 if isinstance(rows[0], tuple) else 2)
    first, second = groups[2][0][0].shape[1], groups[3][0][0].shape[1]
    tile = 512

    def tall(half):
        return pl.BlockSpec((tokens, tile), lambda i: (half, i))

    def whole(width, half):
        return pl.BlockSpec((tokens, width), lambda i: (half, 0), pipeline_mode=pl.Buffered(1))

    return pl.pallas_call(
        functools.partial(grads_kernel, count),
        grid=(D // tile,),
        in_specs=[tall(half) for _, half in groups[0] + groups[1]]
        + [whole(first, half) for _, half in groups[2]]
        + [whole(second, half) for _, half in groups[3]],
        out_specs=pl.BlockSpec((tile, first + second), lambda i: (i, 0)),
        out_shape=jax.ShapeDtypeStruct((D, first + second), BF),
        compiler_params=pltpu.CompilerParams(vmem_limit_bytes=VMEM_LIMIT),
        cost_estimate=pl.CostEstimate(
            flops=2 * count * tokens * D * (first + second),
            bytes_accessed=2 * (2 * count * tokens * D + (count * tokens + D) * (first + second)),
            transcendentals=0,
        ),
        name="weight_grads",
    )(*[a for group in groups for a, _ in group])


RATE_QKV = D ** (-0.5)
RATE_OUT = 4.0 * (HEADS * HEAD_DIM) ** (-0.5)
RATE_DOWN = FF ** (-0.5)


def clip_factor(small):
    row = lax.broadcasted_iota(jnp.int32, small.shape, 0)
    lane = lax.broadcasted_iota(jnp.int32, small.shape, 1)
    summed = (row == small.shape[0] - 1) & (lane >= HEADS)
    squares = jnp.sum(jnp.where(summed, small, small * small), axis=(0, 1), keepdims=True)
    grad_norm = jnp.sqrt(squares)
    return grad_norm, jnp.minimum(1.0, CLIP / (grad_norm + 1e-06))


def adam_kernel(place_ref, small_ref, *refs):
    ins, grads, outs = refs[:12], refs[12:16], refs[16:]
    factor = clip_factor(small_ref[...])[1]
    is_low = place_ref[0] == 0

    def put(number, place, gradient, rate):
        weight, moment, second = (r[place] for r in ins[3 * number : 3 * number + 3])
        new = adam_update(weight, moment, second, gradient.astype(F32), factor, rate, DECAY)
        for ref, value in zip(outs[3 * number : 3 * number + 3], new):
            ref[place] = value

    mine, theirs = grads[0][...], grads[1][...]
    sides = (jnp.where(is_low, mine, theirs), jnp.where(is_low, theirs, mine))
    width = mine.shape[1] // 4
    everything = slice(None)
    for s, side in enumerate(sides):
        cols = slice(s * width, (s + 1) * width)
        for part in range(3):
            put(0, (part, everything, cols), side[:, part * width : (part + 1) * width], RATE_QKV)
        put(1, (everything, cols), side[:, 3 * width :], RATE_OUT)
    put(2, (everything, everything), grads[2][...], RATE_QKV)
    put(2 + 1, (everything, everything), grads[3][...], RATE_DOWN)


def mlp_view(t):
    rows, _, width_ff = t.shape
    return t.reshape(rows, 2, width_ff // 128, 128).transpose(0, 2, 1, 3).reshape(-1, 128)


def adam_all(small, x_place, arrays, att_mine, att_theirs, grad_mlp, grad_down):
    rows, _, width_ff = arrays[6].shape
    lanes = width_ff // 128

    def qkv_view(t):
        return jnp.transpose(t, (1, 0, 2))

    def mlp_back(t):
        return t.reshape(rows, lanes, 2, 128).transpose(0, 2, 1, 3).reshape(rows, 2, width_ff)

    views = [qkv_view(t) for t in arrays[:3]] + list(arrays[3:6])
    views += [mlp_view(t) for t in arrays[6:9]] + list(arrays[9:])
    grads = [att_mine, att_theirs, grad_mlp, grad_down]
    steps = 8

    def spec(t):
        axis = t.ndim - 2
        block = list(t.shape)
        block[axis] //= steps
        return pl.BlockSpec(tuple(block), lambda i: (0,) * axis + (i, 0))

    new = pl.pallas_call(
        adam_kernel,
        grid=(steps,),
        in_specs=[
            pl.BlockSpec(memory_space=pltpu.SMEM),
            pl.BlockSpec(small.shape, lambda i: (0, 0)),
        ]
        + [spec(t) for t in views + grads],
        out_specs=[spec(t) for t in views],
        out_shape=[jax.ShapeDtypeStruct(t.shape, F32) for t in views],
        compiler_params=pltpu.CompilerParams(vmem_limit_bytes=VMEM_LIMIT),
        cost_estimate=pl.CostEstimate(
            flops=20 * sum(t.size for t in views) // 3,
            bytes_accessed=8 * sum(t.size for t in views),
            transcendentals=0,
        ),
        name="adam",
    )(x_place[None], small, *views, *grads)
    new = list(new)
    return (
        [qkv_view(t) for t in new[:3]] + new[3:6] + [mlp_back(t) for t in new[6:9]] + new[9:]
    )


def on_device(
    inputs,
    doc_ids,
    cotangent,
    weight_qkv,
    moment_qkv,
    second_qkv,
    weight_out,
    moment_out,
    second_out,
    weight_mlp,
    moment_mlp,
    second_mlp,
    weight_down,
    moment_down,
    second_down,
    norm_gains,
    moment_gains,
    second_gains,
    gate_logit,
    moment_gate,
    second_gate,
):
    micro_count, _, seg_count, own_len, _ = inputs.shape
    own_tokens = seg_count * own_len
    x_place = lax.axis_index("x")
    y_place = lax.axis_index("y")
    c_place = lax.axis_index("c")
    is_low = x_place == 0
    orders = [("x", "y") if m % 2 == 0 else ("y", "x") for m in range(micro_count)]

    z_count = D // (2 * weight_qkv.shape[0])

    def half_columns(weight, which):
        width = weight.shape[-1] // 2
        return lax.dynamic_slice_in_dim(weight, which * width, width, axis=weight.ndim - 1)

    def by_place(own, other, axis):
        return jnp.where(
            is_low,
            jnp.concatenate([own, other], axis=axis),
            jnp.concatenate([other, own], axis=axis),
        )

    def exchange_rows(columns_for, send, *earlier):
        theirs = swap(tie(send, *earlier), "x")
        mine = columns_for(x_place)
        both = jnp.zeros((2 * rows, mine.shape[1]), BF)
        both = lax.dynamic_update_slice_in_dim(both, mine, x_place * rows, axis=0)
        return lax.dynamic_update_slice_in_dim(both, theirs, (1 - x_place) * rows, axis=0)

    def fetch(block):
        return lax.all_gather(block, "z", axis=0, tiled=True)

    rows = weight_qkv.shape[0]
    heads = weight_qkv.shape[2] // (2 * HEAD_DIM)
    width_att = heads * HEAD_DIM
    width_ff = weight_down.shape[1] // 2
    width = width_ff // CHUNKS

    def att_columns(which):
        qkv = half_columns(weight_qkv, which).astype(BF).reshape(rows, -1)
        return jnp.concatenate([qkv, half_columns(weight_out, which).astype(BF)], axis=1)

    def ff_columns(k, which):
        start = which * width_ff + k * width
        mlp = lax.dynamic_slice_in_dim(weight_mlp, start, width, axis=2).astype(BF)
        down = lax.dynamic_slice_in_dim(weight_down, start, width, axis=1).astype(BF)
        return jnp.concatenate([mlp[:, 0], mlp[:, 1], down], axis=1)

    send_att = att_columns(1 - x_place)
    shard_att = exchange_rows(att_columns, send_att)
    full_att = fetch(shard_att)
    full_qkv = full_att[:, : 3 * width_att]
    full_out = full_att[:, 3 * width_att :]

    head_start = (y_place * 2 + c_place) * (2 * heads) + x_place * heads
    gate_local = lax.dynamic_slice_in_dim(gate_logit, head_start, heads)
    mixing = jax.nn.sigmoid(gate_local)
    gate_rows = jnp.broadcast_to(mixing[:, None], (heads, HEAD_DIM))

    micros = range(micro_count)
    tokens = 8 * own_tokens
    token_rows = [
        tie(inputs[m, 0], send_att).reshape(own_tokens, D).astype(F32) for m in micros
    ]
    back_low = [cotangent[m, 0].reshape(own_tokens, D) for m in micros]
    normed_att = [rms_norm(t, norm_gains[0]).astype(BF) for t in token_rows]
    att_pairs = [gather_tokens(normed_att[m], *orders[m], shard_att) for m in micros]
    att_rows = [jnp.concatenate(pair, axis=0) for pair in att_pairs]
    all_ids = doc_ids[:, 0]
    for axis in ("y", "x", "c"):
        all_ids = jnp.stack([all_ids, swap(all_ids, axis)], axis=0)

    shard_ff = []
    full_ff = []
    for k in range(CHUNKS):
        columns_for = functools.partial(ff_columns, k)
        earlier = [p[0] for p in att_pairs] if k == 0 else [shard_ff[-1]]
        shard_ff.append(exchange_rows(columns_for, columns_for(1 - x_place), *earlier))
        full_ff.append(fetch(shard_ff[-1]))

    rel_c = jnp.arange(2)[:, None, None] ^ c_place
    rel_y = jnp.arange(2)[None, :, None] ^ y_place
    places = ((rel_y * 2 + rel_c) * own_len + jnp.arange(own_len)).reshape(-1)
    causal = places[:, None] >= places[None, :]
    masks = []
    columns = []
    for m in micros:
        ids = jnp.transpose(all_ids[:, :, :, m], (1, 3, 0, 2, 4)).reshape(2, seg_count, -1)
        same = ids[:, :, :, None] == ids[:, :, None, :]
        masks.append((same & causal).astype(F32))
        last = jnp.max(ids, axis=2)
        previous = jnp.concatenate([jnp.full((2, 1), -1, last.dtype), last[:, :-1]], axis=1)
        reading = ids == previous[:, :, None]
        writing = ids == last[:, :, None]
        keep = jnp.broadcast_to((last == previous)[:, :, None], ids.shape)
        columns.append(jnp.stack([reading, writing, keep], axis=-1).astype(F32))

    slots = (2, 2, 2, seg_count, own_len)
    wheres = [1 if orders[m][0] == "x" else 2 for m in micros]
    projected = []
    combined = []
    hidden = []
    mlp_rows = []
    back_states = [
        gather_start(tie(back_low[m], *[p[0] for p in att_pairs]), *orders[m], shard_ff[0])
        for m in micros
    ]
    for m in micros:
        rows_in = att_rows[m]
        if m == 0:
            rows_in = tie(rows_in, *[t for state in back_states for t in state])
        proj = mm(rows_in, full_qkv, NN).astype(BF)
        projected.append(proj.reshape(slots + (3 * width_att,)))
        comb = attention_fwd(projected[m], masks[m], columns[m], gate_rows, wheres[m])
        combined.append(comb.reshape(tokens, width_att))
    half = tokens // 2
    back_states = [gather_across(back_states[m], orders[m][0]) for m in micros]
    back_rows = [gather_core(state) for state in back_states]
    for m in micros:
        ready = combined[m]
        if m > 0:
            ready = tie(ready, *shard_ff, *[state[-1] for state in back_states])
        other = mm(ready[half:], full_out, NT).astype(BF)
        mine = mm(ready[:half], full_out, NT).astype(BF)
        state = scatter_outer(scatter_core(mine, other, own_tokens), orders[m][0])
        hidden.append(token_rows[m] + scatter_inner(state, orders[m][1]))
        normed_mlp = rms_norm(hidden[m], norm_gains[1]).astype(BF)
        mlp_rows.append(gather_tokens(normed_mlp, *orders[m]))

    def reduce_rows(partial):
        return lax.psum_scatter(partial, "z", scatter_dimension=0, tiled=True)

    def products(left, right, totals, dtype):
        terms = [mm(left[p], right, NT) for p in (1, 0)][::-1]
        if totals is not None:
            terms = [a + b for a, b in zip(totals, terms)]
        return tuple(t.astype(dtype) for t in terms)

    active = []
    d_gate_up = []
    own_ff = []
    d_total = [None] * micro_count
    out_total = [None] * micro_count
    states = [None] * micro_count
    for k in range(CHUNKS):
        active.append([])
        d_gate_up.append([])
        last = k == CHUNKS - 1
        for m in micros:
            rows_in = mlp_rows[m]
            if last and m > 0:
                rows_in = (tie(rows_in[0], *d_total[m - 1]), rows_in[1])
            act, grad = feed_forward(rows_in, back_rows[m], full_ff[k])
            active[k].append(act)
            d_gate_up[k].append(grad)
            if last and m > 0:
                grad = (grad[0], tie(grad[1], states[m - 1][1]))
            dtype = BF if last else F32
            d_total[m] = products(grad, full_ff[k][:, : 2 * width], d_total[m], dtype)
            if last:
                states[m] = scatter_core(*d_total[m], own_tokens)
            else:
                out_total[m] = products(act, full_ff[k][:, 2 * width :], out_total[m], F32)
        if not last:
            grad_ff = weight_grads(mlp_rows, back_rows, d_gate_up[k], active[k])
            own_ff.append(reduce_rows(grad_ff))
            terms = [t for pair in d_total + out_total for t in pair]
            full_ff[k + 1] = tie(full_ff[k + 1], grad_ff, *terms)

    last_active = [(active[-1][m][0], tie(active[-1][m][1], states[-1][1])) for m in micros]
    grad_ff = weight_grads(mlp_rows, back_rows, d_gate_up[-1], last_active)
    own_ff.append(reduce_rows(grad_ff))

    gain_grad_att = jnp.zeros((D,), F32)
    gain_grad_mlp = jnp.zeros((D,), F32)
    d_hidden = []
    att_grads = []
    for m in micros:
        state = tie_send(scatter_outer(states[m], orders[m][0]), grad_ff)
        d_normed = scatter_inner(state, orders[m][1])
        ignored, norm_back = jax.vjp(rms_norm, hidden[m], norm_gains[1])
        d_norm, d_gain = norm_back(d_normed)
        gain_grad_mlp = gain_grad_mlp + d_gain
        d_hidden.append(back_low[m].astype(F32) + d_norm)
        att_grads.append(gather_tokens(d_hidden[m].astype(BF), *orders[m]))

    gate_sum = jnp.zeros((heads,), F32)
    d_projs = []
    out_states = []
    for m in micros:
        act = (last_active[m][0], tie(last_active[m][1], d_hidden[m]))
        out_total[m] = products(act, full_ff[-1][:, 2 * width :], out_total[m], BF)
        other = att_grads[m][1] if m > 0 else tie(att_grads[m][1], own_ff[0])
        d_combined = jnp.concatenate(
            [mm(att_grads[m][0], full_out, NN), mm(other, full_out, NN)], axis=0
        )
        d_proj, gate_part = attention_bwd(
            projected[m],
            d_combined.reshape(slots + (width_att,)),
            masks[m],
            columns[m],
            gate_rows,
            wheres[m],
        )
        gate_sum = gate_sum + jnp.sum(gate_part, axis=(0, 2))
        d_projs.append(d_proj.reshape(tokens, 3 * width_att))
    for m in micros:
        mine, other = out_total[m]
        other = tie(other, *[pair[1] for pair in att_grads])
        out_states.append(tie_send(scatter_core(mine, other, own_tokens), d_projs[0]))
    grad_att = weight_grads(att_rows, att_grads, d_projs, combined)
    own_att = reduce_rows(grad_att)

    def exchange_grad(grad):
        mine = lax.dynamic_slice_in_dim(grad, x_place * rows, rows, axis=0)
        theirs = swap(lax.dynamic_slice_in_dim(grad, (1 - x_place) * rows, rows, axis=0), "x")
        return mine, theirs

    def squares_of(grad):
        wide = grad.astype(F32)
        return jnp.sum(wide * wide)

    pairs = [exchange_grad(g) for g in own_ff]

    def ff_part(start, stop):
        low = jnp.concatenate([p[0][:, start * width : stop * width] for p in pairs], axis=1)
        high = jnp.concatenate([p[1][:, start * width : stop * width] for p in pairs], axis=1)
        return by_place(low, high, 1)

    grad_mlp = mlp_view(jnp.stack([ff_part(0, 1), ff_part(1, 2)], axis=1))
    grad_down = ff_part(2, 3)
    ff_owned = sum(squares_of(g) for g in own_ff)

    grad_rows = []
    block_out = []
    in_states = []
    for m in micros:
        d_proj = tie(d_projs[m], grad_att)
        other = mm(d_proj[half:], full_qkv, NT).astype(BF)
        mine = mm(d_proj[:half], full_qkv, NT).astype(BF)
        in_states.append(scatter_core(mine, other, own_tokens))
    for m in micros:
        state = tie_send(scatter_outer(in_states[m], orders[m][0]), own_ff[-1])
        d_normed = scatter_inner(state, orders[m][1])
        ignored, norm_first = jax.vjp(rms_norm, token_rows[m], norm_gains[0])
        d_norm, d_gain = norm_first(d_normed)
        gain_grad_att = gain_grad_att + d_gain
        grad_rows.append((d_hidden[m] + d_norm).astype(BF))
    for m in micros:
        state = tie_send(scatter_outer(out_states[m], orders[m][0]), in_states[-1][1])
        block_out.append((hidden[m] + scatter_inner(state, orders[m][1])).astype(BF))

    att_mine, att_theirs = exchange_grad(own_att)

    gate_grad = gate_sum * mixing * (1.0 - mixing)
    gate_padded = lax.dynamic_update_slice(
        jnp.zeros(gate_logit.shape, F32), gate_grad, (head_start,)
    )
    ff_owned = tie(ff_owned, grad_mlp, grad_down)
    owned = squares_of(own_att) + ff_owned
    small = jnp.concatenate(
        [gain_grad_att, gain_grad_mlp, gate_padded, owned[None], jnp.zeros((111,), F32)]
    ).reshape(-1, 128)
    small = sum_everywhere(small, z_count, att_theirs)
    grad_norm, factor = (t.reshape(()) for t in clip_factor(small))
    flat = small.reshape(-1)
    gains_total = flat[: 2 * D].reshape(2, D)
    gate_total = flat[2 * D : 2 * D + HEADS]
    arrays = [
        weight_qkv,
        moment_qkv,
        second_qkv,
        weight_out,
        moment_out,
        second_out,
        weight_mlp,
        moment_mlp,
        second_mlp,
        weight_down,
        moment_down,
        second_down,
    ]
    new = adam_all(small, x_place, arrays, att_mine, att_theirs, grad_mlp, grad_down)
    gains_new = adam_update(norm_gains, moment_gains, second_gains, gains_total, factor, 0.5, 0.0)
    gate_new = adam_update(gate_logit, moment_gate, second_gate, gate_total, factor, 1.0, 0.0)
    shape = (micro_count, 1, seg_count, own_len, D)
    return (
        jnp.stack(block_out, axis=0).reshape(shape),
        jnp.stack(grad_rows, axis=0).reshape(shape),
        grad_norm,
        *new,
        *gains_new,
        *gate_new,
    )


def solution(mesh):
    seq_count, ctx_count = mesh.devices.shape
    inner = Mesh(
        mesh.devices.reshape(seq_count // 2, 2, ctx_count // 2, 2), ("z", "x", "y", "c")
    )
    seq, ctx = ("z", "x"), ("y", "c")
    rows = P(None, seq, None, ctx, None)
    wide = P(seq, None, ctx)
    flat = P(seq, ctx)
    weights = (wide,) * 3 + (flat,) * 3 + (wide,) * 3 + (flat,) * 3 + (P(),) * 6
    return jax.shard_map(
        on_device,
        mesh=inner,
        in_specs=(rows, P(None, seq, None, ctx), rows) + weights,
        out_specs=(rows, rows, P()) + weights,
        check_vma=False,
    )
```

```python
import functools

import jax
import jax.numpy as jnp
from jax import lax
from jax.experimental import pallas as pl
from jax.experimental.pallas import tpu as pltpu
from jax.sharding import Mesh
from jax.sharding import PartitionSpec as P

D = 2048
HEADS = 16
HEAD_DIM = 128
FF = 8192
STEP_COUNT = 10
CHUNKS = 2

EPS = 1e-06
NEG = -1e30
CLIP = 1.0
BETA1 = 0.9
BETA2 = 0.95
ADAM_EPS = 1e-08
DECAY = 0.1
BF = jnp.bfloat16
F32 = jnp.float32
SCALING = HEAD_DIM ** (-0.5)
VMEM_LIMIT = 48 * 1024 * 1024


def rms_norm(tensor, scaling):
    return tensor * lax.rsqrt(jnp.mean(tensor * tensor, axis=-1, keepdims=True) + EPS) * scaling


def adam_update(weight, moment, second, gradient, factor, step_rate, decay):
    clipped = gradient * factor
    moment = BETA1 * moment + (1.0 - BETA1) * clipped
    second = BETA2 * second + (1.0 - BETA2) * clipped * clipped
    fixed_first = moment / (1.0 - BETA1**STEP_COUNT)
    fixed_second = second / (1.0 - BETA2**STEP_COUNT)
    updated = weight - step_rate * (
        fixed_first / (jnp.sqrt(fixed_second) + ADAM_EPS) + decay * weight
    )
    return (moment, second, updated)


def swap(tensor, axis):
    return lax.ppermute(tensor, axis, [(0, 1), (1, 0)])


def tie(tensor, *earlier):
    return lax.optimization_barrier((tensor,) + earlier)[0]


def gather_start(own, outer, inner, *before_x):
    start = {"x": tie(own, *before_x), "y": own}
    return own, swap(start[inner], inner), swap(start[outer], outer)


def gather_across(state, outer):
    return state + (swap(state[1], outer),)


def gather_core(state):
    mine = jnp.concatenate(state, axis=0)
    return mine, swap(mine, "c")


def gather_tokens(own, outer, inner, *before_x):
    return gather_core(gather_across(gather_start(own, outer, inner, *before_x), outer))


def scatter_core(mine, other, units):
    came = swap(other, "c").reshape(4, units, -1)
    mine = mine.reshape(4, units, -1)
    send = (mine[2:].astype(F32) + came[2:].astype(F32)).astype(BF)
    return mine[:2].astype(F32) + came[:2].astype(F32), send


def scatter_outer(state, outer, *later):
    keep, send = state
    came = tie(swap(send, outer), *later)
    send = (keep[1] + came[1].astype(F32)).astype(BF)
    return keep[0] + came[0].astype(F32), send


def scatter_inner(state, inner):
    keep, send = state
    return keep + swap(send, inner).astype(F32)


def tie_send(state, *earlier):
    return state[0], tie(state[1], *earlier)


def sum_everywhere(tensor, z_count, beside):
    reach = 1
    while reach < z_count:
        tensor = tensor + lax.ppermute(tensor, "z", [(i, i ^ reach) for i in range(z_count)])
        reach *= 2
    tensor = tie(tensor + swap(tensor, "c"), beside)
    for axis in ("y", "x"):
        tensor = tensor + swap(tensor, axis)
    return tensor


def mm(a, b, dims):
    return lax.dot_general(a, b, (dims, ((), ())), preferred_element_type=F32)


NN = ((1,), (0,))
NT = ((1,), (1,))
TN = ((0,), (0,))


def mm_mem(a, b, dims):
    return mm(a.astype(BF), b.astype(BF), dims)


def elu_one(tensor):
    return jnp.where(tensor > 0, tensor + 1.0, jnp.exp(jnp.minimum(tensor, 0.0)))


def elu_slope(tensor):
    low = jnp.where(tensor == 0, 0.5, jnp.exp(jnp.minimum(tensor, 0.0)))
    return jnp.where(tensor > 0, 1.0, low)


def segment_of(ref, r, part):
    block = ref[:, :, r, :, part * HEAD_DIM : (part + 1) * HEAD_DIM]
    return block.reshape(-1, HEAD_DIM)


def memory_forward(qs, ks, vs, cols):
    seg_count = len(qs)
    saved = []
    memory = normer = None
    for r in range(seg_count):
        reading, writing, keep = cols[r]
        sq = elu_one(qs[r].astype(F32))
        sk = elu_one(ks[r].astype(F32))
        value = vs[r].astype(F32)
        rows = sq.shape[0]
        item = dict(sq=sq, sk=sk)
        if r == 0:
            item["recalled"] = jnp.zeros_like(sq)
            change = value
        else:
            both = mm_mem(jnp.concatenate([sq, sk], axis=0), memory, NN)
            num = both[:rows]
            den = 1.0 + jnp.sum(sq * normer, axis=-1, keepdims=True)
            item["recalled"] = reading * num / den
            before = keep * both[rows:]
            kden = 1.0 + keep * jnp.sum(sk * normer, axis=-1, keepdims=True)
            change = value - before / kden
            item.update(num=num, den=den, before=before, kden=kden, memory=memory, normer=normer)
        item["change"] = change
        if r < seg_count - 1:
            write = sk * writing
            fresh = mm_mem(write, change, TN)
            fresh_norm = jnp.sum(write, axis=0, keepdims=True)
            memory = fresh if r == 0 else keep * memory + fresh
            normer = fresh_norm if r == 0 else keep[:1] * normer + fresh_norm
        saved.append(item)
    return saved


def local_probs(query, key, allowed):
    scores = jnp.where(allowed > 0, mm(query, key, NT) * SCALING, NEG)
    exponent = jnp.exp(scores - jnp.max(scores, axis=-1, keepdims=True))
    return exponent / jnp.sum(exponent, axis=-1, keepdims=True)


def columns_of(cols_ref, r):
    cols = cols_ref[r]
    return cols[:, 0:1], cols[:, 1:2], cols[:, 2:3]


def attention_fwd_kernel(heads, proj_ref, mask_ref, cols_ref, gate_ref, out_ref):
    seg_count = mask_ref.shape[0]
    cols = [columns_of(cols_ref, r) for r in range(seg_count)]
    for h in range(heads):
        qs = [segment_of(proj_ref, r, h) for r in range(seg_count)]
        ks = [segment_of(proj_ref, r, heads + h) for r in range(seg_count)]
        vs = [segment_of(proj_ref, r, 2 * heads + h) for r in range(seg_count)]
        saved = memory_forward(qs, ks, vs, cols)
        mixing = gate_ref[h : h + 1]
        for r in range(seg_count):
            prob_low = local_probs(qs[r], ks[r], mask_ref[r]).astype(BF)
            local_out = mm(prob_low, vs[r], NN)
            combined = mixing * saved[r]["recalled"] + (1.0 - mixing) * local_out
            out_ref[:, :, r, :, h * HEAD_DIM : (h + 1) * HEAD_DIM] = combined.astype(BF).reshape(
                out_ref.shape[0], out_ref.shape[1], out_ref.shape[3], HEAD_DIM
            )


def attention_bwd_kernel(
    heads, proj_ref, grad_ref, mask_ref, cols_ref, gate_ref, out_ref, gate_out_ref
):
    seg_count = mask_ref.shape[0]
    cols = [columns_of(cols_ref, r) for r in range(seg_count)]

    def put(r, part, value):
        out_ref[:, :, r, :, part * HEAD_DIM : (part + 1) * HEAD_DIM] = value.astype(BF).reshape(
            out_ref.shape[0], out_ref.shape[1], out_ref.shape[3], HEAD_DIM
        )

    for h in range(heads):
        qs = [segment_of(proj_ref, r, h) for r in range(seg_count)]
        ks = [segment_of(proj_ref, r, heads + h) for r in range(seg_count)]
        vs = [segment_of(proj_ref, r, 2 * heads + h) for r in range(seg_count)]
        saved = memory_forward(qs, ks, vs, cols)
        mixing = gate_ref[h : h + 1]
        gate_sum = jnp.zeros((1, HEAD_DIM), F32)
        d_memory = d_normer = None
        for r in reversed(range(seg_count)):
            reading, writing, keep = cols[r]
            item = saved[r]
            sq, sk = item["sq"], item["sk"]
            rows = sq.shape[0]
            d_combined = segment_of(grad_ref, r, h).astype(F32)
            d_recalled = mixing * d_combined
            d_local = ((1.0 - mixing) * d_combined).astype(BF)
            probs = local_probs(qs[r], ks[r], mask_ref[r])
            prob_low = probs.astype(BF)
            local_out = mm(prob_low, vs[r], NN)
            gate_sum = gate_sum + jnp.sum(
                d_combined * (item["recalled"] - local_out), axis=0, keepdims=True
            )
            d_prob = mm(d_local, vs[r], NT)
            d_value = mm(prob_low, d_local, TN)
            d_scores = (
                probs * (d_prob - jnp.sum(d_prob * probs, axis=-1, keepdims=True))
            ).astype(BF)
            d_query = mm(d_scores, ks[r], NN) * SCALING
            d_key = mm(d_scores, qs[r], TN) * SCALING
            d_sk = None
            d_before = d_kden = None
            if r < seg_count - 1:
                d_change = writing * mm_mem(sk, d_memory, NN)
                d_sk = writing * (mm_mem(item["change"], d_memory, NT) + d_normer)
                d_value = d_value + d_change
                if r > 0:
                    d_before = keep * (-d_change / item["kden"])
                    d_kden = keep * (
                        jnp.sum(d_change * item["before"], axis=-1, keepdims=True)
                        / (item["kden"] * item["kden"])
                    )
            if r > 0:
                d_num = reading * d_recalled / item["den"]
                d_den = -reading * (
                    jnp.sum(d_recalled * item["num"], axis=-1, keepdims=True)
                    / (item["den"] * item["den"])
                )
                if d_before is None:
                    d_sq = mm_mem(d_num, item["memory"], NT) + d_den * item["normer"]
                    new_memory = mm_mem(sq, d_num, TN)
                    new_normer = jnp.sum(sq * d_den, axis=0, keepdims=True)
                else:
                    stacked = jnp.concatenate([d_num, d_before], axis=0)
                    both = mm_mem(stacked, item["memory"], NT)
                    d_sq = both[:rows] + d_den * item["normer"]
                    d_sk = d_sk + both[rows:] + d_kden * item["normer"]
                    new_memory = keep * d_memory + mm_mem(
                        jnp.concatenate([sq, sk], axis=0), stacked, TN
                    )
                    new_normer = keep[:1] * d_normer + jnp.sum(
                        sq * d_den + sk * d_kden, axis=0, keepdims=True
                    )
                d_memory, d_normer = new_memory, new_normer
                d_query = d_query + d_sq * elu_slope(qs[r].astype(F32))
            if d_sk is not None:
                d_key = d_key + d_sk * elu_slope(ks[r].astype(F32))
            put(r, h, d_query)
            put(r, heads + h, d_key)
            put(r, 2 * heads + h, d_value)
        gate_out_ref[h : h + 1] = gate_sum


def block_spec(shape, where):
    dims = list(shape)
    dims[where] = None

    def index(s):
        place = [0] * len(dims)
        place[where] = s
        return tuple(place)

    return pl.BlockSpec(tuple(dims), index)


def attention_fwd(projected, mask, cols, gate_rows, where):
    heads = gate_rows.shape[0]
    out_shape = projected.shape[:-1] + (heads * HEAD_DIM,)
    return pl.pallas_call(
        functools.partial(attention_fwd_kernel, heads),
        grid=(projected.shape[where],),
        in_specs=[
            block_spec(projected.shape, where),
            pl.BlockSpec((None,) + mask.shape[1:], lambda s: (s, 0, 0, 0)),
            pl.BlockSpec((None,) + cols.shape[1:], lambda s: (s, 0, 0, 0)),
            pl.BlockSpec(gate_rows.shape, lambda s: (0, 0)),
        ],
        out_specs=block_spec(out_shape, where),
        out_shape=jax.ShapeDtypeStruct(out_shape, BF),
        compiler_params=pltpu.CompilerParams(vmem_limit_bytes=VMEM_LIMIT),
        cost_estimate=pl.CostEstimate(
            flops=7_600_000_000, bytes_accessed=3_000_000, transcendentals=0
        ),
        name="attention_forward",
    )(projected, mask, cols, gate_rows)


def attention_bwd(projected, d_combined, mask, cols, gate_rows, where):
    heads = gate_rows.shape[0]
    seqs = projected.shape[where]
    return pl.pallas_call(
        functools.partial(attention_bwd_kernel, heads),
        grid=(seqs,),
        in_specs=[
            block_spec(projected.shape, where),
            block_spec(d_combined.shape, where),
            pl.BlockSpec((None,) + mask.shape[1:], lambda s: (s, 0, 0, 0)),
            pl.BlockSpec((None,) + cols.shape[1:], lambda s: (s, 0, 0, 0)),
            pl.BlockSpec(gate_rows.shape, lambda s: (0, 0)),
        ],
        out_specs=[
            block_spec(projected.shape, where),
            pl.BlockSpec((None, heads, HEAD_DIM), lambda s: (s, 0, 0)),
        ],
        out_shape=[
            jax.ShapeDtypeStruct(projected.shape, BF),
            jax.ShapeDtypeStruct((seqs, heads, HEAD_DIM), F32),
        ],
        compiler_params=pltpu.CompilerParams(vmem_limit_bytes=VMEM_LIMIT),
        cost_estimate=pl.CostEstimate(
            flops=14_400_000_000, bytes_accessed=5_000_000, transcendentals=0
        ),
        name="attention_backward",
    )(projected, d_combined, mask, cols, gate_rows)


GELU_A = 0.7978845608028654
GELU_B = 0.044715


def ff_kernel(width, half, x_mine, x_other, g_mine, g_other, w_ref, *outs):
    step = pl.program_id(0)

    @pl.when(step < half)
    def first():
        ff_tile(width, x_mine, g_mine, w_ref, outs[0], outs[2])

    @pl.when(step >= half)
    def second():
        ff_tile(width, x_other, g_other, w_ref, outs[1], outs[3])


def ff_tile(width, x_ref, g_ref, w_ref, act_ref, grad_ref):
    weights = w_ref[...]
    gate_up = mm(x_ref[...], weights[:, : 2 * width], NN)
    d_active = mm(g_ref[...], weights[:, 2 * width :], NN)
    gate = gate_up[:, :width]
    up = gate_up[:, width:]
    square = gate * gate
    tanh = jnp.tanh(GELU_A * gate * (1.0 + GELU_B * square))
    half = 0.5 * (1.0 + tanh)
    gelu = gate * half
    slope = half + 0.5 * gate * (1.0 - tanh * tanh) * GELU_A * (1.0 + 3.0 * GELU_B * square)
    act_ref[...] = (gelu * up).astype(BF)
    grad_ref[:, :width] = (d_active * up * slope).astype(BF)
    grad_ref[:, width:] = (d_active * gelu).astype(BF)


def feed_forward(rows, grads, weights):
    tokens = rows[0].shape[0]
    width = weights.shape[1] // 3
    tile = 256
    half = tokens // tile

    def first(columns):
        return pl.BlockSpec((tile, columns), lambda i: (jnp.minimum(i, half - 1), 0))

    def second(columns):
        return pl.BlockSpec((tile, columns), lambda i: (jnp.maximum(i - half, 0), 0))

    whole = pl.BlockSpec(weights.shape, lambda i: (0, 0), pipeline_mode=pl.Buffered(1))
    act = jax.ShapeDtypeStruct((tokens, width), BF)
    grad = jax.ShapeDtypeStruct((tokens, 2 * width), BF)
    out = pl.pallas_call(
        functools.partial(ff_kernel, width, half),
        grid=(2 * half,),
        in_specs=[first(D), second(D), first(D), second(D), whole],
        out_specs=[first(width), second(width), first(2 * width), second(2 * width)],
        out_shape=[act, act, grad, grad],
        compiler_params=pltpu.CompilerParams(vmem_limit_bytes=VMEM_LIMIT),
        cost_estimate=pl.CostEstimate(
            flops=26 * tokens * D * width, bytes_accessed=tokens * D, transcendentals=0
        ),
        name="feed_forward",
    )(*rows, *grads, weights)
    return (out[0], out[1]), (out[2], out[3])


def down_kernel(count, half, *refs):
    step = pl.program_id(0)
    mine, other, weights = (refs[k * count : (k + 1) * count] for k in range(3))

    def tile(rows, out_ref):
        terms = [mm(a[...], w[...], NT) for a, w in zip(rows, weights)]
        out_ref[...] = sum(terms[1:], terms[0]).astype(BF)

    @pl.when(step < half)
    def first():
        tile(mine, refs[3 * count])

    @pl.when(step >= half)
    def second():
        tile(other, refs[3 * count + 1])


def down_product(active, weights):
    count = len(active)
    tokens, width = active[0][0].shape
    tile = 256
    half = tokens // tile

    def first(columns):
        return pl.BlockSpec((tile, columns), lambda i: (jnp.minimum(i, half - 1), 0))

    def second(columns):
        return pl.BlockSpec((tile, columns), lambda i: (jnp.maximum(i - half, 0), 0))

    down = pl.BlockSpec((D, width), lambda i: (0, 2), pipeline_mode=pl.Buffered(1))
    return pl.pallas_call(
        functools.partial(down_kernel, count, half),
        grid=(2 * half,),
        in_specs=[first(width)] * count + [second(width)] * count + [down] * count,
        out_specs=[first(D), second(D)],
        out_shape=[jax.ShapeDtypeStruct((tokens, D), BF)] * 2,
        compiler_params=pltpu.CompilerParams(vmem_limit_bytes=VMEM_LIMIT),
        cost_estimate=pl.CostEstimate(
            flops=4 * count * tokens * D * width,
            bytes_accessed=2 * D * (count * width + 2 * tokens),
            transcendentals=0,
        ),
        name="down_product",
    )(*[a for a, _ in active], *[b for _, b in active], *weights)


def grads_kernel(count, *refs):
    rows, grads, by_rows, by_grads = (refs[k * count : (k + 1) * count] for k in range(4))
    out_ref = refs[4 * count]
    split = by_rows[0].shape[1]

    def total(left, right):
        acc = None
        for a, b in zip(left, right):
            term = mm(a[...], b[...], TN)
            acc = term if acc is None else acc + term
        return acc

    out_ref[:, :split] = total(rows, by_rows).astype(BF)
    out_ref[:, split:] = total(grads, by_grads).astype(BF)


def weight_grads(rows, grads, by_rows, by_grads):
    def halves(arrays):
        parts = []
        for a in arrays:
            parts += [(a[0], 0), (a[1], 0)] if isinstance(a, tuple) else [(a, 0), (a, 1)]
        return parts

    groups = [halves(a) for a in (rows, grads, by_rows, by_grads)]
    count = len(groups[0])
    tokens = groups[0][0][0].shape[0] // (1 if isinstance(rows[0], tuple) else 2)
    first, second = groups[2][0][0].shape[1], groups[3][0][0].shape[1]
    tile = 512

    def tall(half):
        return pl.BlockSpec((tokens, tile), lambda i: (half, i))

    def whole(width, half):
        return pl.BlockSpec((tokens, width), lambda i: (half, 0), pipeline_mode=pl.Buffered(1))

    return pl.pallas_call(
        functools.partial(grads_kernel, count),
        grid=(D // tile,),
        in_specs=[tall(half) for _, half in groups[0] + groups[1]]
        + [whole(first, half) for _, half in groups[2]]
        + [whole(second, half) for _, half in groups[3]],
        out_specs=pl.BlockSpec((tile, first + second), lambda i: (i, 0)),
        out_shape=jax.ShapeDtypeStruct((D, first + second), BF),
        compiler_params=pltpu.CompilerParams(vmem_limit_bytes=VMEM_LIMIT),
        cost_estimate=pl.CostEstimate(
            flops=3 * count * tokens * D * (first + second),
            bytes_accessed=2 * (2 * count * tokens * D + (count * tokens + D) * (first + second)),
            transcendentals=0,
        ),
        name="weight_grads",
    )(*[a for group in groups for a, _ in group])


RATE_QKV = D ** (-0.5)
RATE_OUT = 4.0 * (HEADS * HEAD_DIM) ** (-0.5)
RATE_DOWN = FF ** (-0.5)


def clip_factor(small):
    row = lax.broadcasted_iota(jnp.int32, small.shape, 0)
    lane = lax.broadcasted_iota(jnp.int32, small.shape, 1)
    summed = (row == small.shape[0] - 1) & (lane >= HEADS)
    squares = jnp.sum(jnp.where(summed, small, small * small), axis=(0, 1), keepdims=True)
    grad_norm = jnp.sqrt(squares)
    return grad_norm, jnp.minimum(1.0, CLIP / (grad_norm + 1e-06))


def adam_kernel(place_ref, small_ref, *refs):
    ins, grads, outs = refs[:12], refs[12:16], refs[16:]
    factor = clip_factor(small_ref[...])[1]
    is_low = place_ref[0] == 0

    def put(number, place, gradient, rate):
        weight, moment, second = (r[place] for r in ins[3 * number : 3 * number + 3])
        new = adam_update(weight, moment, second, gradient.astype(F32), factor, rate, DECAY)
        for ref, value in zip(outs[3 * number : 3 * number + 3], new):
            ref[place] = value

    mine, theirs = grads[0][...], grads[1][...]
    sides = (jnp.where(is_low, mine, theirs), jnp.where(is_low, theirs, mine))
    width = mine.shape[1] // 4
    everything = slice(None)
    for s, side in enumerate(sides):
        cols = slice(s * width, (s + 1) * width)
        for part in range(3):
            put(0, (part, everything, cols), side[:, part * width : (part + 1) * width], RATE_QKV)
        put(1, (everything, cols), side[:, 3 * width :], RATE_OUT)
    put(2, (everything, everything), grads[2][...], RATE_QKV)
    put(2 + 1, (everything, everything), grads[3][...], RATE_DOWN)


def mlp_view(t):
    rows, _, width_ff = t.shape
    return t.reshape(rows, 2, width_ff // 128, 128).transpose(0, 2, 1, 3).reshape(-1, 128)


def adam_all(small, x_place, arrays, att_mine, att_theirs, grad_mlp, grad_down):
    rows, _, width_ff = arrays[6].shape
    lanes = width_ff // 128

    def qkv_view(t):
        return jnp.transpose(t, (1, 0, 2))

    def mlp_back(t):
        return t.reshape(rows, lanes, 2, 128).transpose(0, 2, 1, 3).reshape(rows, 2, width_ff)

    views = [qkv_view(t) for t in arrays[:3]] + list(arrays[3:6])
    views += [mlp_view(t) for t in arrays[6:9]] + list(arrays[9:])
    grads = [att_mine, att_theirs, grad_mlp, grad_down]
    steps = 8

    def spec(t):
        axis = t.ndim - 2
        block = list(t.shape)
        block[axis] //= steps
        return pl.BlockSpec(tuple(block), lambda i: (0,) * axis + (i, 0))

    new = pl.pallas_call(
        adam_kernel,
        grid=(steps,),
        in_specs=[
            pl.BlockSpec(memory_space=pltpu.SMEM),
            pl.BlockSpec(small.shape, lambda i: (0, 0)),
        ]
        + [spec(t) for t in views + grads],
        out_specs=[spec(t) for t in views],
        out_shape=[jax.ShapeDtypeStruct(t.shape, F32) for t in views],
        compiler_params=pltpu.CompilerParams(vmem_limit_bytes=VMEM_LIMIT),
        cost_estimate=pl.CostEstimate(
            flops=20 * sum(t.size for t in views) // 3,
            bytes_accessed=8 * sum(t.size for t in views),
            transcendentals=0,
        ),
        name="adam",
    )(x_place[None], small, *views, *grads)
    new = list(new)
    return (
        [qkv_view(t) for t in new[:3]] + new[3:6] + [mlp_back(t) for t in new[6:9]] + new[9:]
    )


def on_device(
    inputs,
    doc_ids,
    cotangent,
    weight_qkv,
    moment_qkv,
    second_qkv,
    weight_out,
    moment_out,
    second_out,
    weight_mlp,
    moment_mlp,
    second_mlp,
    weight_down,
    moment_down,
    second_down,
    norm_gains,
    moment_gains,
    second_gains,
    gate_logit,
    moment_gate,
    second_gate,
):
    micro_count, _, seg_count, own_len, _ = inputs.shape
    own_tokens = seg_count * own_len
    x_place = lax.axis_index("x")
    y_place = lax.axis_index("y")
    c_place = lax.axis_index("c")
    is_low = x_place == 0
    orders = [("x", "y") if m % 2 == 0 else ("y", "x") for m in range(micro_count)]

    z_count = D // (2 * weight_qkv.shape[0])

    def half_columns(weight, which):
        width = weight.shape[-1] // 2
        return lax.dynamic_slice_in_dim(weight, which * width, width, axis=weight.ndim - 1)

    def by_place(own, other, axis):
        return jnp.where(
            is_low,
            jnp.concatenate([own, other], axis=axis),
            jnp.concatenate([other, own], axis=axis),
        )

    def exchange_rows(columns_for, send, *earlier):
        theirs = swap(tie(send, *earlier), "x")
        mine = columns_for(x_place)
        both = jnp.zeros((2 * rows, mine.shape[1]), BF)
        both = lax.dynamic_update_slice_in_dim(both, mine, x_place * rows, axis=0)
        return lax.dynamic_update_slice_in_dim(both, theirs, (1 - x_place) * rows, axis=0)

    def fetch(block):
        return lax.all_gather(block, "z", axis=0, tiled=True)

    rows = weight_qkv.shape[0]
    heads = weight_qkv.shape[2] // (2 * HEAD_DIM)
    width_att = heads * HEAD_DIM
    width_ff = weight_down.shape[1] // 2
    width = width_ff // CHUNKS

    def att_columns(which):
        qkv = half_columns(weight_qkv, which).astype(BF).reshape(rows, -1)
        return jnp.concatenate([qkv, half_columns(weight_out, which).astype(BF)], axis=1)

    def ff_columns(k, which):
        start = which * width_ff + k * width
        mlp = lax.dynamic_slice_in_dim(weight_mlp, start, width, axis=2).astype(BF)
        down = lax.dynamic_slice_in_dim(weight_down, start, width, axis=1).astype(BF)
        return jnp.concatenate([mlp[:, 0], mlp[:, 1], down], axis=1)

    send_att = att_columns(1 - x_place)
    shard_att = exchange_rows(att_columns, send_att)
    full_att = fetch(shard_att)
    full_qkv = full_att[:, : 3 * width_att]
    full_out = full_att[:, 3 * width_att :]

    head_start = (y_place * 2 + c_place) * (2 * heads) + x_place * heads
    gate_local = lax.dynamic_slice_in_dim(gate_logit, head_start, heads)
    mixing = jax.nn.sigmoid(gate_local)
    gate_rows = jnp.broadcast_to(mixing[:, None], (heads, HEAD_DIM))

    micros = range(micro_count)
    tokens = 8 * own_tokens
    token_rows = [
        tie(inputs[m, 0], send_att).reshape(own_tokens, D).astype(F32) for m in micros
    ]
    back_low = [cotangent[m, 0].reshape(own_tokens, D) for m in micros]
    all_ids = doc_ids[:, 0]
    for axis in ("y", "c", "x"):
        all_ids = jnp.stack([all_ids, swap(all_ids, axis)], axis=0)
    normed_att = [rms_norm(t, norm_gains[0]).astype(BF) for t in token_rows]
    att_rows = [
        gather_tokens(normed_att[m], *orders[m], shard_att, all_ids) for m in micros
    ]

    shard_ff = []
    full_ff = []
    for k in range(CHUNKS):
        columns_for = functools.partial(ff_columns, k)
        earlier = [p[0] for p in att_rows] if k == 0 else [shard_ff[-1]]
        shard_ff.append(exchange_rows(columns_for, columns_for(1 - x_place), *earlier))
        full_ff.append(fetch(shard_ff[-1]))

    rel_c = jnp.arange(2)[:, None, None] ^ c_place
    rel_y = jnp.arange(2)[None, :, None] ^ y_place
    places = ((rel_y * 2 + rel_c) * own_len + jnp.arange(own_len)).reshape(-1)
    causal = places[:, None] >= places[None, :]
    masks = []
    columns = []
    for m in micros:
        ids = jnp.transpose(all_ids[:, :, :, m], (0, 3, 1, 2, 4)).reshape(2, seg_count, -1)
        same = ids[:, :, :, None] == ids[:, :, None, :]
        masks.append((same & causal).astype(F32))
        last = jnp.max(ids, axis=2)
        previous = jnp.concatenate([jnp.full((2, 1), -1, last.dtype), last[:, :-1]], axis=1)
        reading = ids == previous[:, :, None]
        writing = ids == last[:, :, None]
        keep = jnp.broadcast_to((last == previous)[:, :, None], ids.shape)
        columns.append(jnp.stack([reading, writing, keep], axis=-1).astype(F32))

    slots = (2, 2, 2, seg_count, own_len)
    wheres = [1 if orders[m][0] == "x" else 2 for m in micros]
    projected = []
    combined = []
    hidden = []
    mlp_rows = []
    back_states = [
        gather_start(tie(back_low[m], *[p[0] for p in att_rows]), *orders[m])
        for m in micros
    ]
    for m in micros:
        mine, other = att_rows[m]
        if m == 0:
            mine = tie(mine, *[t for state in back_states for t in state])
        proj = jnp.concatenate([mm(p, full_qkv, NN).astype(BF) for p in (mine, other)], axis=0)
        projected.append(proj.reshape(slots + (3 * width_att,)))
        comb = attention_fwd(projected[m], masks[m], columns[m], gate_rows, wheres[m])
        combined.append(comb.reshape(tokens, width_att))
    half = tokens // 2
    back_states = [gather_across(back_states[m], orders[m][0]) for m in micros]
    back_rows = [gather_core(state) for state in back_states]
    for m in micros:
        ready = combined[m]
        if m > 0:
            ready = tie(ready, *shard_ff, *[state[-1] for state in back_states])
        other = mm(ready[half:], full_out, NT).astype(BF)
        mine = mm(ready[:half], full_out, NT).astype(BF)
        state = scatter_outer(scatter_core(mine, other, own_tokens), orders[m][0])
        hidden.append(token_rows[m] + scatter_inner(state, orders[m][1]))
        normed_mlp = rms_norm(hidden[m], norm_gains[1]).astype(BF)
        mlp_rows.append(gather_tokens(normed_mlp, *orders[m]))

    def exchange_grad(grad):
        mine = lax.dynamic_slice_in_dim(grad, x_place * rows, rows, axis=0)
        theirs = swap(lax.dynamic_slice_in_dim(grad, (1 - x_place) * rows, rows, axis=0), "x")
        return mine, theirs

    def squares_of(grad):
        wide = grad.astype(F32)
        return jnp.sum(wide * wide)

    def reduce_rows(partial):
        return lax.psum_scatter(partial, "z", scatter_dimension=0, tiled=True)

    def products(left, right, totals, dtype):
        terms = [mm(left[p], right, NT) for p in (1, 0)][::-1]
        if totals is not None:
            terms = [a + b for a, b in zip(totals, terms)]
        return tuple(t.astype(dtype) for t in terms)

    active = []
    d_gate_up = []
    own_ff = []
    d_total = [None] * micro_count
    states = [None] * micro_count
    for k in range(CHUNKS):
        active.append([])
        d_gate_up.append([])
        last = k == CHUNKS - 1
        for m in micros:
            rows_in = mlp_rows[m]
            if last and m > 0:
                rows_in = (tie(rows_in[0], *d_total[m - 1]), rows_in[1])
            act, grad = feed_forward(rows_in, back_rows[m], full_ff[k])
            active[k].append(act)
            d_gate_up[k].append(grad)
            if last and m > 0:
                grad = (grad[0], tie(grad[1], states[m - 1][1]))
            dtype = BF if last else F32
            d_total[m] = products(grad, full_ff[k][:, : 2 * width], d_total[m], dtype)
            if last:
                states[m] = scatter_core(*d_total[m], own_tokens)
        if not last:
            grad_ff = weight_grads(mlp_rows, back_rows, d_gate_up[k], active[k])
            own_ff.append(reduce_rows(grad_ff))
            terms = [t for pair in d_total for t in pair]
            full_ff[k + 1] = tie(full_ff[k + 1], grad_ff, *terms)

    outer_states = [scatter_outer(states[m], orders[m][0]) for m in micros]
    last_active = [
        (active[-1][m][0], tie(active[-1][m][1], *[t[1] for t in outer_states])) for m in micros
    ]
    grad_ff = weight_grads(mlp_rows, back_rows, d_gate_up[-1], last_active)
    own_ff.append(reduce_rows(grad_ff))

    gain_grad_att = jnp.zeros((D,), F32)
    gain_grad_mlp = jnp.zeros((D,), F32)
    d_hidden = []
    grad_states = []
    for m in micros:
        keep, send = outer_states[m]
        d_normed = scatter_inner((tie(keep, grad_ff), send), orders[m][1])
        ignored, norm_back = jax.vjp(rms_norm, hidden[m], norm_gains[1])
        d_norm, d_gain = norm_back(d_normed)
        gain_grad_mlp = gain_grad_mlp + d_gain
        d_hidden.append(back_low[m].astype(F32) + d_norm)
        state = gather_start(d_hidden[m].astype(BF), *orders[m])
        grad_states.append(gather_across(state, orders[m][0]))

    gate_sum = jnp.zeros((heads,), F32)
    d_projs = []
    out_states = []
    for m in micros:
        act = [active[k][m] for k in range(CHUNKS)]
        act[-1] = (last_active[m][0], tie(last_active[m][1], *d_hidden))
        mine, other = down_product(act, full_ff)
        out_states.append(scatter_core(mine, other, own_tokens))
    sends = [t[1] for t in out_states]
    out_states = [tie_send(t, *[g[-1] for g in grad_states]) for t in out_states]
    att_grads = [gather_core((tie(g[0], *sends),) + g[1:]) for g in grad_states]
    ff_pairs = [exchange_grad(own_ff[0])]
    for m in micros:
        mine, other = att_grads[m]
        if m == 0:
            other = tie(other, own_ff[0])
        d_combined = jnp.concatenate(
            [mm(mine, full_out, NN), mm(other, full_out, NN)], axis=0
        )
        d_proj, gate_part = attention_bwd(
            projected[m],
            d_combined.reshape(slots + (width_att,)),
            masks[m],
            columns[m],
            gate_rows,
            wheres[m],
        )
        gate_sum = gate_sum + jnp.sum(gate_part, axis=(0, 2))
        d_projs.append(d_proj.reshape(tokens, 3 * width_att))
    out_states = [scatter_outer(out_states[m], orders[m][0], *d_projs) for m in micros]
    by_rows = [d_projs[0], tie(d_projs[-1], *[t[1] for t in out_states])]
    grad_att = weight_grads(att_rows, att_grads, by_rows, combined)
    own_att = reduce_rows(grad_att)
    mlp_out = [scatter_inner(out_states[m], orders[m][1]) for m in micros]
    block_out = [(hidden[m] + mlp_out[m]).astype(BF) for m in micros]

    ff_pairs += [exchange_grad(g) for g in own_ff[1:]]

    def ff_part(start, stop):
        cols = slice(start * width, stop * width)
        low = jnp.concatenate([p[0][:, cols] for p in ff_pairs], axis=1)
        high = jnp.concatenate([p[1][:, cols] for p in ff_pairs], axis=1)
        return by_place(low, high, 1)

    grad_mlp = mlp_view(jnp.stack([ff_part(0, 1), ff_part(1, 2)], axis=1))
    grad_down = ff_part(2, 3)
    ff_owned = sum(squares_of(g) for g in own_ff)

    grad_rows = []
    in_states = []
    for m in micros:
        d_proj = tie(d_projs[m], grad_att, *block_out, own_ff[-1], ff_pairs[0][1])
        other = mm(d_proj[half:], full_qkv, NT).astype(BF)
        mine = mm(d_proj[:half], full_qkv, NT).astype(BF)
        in_states.append(scatter_core(mine, other, own_tokens))
    for m in micros:
        state = scatter_outer(in_states[m], orders[m][0])
        state = tie_send(state, ff_pairs[-1][1], *([grad_mlp, grad_down] if m > 0 else []))
        d_normed = scatter_inner(state, orders[m][1])
        ignored, norm_first = jax.vjp(rms_norm, token_rows[m], norm_gains[0])
        d_norm, d_gain = norm_first(d_normed)
        gain_grad_att = gain_grad_att + d_gain
        grad_rows.append((d_hidden[m] + d_norm).astype(BF))

    att_mine, att_theirs = exchange_grad(own_att)

    gate_grad = gate_sum * mixing * (1.0 - mixing)
    gate_padded = lax.dynamic_update_slice(
        jnp.zeros(gate_logit.shape, F32), gate_grad, (head_start,)
    )
    ff_owned = tie(ff_owned, grad_mlp, grad_down)
    owned = squares_of(own_att) + ff_owned
    small = jnp.concatenate(
        [gain_grad_att, gain_grad_mlp, gate_padded, owned[None], jnp.zeros((111,), F32)]
    ).reshape(-1, 128)
    small = sum_everywhere(small, z_count, att_theirs)
    grad_norm, factor = (t.reshape(()) for t in clip_factor(small))
    flat = small.reshape(-1)
    gains_total = flat[: 2 * D].reshape(2, D)
    gate_total = flat[2 * D : 2 * D + HEADS]
    arrays = [
        weight_qkv,
        moment_qkv,
        second_qkv,
        weight_out,
        moment_out,
        second_out,
        weight_mlp,
        moment_mlp,
        second_mlp,
        weight_down,
        moment_down,
        second_down,
    ]
    new = adam_all(small, x_place, arrays, att_mine, att_theirs, grad_mlp, grad_down)
    gains_new = adam_update(norm_gains, moment_gains, second_gains, gains_total, factor, 0.5, 0.0)
    gate_new = adam_update(gate_logit, moment_gate, second_gate, gate_total, factor, 1.0, 0.0)
    shape = (micro_count, 1, seg_count, own_len, D)
    return (
        jnp.stack(block_out, axis=0).reshape(shape),
        jnp.stack(grad_rows, axis=0).reshape(shape),
        grad_norm,
        *new,
        *gains_new,
        *gate_new,
    )


def solution(mesh):
    seq_count, ctx_count = mesh.devices.shape
    inner = Mesh(
        mesh.devices.reshape(seq_count // 2, 2, ctx_count // 2, 2), ("z", "x", "y", "c")
    )
    seq, ctx = ("z", "x"), ("y", "c")
    rows = P(None, seq, None, ctx, None)
    wide = P(seq, None, ctx)
    flat = P(seq, ctx)
    weights = (wide,) * 3 + (flat,) * 3 + (wide,) * 3 + (flat,) * 3 + (P(),) * 6
    return jax.shard_map(
        on_device,
        mesh=inner,
        in_specs=(rows, P(None, seq, None, ctx), rows) + weights,
        out_specs=(rows, rows, P()) + weights,
        check_vma=False,
    )
```

```python
import functools

import jax
import jax.numpy as jnp
from jax import lax
from jax.experimental import pallas as pl
from jax.experimental.pallas import tpu as pltpu
from jax.sharding import Mesh
from jax.sharding import PartitionSpec as P

D = 2048
HEADS = 16
HEAD_DIM = 128
FF = 8192
STEP_COUNT = 10
CHUNKS = 2

EPS = 1e-06
NEG = -1e30
CLIP = 1.0
BETA1 = 0.9
BETA2 = 0.95
ADAM_EPS = 1e-08
DECAY = 0.1
BF = jnp.bfloat16
F32 = jnp.float32
SCALING = HEAD_DIM ** (-0.5)
VMEM_LIMIT = 48 * 1024 * 1024


def rms_norm(tensor, scaling):
    return tensor * lax.rsqrt(jnp.mean(tensor * tensor, axis=-1, keepdims=True) + EPS) * scaling


def adam_update(weight, moment, second, gradient, factor, step_rate, decay):
    clipped = gradient * factor
    moment = BETA1 * moment + (1.0 - BETA1) * clipped
    second = BETA2 * second + (1.0 - BETA2) * clipped * clipped
    fixed_first = moment / (1.0 - BETA1**STEP_COUNT)
    fixed_second = second / (1.0 - BETA2**STEP_COUNT)
    updated = weight - step_rate * (
        fixed_first / (jnp.sqrt(fixed_second) + ADAM_EPS) + decay * weight
    )
    return (moment, second, updated)


def swap(tensor, axis):
    return lax.ppermute(tensor, axis, [(0, 1), (1, 0)])


def tie(tensor, *earlier):
    return lax.optimization_barrier((tensor,) + earlier)[0]


def gather_start(own, outer, inner, *before_x):
    start = {"x": tie(own, *before_x), "y": own}
    return own, swap(start[inner], inner), swap(start[outer], outer)


def gather_across(state, outer):
    return state + (swap(state[1], outer),)


def gather_core(state):
    mine = jnp.concatenate(state, axis=0)
    return mine, swap(mine, "c")


def gather_tokens(own, outer, inner, *before_x):
    return gather_core(gather_across(gather_start(own, outer, inner, *before_x), outer))


def scatter_core(mine, other, units):
    came = swap(other, "c").reshape(4, units, -1)
    mine = mine.reshape(4, units, -1)
    send = (mine[2:].astype(F32) + came[2:].astype(F32)).astype(BF)
    return mine[:2].astype(F32) + came[:2].astype(F32), send


def scatter_outer(state, outer, *later):
    keep, send = state
    came = tie(swap(send, outer), *later)
    send = (keep[1] + came[1].astype(F32)).astype(BF)
    return keep[0] + came[0].astype(F32), send


def scatter_inner(state, inner):
    keep, send = state
    return keep + swap(send, inner).astype(F32)


def tie_send(state, *earlier):
    return state[0], tie(state[1], *earlier)


def sum_everywhere(tensor, z_count, beside):
    reach = 1
    while reach < z_count:
        tensor = tensor + lax.ppermute(tensor, "z", [(i, i ^ reach) for i in range(z_count)])
        reach *= 2
    tensor = tie(tensor + swap(tensor, "c"), beside)
    for axis in ("y", "x"):
        tensor = tensor + swap(tensor, axis)
    return tensor


def mm(a, b, dims):
    return lax.dot_general(a, b, (dims, ((), ())), preferred_element_type=F32)


NN = ((1,), (0,))
NT = ((1,), (1,))
TN = ((0,), (0,))


def mm_mem(a, b, dims):
    return mm(a.astype(BF), b.astype(BF), dims)


def elu_one(tensor):
    return jnp.where(tensor > 0, tensor + 1.0, jnp.exp(jnp.minimum(tensor, 0.0)))


def elu_slope(tensor):
    low = jnp.where(tensor == 0, 0.5, jnp.exp(jnp.minimum(tensor, 0.0)))
    return jnp.where(tensor > 0, 1.0, low)


def segment_of(ref, r, part):
    block = ref[:, :, r, :, part * HEAD_DIM : (part + 1) * HEAD_DIM]
    return block.reshape(-1, HEAD_DIM)


def memory_forward(qs, ks, vs, cols):
    seg_count = len(qs)
    saved = []
    memory = normer = None
    for r in range(seg_count):
        reading, writing, keep = cols[r]
        sq = elu_one(qs[r].astype(F32))
        sk = elu_one(ks[r].astype(F32))
        value = vs[r].astype(F32)
        rows = sq.shape[0]
        item = dict(sq=sq, sk=sk)
        if r == 0:
            item["recalled"] = jnp.zeros_like(sq)
            change = value
        else:
            both = mm_mem(jnp.concatenate([sq, sk], axis=0), memory, NN)
            num = both[:rows]
            den = 1.0 + jnp.sum(sq * normer, axis=-1, keepdims=True)
            item["recalled"] = reading * num / den
            before = keep * both[rows:]
            kden = 1.0 + keep * jnp.sum(sk * normer, axis=-1, keepdims=True)
            change = value - before / kden
            item.update(num=num, den=den, before=before, kden=kden, memory=memory, normer=normer)
        item["change"] = change
        if r < seg_count - 1:
            write = sk * writing
            fresh = mm_mem(write, change, TN)
            fresh_norm = jnp.sum(write, axis=0, keepdims=True)
            memory = fresh if r == 0 else keep * memory + fresh
            normer = fresh_norm if r == 0 else keep[:1] * normer + fresh_norm
        saved.append(item)
    return saved


def local_probs(query, key, allowed):
    scores = jnp.where(allowed > 0, mm(query, key, NT) * SCALING, NEG)
    exponent = jnp.exp(scores - jnp.max(scores, axis=-1, keepdims=True))
    return exponent / jnp.sum(exponent, axis=-1, keepdims=True)


def columns_of(cols_ref, r):
    cols = cols_ref[r]
    return cols[:, 0:1], cols[:, 1:2], cols[:, 2:3]


def attention_fwd_kernel(heads, proj_ref, mask_ref, cols_ref, gate_ref, out_ref):
    seg_count = mask_ref.shape[0]
    cols = [columns_of(cols_ref, r) for r in range(seg_count)]
    for h in range(heads):
        qs = [segment_of(proj_ref, r, h) for r in range(seg_count)]
        ks = [segment_of(proj_ref, r, heads + h) for r in range(seg_count)]
        vs = [segment_of(proj_ref, r, 2 * heads + h) for r in range(seg_count)]
        saved = memory_forward(qs, ks, vs, cols)
        mixing = gate_ref[h : h + 1]
        for r in range(seg_count):
            prob_low = local_probs(qs[r], ks[r], mask_ref[r]).astype(BF)
            local_out = mm(prob_low, vs[r], NN)
            combined = mixing * saved[r]["recalled"] + (1.0 - mixing) * local_out
            out_ref[:, :, r, :, h * HEAD_DIM : (h + 1) * HEAD_DIM] = combined.astype(BF).reshape(
                out_ref.shape[0], out_ref.shape[1], out_ref.shape[3], HEAD_DIM
            )


def attention_bwd_kernel(
    heads, proj_ref, grad_ref, mask_ref, cols_ref, gate_ref, out_ref, gate_out_ref
):
    seg_count = mask_ref.shape[0]
    cols = [columns_of(cols_ref, r) for r in range(seg_count)]

    def put(r, part, value):
        out_ref[:, :, r, :, part * HEAD_DIM : (part + 1) * HEAD_DIM] = value.astype(BF).reshape(
            out_ref.shape[0], out_ref.shape[1], out_ref.shape[3], HEAD_DIM
        )

    for h in range(heads):
        qs = [segment_of(proj_ref, r, h) for r in range(seg_count)]
        ks = [segment_of(proj_ref, r, heads + h) for r in range(seg_count)]
        vs = [segment_of(proj_ref, r, 2 * heads + h) for r in range(seg_count)]
        saved = memory_forward(qs, ks, vs, cols)
        mixing = gate_ref[h : h + 1]
        gate_sum = jnp.zeros((1, HEAD_DIM), F32)
        d_memory = d_normer = None
        for r in reversed(range(seg_count)):
            reading, writing, keep = cols[r]
            item = saved[r]
            sq, sk = item["sq"], item["sk"]
            rows = sq.shape[0]
            d_combined = segment_of(grad_ref, r, h).astype(F32)
            d_recalled = mixing * d_combined
            d_local = ((1.0 - mixing) * d_combined).astype(BF)
            probs = local_probs(qs[r], ks[r], mask_ref[r])
            prob_low = probs.astype(BF)
            local_out = mm(prob_low, vs[r], NN)
            gate_sum = gate_sum + jnp.sum(
                d_combined * (item["recalled"] - local_out), axis=0, keepdims=True
            )
            d_prob = mm(d_local, vs[r], NT)
            d_value = mm(prob_low, d_local, TN)
            d_scores = (
                probs * (d_prob - jnp.sum(d_prob * probs, axis=-1, keepdims=True))
            ).astype(BF)
            d_query = mm(d_scores, ks[r], NN) * SCALING
            d_key = mm(d_scores, qs[r], TN) * SCALING
            d_sk = None
            d_before = d_kden = None
            if r < seg_count - 1:
                d_change = writing * mm_mem(sk, d_memory, NN)
                d_sk = writing * (mm_mem(item["change"], d_memory, NT) + d_normer)
                d_value = d_value + d_change
                if r > 0:
                    d_before = keep * (-d_change / item["kden"])
                    d_kden = keep * (
                        jnp.sum(d_change * item["before"], axis=-1, keepdims=True)
                        / (item["kden"] * item["kden"])
                    )
            if r > 0:
                d_num = reading * d_recalled / item["den"]
                d_den = -reading * (
                    jnp.sum(d_recalled * item["num"], axis=-1, keepdims=True)
                    / (item["den"] * item["den"])
                )
                if d_before is None:
                    d_sq = mm_mem(d_num, item["memory"], NT) + d_den * item["normer"]
                    new_memory = mm_mem(sq, d_num, TN)
                    new_normer = jnp.sum(sq * d_den, axis=0, keepdims=True)
                else:
                    stacked = jnp.concatenate([d_num, d_before], axis=0)
                    both = mm_mem(stacked, item["memory"], NT)
                    d_sq = both[:rows] + d_den * item["normer"]
                    d_sk = d_sk + both[rows:] + d_kden * item["normer"]
                    new_memory = keep * d_memory + mm_mem(
                        jnp.concatenate([sq, sk], axis=0), stacked, TN
                    )
                    new_normer = keep[:1] * d_normer + jnp.sum(
                        sq * d_den + sk * d_kden, axis=0, keepdims=True
                    )
                d_memory, d_normer = new_memory, new_normer
                d_query = d_query + d_sq * elu_slope(qs[r].astype(F32))
            if d_sk is not None:
                d_key = d_key + d_sk * elu_slope(ks[r].astype(F32))
            put(r, h, d_query)
            put(r, heads + h, d_key)
            put(r, 2 * heads + h, d_value)
        gate_out_ref[h : h + 1] = gate_sum


def block_spec(shape, where):
    dims = list(shape)
    dims[where] = None

    def index(s):
        place = [0] * len(dims)
        place[where] = s
        return tuple(place)

    return pl.BlockSpec(tuple(dims), index)


def attention_fwd(projected, mask, cols, gate_rows, where):
    heads = gate_rows.shape[0]
    out_shape = projected.shape[:-1] + (heads * HEAD_DIM,)
    return pl.pallas_call(
        functools.partial(attention_fwd_kernel, heads),
        grid=(projected.shape[where],),
        in_specs=[
            block_spec(projected.shape, where),
            pl.BlockSpec((None,) + mask.shape[1:], lambda s: (s, 0, 0, 0)),
            pl.BlockSpec((None,) + cols.shape[1:], lambda s: (s, 0, 0, 0)),
            pl.BlockSpec(gate_rows.shape, lambda s: (0, 0)),
        ],
        out_specs=block_spec(out_shape, where),
        out_shape=jax.ShapeDtypeStruct(out_shape, BF),
        compiler_params=pltpu.CompilerParams(vmem_limit_bytes=VMEM_LIMIT),
        cost_estimate=pl.CostEstimate(
            flops=7_600_000_000, bytes_accessed=3_000_000, transcendentals=0
        ),
        name="attention_forward",
    )(projected, mask, cols, gate_rows)


def attention_bwd(projected, d_combined, mask, cols, gate_rows, where):
    heads = gate_rows.shape[0]
    seqs = projected.shape[where]
    return pl.pallas_call(
        functools.partial(attention_bwd_kernel, heads),
        grid=(seqs,),
        in_specs=[
            block_spec(projected.shape, where),
            block_spec(d_combined.shape, where),
            pl.BlockSpec((None,) + mask.shape[1:], lambda s: (s, 0, 0, 0)),
            pl.BlockSpec((None,) + cols.shape[1:], lambda s: (s, 0, 0, 0)),
            pl.BlockSpec(gate_rows.shape, lambda s: (0, 0)),
        ],
        out_specs=[
            block_spec(projected.shape, where),
            pl.BlockSpec((None, heads, HEAD_DIM), lambda s: (s, 0, 0)),
        ],
        out_shape=[
            jax.ShapeDtypeStruct(projected.shape, BF),
            jax.ShapeDtypeStruct((seqs, heads, HEAD_DIM), F32),
        ],
        compiler_params=pltpu.CompilerParams(vmem_limit_bytes=VMEM_LIMIT),
        cost_estimate=pl.CostEstimate(
            flops=14_400_000_000, bytes_accessed=5_000_000, transcendentals=0
        ),
        name="attention_backward",
    )(projected, d_combined, mask, cols, gate_rows)


GELU_A = 0.7978845608028654
GELU_B = 0.044715


def ff_kernel(width, half, x_mine, x_other, g_mine, g_other, w_ref, *outs):
    step = pl.program_id(0)

    @pl.when(step < half)
    def first():
        ff_tile(width, x_mine, g_mine, w_ref, outs[0], outs[2])

    @pl.when(step >= half)
    def second():
        ff_tile(width, x_other, g_other, w_ref, outs[1], outs[3])


def ff_tile(width, x_ref, g_ref, w_ref, act_ref, grad_ref):
    weights = w_ref[...]
    gate_up = mm(x_ref[...], weights[:, : 2 * width], NN)
    d_active = mm(g_ref[...], weights[:, 2 * width :], NN)
    gate = gate_up[:, :width]
    up = gate_up[:, width:]
    square = gate * gate
    tanh = jnp.tanh(GELU_A * gate * (1.0 + GELU_B * square))
    half = 0.5 * (1.0 + tanh)
    gelu = gate * half
    slope = half + 0.5 * gate * (1.0 - tanh * tanh) * GELU_A * (1.0 + 3.0 * GELU_B * square)
    act_ref[...] = (gelu * up).astype(BF)
    grad_ref[:, :width] = (d_active * up * slope).astype(BF)
    grad_ref[:, width:] = (d_active * gelu).astype(BF)


def feed_forward(rows, grads, weights):
    tokens = rows[0].shape[0]
    width = weights.shape[1] // 3
    tile = 256
    half = tokens // tile

    def first(columns):
        return pl.BlockSpec((tile, columns), lambda i: (jnp.minimum(i, half - 1), 0))

    def second(columns):
        return pl.BlockSpec((tile, columns), lambda i: (jnp.maximum(i - half, 0), 0))

    whole = pl.BlockSpec(weights.shape, lambda i: (0, 0), pipeline_mode=pl.Buffered(1))
    act = jax.ShapeDtypeStruct((tokens, width), BF)
    grad = jax.ShapeDtypeStruct((tokens, 2 * width), BF)
    out = pl.pallas_call(
        functools.partial(ff_kernel, width, half),
        grid=(2 * half,),
        in_specs=[first(D), second(D), first(D), second(D), whole],
        out_specs=[first(width), second(width), first(2 * width), second(2 * width)],
        out_shape=[act, act, grad, grad],
        compiler_params=pltpu.CompilerParams(vmem_limit_bytes=VMEM_LIMIT),
        cost_estimate=pl.CostEstimate(
            flops=26 * tokens * D * width, bytes_accessed=tokens * D, transcendentals=0
        ),
        name="feed_forward",
    )(*rows, *grads, weights)
    return (out[0], out[1]), (out[2], out[3])


def down_kernel(count, half, *refs):
    step = pl.program_id(0)
    mine, other, weights = (refs[k * count : (k + 1) * count] for k in range(3))

    def tile(rows, out_ref):
        terms = [mm(a[...], w[...], NT) for a, w in zip(rows, weights)]
        out_ref[...] = sum(terms[1:], terms[0]).astype(BF)

    @pl.when(step < half)
    def first():
        tile(mine, refs[3 * count])

    @pl.when(step >= half)
    def second():
        tile(other, refs[3 * count + 1])


def down_product(active, weights):
    count = len(active)
    tokens, width = active[0][0].shape
    tile = 256
    half = tokens // tile

    def first(columns):
        return pl.BlockSpec((tile, columns), lambda i: (jnp.minimum(i, half - 1), 0))

    def second(columns):
        return pl.BlockSpec((tile, columns), lambda i: (jnp.maximum(i - half, 0), 0))

    down = pl.BlockSpec((D, width), lambda i: (0, 2), pipeline_mode=pl.Buffered(1))
    return pl.pallas_call(
        functools.partial(down_kernel, count, half),
        grid=(2 * half,),
        in_specs=[first(width)] * count + [second(width)] * count + [down] * count,
        out_specs=[first(D), second(D)],
        out_shape=[jax.ShapeDtypeStruct((tokens, D), BF)] * 2,
        compiler_params=pltpu.CompilerParams(vmem_limit_bytes=VMEM_LIMIT),
        cost_estimate=pl.CostEstimate(
            flops=4 * count * tokens * D * width,
            bytes_accessed=2 * D * (count * width + 2 * tokens),
            transcendentals=0,
        ),
        name="down_product",
    )(*[a for a, _ in active], *[b for _, b in active], *weights)


def grads_kernel(count, *refs):
    rows, grads, by_rows, by_grads = (refs[k * count : (k + 1) * count] for k in range(4))
    out_ref = refs[4 * count]
    split = by_rows[0].shape[1]

    def total(left, right):
        acc = None
        for a, b in zip(left, right):
            term = mm(a[...], b[...], TN)
            acc = term if acc is None else acc + term
        return acc

    out_ref[:, :split] = total(rows, by_rows).astype(BF)
    out_ref[:, split:] = total(grads, by_grads).astype(BF)


def weight_grads(rows, grads, by_rows, by_grads):
    def halves(arrays):
        parts = []
        for a in arrays:
            parts += [(a[0], 0), (a[1], 0)] if isinstance(a, tuple) else [(a, 0), (a, 1)]
        return parts

    groups = [halves(a) for a in (rows, grads, by_rows, by_grads)]
    count = len(groups[0])
    tokens = groups[0][0][0].shape[0] // (1 if isinstance(rows[0], tuple) else 2)
    first, second = groups[2][0][0].shape[1], groups[3][0][0].shape[1]
    tile = 512

    def tall(half):
        return pl.BlockSpec((tokens, tile), lambda i: (half, i))

    def whole(width, half):
        return pl.BlockSpec((tokens, width), lambda i: (half, 0), pipeline_mode=pl.Buffered(1))

    return pl.pallas_call(
        functools.partial(grads_kernel, count),
        grid=(D // tile,),
        in_specs=[tall(half) for _, half in groups[0] + groups[1]]
        + [whole(first, half) for _, half in groups[2]]
        + [whole(second, half) for _, half in groups[3]],
        out_specs=pl.BlockSpec((tile, first + second), lambda i: (i, 0)),
        out_shape=jax.ShapeDtypeStruct((D, first + second), BF),
        compiler_params=pltpu.CompilerParams(vmem_limit_bytes=VMEM_LIMIT),
        cost_estimate=pl.CostEstimate(
            flops=3 * count * tokens * D * (first + second),
            bytes_accessed=2 * (2 * count * tokens * D + (count * tokens + D) * (first + second)),
            transcendentals=0,
        ),
        name="weight_grads",
    )(*[a for group in groups for a, _ in group])


RATE_QKV = D ** (-0.5)
RATE_OUT = 4.0 * (HEADS * HEAD_DIM) ** (-0.5)
RATE_DOWN = FF ** (-0.5)


def clip_factor(small):
    row = lax.broadcasted_iota(jnp.int32, small.shape, 0)
    lane = lax.broadcasted_iota(jnp.int32, small.shape, 1)
    summed = (row == small.shape[0] - 1) & (lane >= HEADS)
    squares = jnp.sum(jnp.where(summed, small, small * small), axis=(0, 1), keepdims=True)
    grad_norm = jnp.sqrt(squares)
    return grad_norm, jnp.minimum(1.0, CLIP / (grad_norm + 1e-06))


def adam_kernel(steps, chunks, place_ref, small_ref, *refs):
    ins, refs = refs[:15], refs[15:]
    grads, refs = refs[: 2 + 2 * chunks], refs[2 + 2 * chunks :]
    outs, scratch = refs[:15], refs[15]
    factor = clip_factor(small_ref[...])[1]
    is_low = place_ref[0] == 0
    everything = slice(None)

    def put(number, place, gradient, rate, decay=DECAY):
        weight, moment, second = (r[place] for r in ins[3 * number : 3 * number + 3])
        new = adam_update(weight, moment, second, gradient.astype(F32), factor, rate, decay)
        for ref, value in zip(outs[3 * number : 3 * number + 3], new):
            ref[place] = value

    def sides_of(mine, theirs):
        mine, theirs = mine[...], theirs[...]
        return jnp.where(is_low, mine, theirs), jnp.where(is_low, theirs, mine)

    for s, side in enumerate(sides_of(*grads[:2])):
        width = side.shape[1] // 4
        cols = slice(s * width, (s + 1) * width)
        for part in range(3):
            put(0, (part, everything, cols), side[:, part * width : (part + 1) * width], RATE_QKV)
        put(1, (everything, cols), side[:, 3 * width :], RATE_OUT)
    rows, width_ff = ins[9].shape
    lanes = width_ff // 128
    for k in range(chunks):
        for s, side in enumerate(sides_of(*grads[2 + 2 * k : 4 + 2 * k])):
            side = side.astype(F32)
            width = side.shape[1] // 3
            start = s * (width_ff // 2) + k * width
            put(3, (everything, slice(start, start + width)), side[:, 2 * width :], RATE_DOWN)
            for part in range(2):
                for lane in range(width // 128):
                    place = pl.ds((start // 128 + lane) * 2 + part, rows, stride=2 * lanes)
                    first = part * width + lane * 128
                    scratch[place, :] = side[:, first : first + 128]
    put(2, (everything, everything), scratch[...], RATE_QKV)

    @pl.when(pl.program_id(0) == 0)
    def gains():
        put(4, (everything, everything), small_ref[: ins[12].shape[0]], 0.5, 0.0)


def mlp_view(t):
    rows, _, width_ff = t.shape
    return t.reshape(rows, 2, width_ff // 128, 128).transpose(0, 2, 1, 3).reshape(-1, 128)


def adam_all(small, x_place, arrays, att_sides, ff_sides):
    rows, _, width_ff = arrays[6].shape
    steps = 4

    def qkv_view(t):
        return jnp.transpose(t, (1, 0, 2))

    def mlp_back(t, shape):
        rows, _, width_ff = shape
        t = t.reshape(rows, width_ff // 128, 2, 128).transpose(0, 2, 1, 3)
        return t.reshape(shape)

    views = [qkv_view(t) for t in arrays[:3]] + list(arrays[3:6])
    views += [mlp_view(t) for t in arrays[6:9]] + list(arrays[9:12])
    gains = [mlp_view(t[None]) for t in arrays[12:]]
    grads = list(att_sides) + [t for pair in ff_sides for t in pair]

    def spec(t):
        axis = t.ndim - 2
        block = list(t.shape)
        block[axis] //= steps
        return pl.BlockSpec(tuple(block), lambda i, place: (0,) * axis + (i, 0))

    def whole(t):
        return pl.BlockSpec(t.shape, lambda i, place: (0, 0))

    def mine(t):
        return pl.BlockSpec((rows // steps, t.shape[1]), lambda i, place: (place[0] * steps + i, 0))

    specs = [spec(t) for t in views] + [whole(t) for t in gains]
    new = pl.pallas_call(
        functools.partial(adam_kernel, steps, len(ff_sides)),
        grid_spec=pltpu.PrefetchScalarGridSpec(
            num_scalar_prefetch=1,
            grid=(steps,),
            in_specs=[whole(small)]
            + specs
            + [spec(t) if k % 2 else mine(t) for k, t in enumerate(grads)],
            out_specs=specs,
            scratch_shapes=[pltpu.VMEM((views[6].shape[0] // steps, 128), F32)],
        ),
        out_shape=[jax.ShapeDtypeStruct(t.shape, F32) for t in views + gains],
        compiler_params=pltpu.CompilerParams(vmem_limit_bytes=VMEM_LIMIT),
        cost_estimate=pl.CostEstimate(
            flops=20 * sum(t.size for t in views) // 3,
            bytes_accessed=8 * sum(t.size for t in views),
            transcendentals=0,
        ),
        name="adam",
    )(x_place[None], small, *views, *gains, *grads)
    new = list(new)
    return (
        [qkv_view(t) for t in new[:3]]
        + new[3:6]
        + [mlp_back(t, arrays[6].shape) for t in new[6:9]]
        + new[9:12]
        + [mlp_back(t, (1,) + arrays[12].shape)[0] for t in new[12:]]
    )


def on_device(
    inputs,
    doc_ids,
    cotangent,
    weight_qkv,
    moment_qkv,
    second_qkv,
    weight_out,
    moment_out,
    second_out,
    weight_mlp,
    moment_mlp,
    second_mlp,
    weight_down,
    moment_down,
    second_down,
    norm_gains,
    moment_gains,
    second_gains,
    gate_logit,
    moment_gate,
    second_gate,
):
    micro_count, _, seg_count, own_len, _ = inputs.shape
    own_tokens = seg_count * own_len
    x_place = lax.axis_index("x")
    y_place = lax.axis_index("y")
    c_place = lax.axis_index("c")
    is_low = x_place == 0
    orders = [("x", "y") if m % 2 == 0 else ("y", "x") for m in range(micro_count)]

    z_count = D // (2 * weight_qkv.shape[0])

    def half_columns(weight, which):
        width = weight.shape[-1] // 2
        return lax.dynamic_slice_in_dim(weight, which * width, width, axis=weight.ndim - 1)

    def by_place(own, other, axis):
        return jnp.where(
            is_low,
            jnp.concatenate([own, other], axis=axis),
            jnp.concatenate([other, own], axis=axis),
        )

    def exchange_rows(columns_for, send, *earlier):
        theirs = swap(tie(send, *earlier), "x")
        mine = columns_for(x_place)
        both = jnp.zeros((2 * rows, mine.shape[1]), BF)
        both = lax.dynamic_update_slice_in_dim(both, mine, x_place * rows, axis=0)
        return lax.dynamic_update_slice_in_dim(both, theirs, (1 - x_place) * rows, axis=0)

    def fetch(block):
        return lax.all_gather(block, "z", axis=0, tiled=True)

    rows = weight_qkv.shape[0]
    heads = weight_qkv.shape[2] // (2 * HEAD_DIM)
    width_att = heads * HEAD_DIM
    width_ff = weight_down.shape[1] // 2
    width = width_ff // CHUNKS

    def att_columns(which):
        qkv = half_columns(weight_qkv, which).astype(BF).reshape(rows, -1)
        return jnp.concatenate([qkv, half_columns(weight_out, which).astype(BF)], axis=1)

    def ff_columns(k, which):
        start = which * width_ff + k * width
        mlp = lax.dynamic_slice_in_dim(weight_mlp, start, width, axis=2).astype(BF)
        down = lax.dynamic_slice_in_dim(weight_down, start, width, axis=1).astype(BF)
        return jnp.concatenate([mlp[:, 0], mlp[:, 1], down], axis=1)

    send_att = att_columns(1 - x_place)
    shard_att = exchange_rows(att_columns, send_att)
    full_att = fetch(shard_att)
    full_qkv = full_att[:, : 3 * width_att]
    full_out = full_att[:, 3 * width_att :]

    head_start = (y_place * 2 + c_place) * (2 * heads) + x_place * heads
    gate_local = lax.dynamic_slice_in_dim(gate_logit, head_start, heads)
    mixing = jax.nn.sigmoid(gate_local)
    gate_rows = jnp.broadcast_to(mixing[:, None], (heads, HEAD_DIM))

    micros = range(micro_count)
    tokens = 8 * own_tokens
    token_rows = [
        tie(inputs[m, 0], send_att).reshape(own_tokens, D).astype(F32) for m in micros
    ]
    back_low = [cotangent[m, 0].reshape(own_tokens, D) for m in micros]
    all_ids = tie(doc_ids[:, 0], shard_att)
    for axis in ("y", "c", "x"):
        all_ids = jnp.stack([all_ids, swap(all_ids, axis)], axis=0)
    normed_att = [rms_norm(t, norm_gains[0]).astype(BF) for t in token_rows]
    att_rows = [
        gather_tokens(normed_att[m], *orders[m], shard_att) for m in micros
    ]

    shard_ff = []
    full_ff = []
    for k in range(CHUNKS):
        columns_for = functools.partial(ff_columns, k)
        earlier = [p[0] for p in att_rows] if k == 0 else [shard_ff[-1]]
        shard_ff.append(exchange_rows(columns_for, columns_for(1 - x_place), *earlier))
        full_ff.append(fetch(shard_ff[-1]))

    rel_c = jnp.arange(2)[:, None, None] ^ c_place
    rel_y = jnp.arange(2)[None, :, None] ^ y_place
    places = ((rel_y * 2 + rel_c) * own_len + jnp.arange(own_len)).reshape(-1)
    causal = places[:, None] >= places[None, :]
    masks = []
    columns = []
    for m in micros:
        ids = jnp.transpose(all_ids[:, :, :, m], (0, 3, 1, 2, 4)).reshape(2, seg_count, -1)
        same = ids[:, :, :, None] == ids[:, :, None, :]
        masks.append((same & causal).astype(F32))
        last = jnp.max(ids, axis=2)
        previous = jnp.concatenate([jnp.full((2, 1), -1, last.dtype), last[:, :-1]], axis=1)
        reading = ids == previous[:, :, None]
        writing = ids == last[:, :, None]
        keep = jnp.broadcast_to((last == previous)[:, :, None], ids.shape)
        columns.append(jnp.stack([reading, writing, keep], axis=-1).astype(F32))

    slots = (2, 2, 2, seg_count, own_len)
    wheres = [1 if orders[m][0] == "x" else 2 for m in micros]
    projected = []
    combined = []
    hidden = []
    mlp_rows = []
    back_states = [
        gather_start(tie(back_low[m], all_ids, *[p[0] for p in att_rows]), *orders[m])
        for m in micros
    ]
    for m in micros:
        mine, other = att_rows[m]
        if m == 0:
            mine = tie(mine, *[t for state in back_states for t in state])
        proj = jnp.concatenate([mm(p, full_qkv, NN).astype(BF) for p in (mine, other)], axis=0)
        projected.append(proj.reshape(slots + (3 * width_att,)))
        comb = attention_fwd(projected[m], masks[m], columns[m], gate_rows, wheres[m])
        combined.append(comb.reshape(tokens, width_att))
    half = tokens // 2
    back_states = [gather_across(back_states[m], orders[m][0]) for m in micros]
    back_rows = [gather_core(state) for state in back_states]
    for m in micros:
        ready = combined[m]
        if m > 0:
            ready = tie(ready, *shard_ff, *[state[-1] for state in back_states])
        other = mm(ready[half:], full_out, NT).astype(BF)
        mine = mm(ready[:half], full_out, NT).astype(BF)
        state = scatter_outer(scatter_core(mine, other, own_tokens), orders[m][0])
        hidden.append(token_rows[m] + scatter_inner(state, orders[m][1]))
        normed_mlp = rms_norm(hidden[m], norm_gains[1]).astype(BF)
        mlp_rows.append(gather_tokens(normed_mlp, *orders[m]))

    def exchange_grad(grad):
        return grad, swap(lax.dynamic_slice_in_dim(grad, (1 - x_place) * rows, rows, axis=0), "x")

    def squares_of(grad):
        wide = grad.astype(F32)
        return jnp.sum(wide * wide)

    def reduce_rows(partial):
        return lax.psum_scatter(partial, "z", scatter_dimension=0, tiled=True)

    def products(left, right, totals, dtype):
        terms = [mm(left[p], right, NT) for p in (1, 0)][::-1]
        if totals is not None:
            terms = [a + b for a, b in zip(totals, terms)]
        return tuple(t.astype(dtype) for t in terms)

    active = []
    d_gate_up = []
    own_ff = []
    d_total = [None] * micro_count
    states = [None] * micro_count
    for k in range(CHUNKS):
        active.append([])
        d_gate_up.append([])
        last = k == CHUNKS - 1
        for m in micros:
            rows_in = mlp_rows[m]
            if last and m > 0:
                rows_in = (tie(rows_in[0], *d_total[m - 1]), rows_in[1])
            act, grad = feed_forward(rows_in, back_rows[m], full_ff[k])
            active[k].append(act)
            d_gate_up[k].append(grad)
            if last and m > 0:
                grad = (grad[0], tie(grad[1], states[m - 1][1]))
            dtype = BF if last else F32
            d_total[m] = products(grad, full_ff[k][:, : 2 * width], d_total[m], dtype)
            if last:
                states[m] = scatter_core(*d_total[m], own_tokens)
        if not last:
            grad_ff = weight_grads(mlp_rows, back_rows, d_gate_up[k], active[k])
            own_ff.append(reduce_rows(grad_ff))
            terms = [t for pair in d_total for t in pair]
            full_ff[k + 1] = tie(full_ff[k + 1], grad_ff, *terms)

    outer_states = [scatter_outer(states[m], orders[m][0]) for m in micros]
    last_active = [
        (active[-1][m][0], tie(active[-1][m][1], *[t[1] for t in outer_states])) for m in micros
    ]
    grad_ff = weight_grads(mlp_rows, back_rows, d_gate_up[-1], last_active)
    own_ff.append(reduce_rows(grad_ff))

    gain_grad_att = jnp.zeros((D,), F32)
    gain_grad_mlp = jnp.zeros((D,), F32)
    d_hidden = []
    grad_states = []
    for m in micros:
        keep, send = outer_states[m]
        d_normed = scatter_inner((tie(keep, grad_ff), send), orders[m][1])
        ignored, norm_back = jax.vjp(rms_norm, hidden[m], norm_gains[1])
        d_norm, d_gain = norm_back(d_normed)
        gain_grad_mlp = gain_grad_mlp + d_gain
        d_hidden.append(back_low[m].astype(F32) + d_norm)
        state = gather_start(d_hidden[m].astype(BF), *orders[m])
        grad_states.append(gather_across(state, orders[m][0]))

    gate_sum = jnp.zeros((heads,), F32)
    d_projs = []
    out_states = []
    for m in micros:
        act = [active[k][m] for k in range(CHUNKS)]
        act[-1] = (last_active[m][0], tie(last_active[m][1], *d_hidden))
        mine, other = down_product(act, full_ff)
        out_states.append(scatter_core(mine, other, own_tokens))
    sends = [t[1] for t in out_states]
    out_states = [tie_send(t, *[g[-1] for g in grad_states]) for t in out_states]
    att_grads = [gather_core((tie(g[0], *sends),) + g[1:]) for g in grad_states]
    ff_pairs = [exchange_grad(own_ff[0])]
    for m in micros:
        mine, other = att_grads[m]
        if m == 0:
            other = tie(other, own_ff[0])
        d_combined = jnp.concatenate(
            [mm(mine, full_out, NN), mm(other, full_out, NN)], axis=0
        )
        d_proj, gate_part = attention_bwd(
            projected[m],
            d_combined.reshape(slots + (width_att,)),
            masks[m],
            columns[m],
            gate_rows,
            wheres[m],
        )
        gate_sum = gate_sum + jnp.sum(gate_part, axis=(0, 2))
        d_projs.append(d_proj.reshape(tokens, 3 * width_att))
    out_states = [scatter_outer(out_states[m], orders[m][0], d_projs[0]) for m in micros]
    by_rows = [d_projs[0], tie(d_projs[-1], ff_pairs[0][1], *[t[1] for t in out_states])]
    grad_att = weight_grads(att_rows, att_grads, by_rows, combined)
    own_att = reduce_rows(grad_att)
    mlp_out = [scatter_inner(out_states[m], orders[m][1]) for m in micros]
    block_out = [(hidden[m] + mlp_out[m]).astype(BF) for m in micros]

    ff_pairs += [exchange_grad(g) for g in own_ff[1:]]

    ff_owned = sum(squares_of(g) for g in own_ff)

    grad_rows = []
    in_states = []
    for m in micros:
        d_proj = tie(d_projs[m], grad_att)
        other = mm(d_proj[half:], full_qkv, NT).astype(BF)
        mine = mm(d_proj[:half], full_qkv, NT).astype(BF)
        in_states.append(scatter_core(mine, other, own_tokens))
    for m in micros:
        state = scatter_outer(in_states[m], orders[m][0])
        if m > 0:
            state = tie_send(state, ff_pairs[-1][1])
        d_normed = scatter_inner(state, orders[m][1])
        ignored, norm_first = jax.vjp(rms_norm, token_rows[m], norm_gains[0])
        d_norm, d_gain = norm_first(d_normed)
        gain_grad_att = gain_grad_att + d_gain
        grad_rows.append((d_hidden[m] + d_norm).astype(BF))

    att_mine, att_theirs = exchange_grad(own_att)

    gate_grad = gate_sum * mixing * (1.0 - mixing)
    gate_padded = lax.dynamic_update_slice(
        jnp.zeros(gate_logit.shape, F32), gate_grad, (head_start,)
    )
    owned = squares_of(own_att) + ff_owned
    gain_grad = mlp_view(jnp.stack([gain_grad_att, gain_grad_mlp], axis=0)[None])
    last_row = jnp.concatenate([gate_padded, owned[None], jnp.zeros((127 - HEADS,), F32)])
    small = jnp.concatenate([gain_grad, last_row[None]], axis=0)
    small = sum_everywhere(small, z_count, att_theirs)
    arrays = [
        weight_qkv,
        moment_qkv,
        second_qkv,
        weight_out,
        moment_out,
        second_out,
        weight_mlp,
        moment_mlp,
        second_mlp,
        weight_down,
        moment_down,
        second_down,
        norm_gains,
        moment_gains,
        second_gains,
    ]
    new = adam_all(small, x_place, arrays, (att_mine, att_theirs), ff_pairs)
    new = [new[3 * n + k] for n in range(5) for k in (0, 1, 2)]
    grad_norm, factor = (t.reshape(()) for t in clip_factor(tie(small, new[0])))
    gate_total = small[-1, :HEADS]
    gate_new = adam_update(gate_logit, moment_gate, second_gate, gate_total, factor, 1.0, 0.0)
    shape = (micro_count, 1, seg_count, own_len, D)
    return (
        jnp.stack(block_out, axis=0).reshape(shape),
        jnp.stack(grad_rows, axis=0).reshape(shape),
        grad_norm,
        *new,
        *gate_new,
    )


def solution(mesh):
    seq_count, ctx_count = mesh.devices.shape
    inner = Mesh(
        mesh.devices.reshape(seq_count // 2, 2, ctx_count // 2, 2), ("z", "x", "y", "c")
    )
    seq, ctx = ("z", "x"), ("y", "c")
    rows = P(None, seq, None, ctx, None)
    wide = P(seq, None, ctx)
    flat = P(seq, ctx)
    weights = (wide,) * 3 + (flat,) * 3 + (wide,) * 3 + (flat,) * 3 + (P(),) * 6
    return jax.shard_map(
        on_device,
        mesh=inner,
        in_specs=(rows, P(None, seq, None, ctx), rows) + weights,
        out_specs=(rows, rows, P()) + weights,
        check_vma=False,
    )
```

```python
import functools

import jax
import jax.numpy as jnp
from jax import lax
from jax.experimental import pallas as pl
from jax.experimental.pallas import tpu as pltpu
from jax.sharding import Mesh
from jax.sharding import PartitionSpec as P

D = 2048
HEADS = 16
HEAD_DIM = 128
FF = 8192
STEP_COUNT = 10
CHUNKS = 2

EPS = 1e-06
NEG = -1e30
CLIP = 1.0
BETA1 = 0.9
BETA2 = 0.95
ADAM_EPS = 1e-08
DECAY = 0.1
BF = jnp.bfloat16
F32 = jnp.float32
SCALING = HEAD_DIM ** (-0.5)
VMEM_LIMIT = 48 * 1024 * 1024


def rms_norm(tensor, scaling):
    return tensor * lax.rsqrt(jnp.mean(tensor * tensor, axis=-1, keepdims=True) + EPS) * scaling


def adam_update(weight, moment, second, gradient, factor, step_rate, decay):
    clipped = gradient * factor
    moment = BETA1 * moment + (1.0 - BETA1) * clipped
    second = BETA2 * second + (1.0 - BETA2) * clipped * clipped
    fixed_first = moment / (1.0 - BETA1**STEP_COUNT)
    fixed_second = second / (1.0 - BETA2**STEP_COUNT)
    updated = weight - step_rate * (
        fixed_first / (jnp.sqrt(fixed_second) + ADAM_EPS) + decay * weight
    )
    return (moment, second, updated)


def swap(tensor, axis):
    return lax.ppermute(tensor, axis, [(0, 1), (1, 0)])


def tie(tensor, *earlier):
    return lax.optimization_barrier((tensor,) + earlier)[0]


def gather_start(own, outer, inner, *before_x):
    start = {"x": tie(own, *before_x), "y": own}
    return own, swap(start[inner], inner), swap(start[outer], outer)


def gather_across(state, outer):
    return state + (swap(state[1], outer),)


def gather_core(state):
    mine = jnp.concatenate(state, axis=0)
    return mine, swap(mine, "c")


def gather_tokens(own, outer, inner, *before_x):
    return gather_core(gather_across(gather_start(own, outer, inner, *before_x), outer))


def scatter_core(mine, other, units):
    came = swap(other, "c").reshape(4, units, -1)
    mine = mine.reshape(4, units, -1)
    send = (mine[2:].astype(F32) + came[2:].astype(F32)).astype(BF)
    return mine[:2].astype(F32) + came[:2].astype(F32), send


def scatter_outer(state, outer, *later):
    keep, send = state
    came = tie(swap(send, outer), *later)
    send = (keep[1] + came[1].astype(F32)).astype(BF)
    return keep[0] + came[0].astype(F32), send


def scatter_inner(state, inner):
    keep, send = state
    return keep + swap(send, inner).astype(F32)


def tie_pair(pair, *earlier):
    return pair[0], tie(pair[1], *earlier)


def tie_send(state, *earlier):
    return state[0], tie(state[1], *earlier)


def sum_everywhere(tensor, z_count, beside):
    def add(tensor, axis, pairs):
        return tensor + lax.ppermute(tensor, axis, pairs)

    tensor = add(tensor, "x", [(0, 1), (1, 0)])
    reach = 1
    while reach < z_count:
        tensor = add(tensor, "z", [(i, i ^ reach) for i in range(z_count)])
        reach *= 2
    tensor = add(tensor, "c", [(0, 1), (1, 0)])
    return add(tie(tensor, beside), "y", [(0, 1), (1, 0)])


def mm(a, b, dims):
    return lax.dot_general(a, b, (dims, ((), ())), preferred_element_type=F32)


NN = ((1,), (0,))
NT = ((1,), (1,))
TN = ((0,), (0,))


def mm_mem(a, b, dims):
    return mm(a.astype(BF), b.astype(BF), dims)


def elu_one(tensor):
    return jnp.where(tensor > 0, tensor + 1.0, jnp.exp(jnp.minimum(tensor, 0.0)))


def elu_slope(tensor):
    low = jnp.where(tensor == 0, 0.5, jnp.exp(jnp.minimum(tensor, 0.0)))
    return jnp.where(tensor > 0, 1.0, low)


def segment_of(ref, r, part):
    block = ref[:, :, r, :, part * HEAD_DIM : (part + 1) * HEAD_DIM]
    return block.reshape(-1, HEAD_DIM)


def memory_forward(qs, ks, vs, cols):
    seg_count = len(qs)
    saved = []
    memory = normer = None
    for r in range(seg_count):
        reading, writing, keep = cols[r]
        sq = elu_one(qs[r].astype(F32))
        sk = elu_one(ks[r].astype(F32))
        value = vs[r].astype(F32)
        rows = sq.shape[0]
        item = dict(sq=sq, sk=sk)
        if r == 0:
            item["recalled"] = jnp.zeros_like(sq)
            change = value
        else:
            both = mm_mem(jnp.concatenate([sq, sk], axis=0), memory, NN)
            num = both[:rows]
            den = 1.0 + jnp.sum(sq * normer, axis=-1, keepdims=True)
            item["recalled"] = reading * num / den
            before = keep * both[rows:]
            kden = 1.0 + keep * jnp.sum(sk * normer, axis=-1, keepdims=True)
            change = value - before / kden
            item.update(num=num, den=den, before=before, kden=kden, memory=memory, normer=normer)
        item["change"] = change
        if r < seg_count - 1:
            write = sk * writing
            fresh = mm_mem(write, change, TN)
            fresh_norm = jnp.sum(write, axis=0, keepdims=True)
            memory = fresh if r == 0 else keep * memory + fresh
            normer = fresh_norm if r == 0 else keep[:1] * normer + fresh_norm
        saved.append(item)
    return saved


def local_probs(query, key, allowed):
    scores = jnp.where(allowed > 0, mm(query, key, NT) * SCALING, NEG)
    exponent = jnp.exp(scores - jnp.max(scores, axis=-1, keepdims=True))
    return exponent / jnp.sum(exponent, axis=-1, keepdims=True)


def columns_of(cols_ref, r):
    cols = cols_ref[r]
    return cols[:, 0:1], cols[:, 1:2], cols[:, 2:3]


def attention_fwd_kernel(heads, proj_ref, mask_ref, cols_ref, gate_ref, out_ref):
    seg_count = mask_ref.shape[0]
    cols = [columns_of(cols_ref, r) for r in range(seg_count)]
    for h in range(heads):
        qs = [segment_of(proj_ref, r, h) for r in range(seg_count)]
        ks = [segment_of(proj_ref, r, heads + h) for r in range(seg_count)]
        vs = [segment_of(proj_ref, r, 2 * heads + h) for r in range(seg_count)]
        saved = memory_forward(qs, ks, vs, cols)
        mixing = gate_ref[h : h + 1]
        for r in range(seg_count):
            prob_low = local_probs(qs[r], ks[r], mask_ref[r]).astype(BF)
            local_out = mm(prob_low, vs[r], NN)
            combined = mixing * saved[r]["recalled"] + (1.0 - mixing) * local_out
            out_ref[:, :, r, :, h * HEAD_DIM : (h + 1) * HEAD_DIM] = combined.astype(BF).reshape(
                out_ref.shape[0], out_ref.shape[1], out_ref.shape[3], HEAD_DIM
            )


def attention_bwd_kernel(
    heads, proj_ref, grad_ref, mask_ref, cols_ref, gate_ref, out_ref, gate_out_ref
):
    seg_count = mask_ref.shape[0]
    cols = [columns_of(cols_ref, r) for r in range(seg_count)]

    def put(r, part, value):
        out_ref[:, :, r, :, part * HEAD_DIM : (part + 1) * HEAD_DIM] = value.astype(BF).reshape(
            out_ref.shape[0], out_ref.shape[1], out_ref.shape[3], HEAD_DIM
        )

    for h in range(heads):
        qs = [segment_of(proj_ref, r, h) for r in range(seg_count)]
        ks = [segment_of(proj_ref, r, heads + h) for r in range(seg_count)]
        vs = [segment_of(proj_ref, r, 2 * heads + h) for r in range(seg_count)]
        saved = memory_forward(qs, ks, vs, cols)
        mixing = gate_ref[h : h + 1]
        gate_sum = jnp.zeros((1, HEAD_DIM), F32)
        d_memory = d_normer = None
        for r in reversed(range(seg_count)):
            reading, writing, keep = cols[r]
            item = saved[r]
            sq, sk = item["sq"], item["sk"]
            rows = sq.shape[0]
            d_combined = segment_of(grad_ref, r, h).astype(F32)
            d_recalled = mixing * d_combined
            d_local = ((1.0 - mixing) * d_combined).astype(BF)
            probs = local_probs(qs[r], ks[r], mask_ref[r])
            prob_low = probs.astype(BF)
            local_out = mm(prob_low, vs[r], NN)
            gate_sum = gate_sum + jnp.sum(
                d_combined * (item["recalled"] - local_out), axis=0, keepdims=True
            )
            d_prob = mm(d_local, vs[r], NT)
            d_value = mm(prob_low, d_local, TN)
            d_scores = (
                probs * (d_prob - jnp.sum(d_prob * probs, axis=-1, keepdims=True))
            ).astype(BF)
            d_query = mm(d_scores, ks[r], NN) * SCALING
            d_key = mm(d_scores, qs[r], TN) * SCALING
            d_sk = None
            d_before = d_kden = None
            if r < seg_count - 1:
                d_change = writing * mm_mem(sk, d_memory, NN)
                d_sk = writing * (mm_mem(item["change"], d_memory, NT) + d_normer)
                d_value = d_value + d_change
                if r > 0:
                    d_before = keep * (-d_change / item["kden"])
                    d_kden = keep * (
                        jnp.sum(d_change * item["before"], axis=-1, keepdims=True)
                        / (item["kden"] * item["kden"])
                    )
            if r > 0:
                d_num = reading * d_recalled / item["den"]
                d_den = -reading * (
                    jnp.sum(d_recalled * item["num"], axis=-1, keepdims=True)
                    / (item["den"] * item["den"])
                )
                if d_before is None:
                    d_sq = mm_mem(d_num, item["memory"], NT) + d_den * item["normer"]
                    new_memory = mm_mem(sq, d_num, TN)
                    new_normer = jnp.sum(sq * d_den, axis=0, keepdims=True)
                else:
                    stacked = jnp.concatenate([d_num, d_before], axis=0)
                    both = mm_mem(stacked, item["memory"], NT)
                    d_sq = both[:rows] + d_den * item["normer"]
                    d_sk = d_sk + both[rows:] + d_kden * item["normer"]
                    new_memory = keep * d_memory + mm_mem(
                        jnp.concatenate([sq, sk], axis=0), stacked, TN
                    )
                    new_normer = keep[:1] * d_normer + jnp.sum(
                        sq * d_den + sk * d_kden, axis=0, keepdims=True
                    )
                d_memory, d_normer = new_memory, new_normer
                d_query = d_query + d_sq * elu_slope(qs[r].astype(F32))
            if d_sk is not None:
                d_key = d_key + d_sk * elu_slope(ks[r].astype(F32))
            put(r, h, d_query)
            put(r, heads + h, d_key)
            put(r, 2 * heads + h, d_value)
        gate_out_ref[h : h + 1] = gate_sum


def block_spec(shape, where):
    dims = list(shape)
    dims[where] = None

    def index(s):
        place = [0] * len(dims)
        place[where] = s
        return tuple(place)

    return pl.BlockSpec(tuple(dims), index)


def attention_fwd(projected, mask, cols, gate_rows, where):
    heads = gate_rows.shape[0]
    out_shape = projected.shape[:-1] + (heads * HEAD_DIM,)
    return pl.pallas_call(
        functools.partial(attention_fwd_kernel, heads),
        grid=(projected.shape[where],),
        in_specs=[
            block_spec(projected.shape, where),
            pl.BlockSpec((None,) + mask.shape[1:], lambda s: (s, 0, 0, 0)),
            pl.BlockSpec((None,) + cols.shape[1:], lambda s: (s, 0, 0, 0)),
            pl.BlockSpec(gate_rows.shape, lambda s: (0, 0)),
        ],
        out_specs=block_spec(out_shape, where),
        out_shape=jax.ShapeDtypeStruct(out_shape, BF),
        compiler_params=pltpu.CompilerParams(vmem_limit_bytes=VMEM_LIMIT),
        cost_estimate=pl.CostEstimate(
            flops=7_600_000_000, bytes_accessed=3_000_000, transcendentals=0
        ),
        name="attention_forward",
    )(projected, mask, cols, gate_rows)


def attention_bwd(projected, d_combined, mask, cols, gate_rows, where):
    heads = gate_rows.shape[0]
    seqs = projected.shape[where]
    return pl.pallas_call(
        functools.partial(attention_bwd_kernel, heads),
        grid=(seqs,),
        in_specs=[
            block_spec(projected.shape, where),
            block_spec(d_combined.shape, where),
            pl.BlockSpec((None,) + mask.shape[1:], lambda s: (s, 0, 0, 0)),
            pl.BlockSpec((None,) + cols.shape[1:], lambda s: (s, 0, 0, 0)),
            pl.BlockSpec(gate_rows.shape, lambda s: (0, 0)),
        ],
        out_specs=[
            block_spec(projected.shape, where),
            pl.BlockSpec((None, heads, HEAD_DIM), lambda s: (s, 0, 0)),
        ],
        out_shape=[
            jax.ShapeDtypeStruct(projected.shape, BF),
            jax.ShapeDtypeStruct((seqs, heads, HEAD_DIM), F32),
        ],
        compiler_params=pltpu.CompilerParams(vmem_limit_bytes=VMEM_LIMIT),
        cost_estimate=pl.CostEstimate(
            flops=14_400_000_000, bytes_accessed=5_000_000, transcendentals=0
        ),
        name="attention_backward",
    )(projected, d_combined, mask, cols, gate_rows)


GELU_A = 0.7978845608028654
GELU_B = 0.044715


def ff_kernel(width, half, x_mine, x_other, g_mine, g_other, w_ref, *outs):
    step = pl.program_id(0)

    @pl.when(step < half)
    def first():
        ff_tile(width, x_mine, g_mine, w_ref, outs[0], outs[2])

    @pl.when(step >= half)
    def second():
        ff_tile(width, x_other, g_other, w_ref, outs[1], outs[3])


def ff_tile(width, x_ref, g_ref, w_ref, act_ref, grad_ref):
    weights = w_ref[...]
    gate_up = mm(x_ref[...], weights[:, : 2 * width], NN)
    d_active = mm(g_ref[...], weights[:, 2 * width :], NN)
    gate = gate_up[:, :width]
    up = gate_up[:, width:]
    square = gate * gate
    tanh = jnp.tanh(GELU_A * gate * (1.0 + GELU_B * square))
    half = 0.5 * (1.0 + tanh)
    gelu = gate * half
    slope = half + 0.5 * gate * (1.0 - tanh * tanh) * GELU_A * (1.0 + 3.0 * GELU_B * square)
    act_ref[...] = (gelu * up).astype(BF)
    grad_ref[:, :width] = (d_active * up * slope).astype(BF)
    grad_ref[:, width:] = (d_active * gelu).astype(BF)


def feed_forward(rows, grads, weights):
    tokens = rows[0].shape[0]
    width = weights.shape[1] // 3
    tile = 256
    half = tokens // tile

    def first(columns):
        return pl.BlockSpec((tile, columns), lambda i: (jnp.minimum(i, half - 1), 0))

    def second(columns):
        return pl.BlockSpec((tile, columns), lambda i: (jnp.maximum(i - half, 0), 0))

    whole = pl.BlockSpec(weights.shape, lambda i: (0, 0), pipeline_mode=pl.Buffered(1))
    act = jax.ShapeDtypeStruct((tokens, width), BF)
    grad = jax.ShapeDtypeStruct((tokens, 2 * width), BF)
    out = pl.pallas_call(
        functools.partial(ff_kernel, width, half),
        grid=(2 * half,),
        in_specs=[first(D), second(D), first(D), second(D), whole],
        out_specs=[first(width), second(width), first(2 * width), second(2 * width)],
        out_shape=[act, act, grad, grad],
        compiler_params=pltpu.CompilerParams(vmem_limit_bytes=VMEM_LIMIT),
        cost_estimate=pl.CostEstimate(
            flops=26 * tokens * D * width, bytes_accessed=tokens * D, transcendentals=0
        ),
        name="feed_forward",
    )(*rows, *grads, weights)
    return (out[0], out[1]), (out[2], out[3])


def down_kernel(count, half, *refs):
    step = pl.program_id(0)
    mine, other, weights = (refs[k * count : (k + 1) * count] for k in range(3))

    def tile(rows, out_ref):
        terms = [mm(a[...], w[...], NT) for a, w in zip(rows, weights)]
        out_ref[...] = sum(terms[1:], terms[0]).astype(BF)

    @pl.when(step < half)
    def first():
        tile(mine, refs[3 * count])

    @pl.when(step >= half)
    def second():
        tile(other, refs[3 * count + 1])


def down_product(active, weights):
    count = len(active)
    tokens, width = active[0][0].shape
    tile = 256
    half = tokens // tile

    def first(columns):
        return pl.BlockSpec((tile, columns), lambda i: (jnp.minimum(i, half - 1), 0))

    def second(columns):
        return pl.BlockSpec((tile, columns), lambda i: (jnp.maximum(i - half, 0), 0))

    down = pl.BlockSpec((D, width), lambda i: (0, 2), pipeline_mode=pl.Buffered(1))
    return pl.pallas_call(
        functools.partial(down_kernel, count, half),
        grid=(2 * half,),
        in_specs=[first(width)] * count + [second(width)] * count + [down] * count,
        out_specs=[first(D), second(D)],
        out_shape=[jax.ShapeDtypeStruct((tokens, D), BF)] * 2,
        compiler_params=pltpu.CompilerParams(vmem_limit_bytes=VMEM_LIMIT),
        cost_estimate=pl.CostEstimate(
            flops=4 * count * tokens * D * width,
            bytes_accessed=2 * D * (count * width + 2 * tokens),
            transcendentals=0,
        ),
        name="down_product",
    )(*[a for a, _ in active], *[b for _, b in active], *weights)


def grads_kernel(count, *refs):
    rows, grads, by_rows, by_grads = (refs[k * count : (k + 1) * count] for k in range(4))
    out_ref = refs[4 * count]
    split = by_rows[0].shape[1]

    def total(left, right):
        acc = None
        for a, b in zip(left, right):
            term = mm(a[...], b[...], TN)
            acc = term if acc is None else acc + term
        return acc

    out_ref[:, :split] = total(rows, by_rows).astype(BF)
    out_ref[:, split:] = total(grads, by_grads).astype(BF)


def weight_grads(rows, grads, by_rows, by_grads):
    def halves(arrays):
        parts = []
        for a in arrays:
            parts += [(a[0], 0), (a[1], 0)] if isinstance(a, tuple) else [(a, 0), (a, 1)]
        return parts

    groups = [halves(a) for a in (rows, grads, by_rows, by_grads)]
    count = len(groups[0])
    tokens = groups[0][0][0].shape[0] // (1 if isinstance(rows[0], tuple) else 2)
    first, second = groups[2][0][0].shape[1], groups[3][0][0].shape[1]
    tile = 512

    def tall(half):
        return pl.BlockSpec((tokens, tile), lambda i: (half, i))

    def whole(width, half):
        return pl.BlockSpec((tokens, width), lambda i: (half, 0), pipeline_mode=pl.Buffered(1))

    return pl.pallas_call(
        functools.partial(grads_kernel, count),
        grid=(D // tile,),
        in_specs=[tall(half) for _, half in groups[0] + groups[1]]
        + [whole(first, half) for _, half in groups[2]]
        + [whole(second, half) for _, half in groups[3]],
        out_specs=pl.BlockSpec((tile, first + second), lambda i: (i, 0)),
        out_shape=jax.ShapeDtypeStruct((D, first + second), BF),
        compiler_params=pltpu.CompilerParams(vmem_limit_bytes=VMEM_LIMIT),
        cost_estimate=pl.CostEstimate(
            flops=3 * count * tokens * D * (first + second),
            bytes_accessed=2 * (2 * count * tokens * D + (count * tokens + D) * (first + second)),
            transcendentals=0,
        ),
        name="weight_grads",
    )(*[a for group in groups for a, _ in group])


RATE_QKV = D ** (-0.5)
RATE_OUT = 4.0 * (HEADS * HEAD_DIM) ** (-0.5)
RATE_DOWN = FF ** (-0.5)


def clip_factor(small):
    row = lax.broadcasted_iota(jnp.int32, small.shape, 0)
    lane = lax.broadcasted_iota(jnp.int32, small.shape, 1)
    summed = (row == small.shape[0] - 1) & (lane >= HEADS)
    squares = jnp.sum(jnp.where(summed, small, small * small), axis=(0, 1), keepdims=True)
    grad_norm = jnp.sqrt(squares)
    return grad_norm, jnp.minimum(1.0, CLIP / (grad_norm + 1e-06))


def adam_kernel(steps, chunks, place_ref, small_ref, *refs):
    ins, refs = refs[:18], refs[18:]
    grads, refs = refs[: 2 + 2 * chunks], refs[2 + 2 * chunks :]
    outs, norm_ref, scratch = refs[:18], refs[18], refs[19]
    grad_norm, factor = clip_factor(small_ref[...])
    is_low = place_ref[0] == 0
    everything = slice(None)

    def put(number, place, gradient, rate, decay=DECAY):
        weight, moment, second = (r[place] for r in ins[3 * number : 3 * number + 3])
        new = adam_update(weight, moment, second, gradient.astype(F32), factor, rate, decay)
        for ref, value in zip(outs[3 * number : 3 * number + 3], new):
            ref[place] = value

    def sides_of(mine, theirs):
        mine, theirs = mine[...], theirs[...]
        return jnp.where(is_low, mine, theirs), jnp.where(is_low, theirs, mine)

    for s, side in enumerate(sides_of(*grads[:2])):
        width = side.shape[1] // 4
        cols = slice(s * width, (s + 1) * width)
        for part in range(3):
            put(0, (part, everything, cols), side[:, part * width : (part + 1) * width], RATE_QKV)
        put(1, (everything, cols), side[:, 3 * width :], RATE_OUT)
    rows, width_ff = ins[9].shape
    lanes = width_ff // 128
    for k in range(chunks):
        for s, side in enumerate(sides_of(*grads[2 + 2 * k : 4 + 2 * k])):
            side = side.astype(F32)
            width = side.shape[1] // 3
            start = s * (width_ff // 2) + k * width
            put(3, (everything, slice(start, start + width)), side[:, 2 * width :], RATE_DOWN)
            for part in range(2):
                for lane in range(width // 128):
                    place = pl.ds((start // 128 + lane) * 2 + part, rows, stride=2 * lanes)
                    first = part * width + lane * 128
                    scratch[place, :] = side[:, first : first + 128]
    put(2, (everything, everything), scratch[...], RATE_QKV)

    @pl.when(pl.program_id(0) == 0)
    def small_ones():
        last = ins[12].shape[0]
        put(4, (everything, everything), small_ref[:last], 0.5, 0.0)
        put(5, (everything, everything), small_ref[last:, :HEADS], 1.0, 0.0)
        norm_ref[...] = grad_norm


def mlp_view(t):
    rows, _, width_ff = t.shape
    return t.reshape(rows, 2, width_ff // 128, 128).transpose(0, 2, 1, 3).reshape(-1, 128)


def adam_all(small, x_place, arrays, att_sides, ff_sides):
    rows, _, width_ff = arrays[6].shape
    steps = 4

    def qkv_view(t):
        return jnp.transpose(t, (1, 0, 2))

    def mlp_back(t, shape):
        rows, _, width_ff = shape
        t = t.reshape(rows, width_ff // 128, 2, 128).transpose(0, 2, 1, 3)
        return t.reshape(shape)

    views = [qkv_view(t) for t in arrays[:3]] + list(arrays[3:6])
    views += [mlp_view(t) for t in arrays[6:9]] + list(arrays[9:12])
    gains = [mlp_view(t[None]) for t in arrays[12:15]] + [t[None] for t in arrays[15:]]
    grads = list(att_sides) + [t for pair in ff_sides for t in pair]

    def spec(t):
        axis = t.ndim - 2
        block = list(t.shape)
        block[axis] //= steps
        return pl.BlockSpec(tuple(block), lambda i, place: (0,) * axis + (i, 0))

    def whole(t):
        return pl.BlockSpec(t.shape, lambda i, place: (0, 0))

    def mine(t):
        return pl.BlockSpec((rows // steps, t.shape[1]), lambda i, place: (place[0] * steps + i, 0))

    specs = [spec(t) for t in views] + [whole(t) for t in gains]
    new = pl.pallas_call(
        functools.partial(adam_kernel, steps, len(ff_sides)),
        grid_spec=pltpu.PrefetchScalarGridSpec(
            num_scalar_prefetch=1,
            grid=(steps,),
            in_specs=[whole(small)]
            + specs
            + [spec(t) if k % 2 else mine(t) for k, t in enumerate(grads)],
            out_specs=specs + [pl.BlockSpec((1, 1), lambda i, place: (0, 0))],
            scratch_shapes=[pltpu.VMEM((views[6].shape[0] // steps, 128), F32)],
        ),
        out_shape=[jax.ShapeDtypeStruct(t.shape, F32) for t in views + gains]
        + [jax.ShapeDtypeStruct((1, 1), F32)],
        compiler_params=pltpu.CompilerParams(vmem_limit_bytes=VMEM_LIMIT),
        cost_estimate=pl.CostEstimate(
            flops=20 * sum(t.size for t in views) // 3,
            bytes_accessed=8 * sum(t.size for t in views),
            transcendentals=0,
        ),
        name="adam",
    )(x_place[None], small, *views, *gains, *grads)
    new = list(new)
    return (
        [qkv_view(t) for t in new[:3]]
        + new[3:6]
        + [mlp_back(t, arrays[6].shape) for t in new[6:9]]
        + new[9:12]
        + [mlp_back(t, (1,) + arrays[12].shape)[0] for t in new[12:15]]
        + [t[0] for t in new[15:18]]
        + [new[18].reshape(())]
    )


def on_device(
    inputs,
    doc_ids,
    cotangent,
    weight_qkv,
    moment_qkv,
    second_qkv,
    weight_out,
    moment_out,
    second_out,
    weight_mlp,
    moment_mlp,
    second_mlp,
    weight_down,
    moment_down,
    second_down,
    norm_gains,
    moment_gains,
    second_gains,
    gate_logit,
    moment_gate,
    second_gate,
):
    micro_count, _, seg_count, own_len, _ = inputs.shape
    own_tokens = seg_count * own_len
    x_place = lax.axis_index("x")
    y_place = lax.axis_index("y")
    c_place = lax.axis_index("c")
    orders = [("x", "y") if m % 2 == 0 else ("y", "x") for m in range(micro_count)]

    z_count = D // (2 * weight_qkv.shape[0])

    def half_columns(weight, which):
        width = weight.shape[-1] // 2
        return lax.dynamic_slice_in_dim(weight, which * width, width, axis=weight.ndim - 1)

    def join_rows(mine, theirs):
        both = jnp.zeros((2 * rows, mine.shape[1]), BF)
        both = lax.dynamic_update_slice_in_dim(both, mine, x_place * rows, axis=0)
        return lax.dynamic_update_slice_in_dim(both, theirs, (1 - x_place) * rows, axis=0)

    def fetch(block):
        return lax.all_gather(block, "z", axis=0, tiled=True)

    rows = weight_qkv.shape[0]
    heads = weight_qkv.shape[2] // (2 * HEAD_DIM)
    width_att = heads * HEAD_DIM
    width_ff = weight_down.shape[1] // 2
    width = width_ff // CHUNKS

    def qkv_columns(which):
        return half_columns(weight_qkv, which).astype(BF).reshape(rows, -1)

    def ff_columns(k, which):
        start = which * width_ff + k * width
        mlp = lax.dynamic_slice_in_dim(mlp_later, start, width, axis=2).astype(BF)
        down = lax.dynamic_slice_in_dim(down_later, start, width, axis=1).astype(BF)
        return jnp.concatenate([mlp[:, 0], mlp[:, 1], down], axis=1)

    send_qkv = qkv_columns(1 - x_place)
    all_out = fetch(weight_out.astype(BF))
    all_ids = doc_ids[:, 0]
    for axis in ("y", "c"):
        all_ids = jnp.stack([all_ids, swap(all_ids, axis)], axis=0)
    their_qkv = swap(send_qkv, "x")
    shard_qkv = join_rows(qkv_columns(x_place), tie(their_qkv, all_ids))
    full_qkv = fetch(shard_qkv)

    head_start = (y_place * 2 + c_place) * (2 * heads) + x_place * heads
    gate_local = lax.dynamic_slice_in_dim(gate_logit, head_start, heads)
    mixing = jax.nn.sigmoid(gate_local)
    gate_rows = jnp.broadcast_to(mixing[:, None], (heads, HEAD_DIM))

    micros = range(micro_count)
    tokens = 8 * own_tokens
    token_rows = [
        tie(inputs[m, 0], send_qkv).reshape(own_tokens, D).astype(F32) for m in micros
    ]
    back_low = [cotangent[m, 0].reshape(own_tokens, D) for m in micros]
    all_ids = jnp.stack([all_ids, swap(all_ids, "x")], axis=0)
    normed_att = [rms_norm(t, norm_gains[0]).astype(BF) for t in token_rows]
    att_states = [gather_start(normed_att[m], *orders[m], their_qkv, all_ids) for m in micros]
    mlp_later = tie(weight_mlp, *[t for state in att_states for t in state[1:]])
    down_later = tie(weight_down, *[t for state in att_states for t in state[1:]])
    att_states = [gather_across(att_states[m], orders[m][0]) for m in micros]
    att_rows = [gather_core(state) for state in att_states]

    att_last = [state[-1] for state in att_states]
    back_states = [gather_start(tie(back_low[m], *att_last), *orders[m]) for m in micros]
    back_first = [t for state in back_states for t in state[1:]]
    shard_ff = []
    full_ff = []
    earlier = back_first
    for k in range(CHUNKS):
        theirs = swap(tie(ff_columns(k, 1 - x_place), *earlier), "x")
        shard_ff.append(join_rows(ff_columns(k, x_place), theirs))
        full_ff.append(fetch(shard_ff[k]))
        if k == 0:
            their_out = swap(tie(half_columns(all_out, 1 - x_place), theirs), "x")
            both_out = jnp.zeros((z_count, 2, rows, width_att), BF)
            for part, place in ((half_columns(all_out, x_place), x_place), (their_out, 1 - x_place)):
                part = part.reshape(z_count, 1, rows, width_att)
                both_out = lax.dynamic_update_slice_in_dim(both_out, part, place, axis=1)
            full_out = both_out.reshape(D, width_att)
            back_states = [
                gather_across((state[0], tie(state[1], their_out), state[2]), orders[m][0])
                for m, state in enumerate(back_states)
            ]
            earlier = [state[-1] for state in back_states]
        else:
            earlier = [theirs]
    back_rows = [gather_core(state) for state in back_states]

    rel_c = jnp.arange(2)[:, None, None] ^ c_place
    rel_y = jnp.arange(2)[None, :, None] ^ y_place
    places = ((rel_y * 2 + rel_c) * own_len + jnp.arange(own_len)).reshape(-1)
    causal = places[:, None] >= places[None, :]
    masks = []
    columns = []
    for m in micros:
        ids = jnp.transpose(all_ids[:, :, :, m], (0, 3, 1, 2, 4)).reshape(2, seg_count, -1)
        same = ids[:, :, :, None] == ids[:, :, None, :]
        masks.append((same & causal).astype(F32))
        last = jnp.max(ids, axis=2)
        previous = jnp.concatenate([jnp.full((2, 1), -1, last.dtype), last[:, :-1]], axis=1)
        reading = ids == previous[:, :, None]
        writing = ids == last[:, :, None]
        keep = jnp.broadcast_to((last == previous)[:, :, None], ids.shape)
        columns.append(jnp.stack([reading, writing, keep], axis=-1).astype(F32))

    slots = (2, 2, 2, seg_count, own_len)
    wheres = [1 if orders[m][0] == "x" else 2 for m in micros]
    projected = []
    combined = []
    hidden = []
    mlp_rows = []
    for m in micros:
        mine, other = att_rows[m]
        if m == 0:
            mine = tie(mine, *back_first, shard_ff[0])
        proj = jnp.concatenate([mm(p, full_qkv, NN).astype(BF) for p in (mine, other)], axis=0)
        projected.append(proj.reshape(slots + (3 * width_att,)))
        comb = attention_fwd(projected[m], masks[m], columns[m], gate_rows, wheres[m])
        combined.append(comb.reshape(tokens, width_att))
    half = tokens // 2
    for m in micros:
        ready = combined[m]
        if m > 0:
            ready = tie(ready, *shard_ff, *[state[-1] for state in back_states])
        other = mm(ready[half:], full_out, NT).astype(BF)
        mine = mm(ready[:half], full_out, NT).astype(BF)
        state = scatter_outer(scatter_core(mine, other, own_tokens), orders[m][0])
        hidden.append(token_rows[m] + scatter_inner(state, orders[m][1]))
        normed_mlp = rms_norm(hidden[m], norm_gains[1]).astype(BF)
        mlp_rows.append(gather_tokens(normed_mlp, *orders[m]))

    def exchange_grad(grad):
        return grad, swap(lax.dynamic_slice_in_dim(grad, (1 - x_place) * rows, rows, axis=0), "x")

    def squares_of(grad):
        wide = grad.astype(F32)
        return jnp.sum(wide * wide)

    def reduce_rows(partial):
        return lax.psum_scatter(partial, "z", scatter_dimension=0, tiled=True)

    def products(left, right, totals, dtype):
        terms = [mm(left[p], right, NT) for p in (1, 0)][::-1]
        if totals is not None:
            terms = [a + b for a, b in zip(totals, terms)]
        return tuple(t.astype(dtype) for t in terms)

    active = []
    d_gate_up = []
    own_ff = []
    d_total = [None] * micro_count
    states = [None] * micro_count
    for k in range(CHUNKS):
        active.append([])
        d_gate_up.append([])
        last = k == CHUNKS - 1
        for m in micros:
            rows_in = mlp_rows[m]
            if last and m > 0:
                rows_in = (tie(rows_in[0], *d_total[m - 1]), rows_in[1])
            act, grad = feed_forward(rows_in, back_rows[m], full_ff[k])
            active[k].append(act)
            d_gate_up[k].append(grad)
            if last and m > 0:
                grad = (grad[0], tie(grad[1], states[m - 1][1]))
            dtype = BF if last else F32
            d_total[m] = products(grad, full_ff[k][:, : 2 * width], d_total[m], dtype)
            if last:
                states[m] = scatter_core(*d_total[m], own_tokens)
        if not last:
            grad_ff = weight_grads(mlp_rows, back_rows, d_gate_up[k], active[k])
            own_ff.append(reduce_rows(grad_ff))
            terms = [t for pair in d_total for t in pair]
            full_ff[k + 1] = tie(full_ff[k + 1], grad_ff, *terms)

    out_pairs = []
    for m in micros:
        act = [active[k][m] for k in range(CHUNKS)]
        act[-1] = (act[-1][0], tie(act[-1][1], states[-1][1]))
        out_pairs.append(down_product(act, full_ff))
    products_done = [t for pair in out_pairs for t in pair]
    outer_states = [scatter_outer(states[m], orders[m][0], *products_done) for m in micros]
    last_active = [
        (active[-1][m][0], tie(active[-1][m][1], *[t[1] for t in outer_states])) for m in micros
    ]
    grad_ff = weight_grads(mlp_rows, back_rows, d_gate_up[-1], last_active)
    own_ff.append(reduce_rows(grad_ff))

    gain_grad_att = jnp.zeros((D,), F32)
    gain_grad_mlp = jnp.zeros((D,), F32)
    d_hidden = []
    grad_states = []
    for m in micros:
        keep, send = outer_states[m]
        d_normed = scatter_inner((tie(keep, grad_ff), send), orders[m][1])
        ignored, norm_back = jax.vjp(rms_norm, hidden[m], norm_gains[1])
        d_norm, d_gain = norm_back(d_normed)
        gain_grad_mlp = gain_grad_mlp + d_gain
        d_hidden.append(back_low[m].astype(F32) + d_norm)
        state = gather_start(d_hidden[m].astype(BF), *orders[m])
        grad_states.append(gather_across(state, orders[m][0]))

    gate_sum = jnp.zeros((heads,), F32)
    d_projs = []
    out_states = [scatter_core(*tie_pair(out_pairs[m], *d_hidden), own_tokens) for m in micros]
    sends = [t[1] for t in out_states]
    out_states = [tie_send(t, *[g[-1] for g in grad_states]) for t in out_states]
    att_grads = [gather_core((tie(g[0], *sends),) + g[1:]) for g in grad_states]
    ff_pairs = [exchange_grad(own_ff[0])]
    for m in micros:
        mine, other = att_grads[m]
        if m == 0:
            other = tie(other, own_ff[0])
        d_combined = jnp.concatenate(
            [mm(mine, full_out, NN), mm(other, full_out, NN)], axis=0
        )
        d_proj, gate_part = attention_bwd(
            projected[m],
            d_combined.reshape(slots + (width_att,)),
            masks[m],
            columns[m],
            gate_rows,
            wheres[m],
        )
        gate_sum = gate_sum + jnp.sum(gate_part, axis=(0, 2))
        d_projs.append(d_proj.reshape(tokens, 3 * width_att))
    out_states = [scatter_outer(out_states[m], orders[m][0], d_projs[0]) for m in micros]
    by_rows = [d_projs[0], tie(d_projs[-1], ff_pairs[0][1], *[t[1] for t in out_states])]
    grad_att = weight_grads(att_rows, att_grads, by_rows, combined)
    own_att = reduce_rows(grad_att)
    mlp_out = [scatter_inner(out_states[m], orders[m][1]) for m in micros]
    block_out = [(hidden[m] + mlp_out[m]).astype(BF) for m in micros]

    ff_pairs += [exchange_grad(g) for g in own_ff[1:]]

    ff_owned = sum(squares_of(g) for g in own_ff)

    grad_rows = []
    in_states = []
    for m in micros:
        d_proj = tie(d_projs[m], grad_att)
        other = mm(d_proj[half:], full_qkv, NT).astype(BF)
        mine = mm(d_proj[:half], full_qkv, NT).astype(BF)
        in_states.append(scatter_core(mine, other, own_tokens))
    for m in micros:
        state = scatter_outer(in_states[m], orders[m][0])
        if m > 0:
            state = tie_send(state, ff_pairs[-1][1])
        d_normed = scatter_inner(state, orders[m][1])
        ignored, norm_first = jax.vjp(rms_norm, token_rows[m], norm_gains[0])
        d_norm, d_gain = norm_first(d_normed)
        gain_grad_att = gain_grad_att + d_gain
        grad_rows.append((d_hidden[m] + d_norm).astype(BF))

    att_mine, att_theirs = exchange_grad(own_att)

    gate_grad = gate_sum * mixing * (1.0 - mixing)
    gate_padded = lax.dynamic_update_slice(
        jnp.zeros(gate_logit.shape, F32), gate_grad, (head_start,)
    )
    owned = squares_of(own_att) + ff_owned
    gain_grad = mlp_view(jnp.stack([gain_grad_att, gain_grad_mlp], axis=0)[None])
    last_row = jnp.concatenate([gate_padded, owned[None], jnp.zeros((127 - HEADS,), F32)])
    small = jnp.concatenate([gain_grad, last_row[None]], axis=0)
    small = sum_everywhere(small, z_count, att_theirs)
    arrays = [
        weight_qkv,
        moment_qkv,
        second_qkv,
        weight_out,
        moment_out,
        second_out,
        weight_mlp,
        moment_mlp,
        second_mlp,
        weight_down,
        moment_down,
        second_down,
        norm_gains,
        moment_gains,
        second_gains,
        gate_logit,
        moment_gate,
        second_gate,
    ]
    new = adam_all(small, x_place, arrays, (att_mine, att_theirs), ff_pairs)
    shape = (micro_count, 1, seg_count, own_len, D)
    return (
        jnp.stack(block_out, axis=0).reshape(shape),
        jnp.stack(grad_rows, axis=0).reshape(shape),
        new[-1],
        *new[:-1],
    )


def solution(mesh):
    seq_count, ctx_count = mesh.devices.shape
    inner = Mesh(
        mesh.devices.reshape(seq_count // 2, 2, ctx_count // 2, 2), ("z", "x", "y", "c")
    )
    seq, ctx = ("z", "x"), ("y", "c")
    rows = P(None, seq, None, ctx, None)
    wide = P(seq, None, ctx)
    flat = P(seq, ctx)
    weights = (wide,) * 3 + (flat,) * 3 + (wide,) * 3 + (flat,) * 3 + (P(),) * 6
    return jax.shard_map(
        on_device,
        mesh=inner,
        in_specs=(rows, P(None, seq, None, ctx), rows) + weights,
        out_specs=(rows, rows, P()) + weights,
        check_vma=False,
    )
```

```python
import functools

import jax
import jax.numpy as jnp
from jax import lax
from jax.experimental import pallas as pl
from jax.experimental.pallas import tpu as pltpu
from jax.sharding import Mesh
from jax.sharding import PartitionSpec as P

D = 2048
HEADS = 16
HEAD_DIM = 128
FF = 8192
STEP_COUNT = 10
CHUNKS = 2

EPS = 1e-06
NEG = -1e30
CLIP = 1.0
BETA1 = 0.9
BETA2 = 0.95
ADAM_EPS = 1e-08
DECAY = 0.1
BF = jnp.bfloat16
F32 = jnp.float32
SCALING = HEAD_DIM ** (-0.5)
VMEM_LIMIT = 48 * 1024 * 1024


def rms_norm(tensor, scaling):
    return tensor * lax.rsqrt(jnp.mean(tensor * tensor, axis=-1, keepdims=True) + EPS) * scaling


def adam_update(weight, moment, second, gradient, factor, step_rate, decay):
    clipped = gradient * factor
    moment = BETA1 * moment + (1.0 - BETA1) * clipped
    second = BETA2 * second + (1.0 - BETA2) * clipped * clipped
    fixed_first = moment / (1.0 - BETA1**STEP_COUNT)
    fixed_second = second / (1.0 - BETA2**STEP_COUNT)
    updated = weight - step_rate * (
        fixed_first / (jnp.sqrt(fixed_second) + ADAM_EPS) + decay * weight
    )
    return (moment, second, updated)


def swap(tensor, axis):
    return lax.ppermute(tensor, axis, [(0, 1), (1, 0)])


def tie(tensor, *earlier):
    return lax.optimization_barrier((tensor,) + earlier)[0]


def gather_start(own, outer, inner, x_after=(), y_after=()):
    start = {"x": tie(own, *x_after), "y": tie(own, *y_after)}
    return own, swap(start[inner], inner), swap(start[outer], outer)


def gather_across(state, outer, inner, last):
    own, by_inner, by_outer = state
    return state + (swap(by_inner if last == outer else by_outer, last),)


def gather_steps(owns, orders):
    starts = [gather_start(own, *order) for own, order in zip(owns, orders)]
    firsts = [t for state in starts for t in state[1:]]
    ready = []
    for state, order in zip(starts, orders):
        by_inner = tie(state[1], *firsts)
        ready.append((state[0], by_inner, state[2], swap(by_inner, order[0])))
    lasts = [state[-1] for state in ready]
    return [(tie(state[0], *lasts),) + state[1:] for state in ready]


def gather_core(state):
    mine = jnp.concatenate(state, axis=0)
    return mine, swap(mine, "c")


def scatter_core(mine, other, units, outer, first):
    came = swap(other, "c").reshape(2, 2, units, -1)
    mine = mine.reshape(2, 2, units, -1)
    parts = []
    for p in range(2):
        index = (p,) if first == outer else (slice(None), p)
        parts.append(mine[index].astype(F32) + came[index].astype(F32))
    return parts[0], parts[1].astype(BF)


def scatter_outer(state, axis, *later):
    keep, send = state
    return scatter_add(keep, tie(swap(send, axis), *later))


def scatter_add(keep, came):
    send = (keep[1] + came[1].astype(F32)).astype(BF)
    return keep[0] + came[0].astype(F32), send


def scatter_inner(state, axis):
    keep, send = state
    return keep + swap(send, axis).astype(F32)


def tie_pair(pair, *earlier):
    return pair[0], tie(pair[1], *earlier)


def tie_send(state, *earlier):
    return state[0], tie(state[1], *earlier)


def sum_everywhere(tensor, z_count, beside):
    def add(tensor, axis, pairs):
        return tensor + lax.ppermute(tensor, axis, pairs)

    tensor = add(tensor, "x", [(0, 1), (1, 0)])
    reach = 1
    while reach < z_count:
        tensor = add(tensor, "z", [(i, i ^ reach) for i in range(z_count)])
        reach *= 2
    tensor = add(tensor, "c", [(0, 1), (1, 0)])
    return add(tie(tensor, beside), "y", [(0, 1), (1, 0)])


def mm(a, b, dims):
    return lax.dot_general(a, b, (dims, ((), ())), preferred_element_type=F32)


NN = ((1,), (0,))
NT = ((1,), (1,))
TN = ((0,), (0,))


def mm_mem(a, b, dims):
    return mm(a.astype(BF), b.astype(BF), dims)


def elu_one(tensor):
    return jnp.where(tensor > 0, tensor + 1.0, jnp.exp(jnp.minimum(tensor, 0.0)))


def elu_slope(tensor):
    low = jnp.where(tensor == 0, 0.5, jnp.exp(jnp.minimum(tensor, 0.0)))
    return jnp.where(tensor > 0, 1.0, low)


def segment_of(ref, r, part):
    block = ref[:, :, r, :, part * HEAD_DIM : (part + 1) * HEAD_DIM]
    return block.reshape(-1, HEAD_DIM)


def memory_forward(qs, ks, vs, cols):
    seg_count = len(qs)
    saved = []
    memory = normer = None
    for r in range(seg_count):
        reading, writing, keep = cols[r]
        sq = elu_one(qs[r].astype(F32))
        sk = elu_one(ks[r].astype(F32))
        value = vs[r].astype(F32)
        rows = sq.shape[0]
        item = dict(sq=sq, sk=sk)
        if r == 0:
            item["recalled"] = jnp.zeros_like(sq)
            change = value
        else:
            both = mm_mem(jnp.concatenate([sq, sk], axis=0), memory, NN)
            num = both[:rows]
            den = 1.0 + jnp.sum(sq * normer, axis=-1, keepdims=True)
            item["recalled"] = reading * num / den
            before = keep * both[rows:]
            kden = 1.0 + keep * jnp.sum(sk * normer, axis=-1, keepdims=True)
            change = value - before / kden
            item.update(num=num, den=den, before=before, kden=kden, memory=memory, normer=normer)
        item["change"] = change
        if r < seg_count - 1:
            write = sk * writing
            fresh = mm_mem(write, change, TN)
            fresh_norm = jnp.sum(write, axis=0, keepdims=True)
            memory = fresh if r == 0 else keep * memory + fresh
            normer = fresh_norm if r == 0 else keep[:1] * normer + fresh_norm
        saved.append(item)
    return saved


def local_probs(query, key, allowed):
    scores = jnp.where(allowed > 0, mm(query, key, NT) * SCALING, NEG)
    exponent = jnp.exp(scores - jnp.max(scores, axis=-1, keepdims=True))
    return exponent / jnp.sum(exponent, axis=-1, keepdims=True)


def columns_of(cols_ref, r):
    cols = cols_ref[r]
    return cols[:, 0:1], cols[:, 1:2], cols[:, 2:3]


def attention_fwd_kernel(heads, proj_ref, mask_ref, cols_ref, gate_ref, out_ref):
    seg_count = mask_ref.shape[0]
    cols = [columns_of(cols_ref, r) for r in range(seg_count)]
    for h in range(heads):
        qs = [segment_of(proj_ref, r, h) for r in range(seg_count)]
        ks = [segment_of(proj_ref, r, heads + h) for r in range(seg_count)]
        vs = [segment_of(proj_ref, r, 2 * heads + h) for r in range(seg_count)]
        saved = memory_forward(qs, ks, vs, cols)
        mixing = gate_ref[h : h + 1]
        for r in range(seg_count):
            prob_low = local_probs(qs[r], ks[r], mask_ref[r]).astype(BF)
            local_out = mm(prob_low, vs[r], NN)
            combined = mixing * saved[r]["recalled"] + (1.0 - mixing) * local_out
            out_ref[:, :, r, :, h * HEAD_DIM : (h + 1) * HEAD_DIM] = combined.astype(BF).reshape(
                out_ref.shape[0], out_ref.shape[1], out_ref.shape[3], HEAD_DIM
            )


def attention_bwd_kernel(
    heads, proj_ref, grad_ref, mask_ref, cols_ref, gate_ref, out_ref, gate_out_ref
):
    seg_count = mask_ref.shape[0]
    cols = [columns_of(cols_ref, r) for r in range(seg_count)]

    def put(r, part, value):
        out_ref[:, :, r, :, part * HEAD_DIM : (part + 1) * HEAD_DIM] = value.astype(BF).reshape(
            out_ref.shape[0], out_ref.shape[1], out_ref.shape[3], HEAD_DIM
        )

    for h in range(heads):
        qs = [segment_of(proj_ref, r, h) for r in range(seg_count)]
        ks = [segment_of(proj_ref, r, heads + h) for r in range(seg_count)]
        vs = [segment_of(proj_ref, r, 2 * heads + h) for r in range(seg_count)]
        saved = memory_forward(qs, ks, vs, cols)
        mixing = gate_ref[h : h + 1]
        gate_sum = jnp.zeros((1, HEAD_DIM), F32)
        d_memory = d_normer = None
        for r in reversed(range(seg_count)):
            reading, writing, keep = cols[r]
            item = saved[r]
            sq, sk = item["sq"], item["sk"]
            rows = sq.shape[0]
            d_combined = segment_of(grad_ref, r, h).astype(F32)
            d_recalled = mixing * d_combined
            d_local = ((1.0 - mixing) * d_combined).astype(BF)
            probs = local_probs(qs[r], ks[r], mask_ref[r])
            prob_low = probs.astype(BF)
            local_out = mm(prob_low, vs[r], NN)
            gate_sum = gate_sum + jnp.sum(
                d_combined * (item["recalled"] - local_out), axis=0, keepdims=True
            )
            d_prob = mm(d_local, vs[r], NT)
            d_value = mm(prob_low, d_local, TN)
            d_scores = (
                probs * (d_prob - jnp.sum(d_prob * probs, axis=-1, keepdims=True))
            ).astype(BF)
            d_query = mm(d_scores, ks[r], NN) * SCALING
            d_key = mm(d_scores, qs[r], TN) * SCALING
            d_sk = None
            d_before = d_kden = None
            if r < seg_count - 1:
                d_change = writing * mm_mem(sk, d_memory, NN)
                d_sk = writing * (mm_mem(item["change"], d_memory, NT) + d_normer)
                d_value = d_value + d_change
                if r > 0:
                    d_before = keep * (-d_change / item["kden"])
                    d_kden = keep * (
                        jnp.sum(d_change * item["before"], axis=-1, keepdims=True)
                        / (item["kden"] * item["kden"])
                    )
            if r > 0:
                d_num = reading * d_recalled / item["den"]
                d_den = -reading * (
                    jnp.sum(d_recalled * item["num"], axis=-1, keepdims=True)
                    / (item["den"] * item["den"])
                )
                if d_before is None:
                    d_sq = mm_mem(d_num, item["memory"], NT) + d_den * item["normer"]
                    new_memory = mm_mem(sq, d_num, TN)
                    new_normer = jnp.sum(sq * d_den, axis=0, keepdims=True)
                else:
                    stacked = jnp.concatenate([d_num, d_before], axis=0)
                    both = mm_mem(stacked, item["memory"], NT)
                    d_sq = both[:rows] + d_den * item["normer"]
                    d_sk = d_sk + both[rows:] + d_kden * item["normer"]
                    new_memory = keep * d_memory + mm_mem(
                        jnp.concatenate([sq, sk], axis=0), stacked, TN
                    )
                    new_normer = keep[:1] * d_normer + jnp.sum(
                        sq * d_den + sk * d_kden, axis=0, keepdims=True
                    )
                d_memory, d_normer = new_memory, new_normer
                d_query = d_query + d_sq * elu_slope(qs[r].astype(F32))
            if d_sk is not None:
                d_key = d_key + d_sk * elu_slope(ks[r].astype(F32))
            put(r, h, d_query)
            put(r, heads + h, d_key)
            put(r, 2 * heads + h, d_value)
        gate_out_ref[h : h + 1] = gate_sum


def block_spec(shape, where):
    dims = list(shape)
    dims[where] = None

    def index(s):
        place = [0] * len(dims)
        place[where] = s
        return tuple(place)

    return pl.BlockSpec(tuple(dims), index)


def attention_fwd(projected, mask, cols, gate_rows, where):
    heads = gate_rows.shape[0]
    out_shape = projected.shape[:-1] + (heads * HEAD_DIM,)
    return pl.pallas_call(
        functools.partial(attention_fwd_kernel, heads),
        grid=(projected.shape[where],),
        in_specs=[
            block_spec(projected.shape, where),
            pl.BlockSpec((None,) + mask.shape[1:], lambda s: (s, 0, 0, 0)),
            pl.BlockSpec((None,) + cols.shape[1:], lambda s: (s, 0, 0, 0)),
            pl.BlockSpec(gate_rows.shape, lambda s: (0, 0)),
        ],
        out_specs=block_spec(out_shape, where),
        out_shape=jax.ShapeDtypeStruct(out_shape, BF),
        compiler_params=pltpu.CompilerParams(vmem_limit_bytes=VMEM_LIMIT),
        cost_estimate=pl.CostEstimate(
            flops=7_600_000_000, bytes_accessed=3_000_000, transcendentals=0
        ),
        name="attention_forward",
    )(projected, mask, cols, gate_rows)


def attention_bwd(projected, d_combined, mask, cols, gate_rows, where):
    heads = gate_rows.shape[0]
    seqs = projected.shape[where]
    return pl.pallas_call(
        functools.partial(attention_bwd_kernel, heads),
        grid=(seqs,),
        in_specs=[
            block_spec(projected.shape, where),
            block_spec(d_combined.shape, where),
            pl.BlockSpec((None,) + mask.shape[1:], lambda s: (s, 0, 0, 0)),
            pl.BlockSpec((None,) + cols.shape[1:], lambda s: (s, 0, 0, 0)),
            pl.BlockSpec(gate_rows.shape, lambda s: (0, 0)),
        ],
        out_specs=[
            block_spec(projected.shape, where),
            pl.BlockSpec((None, heads, HEAD_DIM), lambda s: (s, 0, 0)),
        ],
        out_shape=[
            jax.ShapeDtypeStruct(projected.shape, BF),
            jax.ShapeDtypeStruct((seqs, heads, HEAD_DIM), F32),
        ],
        compiler_params=pltpu.CompilerParams(vmem_limit_bytes=VMEM_LIMIT),
        cost_estimate=pl.CostEstimate(
            flops=14_400_000_000, bytes_accessed=5_000_000, transcendentals=0
        ),
        name="attention_backward",
    )(projected, d_combined, mask, cols, gate_rows)


GELU_A = 0.7978845608028654
GELU_B = 0.044715


def ff_kernel(width, half, x_mine, x_other, g_mine, g_other, w_ref, *outs):
    step = pl.program_id(0)

    @pl.when(step < half)
    def first():
        ff_tile(width, x_mine, g_mine, w_ref, outs[0], outs[2])

    @pl.when(step >= half)
    def second():
        ff_tile(width, x_other, g_other, w_ref, outs[1], outs[3])


def ff_tile(width, x_ref, g_ref, w_ref, act_ref, grad_ref):
    weights = w_ref[...]
    gate_up = mm(x_ref[...], weights[:, : 2 * width], NN)
    d_active = mm(g_ref[...], weights[:, 2 * width :], NN)
    gate = gate_up[:, :width]
    up = gate_up[:, width:]
    square = gate * gate
    tanh = jnp.tanh(GELU_A * gate * (1.0 + GELU_B * square))
    half = 0.5 * (1.0 + tanh)
    gelu = gate * half
    slope = half + 0.5 * gate * (1.0 - tanh * tanh) * GELU_A * (1.0 + 3.0 * GELU_B * square)
    act_ref[...] = (gelu * up).astype(BF)
    grad_ref[:, :width] = (d_active * up * slope).astype(BF)
    grad_ref[:, width:] = (d_active * gelu).astype(BF)


def feed_forward(rows, grads, weights):
    tokens = rows[0].shape[0]
    width = weights.shape[1] // 3
    tile = 256
    half = tokens // tile

    def first(columns):
        return pl.BlockSpec((tile, columns), lambda i: (jnp.minimum(i, half - 1), 0))

    def second(columns):
        return pl.BlockSpec((tile, columns), lambda i: (jnp.maximum(i - half, 0), 0))

    whole = pl.BlockSpec(weights.shape, lambda i: (0, 0), pipeline_mode=pl.Buffered(1))
    act = jax.ShapeDtypeStruct((tokens, width), BF)
    grad = jax.ShapeDtypeStruct((tokens, 2 * width), BF)
    out = pl.pallas_call(
        functools.partial(ff_kernel, width, half),
        grid=(2 * half,),
        in_specs=[first(D), second(D), first(D), second(D), whole],
        out_specs=[first(width), second(width), first(2 * width), second(2 * width)],
        out_shape=[act, act, grad, grad],
        compiler_params=pltpu.CompilerParams(vmem_limit_bytes=VMEM_LIMIT),
        cost_estimate=pl.CostEstimate(
            flops=26 * tokens * D * width, bytes_accessed=tokens * D, transcendentals=0
        ),
        name="feed_forward",
    )(*rows, *grads, weights)
    return (out[0], out[1]), (out[2], out[3])


def down_kernel(count, half, *refs):
    step = pl.program_id(0)
    mine, other, weights = (refs[k * count : (k + 1) * count] for k in range(3))

    def tile(rows, out_ref):
        terms = [mm(a[...], w[...], NT) for a, w in zip(rows, weights)]
        out_ref[...] = sum(terms[1:], terms[0]).astype(BF)

    @pl.when(step < half)
    def first():
        tile(mine, refs[3 * count])

    @pl.when(step >= half)
    def second():
        tile(other, refs[3 * count + 1])


def down_product(active, weights):
    count = len(active)
    tokens, width = active[0][0].shape
    tile = 256
    half = tokens // tile

    def first(columns):
        return pl.BlockSpec((tile, columns), lambda i: (jnp.minimum(i, half - 1), 0))

    def second(columns):
        return pl.BlockSpec((tile, columns), lambda i: (jnp.maximum(i - half, 0), 0))

    down = pl.BlockSpec((D, width), lambda i: (0, 2), pipeline_mode=pl.Buffered(1))
    return pl.pallas_call(
        functools.partial(down_kernel, count, half),
        grid=(2 * half,),
        in_specs=[first(width)] * count + [second(width)] * count + [down] * count,
        out_specs=[first(D), second(D)],
        out_shape=[jax.ShapeDtypeStruct((tokens, D), BF)] * 2,
        compiler_params=pltpu.CompilerParams(vmem_limit_bytes=VMEM_LIMIT),
        cost_estimate=pl.CostEstimate(
            flops=4 * count * tokens * D * width,
            bytes_accessed=2 * D * (count * width + 2 * tokens),
            transcendentals=0,
        ),
        name="down_product",
    )(*[a for a, _ in active], *[b for _, b in active], *weights)


def grads_kernel(count, *refs):
    rows, grads, by_rows, by_grads = (refs[k * count : (k + 1) * count] for k in range(4))
    out_ref = refs[4 * count]
    split = by_rows[0].shape[1]

    def total(left, right):
        acc = None
        for a, b in zip(left, right):
            term = mm(a[...], b[...], TN)
            acc = term if acc is None else acc + term
        return acc

    out_ref[:, :split] = total(rows, by_rows).astype(BF)
    out_ref[:, split:] = total(grads, by_grads).astype(BF)


def weight_grads(rows, grads, by_rows, by_grads):
    def halves(arrays):
        parts = []
        for a in arrays:
            parts += [(a[0], 0), (a[1], 0)] if isinstance(a, tuple) else [(a, 0), (a, 1)]
        return parts

    groups = [halves(a) for a in (rows, grads, by_rows, by_grads)]
    count = len(groups[0])
    tokens = groups[0][0][0].shape[0] // (1 if isinstance(rows[0], tuple) else 2)
    first, second = groups[2][0][0].shape[1], groups[3][0][0].shape[1]
    tile = 512

    def tall(half):
        return pl.BlockSpec((tokens, tile), lambda i: (half, i))

    def whole(width, half):
        return pl.BlockSpec((tokens, width), lambda i: (half, 0), pipeline_mode=pl.Buffered(1))

    return pl.pallas_call(
        functools.partial(grads_kernel, count),
        grid=(D // tile,),
        in_specs=[tall(half) for _, half in groups[0] + groups[1]]
        + [whole(first, half) for _, half in groups[2]]
        + [whole(second, half) for _, half in groups[3]],
        out_specs=pl.BlockSpec((tile, first + second), lambda i: (i, 0)),
        out_shape=jax.ShapeDtypeStruct((D, first + second), BF),
        compiler_params=pltpu.CompilerParams(vmem_limit_bytes=VMEM_LIMIT),
        cost_estimate=pl.CostEstimate(
            flops=3 * count * tokens * D * (first + second),
            bytes_accessed=2 * (2 * count * tokens * D + (count * tokens + D) * (first + second)),
            transcendentals=0,
        ),
        name="weight_grads",
    )(*[a for group in groups for a, _ in group])


RATE_QKV = D ** (-0.5)
RATE_OUT = 4.0 * (HEADS * HEAD_DIM) ** (-0.5)
RATE_DOWN = FF ** (-0.5)


def clip_factor(small):
    row = lax.broadcasted_iota(jnp.int32, small.shape, 0)
    lane = lax.broadcasted_iota(jnp.int32, small.shape, 1)
    summed = (row == small.shape[0] - 1) & (lane >= HEADS)
    squares = jnp.sum(jnp.where(summed, small, small * small), axis=(0, 1), keepdims=True)
    grad_norm = jnp.sqrt(squares)
    return grad_norm, jnp.minimum(1.0, CLIP / (grad_norm + 1e-06))


def adam_kernel(steps, chunks, place_ref, small_ref, *refs):
    ins, refs = refs[:18], refs[18:]
    grads, refs = refs[: 2 + 2 * chunks], refs[2 + 2 * chunks :]
    outs, norm_ref, scratch = refs[:18], refs[18], refs[19]
    grad_norm, factor = clip_factor(small_ref[...])
    is_low = place_ref[0] == 0
    everything = slice(None)

    def put(number, place, gradient, rate, decay=DECAY):
        weight, moment, second = (r[place] for r in ins[3 * number : 3 * number + 3])
        new = adam_update(weight, moment, second, gradient.astype(F32), factor, rate, decay)
        for ref, value in zip(outs[3 * number : 3 * number + 3], new):
            ref[place] = value

    def sides_of(mine, theirs):
        mine, theirs = mine[...], theirs[...]
        return jnp.where(is_low, mine, theirs), jnp.where(is_low, theirs, mine)

    for s, side in enumerate(sides_of(*grads[:2])):
        width = side.shape[1] // 4
        cols = slice(s * width, (s + 1) * width)
        for part in range(3):
            put(0, (part, everything, cols), side[:, part * width : (part + 1) * width], RATE_QKV)
        put(1, (everything, cols), side[:, 3 * width :], RATE_OUT)
    rows, width_ff = ins[9].shape
    lanes = width_ff // 128
    for k in range(chunks):
        for s, side in enumerate(sides_of(*grads[2 + 2 * k : 4 + 2 * k])):
            side = side.astype(F32)
            width = side.shape[1] // 3
            start = s * (width_ff // 2) + k * width
            put(3, (everything, slice(start, start + width)), side[:, 2 * width :], RATE_DOWN)
            for part in range(2):
                for lane in range(width // 128):
                    place = pl.ds((start // 128 + lane) * 2 + part, rows, stride=2 * lanes)
                    first = part * width + lane * 128
                    scratch[place, :] = side[:, first : first + 128]
    put(2, (everything, everything), scratch[...], RATE_QKV)

    @pl.when(pl.program_id(0) == 0)
    def small_ones():
        last = ins[12].shape[0]
        put(4, (everything, everything), small_ref[:last], 0.5, 0.0)
        put(5, (everything, everything), small_ref[last:, :HEADS], 1.0, 0.0)
        norm_ref[...] = grad_norm


def mlp_view(t):
    rows, _, width_ff = t.shape
    return t.reshape(rows, 2, width_ff // 128, 128).transpose(0, 2, 1, 3).reshape(-1, 128)


def adam_all(small, x_place, arrays, att_sides, ff_sides):
    rows, _, width_ff = arrays[6].shape
    steps = 4

    def qkv_view(t):
        return jnp.transpose(t, (1, 0, 2))

    def mlp_back(t, shape):
        rows, _, width_ff = shape
        t = t.reshape(rows, width_ff // 128, 2, 128).transpose(0, 2, 1, 3)
        return t.reshape(shape)

    views = [qkv_view(t) for t in arrays[:3]] + list(arrays[3:6])
    views += [mlp_view(t) for t in arrays[6:9]] + list(arrays[9:12])
    gains = [mlp_view(t[None]) for t in arrays[12:15]] + [t[None] for t in arrays[15:]]
    grads = list(att_sides) + [t for pair in ff_sides for t in pair]

    def spec(t):
        axis = t.ndim - 2
        block = list(t.shape)
        block[axis] //= steps
        return pl.BlockSpec(tuple(block), lambda i, place: (0,) * axis + (i, 0))

    def whole(t):
        return pl.BlockSpec(t.shape, lambda i, place: (0, 0))

    def mine(t):
        return pl.BlockSpec((rows // steps, t.shape[1]), lambda i, place: (place[0] * steps + i, 0))

    specs = [spec(t) for t in views] + [whole(t) for t in gains]
    new = pl.pallas_call(
        functools.partial(adam_kernel, steps, len(ff_sides)),
        grid_spec=pltpu.PrefetchScalarGridSpec(
            num_scalar_prefetch=1,
            grid=(steps,),
            in_specs=[whole(small)]
            + specs
            + [spec(t) if k % 2 else mine(t) for k, t in enumerate(grads)],
            out_specs=specs + [pl.BlockSpec((1, 1), lambda i, place: (0, 0))],
            scratch_shapes=[pltpu.VMEM((views[6].shape[0] // steps, 128), F32)],
        ),
        out_shape=[jax.ShapeDtypeStruct(t.shape, F32) for t in views + gains]
        + [jax.ShapeDtypeStruct((1, 1), F32)],
        compiler_params=pltpu.CompilerParams(vmem_limit_bytes=VMEM_LIMIT),
        cost_estimate=pl.CostEstimate(
            flops=20 * sum(t.size for t in views) // 3,
            bytes_accessed=8 * sum(t.size for t in views),
            transcendentals=0,
        ),
        name="adam",
    )(x_place[None], small, *views, *gains, *grads)
    new = list(new)
    return (
        [qkv_view(t) for t in new[:3]]
        + new[3:6]
        + [mlp_back(t, arrays[6].shape) for t in new[6:9]]
        + new[9:12]
        + [mlp_back(t, (1,) + arrays[12].shape)[0] for t in new[12:15]]
        + [t[0] for t in new[15:18]]
        + [new[18].reshape(())]
    )


def on_device(
    inputs,
    doc_ids,
    cotangent,
    weight_qkv,
    moment_qkv,
    second_qkv,
    weight_out,
    moment_out,
    second_out,
    weight_mlp,
    moment_mlp,
    second_mlp,
    weight_down,
    moment_down,
    second_down,
    norm_gains,
    moment_gains,
    second_gains,
    gate_logit,
    moment_gate,
    second_gate,
):
    micro_count, _, seg_count, own_len, _ = inputs.shape
    own_tokens = seg_count * own_len
    x_place = lax.axis_index("x")
    y_place = lax.axis_index("y")
    c_place = lax.axis_index("c")
    orders = [("x", "y") if m % 2 == 0 else ("y", "x") for m in range(micro_count)]

    z_count = D // (2 * weight_qkv.shape[0])

    def half_columns(weight, which):
        width = weight.shape[-1] // 2
        return lax.dynamic_slice_in_dim(weight, which * width, width, axis=weight.ndim - 1)

    def join_rows(mine, theirs):
        both = jnp.zeros((2 * rows, mine.shape[1]), BF)
        both = lax.dynamic_update_slice_in_dim(both, mine, x_place * rows, axis=0)
        return lax.dynamic_update_slice_in_dim(both, theirs, (1 - x_place) * rows, axis=0)

    def fetch(block):
        return lax.all_gather(block, "z", axis=0, tiled=True)

    rows = weight_qkv.shape[0]
    heads = weight_qkv.shape[2] // (2 * HEAD_DIM)
    width_att = heads * HEAD_DIM
    width_ff = weight_down.shape[1] // 2
    width = width_ff // CHUNKS

    def qkv_columns(which):
        return half_columns(weight_qkv, which).astype(BF).reshape(rows, -1)

    def ff_columns(k, which):
        start = which * width_ff + k * width
        mlp = lax.dynamic_slice_in_dim(mlp_later, start, width, axis=2).astype(BF)
        down = lax.dynamic_slice_in_dim(down_later, start, width, axis=1).astype(BF)
        return jnp.concatenate([mlp[:, 0], mlp[:, 1], down], axis=1)

    send_qkv = qkv_columns(1 - x_place)
    all_out = fetch(weight_out.astype(BF))
    all_ids = doc_ids[:, 0]
    for axis in ("y", "c"):
        all_ids = jnp.stack([all_ids, swap(all_ids, axis)], axis=0)
    their_qkv = swap(send_qkv, "x")
    shard_qkv = join_rows(qkv_columns(x_place), tie(their_qkv, all_ids))
    full_qkv = fetch(shard_qkv)

    head_start = (y_place * 2 + c_place) * (2 * heads) + x_place * heads
    gate_local = lax.dynamic_slice_in_dim(gate_logit, head_start, heads)
    mixing = jax.nn.sigmoid(gate_local)
    gate_rows = jnp.broadcast_to(mixing[:, None], (heads, HEAD_DIM))

    micros = range(micro_count)
    tokens = 8 * own_tokens
    token_rows = [
        tie(inputs[m, 0], send_qkv).reshape(own_tokens, D).astype(F32) for m in micros
    ]
    back_low = [cotangent[m, 0].reshape(own_tokens, D) for m in micros]
    all_ids = jnp.stack([all_ids, swap(all_ids, "x")], axis=0)
    normed_att = [rms_norm(t, norm_gains[0]).astype(BF) for t in token_rows]
    att_states = [
        gather_start(normed_att[m], *orders[m], (their_qkv, all_ids)) for m in micros
    ]
    att_by_x = [state[1 + orders[m].index("y")] for m, state in enumerate(att_states)]
    mlp_later = tie(weight_mlp, *att_by_x)
    down_later = tie(weight_down, *att_by_x)
    att_states = [gather_across(state, *orders[m], "y") for m, state in enumerate(att_states)]
    att_rows = [gather_core(state) for state in att_states]

    def their_ff(k, *earlier):
        return swap(tie(ff_columns(k, 1 - x_place), *earlier), "x")

    theirs = their_ff(0, *att_by_x)
    shard_ff = [join_rows(ff_columns(0, x_place), theirs)]
    full_ff = [fetch(shard_ff[0])]
    their_out = swap(tie(half_columns(all_out, 1 - x_place), shard_ff[0]), "x")
    both_out = jnp.zeros((z_count, 2, rows, width_att), BF)
    for part, place in ((half_columns(all_out, x_place), x_place), (their_out, 1 - x_place)):
        part = part.reshape(z_count, 1, rows, width_att)
        both_out = lax.dynamic_update_slice_in_dim(both_out, part, place, axis=1)
    full_out = both_out.reshape(D, width_att)
    att_last = [state[-1] for state in att_states]
    back_states = [
        gather_start(back_low[m], *orders[m], (their_out,), att_last) for m in micros
    ]
    back_first = [t for state in back_states for t in state[1:]]
    back_states = [gather_across(state, *orders[m], "y") for m, state in enumerate(back_states)]
    earlier = back_first

    rel_c = jnp.arange(2)[:, None, None] ^ c_place
    rel_y = jnp.arange(2)[None, :, None] ^ y_place
    places = ((rel_y * 2 + rel_c) * own_len + jnp.arange(own_len)).reshape(-1)
    causal = places[:, None] >= places[None, :]
    masks = []
    columns = []
    for m in micros:
        ids = jnp.transpose(all_ids[:, :, :, m], (0, 3, 1, 2, 4)).reshape(2, seg_count, -1)
        same = ids[:, :, :, None] == ids[:, :, None, :]
        masks.append((same & causal).astype(F32))
        last = jnp.max(ids, axis=2)
        previous = jnp.concatenate([jnp.full((2, 1), -1, last.dtype), last[:, :-1]], axis=1)
        reading = ids == previous[:, :, None]
        writing = ids == last[:, :, None]
        keep = jnp.broadcast_to((last == previous)[:, :, None], ids.shape)
        columns.append(jnp.stack([reading, writing, keep], axis=-1).astype(F32))

    slots = (2, 2, 2, seg_count, own_len)
    wheres = [1 if orders[m][0] == "x" else 2 for m in micros]
    projected = []
    combined = []
    hidden = []
    normed_mlp = []
    for m in micros:
        mine, other = att_rows[m]
        if m == 0:
            mine = tie(mine, *back_first)
        proj = jnp.concatenate([mm(p, full_qkv, NN).astype(BF) for p in (mine, other)], axis=0)
        projected.append(proj.reshape(slots + (3 * width_att,)))
        comb = attention_fwd(projected[m], masks[m], columns[m], gate_rows, wheres[m])
        combined.append(comb.reshape(tokens, width_att))
    half = tokens // 2
    for k in range(1, CHUNKS):
        theirs = their_ff(k, *earlier)
        shard_ff.append(join_rows(ff_columns(k, x_place), tie(theirs, combined[0])))
        full_ff.append(fetch(shard_ff[k]))
        earlier = [theirs]
    back_states = [(tie(state[0], combined[0]),) + state[1:] for state in back_states]
    back_rows = [gather_core(state) for state in back_states]
    for m in micros:
        ready = combined[m]
        if m > 0:
            ready = tie(ready, *shard_ff, *[state[-1] for state in back_states])
        other = mm(ready[half:], full_out, NT).astype(BF)
        mine = mm(ready[:half], full_out, NT).astype(BF)
        state = scatter_core(mine, other, own_tokens, orders[m][0], orders[m][0])
        state = scatter_outer(state, orders[m][0])
        hidden.append(token_rows[m] + scatter_inner(state, orders[m][1]))
        normed_mlp.append(rms_norm(hidden[m], norm_gains[1]).astype(BF))
    mlp_rows = [gather_core(state) for state in gather_steps(normed_mlp, orders)]

    def exchange_grad(grad):
        return grad, swap(lax.dynamic_slice_in_dim(grad, (1 - x_place) * rows, rows, axis=0), "x")

    def squares_of(grad):
        wide = grad.astype(F32)
        return jnp.sum(wide * wide)

    def reduce_rows(partial):
        return lax.psum_scatter(partial, "z", scatter_dimension=0, tiled=True)

    def products(left, right, totals, dtype):
        terms = [mm(left[p], right, NT) for p in (1, 0)][::-1]
        if totals is not None:
            terms = [a + b for a, b in zip(totals, terms)]
        return tuple(t.astype(dtype) for t in terms)

    active = []
    d_gate_up = []
    own_ff = []
    d_total = [None] * micro_count
    states = [None] * micro_count
    for k in range(CHUNKS):
        active.append([])
        d_gate_up.append([])
        last = k == CHUNKS - 1
        for m in micros:
            rows_in = mlp_rows[m]
            if last and m > 0:
                rows_in = (tie(rows_in[0], *d_total[m - 1]), rows_in[1])
            act, grad = feed_forward(rows_in, back_rows[m], full_ff[k])
            active[k].append(act)
            d_gate_up[k].append(grad)
            if last and m > 0:
                grad = (grad[0], tie(grad[1], states[m - 1][1]))
            dtype = BF if last else F32
            d_total[m] = products(grad, full_ff[k][:, : 2 * width], d_total[m], dtype)
            if last:
                states[m] = scatter_core(*d_total[m], own_tokens, orders[m][0], orders[m][0])
        if not last:
            grad_ff = weight_grads(mlp_rows, back_rows, d_gate_up[k], active[k])
            own_ff.append(reduce_rows(grad_ff))
            terms = [t for pair in d_total for t in pair]
            full_ff[k + 1] = tie(full_ff[k + 1], grad_ff, *terms)

    out_pairs = []
    for m in micros:
        act = [active[k][m] for k in range(CHUNKS)]
        act[-1] = (act[-1][0], tie(act[-1][1], states[-1][1]))
        out_pairs.append(down_product(act, full_ff))
    products_done = [t for pair in out_pairs for t in pair]
    outer_states = [scatter_outer(states[m], orders[m][0], *products_done) for m in micros]
    last_active = [
        (active[-1][m][0], tie(active[-1][m][1], *[t[1] for t in outer_states])) for m in micros
    ]
    grad_ff = weight_grads(mlp_rows, back_rows, d_gate_up[-1], last_active)
    own_ff.append(reduce_rows(grad_ff))

    gain_grad_att = jnp.zeros((D,), F32)
    gain_grad_mlp = jnp.zeros((D,), F32)
    d_hidden = []
    for m in micros:
        keep, send = outer_states[m]
        d_normed = scatter_inner((tie(keep, grad_ff), send), orders[m][1])
        ignored, norm_back = jax.vjp(rms_norm, hidden[m], norm_gains[1])
        d_norm, d_gain = norm_back(d_normed)
        gain_grad_mlp = gain_grad_mlp + d_gain
        d_hidden.append(back_low[m].astype(F32) + d_norm)

    gate_sum = jnp.zeros((heads,), F32)
    d_projs = []
    out_states = [
        scatter_core(*tie_pair(out_pairs[m], *d_hidden), own_tokens, orders[m][0], orders[m][0])
        for m in micros
    ]
    grad_states = gather_steps([t.astype(BF) for t in d_hidden], orders)
    sends = [t[1] for t in out_states]
    out_states = [tie_send(t, *[g[-1] for g in grad_states]) for t in out_states]
    att_grads = [gather_core((tie(g[0], *sends),) + g[1:]) for g in grad_states]
    ff_pairs = [exchange_grad(own_ff[0])]
    for m in micros:
        mine, other = att_grads[m]
        if m == 0:
            other = tie(other, own_ff[0])
        d_combined = jnp.concatenate(
            [mm(mine, full_out, NN), mm(other, full_out, NN)], axis=0
        )
        d_proj, gate_part = attention_bwd(
            projected[m],
            d_combined.reshape(slots + (width_att,)),
            masks[m],
            columns[m],
            gate_rows,
            wheres[m],
        )
        gate_sum = gate_sum + jnp.sum(gate_part, axis=(0, 2))
        d_projs.append(d_proj.reshape(tokens, 3 * width_att))
    out_came = [swap(out_states[m][1], orders[m][0]) for m in micros]
    by_rows = [d_projs[0], tie(d_projs[-1], ff_pairs[0][1], *out_came)]
    grad_att = weight_grads(att_rows, att_grads, by_rows, combined)
    own_att = reduce_rows(grad_att)
    mlp_out = []
    for m in micros:
        state = scatter_add(out_states[m][0], tie(out_came[m], grad_att))
        mlp_out.append(scatter_inner(state, orders[m][1]))
    block_out = [(hidden[m] + mlp_out[m]).astype(BF) for m in micros]

    ff_pairs += [exchange_grad(g) for g in own_ff[1:]]

    ff_owned = sum(squares_of(g) for g in own_ff)

    grad_rows = []
    in_states = []
    for m in micros:
        d_proj = tie(d_projs[m], grad_att)
        other = mm(d_proj[half:], full_qkv, NT).astype(BF)
        mine = mm(d_proj[:half], full_qkv, NT).astype(BF)
        in_states.append(scatter_core(mine, other, own_tokens, orders[m][0], orders[m][0]))
    for m in micros:
        state = scatter_outer(in_states[m], orders[m][0])
        if m > 0:
            state = tie_send(state, ff_pairs[-1][1])
        d_normed = scatter_inner(state, orders[m][1])
        ignored, norm_first = jax.vjp(rms_norm, token_rows[m], norm_gains[0])
        d_norm, d_gain = norm_first(d_normed)
        gain_grad_att = gain_grad_att + d_gain
        grad_rows.append((d_hidden[m] + d_norm).astype(BF))

    att_mine, att_theirs = exchange_grad(own_att)

    gate_grad = gate_sum * mixing * (1.0 - mixing)
    gate_padded = lax.dynamic_update_slice(
        jnp.zeros(gate_logit.shape, F32), gate_grad, (head_start,)
    )
    owned = squares_of(own_att) + ff_owned
    gain_grad = mlp_view(jnp.stack([gain_grad_att, gain_grad_mlp], axis=0)[None])
    last_row = jnp.concatenate([gate_padded, owned[None], jnp.zeros((127 - HEADS,), F32)])
    small = jnp.concatenate([gain_grad, last_row[None]], axis=0)
    small = sum_everywhere(small, z_count, att_theirs)
    arrays = [
        weight_qkv,
        moment_qkv,
        second_qkv,
        weight_out,
        moment_out,
        second_out,
        weight_mlp,
        moment_mlp,
        second_mlp,
        weight_down,
        moment_down,
        second_down,
        norm_gains,
        moment_gains,
        second_gains,
        gate_logit,
        moment_gate,
        second_gate,
    ]
    new = adam_all(small, x_place, arrays, (att_mine, att_theirs), ff_pairs)
    shape = (micro_count, 1, seg_count, own_len, D)
    return (
        jnp.stack(block_out, axis=0).reshape(shape),
        jnp.stack(grad_rows, axis=0).reshape(shape),
        new[-1],
        *new[:-1],
    )


def solution(mesh):
    seq_count, ctx_count = mesh.devices.shape
    inner = Mesh(
        mesh.devices.reshape(seq_count // 2, 2, ctx_count // 2, 2), ("z", "x", "y", "c")
    )
    seq, ctx = ("z", "x"), ("y", "c")
    rows = P(None, seq, None, ctx, None)
    wide = P(seq, None, ctx)
    flat = P(seq, ctx)
    weights = (wide,) * 3 + (flat,) * 3 + (wide,) * 3 + (flat,) * 3 + (P(),) * 6
    return jax.shard_map(
        on_device,
        mesh=inner,
        in_specs=(rows, P(None, seq, None, ctx), rows) + weights,
        out_specs=(rows, rows, P()) + weights,
        check_vma=False,
    )
```

```python
import functools

import jax
import jax.numpy as jnp
from jax import lax
from jax.experimental import pallas as pl
from jax.experimental.pallas import tpu as pltpu
from jax.sharding import Mesh
from jax.sharding import PartitionSpec as P

D = 2048
HEADS = 16
HEAD_DIM = 128
FF = 8192
STEP_COUNT = 10
CHUNKS = 2

EPS = 1e-06
NEG = -1e30
CLIP = 1.0
BETA1 = 0.9
BETA2 = 0.95
ADAM_EPS = 1e-08
DECAY = 0.1
BF = jnp.bfloat16
F32 = jnp.float32
SCALING = HEAD_DIM ** (-0.5)
VMEM_LIMIT = 48 * 1024 * 1024


def rms_norm(tensor, scaling):
    return tensor * lax.rsqrt(jnp.mean(tensor * tensor, axis=-1, keepdims=True) + EPS) * scaling


def adam_update(weight, moment, second, gradient, factor, step_rate, decay):
    clipped = gradient * factor
    moment = BETA1 * moment + (1.0 - BETA1) * clipped
    second = BETA2 * second + (1.0 - BETA2) * clipped * clipped
    fixed_first = moment / (1.0 - BETA1**STEP_COUNT)
    fixed_second = second / (1.0 - BETA2**STEP_COUNT)
    updated = weight - step_rate * (
        fixed_first / (jnp.sqrt(fixed_second) + ADAM_EPS) + decay * weight
    )
    return (moment, second, updated)


def swap(tensor, axis):
    return lax.ppermute(tensor, axis, [(0, 1), (1, 0)])


def tie(tensor, *earlier):
    return lax.optimization_barrier((tensor,) + earlier)[0]


def gather_start(own, outer, inner, x_after=(), y_after=()):
    start = {"x": tie(own, *x_after), "y": tie(own, *y_after)}
    return own, swap(start[inner], inner), swap(start[outer], outer)


def gather_across(state, outer, inner, last):
    own, by_inner, by_outer = state
    return state + (swap(by_inner if last == outer else by_outer, last),)


def gather_steps(owns, orders):
    starts = [gather_start(own, *order) for own, order in zip(owns, orders)]
    firsts = [t for state in starts for t in state[1:]]
    ready = []
    for state, order in zip(starts, orders):
        by_inner = tie(state[1], *firsts)
        ready.append((state[0], by_inner, state[2], swap(by_inner, order[0])))
    lasts = [state[-1] for state in ready]
    return [(tie(state[0], *lasts),) + state[1:] for state in ready]


def gather_core(state):
    mine = jnp.concatenate(state, axis=0)
    return mine, swap(mine, "c")


def scatter_core(mine, other, units, outer, first):
    came = swap(other, "c").reshape(2, 2, units, -1)
    mine = mine.reshape(2, 2, units, -1)
    parts = []
    for p in range(2):
        index = (p,) if first == outer else (slice(None), p)
        parts.append(mine[index].astype(F32) + came[index].astype(F32))
    return parts[0], parts[1].astype(BF)


def scatter_outer(state, axis, *later):
    keep, send = state
    return scatter_add(keep, tie(swap(send, axis), *later))


def scatter_add(keep, came):
    send = (keep[1] + came[1].astype(F32)).astype(BF)
    return keep[0] + came[0].astype(F32), send


def scatter_inner(state, axis):
    keep, send = state
    return keep + swap(send, axis).astype(F32)


def tie_pair(pair, *earlier):
    return pair[0], tie(pair[1], *earlier)


def tie_send(state, *earlier):
    return state[0], tie(state[1], *earlier)


def ring_gather(block, z_count):
    rows = block.shape[0]
    place = lax.axis_index("z")
    full = jnp.zeros((z_count * rows, block.shape[1]), block.dtype)
    for step in range(z_count):
        slot = lax.rem(place + z_count - step, z_count)
        full = lax.dynamic_update_slice_in_dim(full, block, slot * rows, axis=0)
        if step < z_count - 1:
            block = lax.ppermute(block, "z", [(i, (i + 1) % z_count) for i in range(z_count)])
    return full


def sum_everywhere(tensor, z_count, beside):
    def add(tensor, axis, pairs):
        return tensor + lax.ppermute(tensor, axis, pairs)

    tensor = add(tensor, "x", [(0, 1), (1, 0)])
    reach = 1
    while reach < z_count:
        tensor = add(tensor, "z", [(i, i ^ reach) for i in range(z_count)])
        reach *= 2
    tensor = add(tensor, "c", [(0, 1), (1, 0)])
    return add(tie(tensor, beside), "y", [(0, 1), (1, 0)])


def mm(a, b, dims):
    return lax.dot_general(a, b, (dims, ((), ())), preferred_element_type=F32)


NN = ((1,), (0,))
NT = ((1,), (1,))
TN = ((0,), (0,))


def mm_mem(a, b, dims):
    return mm(a.astype(BF), b.astype(BF), dims)


def elu_one(tensor):
    return jnp.where(tensor > 0, tensor + 1.0, jnp.exp(jnp.minimum(tensor, 0.0)))


def elu_slope(tensor):
    low = jnp.where(tensor == 0, 0.5, jnp.exp(jnp.minimum(tensor, 0.0)))
    return jnp.where(tensor > 0, 1.0, low)


def segment_of(ref, r, part):
    block = ref[:, :, r, :, part * HEAD_DIM : (part + 1) * HEAD_DIM]
    return block.reshape(-1, HEAD_DIM)


def memory_forward(qs, ks, vs, cols):
    seg_count = len(qs)
    saved = []
    memory = normer = None
    for r in range(seg_count):
        reading, writing, keep = cols[r]
        sq = elu_one(qs[r].astype(F32))
        sk = elu_one(ks[r].astype(F32))
        value = vs[r].astype(F32)
        rows = sq.shape[0]
        item = dict(sq=sq, sk=sk)
        if r == 0:
            item["recalled"] = jnp.zeros_like(sq)
            change = value
        else:
            both = mm_mem(jnp.concatenate([sq, sk], axis=0), memory, NN)
            num = both[:rows]
            den = 1.0 + jnp.sum(sq * normer, axis=-1, keepdims=True)
            item["recalled"] = reading * num / den
            before = keep * both[rows:]
            kden = 1.0 + keep * jnp.sum(sk * normer, axis=-1, keepdims=True)
            change = value - before / kden
            item.update(num=num, den=den, before=before, kden=kden, memory=memory, normer=normer)
        item["change"] = change
        if r < seg_count - 1:
            write = sk * writing
            fresh = mm_mem(write, change, TN)
            fresh_norm = jnp.sum(write, axis=0, keepdims=True)
            memory = fresh if r == 0 else keep * memory + fresh
            normer = fresh_norm if r == 0 else keep[:1] * normer + fresh_norm
        saved.append(item)
    return saved


def local_probs(query, key, allowed):
    scores = jnp.where(allowed > 0, mm(query, key, NT) * SCALING, NEG)
    exponent = jnp.exp(scores - jnp.max(scores, axis=-1, keepdims=True))
    return exponent / jnp.sum(exponent, axis=-1, keepdims=True)


def columns_of(cols_ref, r):
    cols = cols_ref[r]
    return cols[:, 0:1], cols[:, 1:2], cols[:, 2:3]


def attention_fwd_kernel(heads, proj_ref, mask_ref, cols_ref, gate_ref, out_ref):
    seg_count = mask_ref.shape[0]
    cols = [columns_of(cols_ref, r) for r in range(seg_count)]
    for h in range(heads):
        qs = [segment_of(proj_ref, r, h) for r in range(seg_count)]
        ks = [segment_of(proj_ref, r, heads + h) for r in range(seg_count)]
        vs = [segment_of(proj_ref, r, 2 * heads + h) for r in range(seg_count)]
        saved = memory_forward(qs, ks, vs, cols)
        mixing = gate_ref[h : h + 1]
        for r in range(seg_count):
            prob_low = local_probs(qs[r], ks[r], mask_ref[r]).astype(BF)
            local_out = mm(prob_low, vs[r], NN)
            combined = mixing * saved[r]["recalled"] + (1.0 - mixing) * local_out
            out_ref[:, :, r, :, h * HEAD_DIM : (h + 1) * HEAD_DIM] = combined.astype(BF).reshape(
                out_ref.shape[0], out_ref.shape[1], out_ref.shape[3], HEAD_DIM
            )


def attention_bwd_kernel(
    heads, proj_ref, grad_ref, mask_ref, cols_ref, gate_ref, out_ref, gate_out_ref
):
    seg_count = mask_ref.shape[0]
    cols = [columns_of(cols_ref, r) for r in range(seg_count)]

    def put(r, part, value):
        out_ref[:, :, r, :, part * HEAD_DIM : (part + 1) * HEAD_DIM] = value.astype(BF).reshape(
            out_ref.shape[0], out_ref.shape[1], out_ref.shape[3], HEAD_DIM
        )

    for h in range(heads):
        qs = [segment_of(proj_ref, r, h) for r in range(seg_count)]
        ks = [segment_of(proj_ref, r, heads + h) for r in range(seg_count)]
        vs = [segment_of(proj_ref, r, 2 * heads + h) for r in range(seg_count)]
        saved = memory_forward(qs, ks, vs, cols)
        mixing = gate_ref[h : h + 1]
        gate_sum = jnp.zeros((1, HEAD_DIM), F32)
        d_memory = d_normer = None
        for r in reversed(range(seg_count)):
            reading, writing, keep = cols[r]
            item = saved[r]
            sq, sk = item["sq"], item["sk"]
            rows = sq.shape[0]
            d_combined = segment_of(grad_ref, r, h).astype(F32)
            d_recalled = mixing * d_combined
            d_local = ((1.0 - mixing) * d_combined).astype(BF)
            probs = local_probs(qs[r], ks[r], mask_ref[r])
            prob_low = probs.astype(BF)
            local_out = mm(prob_low, vs[r], NN)
            gate_sum = gate_sum + jnp.sum(
                d_combined * (item["recalled"] - local_out), axis=0, keepdims=True
            )
            d_prob = mm(d_local, vs[r], NT)
            d_value = mm(prob_low, d_local, TN)
            d_scores = (
                probs * (d_prob - jnp.sum(d_prob * probs, axis=-1, keepdims=True))
            ).astype(BF)
            d_query = mm(d_scores, ks[r], NN) * SCALING
            d_key = mm(d_scores, qs[r], TN) * SCALING
            d_sk = None
            d_before = d_kden = None
            if r < seg_count - 1:
                d_change = writing * mm_mem(sk, d_memory, NN)
                d_sk = writing * (mm_mem(item["change"], d_memory, NT) + d_normer)
                d_value = d_value + d_change
                if r > 0:
                    d_before = keep * (-d_change / item["kden"])
                    d_kden = keep * (
                        jnp.sum(d_change * item["before"], axis=-1, keepdims=True)
                        / (item["kden"] * item["kden"])
                    )
            if r > 0:
                d_num = reading * d_recalled / item["den"]
                d_den = -reading * (
                    jnp.sum(d_recalled * item["num"], axis=-1, keepdims=True)
                    / (item["den"] * item["den"])
                )
                if d_before is None:
                    d_sq = mm_mem(d_num, item["memory"], NT) + d_den * item["normer"]
                    new_memory = mm_mem(sq, d_num, TN)
                    new_normer = jnp.sum(sq * d_den, axis=0, keepdims=True)
                else:
                    stacked = jnp.concatenate([d_num, d_before], axis=0)
                    both = mm_mem(stacked, item["memory"], NT)
                    d_sq = both[:rows] + d_den * item["normer"]
                    d_sk = d_sk + both[rows:] + d_kden * item["normer"]
                    new_memory = keep * d_memory + mm_mem(
                        jnp.concatenate([sq, sk], axis=0), stacked, TN
                    )
                    new_normer = keep[:1] * d_normer + jnp.sum(
                        sq * d_den + sk * d_kden, axis=0, keepdims=True
                    )
                d_memory, d_normer = new_memory, new_normer
                d_query = d_query + d_sq * elu_slope(qs[r].astype(F32))
            if d_sk is not None:
                d_key = d_key + d_sk * elu_slope(ks[r].astype(F32))
            put(r, h, d_query)
            put(r, heads + h, d_key)
            put(r, 2 * heads + h, d_value)
        gate_out_ref[h : h + 1] = gate_sum


def block_spec(shape, where):
    dims = list(shape)
    dims[where] = None

    def index(s):
        place = [0] * len(dims)
        place[where] = s
        return tuple(place)

    return pl.BlockSpec(tuple(dims), index)


def attention_fwd(projected, mask, cols, gate_rows, where):
    heads = gate_rows.shape[0]
    out_shape = projected.shape[:-1] + (heads * HEAD_DIM,)
    return pl.pallas_call(
        functools.partial(attention_fwd_kernel, heads),
        grid=(projected.shape[where],),
        in_specs=[
            block_spec(projected.shape, where),
            pl.BlockSpec((None,) + mask.shape[1:], lambda s: (s, 0, 0, 0)),
            pl.BlockSpec((None,) + cols.shape[1:], lambda s: (s, 0, 0, 0)),
            pl.BlockSpec(gate_rows.shape, lambda s: (0, 0)),
        ],
        out_specs=block_spec(out_shape, where),
        out_shape=jax.ShapeDtypeStruct(out_shape, BF),
        compiler_params=pltpu.CompilerParams(vmem_limit_bytes=VMEM_LIMIT),
        cost_estimate=pl.CostEstimate(
            flops=7_600_000_000, bytes_accessed=3_000_000, transcendentals=0
        ),
        name="attention_forward",
    )(projected, mask, cols, gate_rows)


def attention_bwd(projected, d_combined, mask, cols, gate_rows, where):
    heads = gate_rows.shape[0]
    seqs = projected.shape[where]
    return pl.pallas_call(
        functools.partial(attention_bwd_kernel, heads),
        grid=(seqs,),
        in_specs=[
            block_spec(projected.shape, where),
            block_spec(d_combined.shape, where),
            pl.BlockSpec((None,) + mask.shape[1:], lambda s: (s, 0, 0, 0)),
            pl.BlockSpec((None,) + cols.shape[1:], lambda s: (s, 0, 0, 0)),
            pl.BlockSpec(gate_rows.shape, lambda s: (0, 0)),
        ],
        out_specs=[
            block_spec(projected.shape, where),
            pl.BlockSpec((None, heads, HEAD_DIM), lambda s: (s, 0, 0)),
        ],
        out_shape=[
            jax.ShapeDtypeStruct(projected.shape, BF),
            jax.ShapeDtypeStruct((seqs, heads, HEAD_DIM), F32),
        ],
        compiler_params=pltpu.CompilerParams(vmem_limit_bytes=VMEM_LIMIT),
        cost_estimate=pl.CostEstimate(
            flops=14_400_000_000, bytes_accessed=5_000_000, transcendentals=0
        ),
        name="attention_backward",
    )(projected, d_combined, mask, cols, gate_rows)


GELU_A = 0.7978845608028654
GELU_B = 0.044715


def ff_kernel(width, half, x_mine, x_other, g_mine, g_other, w_ref, *outs):
    step = pl.program_id(0)

    @pl.when(step < half)
    def first():
        ff_tile(width, x_mine, g_mine, w_ref, outs[0], outs[2])

    @pl.when(step >= half)
    def second():
        ff_tile(width, x_other, g_other, w_ref, outs[1], outs[3])


def ff_tile(width, x_ref, g_ref, w_ref, act_ref, grad_ref):
    weights = w_ref[...]
    gate_up = mm(x_ref[...], weights[:, : 2 * width], NN)
    d_active = mm(g_ref[...], weights[:, 2 * width :], NN)
    gate = gate_up[:, :width]
    up = gate_up[:, width:]
    square = gate * gate
    tanh = jnp.tanh(GELU_A * gate * (1.0 + GELU_B * square))
    half = 0.5 * (1.0 + tanh)
    gelu = gate * half
    slope = half + 0.5 * gate * (1.0 - tanh * tanh) * GELU_A * (1.0 + 3.0 * GELU_B * square)
    act_ref[...] = (gelu * up).astype(BF)
    grad_ref[:, :width] = (d_active * up * slope).astype(BF)
    grad_ref[:, width:] = (d_active * gelu).astype(BF)


def feed_forward(rows, grads, weights):
    tokens = rows[0].shape[0]
    width = weights.shape[1] // 3
    tile = 256
    half = tokens // tile

    def first(columns):
        return pl.BlockSpec((tile, columns), lambda i: (jnp.minimum(i, half - 1), 0))

    def second(columns):
        return pl.BlockSpec((tile, columns), lambda i: (jnp.maximum(i - half, 0), 0))

    whole = pl.BlockSpec(weights.shape, lambda i: (0, 0), pipeline_mode=pl.Buffered(1))
    act = jax.ShapeDtypeStruct((tokens, width), BF)
    grad = jax.ShapeDtypeStruct((tokens, 2 * width), BF)
    out = pl.pallas_call(
        functools.partial(ff_kernel, width, half),
        grid=(2 * half,),
        in_specs=[first(D), second(D), first(D), second(D), whole],
        out_specs=[first(width), second(width), first(2 * width), second(2 * width)],
        out_shape=[act, act, grad, grad],
        compiler_params=pltpu.CompilerParams(vmem_limit_bytes=VMEM_LIMIT),
        cost_estimate=pl.CostEstimate(
            flops=26 * tokens * D * width, bytes_accessed=tokens * D, transcendentals=0
        ),
        name="feed_forward",
    )(*rows, *grads, weights)
    return (out[0], out[1]), (out[2], out[3])


def down_kernel(count, half, *refs):
    step = pl.program_id(0)
    mine, other, weights = (refs[k * count : (k + 1) * count] for k in range(3))

    def tile(rows, out_ref):
        terms = [mm(a[...], w[...], NT) for a, w in zip(rows, weights)]
        out_ref[...] = sum(terms[1:], terms[0]).astype(BF)

    @pl.when(step < half)
    def first():
        tile(mine, refs[3 * count])

    @pl.when(step >= half)
    def second():
        tile(other, refs[3 * count + 1])


def down_product(active, weights):
    count = len(active)
    tokens, width = active[0][0].shape
    tile = 256
    half = tokens // tile

    def first(columns):
        return pl.BlockSpec((tile, columns), lambda i: (jnp.minimum(i, half - 1), 0))

    def second(columns):
        return pl.BlockSpec((tile, columns), lambda i: (jnp.maximum(i - half, 0), 0))

    down = pl.BlockSpec((D, width), lambda i: (0, 2), pipeline_mode=pl.Buffered(1))
    return pl.pallas_call(
        functools.partial(down_kernel, count, half),
        grid=(2 * half,),
        in_specs=[first(width)] * count + [second(width)] * count + [down] * count,
        out_specs=[first(D), second(D)],
        out_shape=[jax.ShapeDtypeStruct((tokens, D), BF)] * 2,
        compiler_params=pltpu.CompilerParams(vmem_limit_bytes=VMEM_LIMIT),
        cost_estimate=pl.CostEstimate(
            flops=4 * count * tokens * D * width,
            bytes_accessed=2 * D * (count * width + 2 * tokens),
            transcendentals=0,
        ),
        name="down_product",
    )(*[a for a, _ in active], *[b for _, b in active], *weights)


def grads_kernel(count, *refs):
    rows, grads, by_rows, by_grads = (refs[k * count : (k + 1) * count] for k in range(4))
    out_ref = refs[4 * count]
    split = by_rows[0].shape[1]

    def total(left, right):
        acc = None
        for a, b in zip(left, right):
            term = mm(a[...], b[...], TN)
            acc = term if acc is None else acc + term
        return acc

    out_ref[:, :split] = total(rows, by_rows).astype(BF)
    out_ref[:, split:] = total(grads, by_grads).astype(BF)


def weight_grads(rows, grads, by_rows, by_grads):
    def halves(arrays):
        parts = []
        for a in arrays:
            parts += [(a[0], 0), (a[1], 0)] if isinstance(a, tuple) else [(a, 0), (a, 1)]
        return parts

    groups = [halves(a) for a in (rows, grads, by_rows, by_grads)]
    count = len(groups[0])
    tokens = groups[0][0][0].shape[0] // (1 if isinstance(rows[0], tuple) else 2)
    first, second = groups[2][0][0].shape[1], groups[3][0][0].shape[1]
    tile = 512

    def tall(half):
        return pl.BlockSpec((tokens, tile), lambda i: (half, i))

    def whole(width, half):
        return pl.BlockSpec((tokens, width), lambda i: (half, 0), pipeline_mode=pl.Buffered(1))

    return pl.pallas_call(
        functools.partial(grads_kernel, count),
        grid=(D // tile,),
        in_specs=[tall(half) for _, half in groups[0] + groups[1]]
        + [whole(first, half) for _, half in groups[2]]
        + [whole(second, half) for _, half in groups[3]],
        out_specs=pl.BlockSpec((tile, first + second), lambda i: (i, 0)),
        out_shape=jax.ShapeDtypeStruct((D, first + second), BF),
        compiler_params=pltpu.CompilerParams(vmem_limit_bytes=VMEM_LIMIT),
        cost_estimate=pl.CostEstimate(
            flops=3 * count * tokens * D * (first + second),
            bytes_accessed=2 * (2 * count * tokens * D + (count * tokens + D) * (first + second)),
            transcendentals=0,
        ),
        name="weight_grads",
    )(*[a for group in groups for a, _ in group])


RATE_QKV = D ** (-0.5)
RATE_OUT = 4.0 * (HEADS * HEAD_DIM) ** (-0.5)
RATE_DOWN = FF ** (-0.5)


def clip_factor(small):
    row = lax.broadcasted_iota(jnp.int32, small.shape, 0)
    lane = lax.broadcasted_iota(jnp.int32, small.shape, 1)
    summed = (row == small.shape[0] - 1) & (lane >= HEADS)
    squares = jnp.sum(jnp.where(summed, small, small * small), axis=(0, 1), keepdims=True)
    grad_norm = jnp.sqrt(squares)
    return grad_norm, jnp.minimum(1.0, CLIP / (grad_norm + 1e-06))


def adam_kernel(steps, chunks, place_ref, small_ref, *refs):
    ins, refs = refs[:18], refs[18:]
    grads, refs = refs[: 2 + 2 * chunks], refs[2 + 2 * chunks :]
    outs, norm_ref, scratch = refs[:18], refs[18], refs[19]
    grad_norm, factor = clip_factor(small_ref[...])
    is_low = place_ref[0] == 0
    everything = slice(None)

    def put(number, place, gradient, rate, decay=DECAY):
        weight, moment, second = (r[place] for r in ins[3 * number : 3 * number + 3])
        new = adam_update(weight, moment, second, gradient.astype(F32), factor, rate, decay)
        for ref, value in zip(outs[3 * number : 3 * number + 3], new):
            ref[place] = value

    def sides_of(mine, theirs):
        mine, theirs = mine[...], theirs[...]
        return jnp.where(is_low, mine, theirs), jnp.where(is_low, theirs, mine)

    for s, side in enumerate(sides_of(*grads[:2])):
        width = side.shape[1] // 4
        cols = slice(s * width, (s + 1) * width)
        for part in range(3):
            put(0, (part, everything, cols), side[:, part * width : (part + 1) * width], RATE_QKV)
        put(1, (everything, cols), side[:, 3 * width :], RATE_OUT)
    rows, width_ff = ins[9].shape
    lanes = width_ff // 128
    for k in range(chunks):
        for s, side in enumerate(sides_of(*grads[2 + 2 * k : 4 + 2 * k])):
            side = side.astype(F32)
            width = side.shape[1] // 3
            start = s * (width_ff // 2) + k * width
            put(3, (everything, slice(start, start + width)), side[:, 2 * width :], RATE_DOWN)
            for part in range(2):
                for lane in range(width // 128):
                    place = pl.ds((start // 128 + lane) * 2 + part, rows, stride=2 * lanes)
                    first = part * width + lane * 128
                    scratch[place, :] = side[:, first : first + 128]
    put(2, (everything, everything), scratch[...], RATE_QKV)

    @pl.when(pl.program_id(0) == 0)
    def small_ones():
        last = ins[12].shape[0]
        put(4, (everything, everything), small_ref[:last], 0.5, 0.0)
        put(5, (everything, everything), small_ref[last:, :HEADS], 1.0, 0.0)
        norm_ref[...] = grad_norm


def mlp_view(t):
    rows, _, width_ff = t.shape
    return t.reshape(rows, 2, width_ff // 128, 128).transpose(0, 2, 1, 3).reshape(-1, 128)


def adam_all(small, x_place, arrays, att_sides, ff_sides):
    rows, _, width_ff = arrays[6].shape
    steps = 4

    def qkv_view(t):
        return jnp.transpose(t, (1, 0, 2))

    def mlp_back(t, shape):
        rows, _, width_ff = shape
        t = t.reshape(rows, width_ff // 128, 2, 128).transpose(0, 2, 1, 3)
        return t.reshape(shape)

    views = [qkv_view(t) for t in arrays[:3]] + list(arrays[3:6])
    views += [mlp_view(t) for t in arrays[6:9]] + list(arrays[9:12])
    gains = [mlp_view(t[None]) for t in arrays[12:15]] + [t[None] for t in arrays[15:]]
    grads = list(att_sides) + [t for pair in ff_sides for t in pair]

    def spec(t):
        axis = t.ndim - 2
        block = list(t.shape)
        block[axis] //= steps
        return pl.BlockSpec(tuple(block), lambda i, place: (0,) * axis + (i, 0))

    def whole(t):
        return pl.BlockSpec(t.shape, lambda i, place: (0, 0))

    def mine(t):
        return pl.BlockSpec((rows // steps, t.shape[1]), lambda i, place: (place[0] * steps + i, 0))

    specs = [spec(t) for t in views] + [whole(t) for t in gains]
    new = pl.pallas_call(
        functools.partial(adam_kernel, steps, len(ff_sides)),
        grid_spec=pltpu.PrefetchScalarGridSpec(
            num_scalar_prefetch=1,
            grid=(steps,),
            in_specs=[whole(small)]
            + specs
            + [spec(t) if k % 2 else mine(t) for k, t in enumerate(grads)],
            out_specs=specs + [pl.BlockSpec((1, 1), lambda i, place: (0, 0))],
            scratch_shapes=[pltpu.VMEM((views[6].shape[0] // steps, 128), F32)],
        ),
        out_shape=[jax.ShapeDtypeStruct(t.shape, F32) for t in views + gains]
        + [jax.ShapeDtypeStruct((1, 1), F32)],
        compiler_params=pltpu.CompilerParams(vmem_limit_bytes=VMEM_LIMIT),
        cost_estimate=pl.CostEstimate(
            flops=20 * sum(t.size for t in views) // 3,
            bytes_accessed=8 * sum(t.size for t in views),
            transcendentals=0,
        ),
        name="adam",
    )(x_place[None], small, *views, *gains, *grads)
    new = list(new)
    return (
        [qkv_view(t) for t in new[:3]]
        + new[3:6]
        + [mlp_back(t, arrays[6].shape) for t in new[6:9]]
        + new[9:12]
        + [mlp_back(t, (1,) + arrays[12].shape)[0] for t in new[12:15]]
        + [t[0] for t in new[15:18]]
        + [new[18].reshape(())]
    )


def on_device(
    inputs,
    doc_ids,
    cotangent,
    weight_qkv,
    moment_qkv,
    second_qkv,
    weight_out,
    moment_out,
    second_out,
    weight_mlp,
    moment_mlp,
    second_mlp,
    weight_down,
    moment_down,
    second_down,
    norm_gains,
    moment_gains,
    second_gains,
    gate_logit,
    moment_gate,
    second_gate,
):
    micro_count, _, seg_count, own_len, _ = inputs.shape
    own_tokens = seg_count * own_len
    x_place = lax.axis_index("x")
    y_place = lax.axis_index("y")
    c_place = lax.axis_index("c")
    orders = [("x", "y") if m % 2 == 0 else ("y", "x") for m in range(micro_count)]

    z_count = D // (2 * weight_qkv.shape[0])

    def half_columns(weight, which):
        width = weight.shape[-1] // 2
        return lax.dynamic_slice_in_dim(weight, which * width, width, axis=weight.ndim - 1)

    def join_rows(mine, theirs):
        both = jnp.zeros((2 * rows, mine.shape[1]), BF)
        both = lax.dynamic_update_slice_in_dim(both, mine, x_place * rows, axis=0)
        return lax.dynamic_update_slice_in_dim(both, theirs, (1 - x_place) * rows, axis=0)

    def fetch(block):
        return lax.all_gather(block, "z", axis=0, tiled=True)

    rows = weight_qkv.shape[0]
    heads = weight_qkv.shape[2] // (2 * HEAD_DIM)
    width_att = heads * HEAD_DIM
    width_ff = weight_down.shape[1] // 2
    width = width_ff // CHUNKS

    def qkv_columns(which):
        return half_columns(weight_qkv, which).astype(BF).reshape(rows, -1)

    def ff_columns(k, which):
        start = which * width_ff + k * width
        mlp = lax.dynamic_slice_in_dim(mlp_later, start, width, axis=2).astype(BF)
        down = lax.dynamic_slice_in_dim(down_later, start, width, axis=1).astype(BF)
        return jnp.concatenate([mlp[:, 0], mlp[:, 1], down], axis=1)

    send_qkv = qkv_columns(1 - x_place)
    all_out = ring_gather(tie(weight_out, send_qkv).astype(BF), z_count)
    all_ids = tie(doc_ids[:, 0], send_qkv)
    for axis in ("y", "c"):
        all_ids = jnp.stack([all_ids, swap(all_ids, axis)], axis=0)
    their_qkv = swap(send_qkv, "x")
    shard_qkv = join_rows(qkv_columns(x_place), tie(their_qkv, all_ids))
    full_qkv = fetch(shard_qkv)

    head_start = (y_place * 2 + c_place) * (2 * heads) + x_place * heads
    gate_local = lax.dynamic_slice_in_dim(gate_logit, head_start, heads)
    mixing = jax.nn.sigmoid(gate_local)
    gate_rows = jnp.broadcast_to(mixing[:, None], (heads, HEAD_DIM))

    micros = range(micro_count)
    tokens = 8 * own_tokens
    token_rows = [
        tie(inputs[m, 0], send_qkv).reshape(own_tokens, D).astype(F32) for m in micros
    ]
    back_low = [cotangent[m, 0].reshape(own_tokens, D) for m in micros]
    all_ids = jnp.stack([all_ids, swap(all_ids, "x")], axis=0)
    normed_att = [rms_norm(t, norm_gains[0]).astype(BF) for t in token_rows]
    att_states = [
        gather_start(normed_att[m], *orders[m], (their_qkv, all_ids)) for m in micros
    ]
    att_by_x = [state[1 + orders[m].index("y")] for m, state in enumerate(att_states)]
    mlp_later = tie(weight_mlp, *att_by_x)
    down_later = tie(weight_down, *att_by_x)
    att_states = [gather_across(state, *orders[m], "y") for m, state in enumerate(att_states)]
    att_rows = [gather_core(state) for state in att_states]

    def their_ff(k, *earlier):
        return swap(tie(ff_columns(k, 1 - x_place), *earlier), "x")

    theirs = their_ff(0, *att_by_x)
    shard_ff = [join_rows(ff_columns(0, x_place), theirs)]
    full_ff = [fetch(shard_ff[0])]
    their_out = swap(tie(half_columns(all_out, 1 - x_place), shard_ff[0]), "x")
    both_out = jnp.zeros((z_count, 2, rows, width_att), BF)
    for part, place in ((half_columns(all_out, x_place), x_place), (their_out, 1 - x_place)):
        part = part.reshape(z_count, 1, rows, width_att)
        both_out = lax.dynamic_update_slice_in_dim(both_out, part, place, axis=1)
    full_out = both_out.reshape(D, width_att)
    att_last = [state[-1] for state in att_states]
    back_states = [
        gather_start(back_low[m], *orders[m], (their_out,), att_last) for m in micros
    ]
    back_first = [t for state in back_states for t in state[1:]]
    back_states = [gather_across(state, *orders[m], "y") for m, state in enumerate(back_states)]
    earlier = back_first

    rel_c = jnp.arange(2)[:, None, None] ^ c_place
    rel_y = jnp.arange(2)[None, :, None] ^ y_place
    places = ((rel_y * 2 + rel_c) * own_len + jnp.arange(own_len)).reshape(-1)
    causal = places[:, None] >= places[None, :]
    masks = []
    columns = []
    for m in micros:
        ids = jnp.transpose(all_ids[:, :, :, m], (0, 3, 1, 2, 4)).reshape(2, seg_count, -1)
        same = ids[:, :, :, None] == ids[:, :, None, :]
        masks.append((same & causal).astype(F32))
        last = jnp.max(ids, axis=2)
        previous = jnp.concatenate([jnp.full((2, 1), -1, last.dtype), last[:, :-1]], axis=1)
        reading = ids == previous[:, :, None]
        writing = ids == last[:, :, None]
        keep = jnp.broadcast_to((last == previous)[:, :, None], ids.shape)
        columns.append(jnp.stack([reading, writing, keep], axis=-1).astype(F32))

    slots = (2, 2, 2, seg_count, own_len)
    wheres = [1 if orders[m][0] == "x" else 2 for m in micros]
    projected = []
    combined = []
    hidden = []
    normed_mlp = []
    for m in micros:
        mine, other = att_rows[m]
        if m == 0:
            mine = tie(mine, *back_first)
        proj = jnp.concatenate([mm(p, full_qkv, NN).astype(BF) for p in (mine, other)], axis=0)
        projected.append(proj.reshape(slots + (3 * width_att,)))
        comb = attention_fwd(projected[m], masks[m], columns[m], gate_rows, wheres[m])
        combined.append(comb.reshape(tokens, width_att))
    half = tokens // 2
    for k in range(1, CHUNKS):
        theirs = their_ff(k, *earlier)
        shard_ff.append(join_rows(ff_columns(k, x_place), tie(theirs, combined[0])))
        full_ff.append(fetch(shard_ff[k]))
        earlier = [theirs]
    back_states = [(tie(state[0], combined[0]),) + state[1:] for state in back_states]
    back_rows = [gather_core(state) for state in back_states]
    for m in micros:
        ready = combined[m]
        if m > 0:
            ready = tie(ready, *shard_ff, *[state[-1] for state in back_states])
        other = mm(ready[half:], full_out, NT).astype(BF)
        mine = mm(ready[:half], full_out, NT).astype(BF)
        state = scatter_core(mine, other, own_tokens, orders[m][0], orders[m][0])
        state = scatter_outer(state, orders[m][0])
        hidden.append(token_rows[m] + scatter_inner(state, orders[m][1]))
        normed_mlp.append(rms_norm(hidden[m], norm_gains[1]).astype(BF))
    mlp_rows = [gather_core(state) for state in gather_steps(normed_mlp, orders)]

    def exchange_grad(grad):
        return grad, swap(lax.dynamic_slice_in_dim(grad, (1 - x_place) * rows, rows, axis=0), "x")

    def squares_of(grad):
        wide = grad.astype(F32)
        return jnp.sum(wide * wide)

    def reduce_rows(partial):
        return lax.psum_scatter(partial, "z", scatter_dimension=0, tiled=True)

    def products(left, right, totals, dtype):
        terms = [mm(left[p], right, NT) for p in (1, 0)][::-1]
        if totals is not None:
            terms = [a + b for a, b in zip(totals, terms)]
        return tuple(t.astype(dtype) for t in terms)

    active = []
    d_gate_up = []
    own_ff = []
    d_total = [None] * micro_count
    states = [None] * micro_count
    for k in range(CHUNKS):
        active.append([])
        d_gate_up.append([])
        last = k == CHUNKS - 1
        for m in micros:
            rows_in = mlp_rows[m]
            if last and m > 0:
                rows_in = (tie(rows_in[0], *d_total[m - 1]), rows_in[1])
            act, grad = feed_forward(rows_in, back_rows[m], full_ff[k])
            active[k].append(act)
            d_gate_up[k].append(grad)
            if last and m > 0:
                grad = (grad[0], tie(grad[1], states[m - 1][1]))
            dtype = BF if last else F32
            d_total[m] = products(grad, full_ff[k][:, : 2 * width], d_total[m], dtype)
            if last:
                states[m] = scatter_core(*d_total[m], own_tokens, orders[m][0], orders[m][0])
        if not last:
            grad_ff = weight_grads(mlp_rows, back_rows, d_gate_up[k], active[k])
            own_ff.append(reduce_rows(grad_ff))
            terms = [t for pair in d_total for t in pair]
            full_ff[k + 1] = tie(full_ff[k + 1], grad_ff, *terms)

    out_pairs = []
    for m in micros:
        act = [active[k][m] for k in range(CHUNKS)]
        act[-1] = (act[-1][0], tie(act[-1][1], states[-1][1]))
        out_pairs.append(down_product(act, full_ff))
    products_done = [t for pair in out_pairs for t in pair]
    outer_states = [scatter_outer(states[m], orders[m][0], *products_done) for m in micros]
    last_active = [
        (active[-1][m][0], tie(active[-1][m][1], *[t[1] for t in outer_states])) for m in micros
    ]
    grad_ff = weight_grads(mlp_rows, back_rows, d_gate_up[-1], last_active)
    own_ff.append(reduce_rows(grad_ff))

    gain_grad_att = jnp.zeros((D,), F32)
    gain_grad_mlp = jnp.zeros((D,), F32)
    d_hidden = []
    for m in micros:
        keep, send = outer_states[m]
        d_normed = scatter_inner((tie(keep, grad_ff), send), orders[m][1])
        ignored, norm_back = jax.vjp(rms_norm, hidden[m], norm_gains[1])
        d_norm, d_gain = norm_back(d_normed)
        gain_grad_mlp = gain_grad_mlp + d_gain
        d_hidden.append(back_low[m].astype(F32) + d_norm)

    gate_sum = jnp.zeros((heads,), F32)
    d_projs = []
    out_states = [
        scatter_core(*tie_pair(out_pairs[m], *d_hidden), own_tokens, orders[m][0], orders[m][0])
        for m in micros
    ]
    grad_states = gather_steps([t.astype(BF) for t in d_hidden], orders)
    sends = [t[1] for t in out_states]
    out_states = [tie_send(t, *[g[-1] for g in grad_states]) for t in out_states]
    att_grads = [gather_core((tie(g[0], *sends),) + g[1:]) for g in grad_states]
    ff_pairs = [exchange_grad(own_ff[0])]
    for m in micros:
        mine, other = att_grads[m]
        if m == 0:
            other = tie(other, own_ff[0])
        d_combined = jnp.concatenate(
            [mm(mine, full_out, NN), mm(other, full_out, NN)], axis=0
        )
        d_proj, gate_part = attention_bwd(
            projected[m],
            d_combined.reshape(slots + (width_att,)),
            masks[m],
            columns[m],
            gate_rows,
            wheres[m],
        )
        gate_sum = gate_sum + jnp.sum(gate_part, axis=(0, 2))
        d_projs.append(d_proj.reshape(tokens, 3 * width_att))
    out_came = [swap(out_states[m][1], orders[m][0]) for m in micros]
    by_rows = [d_projs[0], tie(d_projs[-1], ff_pairs[0][1], *out_came)]
    grad_att = weight_grads(att_rows, att_grads, by_rows, combined)
    own_att = reduce_rows(grad_att)
    mlp_out = []
    for m in micros:
        state = scatter_add(out_states[m][0], tie(out_came[m], grad_att))
        mlp_out.append(scatter_inner(state, orders[m][1]))
    block_out = [(hidden[m] + mlp_out[m]).astype(BF) for m in micros]

    ff_pairs += [exchange_grad(g) for g in own_ff[1:]]

    ff_owned = sum(squares_of(g) for g in own_ff)

    grad_rows = []
    in_states = []
    for m in micros:
        d_proj = tie(d_projs[m], grad_att)
        other = mm(d_proj[half:], full_qkv, NT).astype(BF)
        mine = mm(d_proj[:half], full_qkv, NT).astype(BF)
        in_states.append(scatter_core(mine, other, own_tokens, orders[m][0], orders[m][0]))
    for m in micros:
        state = scatter_outer(in_states[m], orders[m][0])
        if m > 0:
            state = tie_send(state, ff_pairs[-1][1])
        d_normed = scatter_inner(state, orders[m][1])
        ignored, norm_first = jax.vjp(rms_norm, token_rows[m], norm_gains[0])
        d_norm, d_gain = norm_first(d_normed)
        gain_grad_att = gain_grad_att + d_gain
        grad_rows.append((d_hidden[m] + d_norm).astype(BF))

    att_mine, att_theirs = exchange_grad(own_att)

    gate_grad = gate_sum * mixing * (1.0 - mixing)
    gate_padded = lax.dynamic_update_slice(
        jnp.zeros(gate_logit.shape, F32), gate_grad, (head_start,)
    )
    owned = squares_of(own_att) + ff_owned
    gain_grad = mlp_view(jnp.stack([gain_grad_att, gain_grad_mlp], axis=0)[None])
    last_row = jnp.concatenate([gate_padded, owned[None], jnp.zeros((127 - HEADS,), F32)])
    small = jnp.concatenate([gain_grad, last_row[None]], axis=0)
    small = sum_everywhere(small, z_count, att_theirs)
    arrays = [
        weight_qkv,
        moment_qkv,
        second_qkv,
        weight_out,
        moment_out,
        second_out,
        weight_mlp,
        moment_mlp,
        second_mlp,
        weight_down,
        moment_down,
        second_down,
        norm_gains,
        moment_gains,
        second_gains,
        gate_logit,
        moment_gate,
        second_gate,
    ]
    new = adam_all(small, x_place, arrays, (att_mine, att_theirs), ff_pairs)
    shape = (micro_count, 1, seg_count, own_len, D)
    return (
        jnp.stack(block_out, axis=0).reshape(shape),
        jnp.stack(grad_rows, axis=0).reshape(shape),
        new[-1],
        *new[:-1],
    )


def solution(mesh):
    seq_count, ctx_count = mesh.devices.shape
    inner = Mesh(
        mesh.devices.reshape(seq_count // 2, 2, ctx_count // 2, 2), ("z", "x", "y", "c")
    )
    seq, ctx = ("z", "x"), ("y", "c")
    rows = P(None, seq, None, ctx, None)
    wide = P(seq, None, ctx)
    flat = P(seq, ctx)
    weights = (wide,) * 3 + (flat,) * 3 + (wide,) * 3 + (flat,) * 3 + (P(),) * 6
    return jax.shard_map(
        on_device,
        mesh=inner,
        in_specs=(rows, P(None, seq, None, ctx), rows) + weights,
        out_specs=(rows, rows, P()) + weights,
        check_vma=False,
    )
```

```python
import functools

import jax
import jax.numpy as jnp
from jax import lax
from jax.experimental import pallas as pl
from jax.experimental.pallas import tpu as pltpu
from jax.sharding import Mesh
from jax.sharding import PartitionSpec as P

D = 2048
HEADS = 16
HEAD_DIM = 128
FF = 8192
STEP_COUNT = 10
CHUNKS = 2

EPS = 1e-06
NEG = -1e30
CLIP = 1.0
BETA1 = 0.9
BETA2 = 0.95
ADAM_EPS = 1e-08
DECAY = 0.1
BF = jnp.bfloat16
F32 = jnp.float32
SCALING = HEAD_DIM ** (-0.5)
VMEM_LIMIT = 48 * 1024 * 1024


def rms_norm(tensor, scaling):
    return tensor * lax.rsqrt(jnp.mean(tensor * tensor, axis=-1, keepdims=True) + EPS) * scaling


def adam_update(weight, moment, second, gradient, factor, step_rate, decay):
    clipped = gradient * factor
    moment = BETA1 * moment + (1.0 - BETA1) * clipped
    second = BETA2 * second + (1.0 - BETA2) * clipped * clipped
    fixed_first = moment / (1.0 - BETA1**STEP_COUNT)
    fixed_second = second / (1.0 - BETA2**STEP_COUNT)
    updated = weight - step_rate * (
        fixed_first / (jnp.sqrt(fixed_second) + ADAM_EPS) + decay * weight
    )
    return (moment, second, updated)


def swap(tensor, axis):
    return lax.ppermute(tensor, axis, [(0, 1), (1, 0)])


def tie(tensor, *earlier):
    return lax.optimization_barrier((tensor,) + earlier)[0]


def gather_start(own, outer, inner, x_after=(), y_after=()):
    start = {"x": tie(own, *x_after), "y": tie(own, *y_after)}
    return own, swap(start[inner], inner), swap(start[outer], outer)


def gather_across(state, outer, inner, last):
    own, by_inner, by_outer = state
    return state + (swap(by_inner if last == outer else by_outer, last),)


def gather_steps(owns, orders):
    starts = [gather_start(own, *order) for own, order in zip(owns, orders)]
    firsts = [t for state in starts for t in state[1:]]
    ready = []
    for state, order in zip(starts, orders):
        by_inner = tie(state[1], *firsts)
        ready.append((state[0], by_inner, state[2], swap(by_inner, order[0])))
    lasts = [state[-1] for state in ready]
    return [(tie(state[0], *lasts),) + state[1:] for state in ready]


def gather_core(state):
    mine = jnp.concatenate(state, axis=0)
    return mine, swap(mine, "c")


def scatter_core(mine, other, units, outer, first):
    came = swap(other, "c").reshape(2, 2, units, -1)
    mine = mine.reshape(2, 2, units, -1)
    parts = []
    for p in range(2):
        index = (p,) if first == outer else (slice(None), p)
        parts.append(mine[index].astype(F32) + came[index].astype(F32))
    return parts[0], parts[1].astype(BF)


def scatter_outer(state, axis, *later):
    keep, send = state
    return scatter_add(keep, tie(swap(send, axis), *later))


def scatter_add(keep, came):
    send = (keep[1] + came[1].astype(F32)).astype(BF)
    return keep[0] + came[0].astype(F32), send


def scatter_inner(state, axis):
    keep, send = state
    return keep + swap(send, axis).astype(F32)


def tie_pair(pair, *earlier):
    return pair[0], tie(pair[1], *earlier)


def tie_send(state, *earlier):
    return state[0], tie(state[1], *earlier)


def direct_gather(block, z_count):
    rows = block.shape[0]
    place = lax.axis_index("z")
    pieces = [block]
    for step in range(1, z_count):
        pairs = [(i, (i + step) % z_count) for i in range(z_count)]
        pieces.append(lax.ppermute(block, "z", pairs))
    full = jnp.zeros((z_count * rows, block.shape[1]), block.dtype)
    for step, piece in enumerate(pieces):
        slot = lax.rem(place + z_count - step, z_count)
        full = lax.dynamic_update_slice_in_dim(full, piece, slot * rows, axis=0)
    return full


def sum_everywhere(tensor, z_count, beside):
    def add(tensor, axis, pairs):
        return tensor + lax.ppermute(tensor, axis, pairs)

    tensor = add(tensor, "x", [(0, 1), (1, 0)])
    reach = 1
    while reach < z_count:
        tensor = add(tensor, "z", [(i, i ^ reach) for i in range(z_count)])
        reach *= 2
    tensor = add(tensor, "c", [(0, 1), (1, 0)])
    return add(tie(tensor, beside), "y", [(0, 1), (1, 0)])


def mm(a, b, dims):
    return lax.dot_general(a, b, (dims, ((), ())), preferred_element_type=F32)


NN = ((1,), (0,))
NT = ((1,), (1,))
TN = ((0,), (0,))


def mm_mem(a, b, dims):
    return mm(a.astype(BF), b.astype(BF), dims)


def elu_one(tensor):
    return jnp.where(tensor > 0, tensor + 1.0, jnp.exp(jnp.minimum(tensor, 0.0)))


def elu_slope(tensor):
    low = jnp.where(tensor == 0, 0.5, jnp.exp(jnp.minimum(tensor, 0.0)))
    return jnp.where(tensor > 0, 1.0, low)


def segment_of(ref, r, part):
    block = ref[:, :, r, :, part * HEAD_DIM : (part + 1) * HEAD_DIM]
    return block.reshape(-1, HEAD_DIM)


def memory_forward(qs, ks, vs, cols):
    seg_count = len(qs)
    saved = []
    memory = normer = None
    for r in range(seg_count):
        reading, writing, keep = cols[r]
        sq = elu_one(qs[r].astype(F32))
        sk = elu_one(ks[r].astype(F32))
        value = vs[r].astype(F32)
        rows = sq.shape[0]
        item = dict(sq=sq, sk=sk)
        if r == 0:
            item["recalled"] = jnp.zeros_like(sq)
            change = value
        else:
            both = mm_mem(jnp.concatenate([sq, sk], axis=0), memory, NN)
            num = both[:rows]
            den = 1.0 + jnp.sum(sq * normer, axis=-1, keepdims=True)
            item["recalled"] = reading * num / den
            before = keep * both[rows:]
            kden = 1.0 + keep * jnp.sum(sk * normer, axis=-1, keepdims=True)
            change = value - before / kden
            item.update(num=num, den=den, before=before, kden=kden, memory=memory, normer=normer)
        item["change"] = change
        if r < seg_count - 1:
            write = sk * writing
            fresh = mm_mem(write, change, TN)
            fresh_norm = jnp.sum(write, axis=0, keepdims=True)
            memory = fresh if r == 0 else keep * memory + fresh
            normer = fresh_norm if r == 0 else keep[:1] * normer + fresh_norm
        saved.append(item)
    return saved


def local_probs(query, key, allowed):
    scores = jnp.where(allowed > 0, mm(query, key, NT) * SCALING, NEG)
    exponent = jnp.exp(scores - jnp.max(scores, axis=-1, keepdims=True))
    return exponent / jnp.sum(exponent, axis=-1, keepdims=True)


def columns_of(cols_ref, r):
    cols = cols_ref[r]
    return cols[:, 0:1], cols[:, 1:2], cols[:, 2:3]


def attention_fwd_kernel(heads, proj_ref, mask_ref, cols_ref, gate_ref, out_ref):
    seg_count = mask_ref.shape[0]
    cols = [columns_of(cols_ref, r) for r in range(seg_count)]
    for h in range(heads):
        qs = [segment_of(proj_ref, r, h) for r in range(seg_count)]
        ks = [segment_of(proj_ref, r, heads + h) for r in range(seg_count)]
        vs = [segment_of(proj_ref, r, 2 * heads + h) for r in range(seg_count)]
        saved = memory_forward(qs, ks, vs, cols)
        mixing = gate_ref[h : h + 1]
        for r in range(seg_count):
            prob_low = local_probs(qs[r], ks[r], mask_ref[r]).astype(BF)
            local_out = mm(prob_low, vs[r], NN)
            combined = mixing * saved[r]["recalled"] + (1.0 - mixing) * local_out
            out_ref[:, :, r, :, h * HEAD_DIM : (h + 1) * HEAD_DIM] = combined.astype(BF).reshape(
                out_ref.shape[0], out_ref.shape[1], out_ref.shape[3], HEAD_DIM
            )


def attention_bwd_kernel(
    heads, proj_ref, grad_ref, mask_ref, cols_ref, gate_ref, out_ref, gate_out_ref
):
    seg_count = mask_ref.shape[0]
    cols = [columns_of(cols_ref, r) for r in range(seg_count)]

    def put(r, part, value):
        out_ref[:, :, r, :, part * HEAD_DIM : (part + 1) * HEAD_DIM] = value.astype(BF).reshape(
            out_ref.shape[0], out_ref.shape[1], out_ref.shape[3], HEAD_DIM
        )

    for h in range(heads):
        qs = [segment_of(proj_ref, r, h) for r in range(seg_count)]
        ks = [segment_of(proj_ref, r, heads + h) for r in range(seg_count)]
        vs = [segment_of(proj_ref, r, 2 * heads + h) for r in range(seg_count)]
        saved = memory_forward(qs, ks, vs, cols)
        mixing = gate_ref[h : h + 1]
        gate_sum = jnp.zeros((1, HEAD_DIM), F32)
        d_memory = d_normer = None
        for r in reversed(range(seg_count)):
            reading, writing, keep = cols[r]
            item = saved[r]
            sq, sk = item["sq"], item["sk"]
            rows = sq.shape[0]
            d_combined = segment_of(grad_ref, r, h).astype(F32)
            d_recalled = mixing * d_combined
            d_local = ((1.0 - mixing) * d_combined).astype(BF)
            probs = local_probs(qs[r], ks[r], mask_ref[r])
            prob_low = probs.astype(BF)
            local_out = mm(prob_low, vs[r], NN)
            gate_sum = gate_sum + jnp.sum(
                d_combined * (item["recalled"] - local_out), axis=0, keepdims=True
            )
            d_prob = mm(d_local, vs[r], NT)
            d_value = mm(prob_low, d_local, TN)
            d_scores = (
                probs * (d_prob - jnp.sum(d_prob * probs, axis=-1, keepdims=True))
            ).astype(BF)
            d_query = mm(d_scores, ks[r], NN) * SCALING
            d_key = mm(d_scores, qs[r], TN) * SCALING
            d_sk = None
            d_before = d_kden = None
            if r < seg_count - 1:
                d_change = writing * mm_mem(sk, d_memory, NN)
                d_sk = writing * (mm_mem(item["change"], d_memory, NT) + d_normer)
                d_value = d_value + d_change
                if r > 0:
                    d_before = keep * (-d_change / item["kden"])
                    d_kden = keep * (
                        jnp.sum(d_change * item["before"], axis=-1, keepdims=True)
                        / (item["kden"] * item["kden"])
                    )
            if r > 0:
                d_num = reading * d_recalled / item["den"]
                d_den = -reading * (
                    jnp.sum(d_recalled * item["num"], axis=-1, keepdims=True)
                    / (item["den"] * item["den"])
                )
                if d_before is None:
                    d_sq = mm_mem(d_num, item["memory"], NT) + d_den * item["normer"]
                    new_memory = mm_mem(sq, d_num, TN)
                    new_normer = jnp.sum(sq * d_den, axis=0, keepdims=True)
                else:
                    stacked = jnp.concatenate([d_num, d_before], axis=0)
                    both = mm_mem(stacked, item["memory"], NT)
                    d_sq = both[:rows] + d_den * item["normer"]
                    d_sk = d_sk + both[rows:] + d_kden * item["normer"]
                    new_memory = keep * d_memory + mm_mem(
                        jnp.concatenate([sq, sk], axis=0), stacked, TN
                    )
                    new_normer = keep[:1] * d_normer + jnp.sum(
                        sq * d_den + sk * d_kden, axis=0, keepdims=True
                    )
                d_memory, d_normer = new_memory, new_normer
                d_query = d_query + d_sq * elu_slope(qs[r].astype(F32))
            if d_sk is not None:
                d_key = d_key + d_sk * elu_slope(ks[r].astype(F32))
            put(r, h, d_query)
            put(r, heads + h, d_key)
            put(r, 2 * heads + h, d_value)
        gate_out_ref[h : h + 1] = gate_sum


def block_spec(shape, where):
    dims = list(shape)
    dims[where] = None

    def index(s):
        place = [0] * len(dims)
        place[where] = s
        return tuple(place)

    return pl.BlockSpec(tuple(dims), index)


def attention_fwd(projected, mask, cols, gate_rows, where):
    heads = gate_rows.shape[0]
    out_shape = projected.shape[:-1] + (heads * HEAD_DIM,)
    return pl.pallas_call(
        functools.partial(attention_fwd_kernel, heads),
        grid=(projected.shape[where],),
        in_specs=[
            block_spec(projected.shape, where),
            pl.BlockSpec((None,) + mask.shape[1:], lambda s: (s, 0, 0, 0)),
            pl.BlockSpec((None,) + cols.shape[1:], lambda s: (s, 0, 0, 0)),
            pl.BlockSpec(gate_rows.shape, lambda s: (0, 0)),
        ],
        out_specs=block_spec(out_shape, where),
        out_shape=jax.ShapeDtypeStruct(out_shape, BF),
        compiler_params=pltpu.CompilerParams(vmem_limit_bytes=VMEM_LIMIT),
        cost_estimate=pl.CostEstimate(
            flops=7_600_000_000, bytes_accessed=3_000_000, transcendentals=0
        ),
        name="attention_forward",
    )(projected, mask, cols, gate_rows)


def attention_bwd(projected, d_combined, mask, cols, gate_rows, where):
    heads = gate_rows.shape[0]
    seqs = projected.shape[where]
    return pl.pallas_call(
        functools.partial(attention_bwd_kernel, heads),
        grid=(seqs,),
        in_specs=[
            block_spec(projected.shape, where),
            block_spec(d_combined.shape, where),
            pl.BlockSpec((None,) + mask.shape[1:], lambda s: (s, 0, 0, 0)),
            pl.BlockSpec((None,) + cols.shape[1:], lambda s: (s, 0, 0, 0)),
            pl.BlockSpec(gate_rows.shape, lambda s: (0, 0)),
        ],
        out_specs=[
            block_spec(projected.shape, where),
            pl.BlockSpec((None, heads, HEAD_DIM), lambda s: (s, 0, 0)),
        ],
        out_shape=[
            jax.ShapeDtypeStruct(projected.shape, BF),
            jax.ShapeDtypeStruct((seqs, heads, HEAD_DIM), F32),
        ],
        compiler_params=pltpu.CompilerParams(vmem_limit_bytes=VMEM_LIMIT),
        cost_estimate=pl.CostEstimate(
            flops=14_400_000_000, bytes_accessed=5_000_000, transcendentals=0
        ),
        name="attention_backward",
    )(projected, d_combined, mask, cols, gate_rows)


GELU_A = 0.7978845608028654
GELU_B = 0.044715


def ff_kernel(width, half, x_mine, x_other, g_mine, g_other, w_ref, *outs):
    step = pl.program_id(0)

    @pl.when(step < half)
    def first():
        ff_tile(width, x_mine, g_mine, w_ref, outs[0], outs[2])

    @pl.when(step >= half)
    def second():
        ff_tile(width, x_other, g_other, w_ref, outs[1], outs[3])


def ff_tile(width, x_ref, g_ref, w_ref, act_ref, grad_ref):
    weights = w_ref[...]
    gate_up = mm(x_ref[...], weights[:, : 2 * width], NN)
    d_active = mm(g_ref[...], weights[:, 2 * width :], NN)
    gate = gate_up[:, :width]
    up = gate_up[:, width:]
    square = gate * gate
    tanh = jnp.tanh(GELU_A * gate * (1.0 + GELU_B * square))
    half = 0.5 * (1.0 + tanh)
    gelu = gate * half
    slope = half + 0.5 * gate * (1.0 - tanh * tanh) * GELU_A * (1.0 + 3.0 * GELU_B * square)
    act_ref[...] = (gelu * up).astype(BF)
    grad_ref[:, :width] = (d_active * up * slope).astype(BF)
    grad_ref[:, width:] = (d_active * gelu).astype(BF)


def feed_forward(rows, grads, weights):
    tokens = rows[0].shape[0]
    width = weights.shape[1] // 3
    tile = 256
    half = tokens // tile

    def first(columns):
        return pl.BlockSpec((tile, columns), lambda i: (jnp.minimum(i, half - 1), 0))

    def second(columns):
        return pl.BlockSpec((tile, columns), lambda i: (jnp.maximum(i - half, 0), 0))

    whole = pl.BlockSpec(weights.shape, lambda i: (0, 0), pipeline_mode=pl.Buffered(1))
    act = jax.ShapeDtypeStruct((tokens, width), BF)
    grad = jax.ShapeDtypeStruct((tokens, 2 * width), BF)
    out = pl.pallas_call(
        functools.partial(ff_kernel, width, half),
        grid=(2 * half,),
        in_specs=[first(D), second(D), first(D), second(D), whole],
        out_specs=[first(width), second(width), first(2 * width), second(2 * width)],
        out_shape=[act, act, grad, grad],
        compiler_params=pltpu.CompilerParams(vmem_limit_bytes=VMEM_LIMIT),
        cost_estimate=pl.CostEstimate(
            flops=26 * tokens * D * width, bytes_accessed=tokens * D, transcendentals=0
        ),
        name="feed_forward",
    )(*rows, *grads, weights)
    return (out[0], out[1]), (out[2], out[3])


def down_kernel(count, half, *refs):
    step = pl.program_id(0)
    mine, other, weights = (refs[k * count : (k + 1) * count] for k in range(3))

    def tile(rows, out_ref):
        terms = [mm(a[...], w[...], NT) for a, w in zip(rows, weights)]
        out_ref[...] = sum(terms[1:], terms[0]).astype(BF)

    @pl.when(step < half)
    def first():
        tile(mine, refs[3 * count])

    @pl.when(step >= half)
    def second():
        tile(other, refs[3 * count + 1])


def down_product(active, weights):
    count = len(active)
    tokens, width = active[0][0].shape
    tile = 256
    half = tokens // tile

    def first(columns):
        return pl.BlockSpec((tile, columns), lambda i: (jnp.minimum(i, half - 1), 0))

    def second(columns):
        return pl.BlockSpec((tile, columns), lambda i: (jnp.maximum(i - half, 0), 0))

    down = pl.BlockSpec((D, width), lambda i: (0, 2), pipeline_mode=pl.Buffered(1))
    return pl.pallas_call(
        functools.partial(down_kernel, count, half),
        grid=(2 * half,),
        in_specs=[first(width)] * count + [second(width)] * count + [down] * count,
        out_specs=[first(D), second(D)],
        out_shape=[jax.ShapeDtypeStruct((tokens, D), BF)] * 2,
        compiler_params=pltpu.CompilerParams(vmem_limit_bytes=VMEM_LIMIT),
        cost_estimate=pl.CostEstimate(
            flops=4 * count * tokens * D * width,
            bytes_accessed=2 * D * (count * width + 2 * tokens),
            transcendentals=0,
        ),
        name="down_product",
    )(*[a for a, _ in active], *[b for _, b in active], *weights)


def grads_kernel(count, *refs):
    rows, grads, by_rows, by_grads = (refs[k * count : (k + 1) * count] for k in range(4))
    out_ref = refs[4 * count]
    split = by_rows[0].shape[1]

    def total(left, right):
        acc = None
        for a, b in zip(left, right):
            term = mm(a[...], b[...], TN)
            acc = term if acc is None else acc + term
        return acc

    out_ref[:, :split] = total(rows, by_rows).astype(BF)
    out_ref[:, split:] = total(grads, by_grads).astype(BF)


def weight_grads(rows, grads, by_rows, by_grads):
    def halves(arrays):
        parts = []
        for a in arrays:
            parts += [(a[0], 0), (a[1], 0)] if isinstance(a, tuple) else [(a, 0), (a, 1)]
        return parts

    groups = [halves(a) for a in (rows, grads, by_rows, by_grads)]
    count = len(groups[0])
    tokens = groups[0][0][0].shape[0] // (1 if isinstance(rows[0], tuple) else 2)
    first, second = groups[2][0][0].shape[1], groups[3][0][0].shape[1]
    tile = 512

    def tall(half):
        return pl.BlockSpec((tokens, tile), lambda i: (half, i))

    def whole(width, half):
        return pl.BlockSpec((tokens, width), lambda i: (half, 0), pipeline_mode=pl.Buffered(1))

    return pl.pallas_call(
        functools.partial(grads_kernel, count),
        grid=(D // tile,),
        in_specs=[tall(half) for _, half in groups[0] + groups[1]]
        + [whole(first, half) for _, half in groups[2]]
        + [whole(second, half) for _, half in groups[3]],
        out_specs=pl.BlockSpec((tile, first + second), lambda i: (i, 0)),
        out_shape=jax.ShapeDtypeStruct((D, first + second), BF),
        compiler_params=pltpu.CompilerParams(vmem_limit_bytes=VMEM_LIMIT),
        cost_estimate=pl.CostEstimate(
            flops=3 * count * tokens * D * (first + second),
            bytes_accessed=2 * (2 * count * tokens * D + (count * tokens + D) * (first + second)),
            transcendentals=0,
        ),
        name="weight_grads",
    )(*[a for group in groups for a, _ in group])


RATE_QKV = D ** (-0.5)
RATE_OUT = 4.0 * (HEADS * HEAD_DIM) ** (-0.5)
RATE_DOWN = FF ** (-0.5)


def small_kernel(owned_ref, att_ref, gains_ref, gate_ref, out_ref):
    wide = att_ref[...].astype(F32)
    squares = jnp.sum(wide * wide, axis=(0, 1), keepdims=True) + owned_ref[0]
    count = gains_ref.shape[0]
    out_ref[:count] = gains_ref[...]
    lane = lax.broadcasted_iota(jnp.int32, gate_ref.shape, 1)
    out_ref[count:] = jnp.where(lane == HEADS, squares, gate_ref[...])


def small_sums(owned, own_att, gains, gate_row):
    return pl.pallas_call(
        small_kernel,
        in_specs=[
            pl.BlockSpec(memory_space=pltpu.SMEM),
            pl.BlockSpec(memory_space=pltpu.VMEM),
            pl.BlockSpec(memory_space=pltpu.VMEM),
            pl.BlockSpec(memory_space=pltpu.VMEM),
        ],
        out_specs=pl.BlockSpec(memory_space=pltpu.VMEM),
        out_shape=jax.ShapeDtypeStruct((gains.shape[0] + 1, 128), F32),
        compiler_params=pltpu.CompilerParams(vmem_limit_bytes=16 * 1024 * 1024),
        name="small_sums",
    )(owned[None], own_att, gains, gate_row)


def clip_factor(small):
    row = lax.broadcasted_iota(jnp.int32, small.shape, 0)
    lane = lax.broadcasted_iota(jnp.int32, small.shape, 1)
    summed = (row == small.shape[0] - 1) & (lane >= HEADS)
    squares = jnp.sum(jnp.where(summed, small, small * small), axis=(0, 1), keepdims=True)
    grad_norm = jnp.sqrt(squares)
    return grad_norm, jnp.minimum(1.0, CLIP / (grad_norm + 1e-06))


def adam_kernel(steps, chunks, place_ref, small_ref, *refs):
    ins, refs = refs[:18], refs[18:]
    grads, refs = refs[: 2 + 2 * chunks], refs[2 + 2 * chunks :]
    outs, norm_ref, scratch = refs[:18], refs[18], refs[19]
    grad_norm, factor = clip_factor(small_ref[...])
    is_low = place_ref[0] == 0
    everything = slice(None)

    def put(number, place, gradient, rate, decay=DECAY):
        weight, moment, second = (r[place] for r in ins[3 * number : 3 * number + 3])
        new = adam_update(weight, moment, second, gradient.astype(F32), factor, rate, decay)
        for ref, value in zip(outs[3 * number : 3 * number + 3], new):
            ref[place] = value

    def sides_of(mine, theirs):
        mine, theirs = mine[...], theirs[...]
        return jnp.where(is_low, mine, theirs), jnp.where(is_low, theirs, mine)

    for s, side in enumerate(sides_of(*grads[:2])):
        width = side.shape[1] // 4
        cols = slice(s * width, (s + 1) * width)
        for part in range(3):
            put(0, (part, everything, cols), side[:, part * width : (part + 1) * width], RATE_QKV)
        put(1, (everything, cols), side[:, 3 * width :], RATE_OUT)
    rows, width_ff = ins[9].shape
    lanes = width_ff // 128
    for k in range(chunks):
        for s, side in enumerate(sides_of(*grads[2 + 2 * k : 4 + 2 * k])):
            side = side.astype(F32)
            width = side.shape[1] // 3
            start = s * (width_ff // 2) + k * width
            put(3, (everything, slice(start, start + width)), side[:, 2 * width :], RATE_DOWN)
            for part in range(2):
                for lane in range(width // 128):
                    place = pl.ds((start // 128 + lane) * 2 + part, rows, stride=2 * lanes)
                    first = part * width + lane * 128
                    scratch[place, :] = side[:, first : first + 128]
    put(2, (everything, everything), scratch[...], RATE_QKV)

    @pl.when(pl.program_id(0) == 0)
    def small_ones():
        last = ins[12].shape[0]
        put(4, (everything, everything), small_ref[:last], 0.5, 0.0)
        put(5, (everything, everything), small_ref[last:, :HEADS], 1.0, 0.0)
        norm_ref[...] = grad_norm


def mlp_view(t):
    rows, _, width_ff = t.shape
    return t.reshape(rows, 2, width_ff // 128, 128).transpose(0, 2, 1, 3).reshape(-1, 128)


def adam_all(small, x_place, arrays, att_sides, ff_sides):
    rows, _, width_ff = arrays[6].shape
    steps = 4

    def qkv_view(t):
        return jnp.transpose(t, (1, 0, 2))

    def mlp_back(t, shape):
        rows, _, width_ff = shape
        t = t.reshape(rows, width_ff // 128, 2, 128).transpose(0, 2, 1, 3)
        return t.reshape(shape)

    views = [qkv_view(t) for t in arrays[:3]] + list(arrays[3:6])
    views += [mlp_view(t) for t in arrays[6:9]] + list(arrays[9:12])
    gains = [mlp_view(t[None]) for t in arrays[12:15]] + [t[None] for t in arrays[15:]]
    grads = list(att_sides) + [t for pair in ff_sides for t in pair]

    def spec(t):
        axis = t.ndim - 2
        block = list(t.shape)
        block[axis] //= steps
        return pl.BlockSpec(tuple(block), lambda i, place: (0,) * axis + (i, 0))

    def whole(t):
        return pl.BlockSpec(t.shape, lambda i, place: (0, 0))

    def mine(t):
        return pl.BlockSpec((rows // steps, t.shape[1]), lambda i, place: (place[0] * steps + i, 0))

    specs = [spec(t) for t in views] + [whole(t) for t in gains]
    new = pl.pallas_call(
        functools.partial(adam_kernel, steps, len(ff_sides)),
        grid_spec=pltpu.PrefetchScalarGridSpec(
            num_scalar_prefetch=1,
            grid=(steps,),
            in_specs=[whole(small)]
            + specs
            + [spec(t) if k % 2 else mine(t) for k, t in enumerate(grads)],
            out_specs=specs + [pl.BlockSpec((1, 1), lambda i, place: (0, 0))],
            scratch_shapes=[pltpu.VMEM((views[6].shape[0] // steps, 128), F32)],
        ),
        out_shape=[jax.ShapeDtypeStruct(t.shape, F32) for t in views + gains]
        + [jax.ShapeDtypeStruct((1, 1), F32)],
        compiler_params=pltpu.CompilerParams(vmem_limit_bytes=VMEM_LIMIT),
        cost_estimate=pl.CostEstimate(
            flops=20 * sum(t.size for t in views) // 3,
            bytes_accessed=8 * sum(t.size for t in views),
            transcendentals=0,
        ),
        name="adam",
    )(x_place[None], small, *views, *gains, *grads)
    new = list(new)
    return (
        [qkv_view(t) for t in new[:3]]
        + new[3:6]
        + [mlp_back(t, arrays[6].shape) for t in new[6:9]]
        + new[9:12]
        + [mlp_back(t, (1,) + arrays[12].shape)[0] for t in new[12:15]]
        + [t[0] for t in new[15:18]]
        + [new[18].reshape(())]
    )


def on_device(
    inputs,
    doc_ids,
    cotangent,
    weight_qkv,
    moment_qkv,
    second_qkv,
    weight_out,
    moment_out,
    second_out,
    weight_mlp,
    moment_mlp,
    second_mlp,
    weight_down,
    moment_down,
    second_down,
    norm_gains,
    moment_gains,
    second_gains,
    gate_logit,
    moment_gate,
    second_gate,
):
    micro_count, _, seg_count, own_len, _ = inputs.shape
    own_tokens = seg_count * own_len
    x_place = lax.axis_index("x")
    y_place = lax.axis_index("y")
    c_place = lax.axis_index("c")
    orders = [("x", "y") if m % 2 == 0 else ("y", "x") for m in range(micro_count)]

    z_count = D // (2 * weight_qkv.shape[0])

    def half_columns(weight, which):
        width = weight.shape[-1] // 2
        return lax.dynamic_slice_in_dim(weight, which * width, width, axis=weight.ndim - 1)

    def join_rows(mine, theirs):
        both = jnp.zeros((2 * rows, mine.shape[1]), BF)
        both = lax.dynamic_update_slice_in_dim(both, mine, x_place * rows, axis=0)
        return lax.dynamic_update_slice_in_dim(both, theirs, (1 - x_place) * rows, axis=0)

    def fetch(block):
        return lax.all_gather(block, "z", axis=0, tiled=True)

    rows = weight_qkv.shape[0]
    heads = weight_qkv.shape[2] // (2 * HEAD_DIM)
    width_att = heads * HEAD_DIM
    width_ff = weight_down.shape[1] // 2
    width = width_ff // CHUNKS

    def qkv_columns(which):
        return half_columns(weight_qkv, which).astype(BF).reshape(rows, -1)

    def ff_columns(k, which):
        start = which * width_ff + k * width
        mlp = lax.dynamic_slice_in_dim(mlp_later, start, width, axis=2).astype(BF)
        down = lax.dynamic_slice_in_dim(down_later, start, width, axis=1).astype(BF)
        return jnp.concatenate([mlp[:, 0], mlp[:, 1], down], axis=1)

    send_qkv = qkv_columns(1 - x_place)
    all_out = direct_gather(tie(weight_out, send_qkv).astype(BF), z_count)
    all_ids = tie(doc_ids[:, 0], send_qkv)
    for axis in ("y", "c"):
        all_ids = jnp.stack([all_ids, swap(all_ids, axis)], axis=0)
    their_qkv = swap(send_qkv, "x")
    shard_qkv = join_rows(qkv_columns(x_place), tie(their_qkv, all_ids))
    full_qkv = fetch(shard_qkv)

    head_start = (y_place * 2 + c_place) * (2 * heads) + x_place * heads
    gate_local = lax.dynamic_slice_in_dim(gate_logit, head_start, heads)
    mixing = jax.nn.sigmoid(gate_local)
    gate_rows = jnp.broadcast_to(mixing[:, None], (heads, HEAD_DIM))

    micros = range(micro_count)
    tokens = 8 * own_tokens
    token_rows = [
        tie(inputs[m, 0], send_qkv).reshape(own_tokens, D).astype(F32) for m in micros
    ]
    back_low = [cotangent[m, 0].reshape(own_tokens, D) for m in micros]
    all_ids = jnp.stack([all_ids, swap(all_ids, "x")], axis=0)
    normed_att = [rms_norm(t, norm_gains[0]).astype(BF) for t in token_rows]
    att_states = [
        gather_start(normed_att[m], *orders[m], (their_qkv, all_ids)) for m in micros
    ]
    att_by_x = [state[1 + orders[m].index("y")] for m, state in enumerate(att_states)]
    mlp_later = tie(weight_mlp, *att_by_x)
    down_later = tie(weight_down, *att_by_x)
    att_states = [gather_across(state, *orders[m], "y") for m, state in enumerate(att_states)]
    att_rows = [gather_core(state) for state in att_states]

    def their_ff(k, *earlier):
        return swap(tie(ff_columns(k, 1 - x_place), *earlier), "x")

    theirs = their_ff(0, *att_by_x)
    shard_ff = [join_rows(ff_columns(0, x_place), theirs)]
    full_ff = [fetch(shard_ff[0])]
    their_out = swap(tie(half_columns(all_out, 1 - x_place), shard_ff[0]), "x")
    both_out = jnp.zeros((z_count, 2, rows, width_att), BF)
    for part, place in ((half_columns(all_out, x_place), x_place), (their_out, 1 - x_place)):
        part = part.reshape(z_count, 1, rows, width_att)
        both_out = lax.dynamic_update_slice_in_dim(both_out, part, place, axis=1)
    full_out = both_out.reshape(D, width_att)
    att_last = [state[-1] for state in att_states]
    back_states = [
        gather_start(back_low[m], *orders[m], (their_out,), att_last) for m in micros
    ]
    back_first = [t for state in back_states for t in state[1:]]
    back_states = [gather_across(state, *orders[m], "y") for m, state in enumerate(back_states)]
    earlier = back_first

    rel_c = jnp.arange(2)[:, None, None] ^ c_place
    rel_y = jnp.arange(2)[None, :, None] ^ y_place
    places = ((rel_y * 2 + rel_c) * own_len + jnp.arange(own_len)).reshape(-1)
    causal = places[:, None] >= places[None, :]
    masks = []
    columns = []
    for m in micros:
        ids = jnp.transpose(all_ids[:, :, :, m], (0, 3, 1, 2, 4)).reshape(2, seg_count, -1)
        same = ids[:, :, :, None] == ids[:, :, None, :]
        masks.append((same & causal).astype(F32))
        last = jnp.max(ids, axis=2)
        previous = jnp.concatenate([jnp.full((2, 1), -1, last.dtype), last[:, :-1]], axis=1)
        reading = ids == previous[:, :, None]
        writing = ids == last[:, :, None]
        keep = jnp.broadcast_to((last == previous)[:, :, None], ids.shape)
        columns.append(jnp.stack([reading, writing, keep], axis=-1).astype(F32))

    slots = (2, 2, 2, seg_count, own_len)
    wheres = [1 if orders[m][0] == "x" else 2 for m in micros]
    projected = []
    combined = []
    hidden = []
    normed_mlp = []
    for m in micros:
        mine, other = att_rows[m]
        if m == 0:
            mine = tie(mine, *back_first)
        proj = jnp.concatenate([mm(p, full_qkv, NN).astype(BF) for p in (mine, other)], axis=0)
        projected.append(proj.reshape(slots + (3 * width_att,)))
        comb = attention_fwd(projected[m], masks[m], columns[m], gate_rows, wheres[m])
        combined.append(comb.reshape(tokens, width_att))
    half = tokens // 2
    for k in range(1, CHUNKS):
        theirs = their_ff(k, *earlier)
        shard_ff.append(join_rows(ff_columns(k, x_place), tie(theirs, combined[0])))
        full_ff.append(fetch(shard_ff[k]))
        earlier = [theirs]
    back_states = [(tie(state[0], combined[0]),) + state[1:] for state in back_states]
    back_rows = [gather_core(state) for state in back_states]
    for m in micros:
        ready = combined[m]
        if m > 0:
            ready = tie(ready, *shard_ff, *[state[-1] for state in back_states])
        other = mm(ready[half:], full_out, NT).astype(BF)
        mine = mm(ready[:half], full_out, NT).astype(BF)
        state = scatter_core(mine, other, own_tokens, orders[m][0], orders[m][0])
        state = scatter_outer(state, orders[m][0])
        hidden.append(token_rows[m] + scatter_inner(state, orders[m][1]))
        normed_mlp.append(rms_norm(hidden[m], norm_gains[1]).astype(BF))
    mlp_rows = [gather_core(state) for state in gather_steps(normed_mlp, orders)]

    def exchange_grad(grad):
        return grad, swap(lax.dynamic_slice_in_dim(grad, (1 - x_place) * rows, rows, axis=0), "x")

    def squares_of(grad):
        wide = grad.astype(F32)
        return jnp.sum(wide * wide)

    def reduce_rows(partial):
        return lax.psum_scatter(partial, "z", scatter_dimension=0, tiled=True)

    def products(left, right, totals, dtype):
        terms = [mm(left[p], right, NT) for p in (1, 0)][::-1]
        if totals is not None:
            terms = [a + b for a, b in zip(totals, terms)]
        return tuple(t.astype(dtype) for t in terms)

    active = []
    d_gate_up = []
    own_ff = []
    d_total = [None] * micro_count
    states = [None] * micro_count
    for k in range(CHUNKS):
        active.append([])
        d_gate_up.append([])
        last = k == CHUNKS - 1
        for m in micros:
            rows_in = mlp_rows[m]
            if last and m > 0:
                rows_in = (tie(rows_in[0], *d_total[m - 1]), rows_in[1])
            act, grad = feed_forward(rows_in, back_rows[m], full_ff[k])
            active[k].append(act)
            d_gate_up[k].append(grad)
            if last and m > 0:
                grad = (grad[0], tie(grad[1], states[m - 1][1]))
            dtype = BF if last else F32
            d_total[m] = products(grad, full_ff[k][:, : 2 * width], d_total[m], dtype)
            if last:
                states[m] = scatter_core(*d_total[m], own_tokens, orders[m][0], orders[m][0])
        if not last:
            grad_ff = weight_grads(mlp_rows, back_rows, d_gate_up[k], active[k])
            own_ff.append(reduce_rows(grad_ff))
            terms = [t for pair in d_total for t in pair]
            full_ff[k + 1] = tie(full_ff[k + 1], grad_ff, *terms)

    out_pairs = []
    for m in micros:
        act = [active[k][m] for k in range(CHUNKS)]
        act[-1] = (act[-1][0], tie(act[-1][1], states[-1][1]))
        out_pairs.append(down_product(act, full_ff))
    products_done = [t for pair in out_pairs for t in pair]
    outer_states = [scatter_outer(states[m], orders[m][0], *products_done) for m in micros]
    last_active = [
        (active[-1][m][0], tie(active[-1][m][1], *[t[1] for t in outer_states])) for m in micros
    ]
    grad_ff = weight_grads(mlp_rows, back_rows, d_gate_up[-1], last_active)
    own_ff.append(reduce_rows(grad_ff))

    gain_grad_att = jnp.zeros((D,), F32)
    gain_grad_mlp = jnp.zeros((D,), F32)
    d_hidden = []
    for m in micros:
        keep, send = outer_states[m]
        d_normed = scatter_inner((tie(keep, grad_ff), send), orders[m][1])
        ignored, norm_back = jax.vjp(rms_norm, hidden[m], norm_gains[1])
        d_norm, d_gain = norm_back(d_normed)
        gain_grad_mlp = gain_grad_mlp + d_gain
        d_hidden.append(back_low[m].astype(F32) + d_norm)

    gate_sum = jnp.zeros((heads,), F32)
    d_projs = []
    out_states = [
        scatter_core(*tie_pair(out_pairs[m], *d_hidden), own_tokens, orders[m][0], orders[m][0])
        for m in micros
    ]
    grad_states = gather_steps([t.astype(BF) for t in d_hidden], orders)
    sends = [t[1] for t in out_states]
    out_states = [tie_send(t, *[g[-1] for g in grad_states]) for t in out_states]
    att_grads = [gather_core((tie(g[0], *sends),) + g[1:]) for g in grad_states]
    ff_pairs = [exchange_grad(own_ff[0])]
    for m in micros:
        mine, other = att_grads[m]
        if m == 0:
            other = tie(other, own_ff[0])
        d_combined = jnp.concatenate(
            [mm(mine, full_out, NN), mm(other, full_out, NN)], axis=0
        )
        d_proj, gate_part = attention_bwd(
            projected[m],
            d_combined.reshape(slots + (width_att,)),
            masks[m],
            columns[m],
            gate_rows,
            wheres[m],
        )
        gate_sum = gate_sum + jnp.sum(gate_part, axis=(0, 2))
        d_projs.append(d_proj.reshape(tokens, 3 * width_att))
    out_came = [swap(out_states[m][1], orders[m][0]) for m in micros]
    by_rows = [d_projs[0], tie(d_projs[-1], ff_pairs[0][1], *out_came)]
    grad_att = weight_grads(att_rows, att_grads, by_rows, combined)
    own_att = reduce_rows(grad_att)
    mlp_out = []
    for m in micros:
        state = scatter_add(out_states[m][0], tie(out_came[m], grad_att))
        mlp_out.append(scatter_inner(state, orders[m][1]))
    block_out = [(hidden[m] + mlp_out[m]).astype(BF) for m in micros]

    ff_pairs += [exchange_grad(g) for g in own_ff[1:]]

    ff_owned = sum(squares_of(g) for g in own_ff)

    grad_rows = []
    in_states = []
    for m in micros:
        d_proj = tie(d_projs[m], grad_att)
        other = mm(d_proj[half:], full_qkv, NT).astype(BF)
        mine = mm(d_proj[:half], full_qkv, NT).astype(BF)
        in_states.append(scatter_core(mine, other, own_tokens, orders[m][0], orders[m][0]))
    for m in micros:
        state = scatter_outer(in_states[m], orders[m][0])
        if m > 0:
            state = tie_send(state, ff_pairs[-1][1])
        d_normed = scatter_inner(state, orders[m][1])
        ignored, norm_first = jax.vjp(rms_norm, token_rows[m], norm_gains[0])
        d_norm, d_gain = norm_first(d_normed)
        gain_grad_att = gain_grad_att + d_gain
        grad_rows.append((d_hidden[m] + d_norm).astype(BF))

    att_mine, att_theirs = exchange_grad(own_att)

    gate_grad = gate_sum * mixing * (1.0 - mixing)
    gate_padded = lax.dynamic_update_slice(
        jnp.zeros(gate_logit.shape, F32), gate_grad, (head_start,)
    )
    gain_grad = mlp_view(jnp.stack([gain_grad_att, gain_grad_mlp], axis=0)[None])
    gate_row = jnp.concatenate([gate_padded, jnp.zeros((128 - HEADS,), F32)])[None]
    small = small_sums(ff_owned, own_att, gain_grad, gate_row)
    small = sum_everywhere(small, z_count, att_theirs)
    arrays = [
        weight_qkv,
        moment_qkv,
        second_qkv,
        weight_out,
        moment_out,
        second_out,
        weight_mlp,
        moment_mlp,
        second_mlp,
        weight_down,
        moment_down,
        second_down,
        norm_gains,
        moment_gains,
        second_gains,
        gate_logit,
        moment_gate,
        second_gate,
    ]
    new = adam_all(small, x_place, arrays, (att_mine, att_theirs), ff_pairs)
    shape = (micro_count, 1, seg_count, own_len, D)
    return (
        jnp.stack(block_out, axis=0).reshape(shape),
        jnp.stack(grad_rows, axis=0).reshape(shape),
        new[-1],
        *new[:-1],
    )


def solution(mesh):
    seq_count, ctx_count = mesh.devices.shape
    inner = Mesh(
        mesh.devices.reshape(seq_count // 2, 2, ctx_count // 2, 2), ("z", "x", "y", "c")
    )
    seq, ctx = ("z", "x"), ("y", "c")
    rows = P(None, seq, None, ctx, None)
    wide = P(seq, None, ctx)
    flat = P(seq, ctx)
    weights = (wide,) * 3 + (flat,) * 3 + (wide,) * 3 + (flat,) * 3 + (P(),) * 6
    return jax.shard_map(
        on_device,
        mesh=inner,
        in_specs=(rows, P(None, seq, None, ctx), rows) + weights,
        out_specs=(rows, rows, P()) + weights,
        check_vma=False,
    )
```

```python
import functools

import jax
import jax.numpy as jnp
from jax import lax
from jax.experimental import pallas as pl
from jax.experimental.pallas import tpu as pltpu
from jax.sharding import Mesh
from jax.sharding import PartitionSpec as P

D = 2048
HEADS = 16
HEAD_DIM = 128
FF = 8192
STEP_COUNT = 10
CHUNKS = 2

EPS = 1e-06
NEG = -1e30
CLIP = 1.0
BETA1 = 0.9
BETA2 = 0.95
ADAM_EPS = 1e-08
DECAY = 0.1
BF = jnp.bfloat16
F32 = jnp.float32
SCALING = HEAD_DIM ** (-0.5)
VMEM_LIMIT = 48 * 1024 * 1024


def rms_norm(tensor, scaling):
    return tensor * lax.rsqrt(jnp.mean(tensor * tensor, axis=-1, keepdims=True) + EPS) * scaling


def adam_update(weight, moment, second, gradient, factor, step_rate, decay):
    clipped = gradient * factor
    moment = BETA1 * moment + (1.0 - BETA1) * clipped
    second = BETA2 * second + (1.0 - BETA2) * clipped * clipped
    fixed_first = moment / (1.0 - BETA1**STEP_COUNT)
    fixed_second = second / (1.0 - BETA2**STEP_COUNT)
    updated = weight - step_rate * (
        fixed_first / (jnp.sqrt(fixed_second) + ADAM_EPS) + decay * weight
    )
    return (moment, second, updated)


def swap(tensor, axis):
    return lax.ppermute(tensor, axis, [(0, 1), (1, 0)])


def tie(tensor, *earlier):
    return lax.optimization_barrier((tensor,) + earlier)[0]


def gather_start(own, outer, inner, x_after=(), y_after=()):
    start = {"x": tie(own, *x_after), "y": tie(own, *y_after)}
    return own, swap(start[inner], inner), swap(start[outer], outer)


def gather_across(state, outer, inner, last):
    own, by_inner, by_outer = state
    return state + (swap(by_inner if last == outer else by_outer, last),)


def gather_steps(owns, orders):
    starts = [gather_start(own, *order) for own, order in zip(owns, orders)]
    firsts = [t for state in starts for t in state[1:]]
    ready = []
    for state, order in zip(starts, orders):
        by_inner = tie(state[1], *firsts)
        ready.append((state[0], by_inner, state[2], swap(by_inner, order[0])))
    lasts = [state[-1] for state in ready]
    return [(tie(state[0], *lasts),) + state[1:] for state in ready]


def gather_core(state):
    mine = jnp.concatenate(state, axis=0)
    return mine, swap(mine, "c")


def scatter_core(mine, other, units, outer, first):
    came = swap(other, "c").reshape(2, 2, units, -1)
    mine = mine.reshape(2, 2, units, -1)
    parts = []
    for p in range(2):
        index = (p,) if first == outer else (slice(None), p)
        parts.append(mine[index].astype(F32) + came[index].astype(F32))
    return parts[0], parts[1].astype(BF)


def scatter_outer(state, axis, *later):
    keep, send = state
    return scatter_add(keep, tie(swap(send, axis), *later))


def scatter_add(keep, came):
    send = (keep[1] + came[1].astype(F32)).astype(BF)
    return keep[0] + came[0].astype(F32), send


def scatter_inner(state, axis):
    keep, send = state
    return keep + swap(send, axis).astype(F32)


def tie_pair(pair, *earlier):
    return pair[0], tie(pair[1], *earlier)


def tie_send(state, *earlier):
    return state[0], tie(state[1], *earlier)


def direct_gather(block, z_count):
    rows = block.shape[0]
    place = lax.axis_index("z")
    pieces = [block]
    for step in range(1, z_count):
        pairs = [(i, (i + step) % z_count) for i in range(z_count)]
        pieces.append(lax.ppermute(block, "z", pairs))
    full = jnp.zeros((z_count * rows, block.shape[1]), block.dtype)
    for step, piece in enumerate(pieces):
        slot = lax.rem(place + z_count - step, z_count)
        full = lax.dynamic_update_slice_in_dim(full, piece, slot * rows, axis=0)
    return full


def sum_everywhere(tensor, z_count, beside):
    def add(tensor, axis, pairs):
        return tensor + lax.ppermute(tensor, axis, pairs)

    tensor = add(tensor, "x", [(0, 1), (1, 0)])
    reach = 1
    while reach < z_count:
        tensor = add(tensor, "z", [(i, i ^ reach) for i in range(z_count)])
        reach *= 2
    tensor = add(tensor, "c", [(0, 1), (1, 0)])
    return add(tie(tensor, beside), "y", [(0, 1), (1, 0)])


def mm(a, b, dims):
    return lax.dot_general(a, b, (dims, ((), ())), preferred_element_type=F32)


NN = ((1,), (0,))
NT = ((1,), (1,))
TN = ((0,), (0,))


def mm_mem(a, b, dims):
    return mm(a.astype(BF), b.astype(BF), dims)


def elu_one(tensor):
    return jnp.where(tensor > 0, tensor + 1.0, jnp.exp(jnp.minimum(tensor, 0.0)))


def elu_slope(tensor):
    low = jnp.where(tensor == 0, 0.5, jnp.exp(jnp.minimum(tensor, 0.0)))
    return jnp.where(tensor > 0, 1.0, low)


def segment_of(ref, r, part):
    block = ref[:, :, r, :, part * HEAD_DIM : (part + 1) * HEAD_DIM]
    return block.reshape(-1, HEAD_DIM)


def memory_forward(qs, ks, vs, cols):
    seg_count = len(qs)
    saved = []
    memory = normer = None
    for r in range(seg_count):
        reading, writing, keep = cols[r]
        sq = elu_one(qs[r].astype(F32))
        sk = elu_one(ks[r].astype(F32))
        value = vs[r].astype(F32)
        rows = sq.shape[0]
        item = dict(sq=sq, sk=sk)
        if r == 0:
            item["recalled"] = jnp.zeros_like(sq)
            change = value
        else:
            both = mm_mem(jnp.concatenate([sq, sk], axis=0), memory, NN)
            num = both[:rows]
            den = 1.0 + jnp.sum(sq * normer, axis=-1, keepdims=True)
            item["recalled"] = reading * num / den
            before = keep * both[rows:]
            kden = 1.0 + keep * jnp.sum(sk * normer, axis=-1, keepdims=True)
            change = value - before / kden
            item.update(num=num, den=den, before=before, kden=kden, memory=memory, normer=normer)
        item["change"] = change
        if r < seg_count - 1:
            write = sk * writing
            fresh = mm_mem(write, change, TN)
            fresh_norm = jnp.sum(write, axis=0, keepdims=True)
            memory = fresh if r == 0 else keep * memory + fresh
            normer = fresh_norm if r == 0 else keep[:1] * normer + fresh_norm
        saved.append(item)
    return saved


def local_probs(query, key, allowed):
    scores = jnp.where(allowed > 0, mm(query, key, NT) * SCALING, NEG)
    exponent = jnp.exp(scores - jnp.max(scores, axis=-1, keepdims=True))
    return exponent / jnp.sum(exponent, axis=-1, keepdims=True)


def columns_of(cols_ref, r):
    cols = cols_ref[r]
    return cols[:, 0:1], cols[:, 1:2], cols[:, 2:3]


def attention_fwd_kernel(heads, proj_ref, mask_ref, cols_ref, gate_ref, out_ref):
    seg_count = mask_ref.shape[0]
    cols = [columns_of(cols_ref, r) for r in range(seg_count)]
    for h in range(heads):
        qs = [segment_of(proj_ref, r, h) for r in range(seg_count)]
        ks = [segment_of(proj_ref, r, heads + h) for r in range(seg_count)]
        vs = [segment_of(proj_ref, r, 2 * heads + h) for r in range(seg_count)]
        saved = memory_forward(qs, ks, vs, cols)
        mixing = gate_ref[h : h + 1]
        for r in range(seg_count):
            prob_low = local_probs(qs[r], ks[r], mask_ref[r]).astype(BF)
            local_out = mm(prob_low, vs[r], NN)
            combined = mixing * saved[r]["recalled"] + (1.0 - mixing) * local_out
            out_ref[:, :, r, :, h * HEAD_DIM : (h + 1) * HEAD_DIM] = combined.astype(BF).reshape(
                out_ref.shape[0], out_ref.shape[1], out_ref.shape[3], HEAD_DIM
            )


def attention_bwd_kernel(
    heads, proj_ref, grad_ref, mask_ref, cols_ref, gate_ref, out_ref, gate_out_ref
):
    seg_count = mask_ref.shape[0]
    cols = [columns_of(cols_ref, r) for r in range(seg_count)]

    def put(r, part, value):
        out_ref[:, :, r, :, part * HEAD_DIM : (part + 1) * HEAD_DIM] = value.astype(BF).reshape(
            out_ref.shape[0], out_ref.shape[1], out_ref.shape[3], HEAD_DIM
        )

    for h in range(heads):
        qs = [segment_of(proj_ref, r, h) for r in range(seg_count)]
        ks = [segment_of(proj_ref, r, heads + h) for r in range(seg_count)]
        vs = [segment_of(proj_ref, r, 2 * heads + h) for r in range(seg_count)]
        saved = memory_forward(qs, ks, vs, cols)
        mixing = gate_ref[h : h + 1]
        gate_sum = jnp.zeros((1, HEAD_DIM), F32)
        d_memory = d_normer = None
        for r in reversed(range(seg_count)):
            reading, writing, keep = cols[r]
            item = saved[r]
            sq, sk = item["sq"], item["sk"]
            rows = sq.shape[0]
            d_combined = segment_of(grad_ref, r, h).astype(F32)
            d_recalled = mixing * d_combined
            d_local = ((1.0 - mixing) * d_combined).astype(BF)
            probs = local_probs(qs[r], ks[r], mask_ref[r])
            prob_low = probs.astype(BF)
            local_out = mm(prob_low, vs[r], NN)
            gate_sum = gate_sum + jnp.sum(
                d_combined * (item["recalled"] - local_out), axis=0, keepdims=True
            )
            d_prob = mm(d_local, vs[r], NT)
            d_value = mm(prob_low, d_local, TN)
            d_scores = (
                probs * (d_prob - jnp.sum(d_prob * probs, axis=-1, keepdims=True))
            ).astype(BF)
            d_query = mm(d_scores, ks[r], NN) * SCALING
            d_key = mm(d_scores, qs[r], TN) * SCALING
            d_sk = None
            d_before = d_kden = None
            if r < seg_count - 1:
                d_change = writing * mm_mem(sk, d_memory, NN)
                d_sk = writing * (mm_mem(item["change"], d_memory, NT) + d_normer)
                d_value = d_value + d_change
                if r > 0:
                    d_before = keep * (-d_change / item["kden"])
                    d_kden = keep * (
                        jnp.sum(d_change * item["before"], axis=-1, keepdims=True)
                        / (item["kden"] * item["kden"])
                    )
            if r > 0:
                d_num = reading * d_recalled / item["den"]
                d_den = -reading * (
                    jnp.sum(d_recalled * item["num"], axis=-1, keepdims=True)
                    / (item["den"] * item["den"])
                )
                if d_before is None:
                    d_sq = mm_mem(d_num, item["memory"], NT) + d_den * item["normer"]
                    new_memory = mm_mem(sq, d_num, TN)
                    new_normer = jnp.sum(sq * d_den, axis=0, keepdims=True)
                else:
                    stacked = jnp.concatenate([d_num, d_before], axis=0)
                    both = mm_mem(stacked, item["memory"], NT)
                    d_sq = both[:rows] + d_den * item["normer"]
                    d_sk = d_sk + both[rows:] + d_kden * item["normer"]
                    new_memory = keep * d_memory + mm_mem(
                        jnp.concatenate([sq, sk], axis=0), stacked, TN
                    )
                    new_normer = keep[:1] * d_normer + jnp.sum(
                        sq * d_den + sk * d_kden, axis=0, keepdims=True
                    )
                d_memory, d_normer = new_memory, new_normer
                d_query = d_query + d_sq * elu_slope(qs[r].astype(F32))
            if d_sk is not None:
                d_key = d_key + d_sk * elu_slope(ks[r].astype(F32))
            put(r, h, d_query)
            put(r, heads + h, d_key)
            put(r, 2 * heads + h, d_value)
        gate_out_ref[h : h + 1] = gate_sum


def block_spec(shape, where):
    dims = list(shape)
    dims[where] = None

    def index(s):
        place = [0] * len(dims)
        place[where] = s
        return tuple(place)

    return pl.BlockSpec(tuple(dims), index)


def attention_fwd(projected, mask, cols, gate_rows, where):
    heads = gate_rows.shape[0]
    out_shape = projected.shape[:-1] + (heads * HEAD_DIM,)
    return pl.pallas_call(
        functools.partial(attention_fwd_kernel, heads),
        grid=(projected.shape[where],),
        in_specs=[
            block_spec(projected.shape, where),
            pl.BlockSpec((None,) + mask.shape[1:], lambda s: (s, 0, 0, 0)),
            pl.BlockSpec((None,) + cols.shape[1:], lambda s: (s, 0, 0, 0)),
            pl.BlockSpec(gate_rows.shape, lambda s: (0, 0)),
        ],
        out_specs=block_spec(out_shape, where),
        out_shape=jax.ShapeDtypeStruct(out_shape, BF),
        compiler_params=pltpu.CompilerParams(vmem_limit_bytes=VMEM_LIMIT),
        cost_estimate=pl.CostEstimate(
            flops=7_600_000_000, bytes_accessed=3_000_000, transcendentals=0
        ),
        name="attention_forward",
    )(projected, mask, cols, gate_rows)


def attention_bwd(projected, d_combined, mask, cols, gate_rows, where):
    heads = gate_rows.shape[0]
    seqs = projected.shape[where]
    return pl.pallas_call(
        functools.partial(attention_bwd_kernel, heads),
        grid=(seqs,),
        in_specs=[
            block_spec(projected.shape, where),
            block_spec(d_combined.shape, where),
            pl.BlockSpec((None,) + mask.shape[1:], lambda s: (s, 0, 0, 0)),
            pl.BlockSpec((None,) + cols.shape[1:], lambda s: (s, 0, 0, 0)),
            pl.BlockSpec(gate_rows.shape, lambda s: (0, 0)),
        ],
        out_specs=[
            block_spec(projected.shape, where),
            pl.BlockSpec((None, heads, HEAD_DIM), lambda s: (s, 0, 0)),
        ],
        out_shape=[
            jax.ShapeDtypeStruct(projected.shape, BF),
            jax.ShapeDtypeStruct((seqs, heads, HEAD_DIM), F32),
        ],
        compiler_params=pltpu.CompilerParams(vmem_limit_bytes=VMEM_LIMIT),
        cost_estimate=pl.CostEstimate(
            flops=14_400_000_000, bytes_accessed=5_000_000, transcendentals=0
        ),
        name="attention_backward",
    )(projected, d_combined, mask, cols, gate_rows)


GELU_A = 0.7978845608028654
GELU_B = 0.044715


def ff_kernel(width, half, x_mine, x_other, g_mine, g_other, w_ref, *outs):
    step = pl.program_id(0)

    @pl.when(step < half)
    def first():
        ff_tile(width, x_mine, g_mine, w_ref, outs[0], outs[2])

    @pl.when(step >= half)
    def second():
        ff_tile(width, x_other, g_other, w_ref, outs[1], outs[3])


def ff_tile(width, x_ref, g_ref, w_ref, act_ref, grad_ref):
    weights = w_ref[...]
    gate_up = mm(x_ref[...], weights[:, : 2 * width], NN)
    d_active = mm(g_ref[...], weights[:, 2 * width :], NN)
    gate = gate_up[:, :width]
    up = gate_up[:, width:]
    square = gate * gate
    tanh = jnp.tanh(GELU_A * gate * (1.0 + GELU_B * square))
    half = 0.5 * (1.0 + tanh)
    gelu = gate * half
    slope = half + 0.5 * gate * (1.0 - tanh * tanh) * GELU_A * (1.0 + 3.0 * GELU_B * square)
    act_ref[...] = (gelu * up).astype(BF)
    grad_ref[:, :width] = (d_active * up * slope).astype(BF)
    grad_ref[:, width:] = (d_active * gelu).astype(BF)


def feed_forward(rows, grads, weights):
    tokens = rows[0].shape[0]
    width = weights.shape[1] // 3
    tile = 256
    half = tokens // tile

    def first(columns):
        return pl.BlockSpec((tile, columns), lambda i: (jnp.minimum(i, half - 1), 0))

    def second(columns):
        return pl.BlockSpec((tile, columns), lambda i: (jnp.maximum(i - half, 0), 0))

    whole = pl.BlockSpec(weights.shape, lambda i: (0, 0), pipeline_mode=pl.Buffered(1))
    act = jax.ShapeDtypeStruct((tokens, width), BF)
    grad = jax.ShapeDtypeStruct((tokens, 2 * width), BF)
    out = pl.pallas_call(
        functools.partial(ff_kernel, width, half),
        grid=(2 * half,),
        in_specs=[first(D), second(D), first(D), second(D), whole],
        out_specs=[first(width), second(width), first(2 * width), second(2 * width)],
        out_shape=[act, act, grad, grad],
        compiler_params=pltpu.CompilerParams(vmem_limit_bytes=VMEM_LIMIT),
        cost_estimate=pl.CostEstimate(
            flops=26 * tokens * D * width, bytes_accessed=tokens * D, transcendentals=0
        ),
        name="feed_forward",
    )(*rows, *grads, weights)
    return (out[0], out[1]), (out[2], out[3])


def down_kernel(count, half, *refs):
    step = pl.program_id(0)
    mine, other, weights = (refs[k * count : (k + 1) * count] for k in range(3))

    def tile(rows, out_ref):
        terms = [mm(a[...], w[...], NT) for a, w in zip(rows, weights)]
        out_ref[...] = sum(terms[1:], terms[0]).astype(BF)

    @pl.when(step < half)
    def first():
        tile(mine, refs[3 * count])

    @pl.when(step >= half)
    def second():
        tile(other, refs[3 * count + 1])


def down_product(active, weights):
    count = len(active)
    tokens, width = active[0][0].shape
    tile = 256
    half = tokens // tile

    def first(columns):
        return pl.BlockSpec((tile, columns), lambda i: (jnp.minimum(i, half - 1), 0))

    def second(columns):
        return pl.BlockSpec((tile, columns), lambda i: (jnp.maximum(i - half, 0), 0))

    down = pl.BlockSpec((D, width), lambda i: (0, 2), pipeline_mode=pl.Buffered(1))
    return pl.pallas_call(
        functools.partial(down_kernel, count, half),
        grid=(2 * half,),
        in_specs=[first(width)] * count + [second(width)] * count + [down] * count,
        out_specs=[first(D), second(D)],
        out_shape=[jax.ShapeDtypeStruct((tokens, D), BF)] * 2,
        compiler_params=pltpu.CompilerParams(vmem_limit_bytes=VMEM_LIMIT),
        cost_estimate=pl.CostEstimate(
            flops=4 * count * tokens * D * width,
            bytes_accessed=2 * D * (count * width + 2 * tokens),
            transcendentals=0,
        ),
        name="down_product",
    )(*[a for a, _ in active], *[b for _, b in active], *weights)


def grads_kernel(count, *refs):
    rows, grads, by_rows, by_grads = (refs[k * count : (k + 1) * count] for k in range(4))
    out_ref = refs[4 * count]
    split = by_rows[0].shape[1]

    def total(left, right):
        acc = None
        for a, b in zip(left, right):
            term = mm(a[...], b[...], TN)
            acc = term if acc is None else acc + term
        return acc

    out_ref[:, :split] = total(rows, by_rows).astype(BF)
    out_ref[:, split:] = total(grads, by_grads).astype(BF)


def weight_grads(rows, grads, by_rows, by_grads):
    def halves(arrays):
        parts = []
        for a in arrays:
            parts += [(a[0], 0), (a[1], 0)] if isinstance(a, tuple) else [(a, 0), (a, 1)]
        return parts

    groups = [halves(a) for a in (rows, grads, by_rows, by_grads)]
    count = len(groups[0])
    tokens = groups[0][0][0].shape[0] // (1 if isinstance(rows[0], tuple) else 2)
    first, second = groups[2][0][0].shape[1], groups[3][0][0].shape[1]
    tile = 512

    def tall(half):
        return pl.BlockSpec((tokens, tile), lambda i: (half, i))

    def whole(width, half):
        return pl.BlockSpec((tokens, width), lambda i: (half, 0), pipeline_mode=pl.Buffered(1))

    return pl.pallas_call(
        functools.partial(grads_kernel, count),
        grid=(D // tile,),
        in_specs=[tall(half) for _, half in groups[0] + groups[1]]
        + [whole(first, half) for _, half in groups[2]]
        + [whole(second, half) for _, half in groups[3]],
        out_specs=pl.BlockSpec((tile, first + second), lambda i: (i, 0)),
        out_shape=jax.ShapeDtypeStruct((D, first + second), BF),
        compiler_params=pltpu.CompilerParams(vmem_limit_bytes=VMEM_LIMIT),
        cost_estimate=pl.CostEstimate(
            flops=3 * count * tokens * D * (first + second),
            bytes_accessed=2 * (2 * count * tokens * D + (count * tokens + D) * (first + second)),
            transcendentals=0,
        ),
        name="weight_grads",
    )(*[a for group in groups for a, _ in group])


RATE_QKV = D ** (-0.5)
RATE_OUT = 4.0 * (HEADS * HEAD_DIM) ** (-0.5)
RATE_DOWN = FF ** (-0.5)


def small_kernel(owned_ref, att_ref, gains_ref, gate_ref, out_ref):
    wide = att_ref[...].astype(F32)
    squares = jnp.sum(wide * wide, axis=(0, 1), keepdims=True) + owned_ref[0]
    count = gains_ref.shape[0]
    out_ref[:count] = gains_ref[...]
    lane = lax.broadcasted_iota(jnp.int32, gate_ref.shape, 1)
    out_ref[count:] = jnp.where(lane == HEADS, squares, gate_ref[...])


def small_sums(owned, own_att, gains, gate_row):
    return pl.pallas_call(
        small_kernel,
        in_specs=[
            pl.BlockSpec(memory_space=pltpu.SMEM),
            pl.BlockSpec(memory_space=pltpu.VMEM),
            pl.BlockSpec(memory_space=pltpu.VMEM),
            pl.BlockSpec(memory_space=pltpu.VMEM),
        ],
        out_specs=pl.BlockSpec(memory_space=pltpu.VMEM),
        out_shape=jax.ShapeDtypeStruct((gains.shape[0] + 1, 128), F32),
        compiler_params=pltpu.CompilerParams(vmem_limit_bytes=16 * 1024 * 1024),
        name="small_sums",
    )(owned[None], own_att, gains, gate_row)


def clip_factor(small):
    row = lax.broadcasted_iota(jnp.int32, small.shape, 0)
    lane = lax.broadcasted_iota(jnp.int32, small.shape, 1)
    summed = (row == small.shape[0] - 1) & (lane >= HEADS)
    squares = jnp.sum(jnp.where(summed, small, small * small), axis=(0, 1), keepdims=True)
    grad_norm = jnp.sqrt(squares)
    return grad_norm, jnp.minimum(1.0, CLIP / (grad_norm + 1e-06))


def adam_kernel(steps, chunks, place_ref, small_ref, *refs):
    ins, refs = refs[:18], refs[18:]
    grads, refs = refs[: 2 + 2 * chunks], refs[2 + 2 * chunks :]
    outs, norm_ref, scratch = refs[:18], refs[18], refs[19]
    grad_norm, factor = clip_factor(small_ref[...])
    is_low = place_ref[0] == 0
    everything = slice(None)

    def put(number, place, gradient, rate, decay=DECAY):
        weight, moment, second = (r[place] for r in ins[3 * number : 3 * number + 3])
        new = adam_update(weight, moment, second, gradient.astype(F32), factor, rate, decay)
        for ref, value in zip(outs[3 * number : 3 * number + 3], new):
            ref[place] = value

    def sides_of(mine, theirs):
        mine, theirs = mine[...], theirs[...]
        return jnp.where(is_low, mine, theirs), jnp.where(is_low, theirs, mine)

    for s, side in enumerate(sides_of(*grads[:2])):
        width = side.shape[1] // 4
        cols = slice(s * width, (s + 1) * width)
        for part in range(3):
            put(0, (part, everything, cols), side[:, part * width : (part + 1) * width], RATE_QKV)
        put(1, (everything, cols), side[:, 3 * width :], RATE_OUT)
    rows, width_ff = ins[9].shape
    lanes = width_ff // 128
    for k in range(chunks):
        for s, side in enumerate(sides_of(*grads[2 + 2 * k : 4 + 2 * k])):
            side = side.astype(F32)
            width = side.shape[1] // 3
            start = s * (width_ff // 2) + k * width
            put(3, (everything, slice(start, start + width)), side[:, 2 * width :], RATE_DOWN)
            for part in range(2):
                for lane in range(width // 128):
                    place = pl.ds((start // 128 + lane) * 2 + part, rows, stride=2 * lanes)
                    first = part * width + lane * 128
                    scratch[place, :] = side[:, first : first + 128]
    put(2, (everything, everything), scratch[...], RATE_QKV)

    @pl.when(pl.program_id(0) == 0)
    def small_ones():
        last = ins[12].shape[0]
        put(4, (everything, everything), small_ref[:last], 0.5, 0.0)
        put(5, (everything, everything), small_ref[last:, :HEADS], 1.0, 0.0)
        norm_ref[...] = grad_norm


def mlp_view(t):
    rows, _, width_ff = t.shape
    return t.reshape(rows, 2, width_ff // 128, 128).transpose(0, 2, 1, 3).reshape(-1, 128)


def adam_all(small, x_place, arrays, att_sides, ff_sides):
    rows, _, width_ff = arrays[6].shape
    steps = 4

    def qkv_view(t):
        return jnp.transpose(t, (1, 0, 2))

    def mlp_back(t, shape):
        rows, _, width_ff = shape
        t = t.reshape(rows, width_ff // 128, 2, 128).transpose(0, 2, 1, 3)
        return t.reshape(shape)

    views = [qkv_view(t) for t in arrays[:3]] + list(arrays[3:6])
    views += [mlp_view(t) for t in arrays[6:9]] + list(arrays[9:12])
    gains = [mlp_view(t[None]) for t in arrays[12:15]] + [t[None] for t in arrays[15:]]
    grads = list(att_sides) + [t for pair in ff_sides for t in pair]

    def spec(t):
        axis = t.ndim - 2
        block = list(t.shape)
        block[axis] //= steps
        return pl.BlockSpec(tuple(block), lambda i, place: (0,) * axis + (i, 0))

    def whole(t):
        return pl.BlockSpec(t.shape, lambda i, place: (0, 0))

    def mine(t):
        return pl.BlockSpec((rows // steps, t.shape[1]), lambda i, place: (place[0] * steps + i, 0))

    specs = [spec(t) for t in views] + [whole(t) for t in gains]
    new = pl.pallas_call(
        functools.partial(adam_kernel, steps, len(ff_sides)),
        grid_spec=pltpu.PrefetchScalarGridSpec(
            num_scalar_prefetch=1,
            grid=(steps,),
            in_specs=[whole(small)]
            + specs
            + [spec(t) if k % 2 else mine(t) for k, t in enumerate(grads)],
            out_specs=specs + [pl.BlockSpec((1, 1), lambda i, place: (0, 0))],
            scratch_shapes=[pltpu.VMEM((views[6].shape[0] // steps, 128), F32)],
        ),
        out_shape=[jax.ShapeDtypeStruct(t.shape, F32) for t in views + gains]
        + [jax.ShapeDtypeStruct((1, 1), F32)],
        compiler_params=pltpu.CompilerParams(vmem_limit_bytes=VMEM_LIMIT),
        cost_estimate=pl.CostEstimate(
            flops=20 * sum(t.size for t in views) // 3,
            bytes_accessed=8 * sum(t.size for t in views),
            transcendentals=0,
        ),
        name="adam",
    )(x_place[None], small, *views, *gains, *grads)
    new = list(new)
    return (
        [qkv_view(t) for t in new[:3]]
        + new[3:6]
        + [mlp_back(t, arrays[6].shape) for t in new[6:9]]
        + new[9:12]
        + [mlp_back(t, (1,) + arrays[12].shape)[0] for t in new[12:15]]
        + [t[0] for t in new[15:18]]
        + [new[18].reshape(())]
    )


def on_device(
    inputs,
    doc_ids,
    cotangent,
    weight_qkv,
    moment_qkv,
    second_qkv,
    weight_out,
    moment_out,
    second_out,
    weight_mlp,
    moment_mlp,
    second_mlp,
    weight_down,
    moment_down,
    second_down,
    norm_gains,
    moment_gains,
    second_gains,
    gate_logit,
    moment_gate,
    second_gate,
):
    micro_count, _, seg_count, own_len, _ = inputs.shape
    own_tokens = seg_count * own_len
    x_place = lax.axis_index("x")
    y_place = lax.axis_index("y")
    c_place = lax.axis_index("c")
    orders = [("x", "y") if m % 2 == 0 else ("y", "x") for m in range(micro_count)]

    z_count = D // (2 * weight_qkv.shape[0])

    def half_columns(weight, which):
        width = weight.shape[-1] // 2
        return lax.dynamic_slice_in_dim(weight, which * width, width, axis=weight.ndim - 1)

    def join_rows(mine, theirs):
        both = jnp.zeros((2 * rows, mine.shape[1]), BF)
        both = lax.dynamic_update_slice_in_dim(both, mine, x_place * rows, axis=0)
        return lax.dynamic_update_slice_in_dim(both, theirs, (1 - x_place) * rows, axis=0)

    def fetch(block):
        return lax.all_gather(block, "z", axis=0, tiled=True)

    rows = weight_qkv.shape[0]
    heads = weight_qkv.shape[2] // (2 * HEAD_DIM)
    width_att = heads * HEAD_DIM
    width_ff = weight_down.shape[1] // 2
    width = width_ff // CHUNKS

    def qkv_columns(which):
        return half_columns(weight_qkv, which).astype(BF).reshape(rows, -1)

    def ff_columns(k, which):
        start = which * width_ff + k * width
        mlp = lax.dynamic_slice_in_dim(mlp_later, start, width, axis=2).astype(BF)
        down = lax.dynamic_slice_in_dim(down_later, start, width, axis=1).astype(BF)
        return jnp.concatenate([mlp[:, 0], mlp[:, 1], down], axis=1)

    send_qkv = qkv_columns(1 - x_place)
    all_out = direct_gather(tie(weight_out, send_qkv).astype(BF), z_count)
    all_ids = tie(doc_ids[:, 0], send_qkv)
    for axis in ("y", "c"):
        all_ids = jnp.stack([all_ids, swap(all_ids, axis)], axis=0)
    micros = range(micro_count)
    tokens = 8 * own_tokens
    token_rows = [
        tie(inputs[m, 0], send_qkv).reshape(own_tokens, D).astype(F32) for m in micros
    ]
    normed_att = [rms_norm(t, norm_gains[0]).astype(BF) for t in token_rows]
    their_qkv = swap(send_qkv, "x")
    shard_qkv = join_rows(qkv_columns(x_place), tie(their_qkv, all_ids, *normed_att))
    full_qkv = fetch(shard_qkv)

    head_start = (y_place * 2 + c_place) * (2 * heads) + x_place * heads
    gate_local = lax.dynamic_slice_in_dim(gate_logit, head_start, heads)
    mixing = jax.nn.sigmoid(gate_local)
    gate_rows = jnp.broadcast_to(mixing[:, None], (heads, HEAD_DIM))

    back_low = [cotangent[m, 0].reshape(own_tokens, D) for m in micros]
    all_ids = jnp.stack([all_ids, swap(all_ids, "x")], axis=0)
    att_states = [
        gather_start(normed_att[m], *orders[m], (their_qkv, all_ids)) for m in micros
    ]
    att_by_x = [state[1 + orders[m].index("y")] for m, state in enumerate(att_states)]
    mlp_later = tie(weight_mlp, *att_by_x)
    down_later = tie(weight_down, *att_by_x)
    att_states = [gather_across(state, *orders[m], "y") for m, state in enumerate(att_states)]
    att_rows = [gather_core(state) for state in att_states]

    def their_ff(k, *earlier):
        return swap(tie(ff_columns(k, 1 - x_place), *earlier), "x")

    theirs = their_ff(0, *att_by_x)
    shard_ff = [join_rows(ff_columns(0, x_place), theirs)]
    full_ff = [fetch(shard_ff[0])]
    their_out = swap(tie(half_columns(all_out, 1 - x_place), shard_ff[0]), "x")
    both_out = jnp.zeros((z_count, 2, rows, width_att), BF)
    for part, place in ((half_columns(all_out, x_place), x_place), (their_out, 1 - x_place)):
        part = part.reshape(z_count, 1, rows, width_att)
        both_out = lax.dynamic_update_slice_in_dim(both_out, part, place, axis=1)
    full_out = both_out.reshape(D, width_att)
    back_states = [
        gather_start(back_low[m], *orders[m], (their_out,), (shard_ff[0],)) for m in micros
    ]
    back_first = [t for state in back_states for t in state[1:]]
    back_states = [gather_across(state, *orders[m], "y") for m, state in enumerate(back_states)]
    earlier = back_first

    rel_c = jnp.arange(2)[:, None, None] ^ c_place
    rel_y = jnp.arange(2)[None, :, None] ^ y_place
    places = ((rel_y * 2 + rel_c) * own_len + jnp.arange(own_len)).reshape(-1)
    causal = places[:, None] >= places[None, :]
    masks = []
    columns = []
    for m in micros:
        ids = jnp.transpose(all_ids[:, :, :, m], (0, 3, 1, 2, 4)).reshape(2, seg_count, -1)
        same = ids[:, :, :, None] == ids[:, :, None, :]
        masks.append((same & causal).astype(F32))
        last = jnp.max(ids, axis=2)
        previous = jnp.concatenate([jnp.full((2, 1), -1, last.dtype), last[:, :-1]], axis=1)
        reading = ids == previous[:, :, None]
        writing = ids == last[:, :, None]
        keep = jnp.broadcast_to((last == previous)[:, :, None], ids.shape)
        columns.append(jnp.stack([reading, writing, keep], axis=-1).astype(F32))

    slots = (2, 2, 2, seg_count, own_len)
    wheres = [1 if orders[m][0] == "x" else 2 for m in micros]
    projected = []
    combined = []
    hidden = []
    normed_mlp = []
    for m in micros:
        mine, other = att_rows[m]
        if m == 0:
            mine = tie(mine, *back_first)
        proj = jnp.concatenate([mm(p, full_qkv, NN).astype(BF) for p in (mine, other)], axis=0)
        projected.append(proj.reshape(slots + (3 * width_att,)))
        comb = attention_fwd(projected[m], masks[m], columns[m], gate_rows, wheres[m])
        combined.append(comb.reshape(tokens, width_att))
    half = tokens // 2
    for k in range(1, CHUNKS):
        theirs = their_ff(k, *earlier)
        shard_ff.append(join_rows(ff_columns(k, x_place), tie(theirs, combined[0])))
        full_ff.append(fetch(shard_ff[k]))
        earlier = [theirs]
    back_states = [(tie(state[0], combined[0]),) + state[1:] for state in back_states]
    back_rows = [gather_core(state) for state in back_states]
    for m in micros:
        ready = combined[m]
        if m > 0:
            ready = tie(ready, *shard_ff, *[state[-1] for state in back_states])
        other = mm(ready[half:], full_out, NT).astype(BF)
        mine = mm(ready[:half], full_out, NT).astype(BF)
        state = scatter_core(mine, other, own_tokens, orders[m][0], orders[m][0])
        state = scatter_outer(state, orders[m][0])
        hidden.append(token_rows[m] + scatter_inner(state, orders[m][1]))
        normed_mlp.append(rms_norm(hidden[m], norm_gains[1]).astype(BF))
    mlp_rows = [gather_core(state) for state in gather_steps(normed_mlp, orders)]

    def exchange_grad(grad):
        return grad, swap(lax.dynamic_slice_in_dim(grad, (1 - x_place) * rows, rows, axis=0), "x")

    def squares_of(grad):
        wide = grad.astype(F32)
        return jnp.sum(wide * wide)

    def reduce_rows(partial):
        return lax.psum_scatter(partial, "z", scatter_dimension=0, tiled=True)

    def products(left, right, totals, dtype):
        terms = [mm(left[p], right, NT) for p in (1, 0)][::-1]
        if totals is not None:
            terms = [a + b for a, b in zip(totals, terms)]
        return tuple(t.astype(dtype) for t in terms)

    active = []
    d_gate_up = []
    own_ff = []
    d_total = [None] * micro_count
    states = [None] * micro_count
    for k in range(CHUNKS):
        active.append([])
        d_gate_up.append([])
        last = k == CHUNKS - 1
        for m in micros:
            rows_in = mlp_rows[m]
            if last and m > 0:
                rows_in = (tie(rows_in[0], *d_total[m - 1]), rows_in[1])
            act, grad = feed_forward(rows_in, back_rows[m], full_ff[k])
            active[k].append(act)
            d_gate_up[k].append(grad)
            if last and m > 0:
                grad = (grad[0], tie(grad[1], states[m - 1][1]))
            dtype = BF if last else F32
            d_total[m] = products(grad, full_ff[k][:, : 2 * width], d_total[m], dtype)
            if last:
                states[m] = scatter_core(*d_total[m], own_tokens, orders[m][0], orders[m][0])
        if not last:
            grad_ff = weight_grads(mlp_rows, back_rows, d_gate_up[k], active[k])
            own_ff.append(reduce_rows(grad_ff))
            terms = [t for pair in d_total for t in pair]
            full_ff[k + 1] = tie(full_ff[k + 1], grad_ff, *terms)

    out_pairs = []
    for m in micros:
        act = [active[k][m] for k in range(CHUNKS)]
        act[-1] = (act[-1][0], tie(act[-1][1], states[-1][1]))
        out_pairs.append(down_product(act, full_ff))
    products_done = [t for pair in out_pairs for t in pair]
    outer_states = [scatter_outer(states[m], orders[m][0], *products_done) for m in micros]
    last_active = [
        (active[-1][m][0], tie(active[-1][m][1], *[t[1] for t in outer_states])) for m in micros
    ]
    grad_ff = weight_grads(mlp_rows, back_rows, d_gate_up[-1], last_active)
    own_ff.append(reduce_rows(grad_ff))

    gain_grad_att = jnp.zeros((D,), F32)
    gain_grad_mlp = jnp.zeros((D,), F32)
    d_hidden = []
    for m in micros:
        keep, send = outer_states[m]
        d_normed = scatter_inner((tie(keep, grad_ff), send), orders[m][1])
        ignored, norm_back = jax.vjp(rms_norm, hidden[m], norm_gains[1])
        d_norm, d_gain = norm_back(d_normed)
        gain_grad_mlp = gain_grad_mlp + d_gain
        d_hidden.append(back_low[m].astype(F32) + d_norm)

    gate_sum = jnp.zeros((heads,), F32)
    d_projs = []
    out_states = [
        scatter_core(*tie_pair(out_pairs[m], *d_hidden), own_tokens, orders[m][0], orders[m][0])
        for m in micros
    ]
    grad_states = gather_steps([t.astype(BF) for t in d_hidden], orders)
    sends = [t[1] for t in out_states]
    out_states = [tie_send(t, *[g[-1] for g in grad_states]) for t in out_states]
    att_grads = [gather_core((tie(g[0], *sends),) + g[1:]) for g in grad_states]
    ff_pairs = [exchange_grad(own_ff[0])]
    for m in micros:
        mine, other = att_grads[m]
        if m == 0:
            other = tie(other, own_ff[0])
        d_combined = jnp.concatenate(
            [mm(mine, full_out, NN), mm(other, full_out, NN)], axis=0
        )
        d_proj, gate_part = attention_bwd(
            projected[m],
            d_combined.reshape(slots + (width_att,)),
            masks[m],
            columns[m],
            gate_rows,
            wheres[m],
        )
        gate_sum = gate_sum + jnp.sum(gate_part, axis=(0, 2))
        d_projs.append(d_proj.reshape(tokens, 3 * width_att))
    out_came = [swap(out_states[m][1], orders[m][0]) for m in micros]
    by_rows = [d_projs[0], tie(d_projs[-1], ff_pairs[0][1], *out_came)]
    grad_att = weight_grads(att_rows, att_grads, by_rows, combined)
    own_att = reduce_rows(grad_att)
    mlp_out = []
    for m in micros:
        state = scatter_add(out_states[m][0], tie(out_came[m], grad_att))
        mlp_out.append(scatter_inner(state, orders[m][1]))
    block_out = [(hidden[m] + mlp_out[m]).astype(BF) for m in micros]

    ff_pairs += [exchange_grad(g) for g in own_ff[1:]]

    ff_owned = sum(squares_of(g) for g in own_ff)

    grad_rows = []
    in_states = []
    for m in micros:
        d_proj = tie(d_projs[m], grad_att)
        other = mm(d_proj[half:], full_qkv, NT).astype(BF)
        mine = mm(d_proj[:half], full_qkv, NT).astype(BF)
        in_states.append(scatter_core(mine, other, own_tokens, orders[m][0], orders[m][0]))
    for m in micros:
        state = scatter_outer(in_states[m], orders[m][0])
        if m > 0:
            state = tie_send(state, ff_pairs[-1][1])
        d_normed = scatter_inner(state, orders[m][1])
        ignored, norm_first = jax.vjp(rms_norm, token_rows[m], norm_gains[0])
        d_norm, d_gain = norm_first(d_normed)
        gain_grad_att = gain_grad_att + d_gain
        grad_rows.append((d_hidden[m] + d_norm).astype(BF))

    att_mine, att_theirs = exchange_grad(own_att)

    gate_grad = gate_sum * mixing * (1.0 - mixing)
    gate_padded = lax.dynamic_update_slice(
        jnp.zeros(gate_logit.shape, F32), gate_grad, (head_start,)
    )
    gain_grad = mlp_view(jnp.stack([gain_grad_att, gain_grad_mlp], axis=0)[None])
    gate_row = jnp.concatenate([gate_padded, jnp.zeros((128 - HEADS,), F32)])[None]
    small = small_sums(ff_owned, own_att, gain_grad, gate_row)
    small = sum_everywhere(small, z_count, att_theirs)
    arrays = [
        weight_qkv,
        moment_qkv,
        second_qkv,
        weight_out,
        moment_out,
        second_out,
        weight_mlp,
        moment_mlp,
        second_mlp,
        weight_down,
        moment_down,
        second_down,
        norm_gains,
        moment_gains,
        second_gains,
        gate_logit,
        moment_gate,
        second_gate,
    ]
    new = adam_all(small, x_place, arrays, (att_mine, att_theirs), ff_pairs)
    shape = (micro_count, 1, seg_count, own_len, D)
    return (
        jnp.stack(block_out, axis=0).reshape(shape),
        jnp.stack(grad_rows, axis=0).reshape(shape),
        new[-1],
        *new[:-1],
    )


def solution(mesh):
    seq_count, ctx_count = mesh.devices.shape
    inner = Mesh(
        mesh.devices.reshape(seq_count // 2, 2, ctx_count // 2, 2), ("z", "x", "y", "c")
    )
    seq, ctx = ("z", "x"), ("y", "c")
    rows = P(None, seq, None, ctx, None)
    wide = P(seq, None, ctx)
    flat = P(seq, ctx)
    weights = (wide,) * 3 + (flat,) * 3 + (wide,) * 3 + (flat,) * 3 + (P(),) * 6
    return jax.shard_map(
        on_device,
        mesh=inner,
        in_specs=(rows, P(None, seq, None, ctx), rows) + weights,
        out_specs=(rows, rows, P()) + weights,
        check_vma=False,
    )
```

```python
import functools

import jax
import jax.numpy as jnp
from jax import lax
from jax.experimental import pallas as pl
from jax.experimental.pallas import tpu as pltpu
from jax.sharding import Mesh
from jax.sharding import PartitionSpec as P

D = 2048
HEADS = 16
HEAD_DIM = 128
FF = 8192
STEP_COUNT = 10
CHUNKS = 2

EPS = 1e-06
NEG = -1e30
CLIP = 1.0
BETA1 = 0.9
BETA2 = 0.95
ADAM_EPS = 1e-08
DECAY = 0.1
BF = jnp.bfloat16
F32 = jnp.float32
SCALING = HEAD_DIM ** (-0.5)
VMEM_LIMIT = 48 * 1024 * 1024


def rms_norm(tensor, scaling):
    return tensor * lax.rsqrt(jnp.mean(tensor * tensor, axis=-1, keepdims=True) + EPS) * scaling


def adam_update(weight, moment, second, gradient, factor, step_rate, decay):
    clipped = gradient * factor
    moment = BETA1 * moment + (1.0 - BETA1) * clipped
    second = BETA2 * second + (1.0 - BETA2) * clipped * clipped
    fixed_first = moment / (1.0 - BETA1**STEP_COUNT)
    fixed_second = second / (1.0 - BETA2**STEP_COUNT)
    updated = weight - step_rate * (
        fixed_first / (jnp.sqrt(fixed_second) + ADAM_EPS) + decay * weight
    )
    return (moment, second, updated)


def swap(tensor, axis):
    return lax.ppermute(tensor, axis, [(0, 1), (1, 0)])


def tie(tensor, *earlier):
    return lax.optimization_barrier((tensor,) + earlier)[0]


def gather_start(own, outer, inner, x_after=(), y_after=()):
    start = {"x": tie(own, *x_after), "y": tie(own, *y_after)}
    return own, swap(start[inner], inner), swap(start[outer], outer)


def gather_across(state, outer, inner, last):
    own, by_inner, by_outer = state
    return state + (swap(by_inner if last == outer else by_outer, last),)


def gather_steps(owns, orders):
    starts = [gather_start(own, *order) for own, order in zip(owns, orders)]
    firsts = [t for state in starts for t in state[1:]]
    ready = []
    for state, order in zip(starts, orders):
        by_inner = tie(state[1], *firsts)
        ready.append((state[0], by_inner, state[2], swap(by_inner, order[0])))
    lasts = [state[-1] for state in ready]
    return [(tie(state[0], *lasts),) + state[1:] for state in ready]


def gather_core(state):
    mine = jnp.concatenate(state, axis=0)
    return mine, swap(mine, "c")


def scatter_core(mine, other, units, outer, first):
    came = swap(other, "c").reshape(2, 2, units, -1)
    mine = mine.reshape(2, 2, units, -1)
    parts = []
    for p in range(2):
        index = (p,) if first == outer else (slice(None), p)
        parts.append(mine[index].astype(F32) + came[index].astype(F32))
    return parts[0], parts[1].astype(BF)


def scatter_outer(state, axis, *later):
    keep, send = state
    return scatter_add(keep, tie(swap(send, axis), *later))


def scatter_add(keep, came):
    send = (keep[1] + came[1].astype(F32)).astype(BF)
    return keep[0] + came[0].astype(F32), send


def scatter_inner(state, axis):
    keep, send = state
    return keep + swap(send, axis).astype(F32)


def tie_pair(pair, *earlier):
    return pair[0], tie(pair[1], *earlier)


def tie_send(state, *earlier):
    return state[0], tie(state[1], *earlier)


def direct_gather(block, z_count):
    rows = block.shape[0]
    place = lax.axis_index("z")
    pieces = [block]
    for step in range(1, z_count):
        pairs = [(i, (i + step) % z_count) for i in range(z_count)]
        pieces.append(lax.ppermute(block, "z", pairs))
    full = jnp.zeros((z_count * rows, block.shape[1]), block.dtype)
    for step, piece in enumerate(pieces):
        slot = lax.rem(place + z_count - step, z_count)
        full = lax.dynamic_update_slice_in_dim(full, piece, slot * rows, axis=0)
    return full


def sum_everywhere(tensor, z_count, beside):
    def add(tensor, axis, pairs):
        return tensor + lax.ppermute(tensor, axis, pairs)

    tensor = add(tensor, "x", [(0, 1), (1, 0)])
    reach = 1
    while reach < z_count:
        tensor = add(tensor, "z", [(i, i ^ reach) for i in range(z_count)])
        reach *= 2
    tensor = add(tensor, "c", [(0, 1), (1, 0)])
    return add(tie(tensor, beside), "y", [(0, 1), (1, 0)])


def mm(a, b, dims):
    return lax.dot_general(a, b, (dims, ((), ())), preferred_element_type=F32)


NN = ((1,), (0,))
NT = ((1,), (1,))
TN = ((0,), (0,))


def mm_mem(a, b, dims):
    return mm(a.astype(BF), b.astype(BF), dims)


def elu_one(tensor):
    return jnp.where(tensor > 0, tensor + 1.0, jnp.exp(jnp.minimum(tensor, 0.0)))


def elu_slope(tensor):
    low = jnp.where(tensor == 0, 0.5, jnp.exp(jnp.minimum(tensor, 0.0)))
    return jnp.where(tensor > 0, 1.0, low)


def segment_of(ref, r, part):
    block = ref[:, :, r, :, part * HEAD_DIM : (part + 1) * HEAD_DIM]
    return block.reshape(-1, HEAD_DIM)


def memory_forward(qs, ks, vs, cols):
    seg_count = len(qs)
    saved = []
    memory = normer = None
    for r in range(seg_count):
        reading, writing, keep = cols[r]
        sq = elu_one(qs[r].astype(F32))
        sk = elu_one(ks[r].astype(F32))
        value = vs[r].astype(F32)
        rows = sq.shape[0]
        item = dict(sq=sq, sk=sk)
        if r == 0:
            item["recalled"] = jnp.zeros_like(sq)
            change = value
        else:
            both = mm_mem(jnp.concatenate([sq, sk], axis=0), memory, NN)
            num = both[:rows]
            den = 1.0 + jnp.sum(sq * normer, axis=-1, keepdims=True)
            item["recalled"] = reading * num / den
            before = keep * both[rows:]
            kden = 1.0 + keep * jnp.sum(sk * normer, axis=-1, keepdims=True)
            change = value - before / kden
            item.update(num=num, den=den, before=before, kden=kden, memory=memory, normer=normer)
        item["change"] = change
        if r < seg_count - 1:
            write = sk * writing
            fresh = mm_mem(write, change, TN)
            fresh_norm = jnp.sum(write, axis=0, keepdims=True)
            memory = fresh if r == 0 else keep * memory + fresh
            normer = fresh_norm if r == 0 else keep[:1] * normer + fresh_norm
        saved.append(item)
    return saved


def local_probs(query, key, allowed):
    scores = jnp.where(allowed > 0, mm(query, key, NT) * SCALING, NEG)
    exponent = jnp.exp(scores - jnp.max(scores, axis=-1, keepdims=True))
    return exponent / jnp.sum(exponent, axis=-1, keepdims=True)


def columns_of(cols_ref, r):
    cols = cols_ref[r]
    return cols[:, 0:1], cols[:, 1:2], cols[:, 2:3]


def attention_fwd_kernel(heads, proj_ref, mask_ref, cols_ref, gate_ref, out_ref):
    seg_count = mask_ref.shape[0]
    cols = [columns_of(cols_ref, r) for r in range(seg_count)]
    for h in range(heads):
        qs = [segment_of(proj_ref, r, h) for r in range(seg_count)]
        ks = [segment_of(proj_ref, r, heads + h) for r in range(seg_count)]
        vs = [segment_of(proj_ref, r, 2 * heads + h) for r in range(seg_count)]
        saved = memory_forward(qs, ks, vs, cols)
        mixing = gate_ref[h : h + 1]
        for r in range(seg_count):
            prob_low = local_probs(qs[r], ks[r], mask_ref[r]).astype(BF)
            local_out = mm(prob_low, vs[r], NN)
            combined = mixing * saved[r]["recalled"] + (1.0 - mixing) * local_out
            out_ref[:, :, r, :, h * HEAD_DIM : (h + 1) * HEAD_DIM] = combined.astype(BF).reshape(
                out_ref.shape[0], out_ref.shape[1], out_ref.shape[3], HEAD_DIM
            )


def attention_bwd_kernel(
    heads, proj_ref, grad_ref, mask_ref, cols_ref, gate_ref, out_ref, gate_out_ref
):
    seg_count = mask_ref.shape[0]
    cols = [columns_of(cols_ref, r) for r in range(seg_count)]

    def put(r, part, value):
        out_ref[:, :, r, :, part * HEAD_DIM : (part + 1) * HEAD_DIM] = value.astype(BF).reshape(
            out_ref.shape[0], out_ref.shape[1], out_ref.shape[3], HEAD_DIM
        )

    for h in range(heads):
        qs = [segment_of(proj_ref, r, h) for r in range(seg_count)]
        ks = [segment_of(proj_ref, r, heads + h) for r in range(seg_count)]
        vs = [segment_of(proj_ref, r, 2 * heads + h) for r in range(seg_count)]
        saved = memory_forward(qs, ks, vs, cols)
        mixing = gate_ref[h : h + 1]
        gate_sum = jnp.zeros((1, HEAD_DIM), F32)
        d_memory = d_normer = None
        for r in reversed(range(seg_count)):
            reading, writing, keep = cols[r]
            item = saved[r]
            sq, sk = item["sq"], item["sk"]
            rows = sq.shape[0]
            d_combined = segment_of(grad_ref, r, h).astype(F32)
            d_recalled = mixing * d_combined
            d_local = ((1.0 - mixing) * d_combined).astype(BF)
            probs = local_probs(qs[r], ks[r], mask_ref[r])
            prob_low = probs.astype(BF)
            local_out = mm(prob_low, vs[r], NN)
            gate_sum = gate_sum + jnp.sum(
                d_combined * (item["recalled"] - local_out), axis=0, keepdims=True
            )
            d_prob = mm(d_local, vs[r], NT)
            d_value = mm(prob_low, d_local, TN)
            d_scores = (
                probs * (d_prob - jnp.sum(d_prob * probs, axis=-1, keepdims=True))
            ).astype(BF)
            d_query = mm(d_scores, ks[r], NN) * SCALING
            d_key = mm(d_scores, qs[r], TN) * SCALING
            d_sk = None
            d_before = d_kden = None
            if r < seg_count - 1:
                d_change = writing * mm_mem(sk, d_memory, NN)
                d_sk = writing * (mm_mem(item["change"], d_memory, NT) + d_normer)
                d_value = d_value + d_change
                if r > 0:
                    d_before = keep * (-d_change / item["kden"])
                    d_kden = keep * (
                        jnp.sum(d_change * item["before"], axis=-1, keepdims=True)
                        / (item["kden"] * item["kden"])
                    )
            if r > 0:
                d_num = reading * d_recalled / item["den"]
                d_den = -reading * (
                    jnp.sum(d_recalled * item["num"], axis=-1, keepdims=True)
                    / (item["den"] * item["den"])
                )
                if d_before is None:
                    d_sq = mm_mem(d_num, item["memory"], NT) + d_den * item["normer"]
                    new_memory = mm_mem(sq, d_num, TN)
                    new_normer = jnp.sum(sq * d_den, axis=0, keepdims=True)
                else:
                    stacked = jnp.concatenate([d_num, d_before], axis=0)
                    both = mm_mem(stacked, item["memory"], NT)
                    d_sq = both[:rows] + d_den * item["normer"]
                    d_sk = d_sk + both[rows:] + d_kden * item["normer"]
                    new_memory = keep * d_memory + mm_mem(
                        jnp.concatenate([sq, sk], axis=0), stacked, TN
                    )
                    new_normer = keep[:1] * d_normer + jnp.sum(
                        sq * d_den + sk * d_kden, axis=0, keepdims=True
                    )
                d_memory, d_normer = new_memory, new_normer
                d_query = d_query + d_sq * elu_slope(qs[r].astype(F32))
            if d_sk is not None:
                d_key = d_key + d_sk * elu_slope(ks[r].astype(F32))
            put(r, h, d_query)
            put(r, heads + h, d_key)
            put(r, 2 * heads + h, d_value)
        gate_out_ref[h : h + 1] = gate_sum


def block_spec(shape, where):
    dims = list(shape)
    dims[where] = None

    def index(s):
        place = [0] * len(dims)
        place[where] = s
        return tuple(place)

    return pl.BlockSpec(tuple(dims), index)


def attention_fwd(projected, mask, cols, gate_rows, where):
    heads = gate_rows.shape[0]
    out_shape = projected.shape[:-1] + (heads * HEAD_DIM,)
    return pl.pallas_call(
        functools.partial(attention_fwd_kernel, heads),
        grid=(projected.shape[where],),
        in_specs=[
            block_spec(projected.shape, where),
            pl.BlockSpec((None,) + mask.shape[1:], lambda s: (s, 0, 0, 0)),
            pl.BlockSpec((None,) + cols.shape[1:], lambda s: (s, 0, 0, 0)),
            pl.BlockSpec(gate_rows.shape, lambda s: (0, 0)),
        ],
        out_specs=block_spec(out_shape, where),
        out_shape=jax.ShapeDtypeStruct(out_shape, BF),
        compiler_params=pltpu.CompilerParams(vmem_limit_bytes=VMEM_LIMIT),
        cost_estimate=pl.CostEstimate(
            flops=100_000_000, bytes_accessed=100_000, transcendentals=0
        ),
        name="attention_forward",
    )(projected, mask, cols, gate_rows)


def attention_bwd(projected, d_combined, mask, cols, gate_rows, where):
    heads = gate_rows.shape[0]
    seqs = projected.shape[where]
    return pl.pallas_call(
        functools.partial(attention_bwd_kernel, heads),
        grid=(seqs,),
        in_specs=[
            block_spec(projected.shape, where),
            block_spec(d_combined.shape, where),
            pl.BlockSpec((None,) + mask.shape[1:], lambda s: (s, 0, 0, 0)),
            pl.BlockSpec((None,) + cols.shape[1:], lambda s: (s, 0, 0, 0)),
            pl.BlockSpec(gate_rows.shape, lambda s: (0, 0)),
        ],
        out_specs=[
            block_spec(projected.shape, where),
            pl.BlockSpec((None, heads, HEAD_DIM), lambda s: (s, 0, 0)),
        ],
        out_shape=[
            jax.ShapeDtypeStruct(projected.shape, BF),
            jax.ShapeDtypeStruct((seqs, heads, HEAD_DIM), F32),
        ],
        compiler_params=pltpu.CompilerParams(vmem_limit_bytes=VMEM_LIMIT),
        cost_estimate=pl.CostEstimate(
            flops=14_400_000_000, bytes_accessed=5_000_000, transcendentals=0
        ),
        name="attention_backward",
    )(projected, d_combined, mask, cols, gate_rows)


GELU_A = 0.7978845608028654
GELU_B = 0.044715


def ff_kernel(width, half, x_mine, x_other, g_mine, g_other, w_ref, *outs):
    step = pl.program_id(0)

    @pl.when(step < half)
    def first():
        ff_tile(width, x_mine, g_mine, w_ref, outs[0], outs[2])

    @pl.when(step >= half)
    def second():
        ff_tile(width, x_other, g_other, w_ref, outs[1], outs[3])


def ff_tile(width, x_ref, g_ref, w_ref, act_ref, grad_ref):
    weights = w_ref[...]
    gate_up = mm(x_ref[...], weights[:, : 2 * width], NN)
    d_active = mm(g_ref[...], weights[:, 2 * width :], NN)
    gate = gate_up[:, :width]
    up = gate_up[:, width:]
    square = gate * gate
    tanh = jnp.tanh(GELU_A * gate * (1.0 + GELU_B * square))
    half = 0.5 * (1.0 + tanh)
    gelu = gate * half
    slope = half + 0.5 * gate * (1.0 - tanh * tanh) * GELU_A * (1.0 + 3.0 * GELU_B * square)
    act_ref[...] = (gelu * up).astype(BF)
    grad_ref[:, :width] = (d_active * up * slope).astype(BF)
    grad_ref[:, width:] = (d_active * gelu).astype(BF)


def feed_forward(rows, grads, weights):
    tokens = rows[0].shape[0]
    width = weights.shape[1] // 3
    tile = 256
    half = tokens // tile

    def first(columns):
        return pl.BlockSpec((tile, columns), lambda i: (jnp.minimum(i, half - 1), 0))

    def second(columns):
        return pl.BlockSpec((tile, columns), lambda i: (jnp.maximum(i - half, 0), 0))

    whole = pl.BlockSpec(weights.shape, lambda i: (0, 0), pipeline_mode=pl.Buffered(1))
    act = jax.ShapeDtypeStruct((tokens, width), BF)
    grad = jax.ShapeDtypeStruct((tokens, 2 * width), BF)
    out = pl.pallas_call(
        functools.partial(ff_kernel, width, half),
        grid=(2 * half,),
        in_specs=[first(D), second(D), first(D), second(D), whole],
        out_specs=[first(width), second(width), first(2 * width), second(2 * width)],
        out_shape=[act, act, grad, grad],
        compiler_params=pltpu.CompilerParams(vmem_limit_bytes=VMEM_LIMIT),
        cost_estimate=pl.CostEstimate(
            flops=26 * tokens * D * width, bytes_accessed=tokens * D, transcendentals=0
        ),
        name="feed_forward",
    )(*rows, *grads, weights)
    return (out[0], out[1]), (out[2], out[3])


def down_kernel(count, half, *refs):
    step = pl.program_id(0)
    mine, other, weights = (refs[k * count : (k + 1) * count] for k in range(3))

    def tile(rows, out_ref):
        terms = [mm(a[...], w[...], NT) for a, w in zip(rows, weights)]
        out_ref[...] = sum(terms[1:], terms[0]).astype(BF)

    @pl.when(step < half)
    def first():
        tile(mine, refs[3 * count])

    @pl.when(step >= half)
    def second():
        tile(other, refs[3 * count + 1])


def down_product(active, weights):
    count = len(active)
    tokens, width = active[0][0].shape
    tile = 256
    half = tokens // tile

    def first(columns):
        return pl.BlockSpec((tile, columns), lambda i: (jnp.minimum(i, half - 1), 0))

    def second(columns):
        return pl.BlockSpec((tile, columns), lambda i: (jnp.maximum(i - half, 0), 0))

    down = pl.BlockSpec((D, width), lambda i: (0, 2), pipeline_mode=pl.Buffered(1))
    return pl.pallas_call(
        functools.partial(down_kernel, count, half),
        grid=(2 * half,),
        in_specs=[first(width)] * count + [second(width)] * count + [down] * count,
        out_specs=[first(D), second(D)],
        out_shape=[jax.ShapeDtypeStruct((tokens, D), BF)] * 2,
        compiler_params=pltpu.CompilerParams(vmem_limit_bytes=VMEM_LIMIT),
        cost_estimate=pl.CostEstimate(
            flops=4 * count * tokens * D * width,
            bytes_accessed=2 * D * (count * width + 2 * tokens),
            transcendentals=0,
        ),
        name="down_product",
    )(*[a for a, _ in active], *[b for _, b in active], *weights)


def grads_kernel(count, *refs):
    rows, grads, by_rows, by_grads = (refs[k * count : (k + 1) * count] for k in range(4))
    out_ref = refs[4 * count]
    split = by_rows[0].shape[1]

    def total(left, right):
        acc = None
        for a, b in zip(left, right):
            term = mm(a[...], b[...], TN)
            acc = term if acc is None else acc + term
        return acc

    out_ref[:, :split] = total(rows, by_rows).astype(BF)
    out_ref[:, split:] = total(grads, by_grads).astype(BF)


def weight_grads(rows, grads, by_rows, by_grads):
    def halves(arrays):
        parts = []
        for a in arrays:
            parts += [(a[0], 0), (a[1], 0)] if isinstance(a, tuple) else [(a, 0), (a, 1)]
        return parts

    groups = [halves(a) for a in (rows, grads, by_rows, by_grads)]
    count = len(groups[0])
    tokens = groups[0][0][0].shape[0] // (1 if isinstance(rows[0], tuple) else 2)
    first, second = groups[2][0][0].shape[1], groups[3][0][0].shape[1]
    tile = 512

    def tall(half):
        return pl.BlockSpec((tokens, tile), lambda i: (half, i))

    def whole(width, half):
        return pl.BlockSpec((tokens, width), lambda i: (half, 0), pipeline_mode=pl.Buffered(1))

    return pl.pallas_call(
        functools.partial(grads_kernel, count),
        grid=(D // tile,),
        in_specs=[tall(half) for _, half in groups[0] + groups[1]]
        + [whole(first, half) for _, half in groups[2]]
        + [whole(second, half) for _, half in groups[3]],
        out_specs=pl.BlockSpec((tile, first + second), lambda i: (i, 0)),
        out_shape=jax.ShapeDtypeStruct((D, first + second), BF),
        compiler_params=pltpu.CompilerParams(vmem_limit_bytes=VMEM_LIMIT),
        cost_estimate=pl.CostEstimate(
            flops=3 * count * tokens * D * (first + second),
            bytes_accessed=2 * (2 * count * tokens * D + (count * tokens + D) * (first + second)),
            transcendentals=0,
        ),
        name="weight_grads",
    )(*[a for group in groups for a, _ in group])


RATE_QKV = D ** (-0.5)
RATE_OUT = 4.0 * (HEADS * HEAD_DIM) ** (-0.5)
RATE_DOWN = FF ** (-0.5)


def small_kernel(owned_ref, att_ref, gains_ref, gate_ref, out_ref):
    wide = att_ref[...].astype(F32)
    squares = jnp.sum(wide * wide, axis=(0, 1), keepdims=True) + owned_ref[0]
    count = gains_ref.shape[0]
    out_ref[:count] = gains_ref[...]
    lane = lax.broadcasted_iota(jnp.int32, gate_ref.shape, 1)
    out_ref[count:] = jnp.where(lane == HEADS, squares, gate_ref[...])


def small_sums(owned, own_att, gains, gate_row):
    return pl.pallas_call(
        small_kernel,
        in_specs=[
            pl.BlockSpec(memory_space=pltpu.SMEM),
            pl.BlockSpec(memory_space=pltpu.VMEM),
            pl.BlockSpec(memory_space=pltpu.VMEM),
            pl.BlockSpec(memory_space=pltpu.VMEM),
        ],
        out_specs=pl.BlockSpec(memory_space=pltpu.VMEM),
        out_shape=jax.ShapeDtypeStruct((gains.shape[0] + 1, 128), F32),
        compiler_params=pltpu.CompilerParams(vmem_limit_bytes=16 * 1024 * 1024),
        name="small_sums",
    )(owned[None], own_att, gains, gate_row)


def clip_factor(small):
    row = lax.broadcasted_iota(jnp.int32, small.shape, 0)
    lane = lax.broadcasted_iota(jnp.int32, small.shape, 1)
    summed = (row == small.shape[0] - 1) & (lane >= HEADS)
    squares = jnp.sum(jnp.where(summed, small, small * small), axis=(0, 1), keepdims=True)
    grad_norm = jnp.sqrt(squares)
    return grad_norm, jnp.minimum(1.0, CLIP / (grad_norm + 1e-06))


def adam_kernel(steps, chunks, place_ref, small_ref, *refs):
    ins, refs = refs[:18], refs[18:]
    grads, refs = refs[: 2 + 2 * chunks], refs[2 + 2 * chunks :]
    outs, norm_ref, scratch = refs[:18], refs[18], refs[19]
    grad_norm, factor = clip_factor(small_ref[...])
    is_low = place_ref[0] == 0
    everything = slice(None)

    def put(number, place, gradient, rate, decay=DECAY):
        weight, moment, second = (r[place] for r in ins[3 * number : 3 * number + 3])
        new = adam_update(weight, moment, second, gradient.astype(F32), factor, rate, decay)
        for ref, value in zip(outs[3 * number : 3 * number + 3], new):
            ref[place] = value

    def sides_of(mine, theirs):
        mine, theirs = mine[...], theirs[...]
        return jnp.where(is_low, mine, theirs), jnp.where(is_low, theirs, mine)

    for s, side in enumerate(sides_of(*grads[:2])):
        width = side.shape[1] // 4
        cols = slice(s * width, (s + 1) * width)
        for part in range(3):
            put(0, (part, everything, cols), side[:, part * width : (part + 1) * width], RATE_QKV)
        put(1, (everything, cols), side[:, 3 * width :], RATE_OUT)
    rows, width_ff = ins[9].shape
    lanes = width_ff // 128
    for k in range(chunks):
        for s, side in enumerate(sides_of(*grads[2 + 2 * k : 4 + 2 * k])):
            side = side.astype(F32)
            width = side.shape[1] // 3
            start = s * (width_ff // 2) + k * width
            put(3, (everything, slice(start, start + width)), side[:, 2 * width :], RATE_DOWN)
            for part in range(2):
                for lane in range(width // 128):
                    place = pl.ds((start // 128 + lane) * 2 + part, rows, stride=2 * lanes)
                    first = part * width + lane * 128
                    scratch[place, :] = side[:, first : first + 128]
    put(2, (everything, everything), scratch[...], RATE_QKV)

    @pl.when(pl.program_id(0) == 0)
    def small_ones():
        last = ins[12].shape[0]
        put(4, (everything, everything), small_ref[:last], 0.5, 0.0)
        put(5, (everything, everything), small_ref[last:, :HEADS], 1.0, 0.0)
        norm_ref[...] = grad_norm


def mlp_view(t):
    rows, _, width_ff = t.shape
    return t.reshape(rows, 2, width_ff // 128, 128).transpose(0, 2, 1, 3).reshape(-1, 128)


def adam_all(small, x_place, arrays, att_sides, ff_sides):
    rows, _, width_ff = arrays[6].shape
    steps = 4

    def qkv_view(t):
        return jnp.transpose(t, (1, 0, 2))

    def mlp_back(t, shape):
        rows, _, width_ff = shape
        t = t.reshape(rows, width_ff // 128, 2, 128).transpose(0, 2, 1, 3)
        return t.reshape(shape)

    views = [qkv_view(t) for t in arrays[:3]] + list(arrays[3:6])
    views += [mlp_view(t) for t in arrays[6:9]] + list(arrays[9:12])
    gains = [mlp_view(t[None]) for t in arrays[12:15]] + [t[None] for t in arrays[15:]]
    grads = list(att_sides) + [t for pair in ff_sides for t in pair]

    def spec(t):
        axis = t.ndim - 2
        block = list(t.shape)
        block[axis] //= steps
        return pl.BlockSpec(tuple(block), lambda i, place: (0,) * axis + (i, 0))

    def whole(t):
        return pl.BlockSpec(t.shape, lambda i, place: (0, 0))

    def mine(t):
        return pl.BlockSpec((rows // steps, t.shape[1]), lambda i, place: (place[0] * steps + i, 0))

    specs = [spec(t) for t in views] + [whole(t) for t in gains]
    new = pl.pallas_call(
        functools.partial(adam_kernel, steps, len(ff_sides)),
        grid_spec=pltpu.PrefetchScalarGridSpec(
            num_scalar_prefetch=1,
            grid=(steps,),
            in_specs=[whole(small)]
            + specs
            + [spec(t) if k % 2 else mine(t) for k, t in enumerate(grads)],
            out_specs=specs + [pl.BlockSpec((1, 1), lambda i, place: (0, 0))],
            scratch_shapes=[pltpu.VMEM((views[6].shape[0] // steps, 128), F32)],
        ),
        out_shape=[jax.ShapeDtypeStruct(t.shape, F32) for t in views + gains]
        + [jax.ShapeDtypeStruct((1, 1), F32)],
        compiler_params=pltpu.CompilerParams(vmem_limit_bytes=VMEM_LIMIT),
        cost_estimate=pl.CostEstimate(
            flops=20 * sum(t.size for t in views) // 3,
            bytes_accessed=8 * sum(t.size for t in views),
            transcendentals=0,
        ),
        name="adam",
    )(x_place[None], small, *views, *gains, *grads)
    new = list(new)
    return (
        [qkv_view(t) for t in new[:3]]
        + new[3:6]
        + [mlp_back(t, arrays[6].shape) for t in new[6:9]]
        + new[9:12]
        + [mlp_back(t, (1,) + arrays[12].shape)[0] for t in new[12:15]]
        + [t[0] for t in new[15:18]]
        + [new[18].reshape(())]
    )


def on_device(
    inputs,
    doc_ids,
    cotangent,
    weight_qkv,
    moment_qkv,
    second_qkv,
    weight_out,
    moment_out,
    second_out,
    weight_mlp,
    moment_mlp,
    second_mlp,
    weight_down,
    moment_down,
    second_down,
    norm_gains,
    moment_gains,
    second_gains,
    gate_logit,
    moment_gate,
    second_gate,
):
    micro_count, _, seg_count, own_len, _ = inputs.shape
    own_tokens = seg_count * own_len
    x_place = lax.axis_index("x")
    y_place = lax.axis_index("y")
    c_place = lax.axis_index("c")
    orders = [("x", "y") if m % 2 == 0 else ("y", "x") for m in range(micro_count)]

    z_count = D // (2 * weight_qkv.shape[0])

    def half_columns(weight, which):
        width = weight.shape[-1] // 2
        return lax.dynamic_slice_in_dim(weight, which * width, width, axis=weight.ndim - 1)

    def join_rows(mine, theirs):
        both = jnp.zeros((2 * rows, mine.shape[1]), BF)
        both = lax.dynamic_update_slice_in_dim(both, mine, x_place * rows, axis=0)
        return lax.dynamic_update_slice_in_dim(both, theirs, (1 - x_place) * rows, axis=0)

    def fetch(block):
        return lax.all_gather(block, "z", axis=0, tiled=True)

    rows = weight_qkv.shape[0]
    heads = weight_qkv.shape[2] // (2 * HEAD_DIM)
    width_att = heads * HEAD_DIM
    width_ff = weight_down.shape[1] // 2
    width = width_ff // CHUNKS

    def qkv_columns(which):
        return half_columns(weight_qkv, which).astype(BF).reshape(rows, -1)

    def ff_columns(k, which):
        start = tie(which * width_ff + k * width, shard_qkv)
        mlp = lax.dynamic_slice_in_dim(weight_mlp, start, width, axis=2).astype(BF)
        down = lax.dynamic_slice_in_dim(weight_down, start, width, axis=1).astype(BF)
        return jnp.concatenate([mlp[:, 0], mlp[:, 1], down], axis=1)

    send_qkv = qkv_columns(1 - x_place)
    all_out = direct_gather(tie(weight_out, send_qkv).astype(BF), z_count)
    all_ids = tie(doc_ids[:, 0], send_qkv)
    for axis in ("y", "c"):
        all_ids = jnp.stack([all_ids, swap(all_ids, axis)], axis=0)
    micros = range(micro_count)
    tokens = 8 * own_tokens
    token_rows = [
        tie(inputs[m, 0], send_qkv).reshape(own_tokens, D).astype(F32) for m in micros
    ]
    normed_att = [rms_norm(t, norm_gains[0]).astype(BF) for t in token_rows]
    their_qkv = swap(send_qkv, "x")
    shard_qkv = join_rows(qkv_columns(x_place), tie(their_qkv, all_ids, *normed_att))
    full_qkv = fetch(shard_qkv)

    head_start = (y_place * 2 + c_place) * (2 * heads) + x_place * heads
    gate_local = lax.dynamic_slice_in_dim(gate_logit, head_start, heads)
    mixing = jax.nn.sigmoid(gate_local)
    gate_rows = jnp.broadcast_to(mixing[:, None], (heads, HEAD_DIM))

    back_low = [cotangent[m, 0].reshape(own_tokens, D) for m in micros]
    all_ids = jnp.stack([all_ids, swap(all_ids, "x")], axis=0)
    their_first = swap(ff_columns(0, 1 - x_place), "x")
    shard_ff = [join_rows(ff_columns(0, x_place), their_first)]
    att_states = [
        gather_start(normed_att[m], *orders[m], (shard_ff[0], all_ids)) for m in micros
    ]
    att_by_x = [state[1 + orders[m].index("y")] for m, state in enumerate(att_states)]
    att_states = [gather_across(state, *orders[m], "y") for m, state in enumerate(att_states)]
    att_rows = [gather_core(state) for state in att_states]

    def their_ff(k, *earlier):
        return swap(tie(ff_columns(k, 1 - x_place), *earlier), "x")

    full_ff = [fetch(shard_ff[0])]
    their_out = swap(tie(half_columns(all_out, 1 - x_place), *att_by_x), "x")
    both_out = jnp.zeros((z_count, 2, rows, width_att), BF)
    for part, place in ((half_columns(all_out, x_place), x_place), (their_out, 1 - x_place)):
        part = part.reshape(z_count, 1, rows, width_att)
        both_out = lax.dynamic_update_slice_in_dim(both_out, part, place, axis=1)
    full_out = both_out.reshape(D, width_att)
    back_states = [
        gather_start(back_low[m], *orders[m], (their_out,), (shard_ff[0],)) for m in micros
    ]
    back_first = [t for state in back_states for t in state[1:]]
    back_states = [gather_across(state, *orders[m], "y") for m, state in enumerate(back_states)]
    earlier = back_first

    rel_c = jnp.arange(2)[:, None, None] ^ c_place
    rel_y = jnp.arange(2)[None, :, None] ^ y_place
    places = ((rel_y * 2 + rel_c) * own_len + jnp.arange(own_len)).reshape(-1)
    causal = places[:, None] >= places[None, :]
    masks = []
    columns = []
    for m in micros:
        ids = jnp.transpose(all_ids[:, :, :, m], (0, 3, 1, 2, 4)).reshape(2, seg_count, -1)
        same = ids[:, :, :, None] == ids[:, :, None, :]
        masks.append((same & causal).astype(F32))
        last = jnp.max(ids, axis=2)
        previous = jnp.concatenate([jnp.full((2, 1), -1, last.dtype), last[:, :-1]], axis=1)
        reading = ids == previous[:, :, None]
        writing = ids == last[:, :, None]
        keep = jnp.broadcast_to((last == previous)[:, :, None], ids.shape)
        columns.append(jnp.stack([reading, writing, keep], axis=-1).astype(F32))

    slots = (2, 2, 2, seg_count, own_len)
    wheres = [1 if orders[m][0] == "x" else 2 for m in micros]
    projected = []
    combined = []
    hidden = []
    normed_mlp = []
    for m in micros:
        mine, other = att_rows[m]
        if m == 0:
            mine = tie(mine, *back_first)
        proj = jnp.concatenate([mm(p, full_qkv, NN).astype(BF) for p in (mine, other)], axis=0)
        projected.append(proj.reshape(slots + (3 * width_att,)))
        comb = attention_fwd(projected[m], masks[m], columns[m], gate_rows, wheres[m])
        combined.append(comb.reshape(tokens, width_att))
    half = tokens // 2
    for k in range(1, CHUNKS):
        theirs = their_ff(k, *earlier)
        shard_ff.append(join_rows(ff_columns(k, x_place), tie(theirs, combined[0])))
        full_ff.append(fetch(shard_ff[k]))
        earlier = [theirs]
    back_states = [(tie(state[0], combined[0]),) + state[1:] for state in back_states]
    back_rows = [gather_core(state) for state in back_states]
    for m in micros:
        ready = combined[m]
        if m > 0:
            ready = tie(ready, *shard_ff, *[state[-1] for state in back_states])
        other = mm(ready[half:], full_out, NT).astype(BF)
        mine = mm(ready[:half], full_out, NT).astype(BF)
        state = scatter_core(mine, other, own_tokens, orders[m][0], orders[m][0])
        state = scatter_outer(state, orders[m][0])
        hidden.append(token_rows[m] + scatter_inner(state, orders[m][1]))
        normed_mlp.append(rms_norm(hidden[m], norm_gains[1]).astype(BF))
    mlp_rows = [gather_core(state) for state in gather_steps(normed_mlp, orders)]

    def exchange_grad(grad):
        return grad, swap(lax.dynamic_slice_in_dim(grad, (1 - x_place) * rows, rows, axis=0), "x")

    def squares_of(grad):
        wide = grad.astype(F32)
        return jnp.sum(wide * wide)

    def reduce_rows(partial):
        return lax.psum_scatter(partial, "z", scatter_dimension=0, tiled=True)

    def products(left, right, totals, dtype):
        terms = [mm(left[p], right, NT) for p in (1, 0)][::-1]
        if totals is not None:
            terms = [a + b for a, b in zip(totals, terms)]
        return tuple(t.astype(dtype) for t in terms)

    active = []
    d_gate_up = []
    own_ff = []
    d_total = [None] * micro_count
    states = [None] * micro_count
    for k in range(CHUNKS):
        active.append([])
        d_gate_up.append([])
        last = k == CHUNKS - 1
        for m in micros:
            rows_in = mlp_rows[m]
            if last and m > 0:
                rows_in = (tie(rows_in[0], *d_total[m - 1]), rows_in[1])
            act, grad = feed_forward(rows_in, back_rows[m], full_ff[k])
            active[k].append(act)
            d_gate_up[k].append(grad)
            if last and m > 0:
                grad = (grad[0], tie(grad[1], states[m - 1][1]))
            dtype = BF if last else F32
            d_total[m] = products(grad, full_ff[k][:, : 2 * width], d_total[m], dtype)
            if last:
                states[m] = scatter_core(*d_total[m], own_tokens, orders[m][0], orders[m][0])
        if not last:
            grad_ff = weight_grads(mlp_rows, back_rows, d_gate_up[k], active[k])
            own_ff.append(reduce_rows(grad_ff))
            terms = [t for pair in d_total for t in pair]
            full_ff[k + 1] = tie(full_ff[k + 1], grad_ff, *terms)

    out_pairs = []
    for m in micros:
        act = [active[k][m] for k in range(CHUNKS)]
        act[-1] = (act[-1][0], tie(act[-1][1], states[-1][1]))
        out_pairs.append(down_product(act, full_ff))
    products_done = [t for pair in out_pairs for t in pair]
    outer_states = [scatter_outer(states[m], orders[m][0], *products_done) for m in micros]
    last_active = [
        (active[-1][m][0], tie(active[-1][m][1], *[t[1] for t in outer_states])) for m in micros
    ]
    grad_ff = weight_grads(mlp_rows, back_rows, d_gate_up[-1], last_active)
    own_ff.append(reduce_rows(grad_ff))

    gain_grad_att = jnp.zeros((D,), F32)
    gain_grad_mlp = jnp.zeros((D,), F32)
    d_hidden = []
    for m in micros:
        keep, send = outer_states[m]
        d_normed = scatter_inner((tie(keep, grad_ff), send), orders[m][1])
        ignored, norm_back = jax.vjp(rms_norm, hidden[m], norm_gains[1])
        d_norm, d_gain = norm_back(d_normed)
        gain_grad_mlp = gain_grad_mlp + d_gain
        d_hidden.append(back_low[m].astype(F32) + d_norm)

    gate_sum = jnp.zeros((heads,), F32)
    d_projs = []
    out_states = [
        scatter_core(*tie_pair(out_pairs[m], *d_hidden), own_tokens, orders[m][0], orders[m][0])
        for m in micros
    ]
    grad_states = gather_steps([t.astype(BF) for t in d_hidden], orders)
    sends = [t[1] for t in out_states]
    out_states = [tie_send(t, *[g[-1] for g in grad_states]) for t in out_states]
    att_grads = [gather_core((tie(g[0], *sends),) + g[1:]) for g in grad_states]
    ff_pairs = [exchange_grad(own_ff[0])]
    for m in micros:
        mine, other = att_grads[m]
        if m == 0:
            other = tie(other, own_ff[0])
        d_combined = jnp.concatenate(
            [mm(mine, full_out, NN), mm(other, full_out, NN)], axis=0
        )
        d_proj, gate_part = attention_bwd(
            projected[m],
            d_combined.reshape(slots + (width_att,)),
            masks[m],
            columns[m],
            gate_rows,
            wheres[m],
        )
        gate_sum = gate_sum + jnp.sum(gate_part, axis=(0, 2))
        d_projs.append(d_proj.reshape(tokens, 3 * width_att))
    out_came = [swap(out_states[m][1], orders[m][0]) for m in micros]
    by_rows = [d_projs[0], tie(d_projs[-1], ff_pairs[0][1], *out_came)]
    grad_att = weight_grads(att_rows, att_grads, by_rows, combined)
    own_att = reduce_rows(grad_att)
    mlp_out = []
    for m in micros:
        state = scatter_add(out_states[m][0], tie(out_came[m], grad_att))
        mlp_out.append(scatter_inner(state, orders[m][1]))
    block_out = [(hidden[m] + mlp_out[m]).astype(BF) for m in micros]

    ff_pairs += [exchange_grad(g) for g in own_ff[1:]]

    ff_owned = sum(squares_of(g) for g in own_ff)

    grad_rows = []
    in_states = []
    for m in micros:
        d_proj = tie(d_projs[m], grad_att)
        other = mm(d_proj[half:], full_qkv, NT).astype(BF)
        mine = mm(d_proj[:half], full_qkv, NT).astype(BF)
        in_states.append(scatter_core(mine, other, own_tokens, orders[m][0], orders[m][0]))
    for m in micros:
        state = scatter_outer(in_states[m], orders[m][0])
        if m > 0:
            state = tie_send(state, ff_pairs[-1][1])
        d_normed = scatter_inner(state, orders[m][1])
        ignored, norm_first = jax.vjp(rms_norm, token_rows[m], norm_gains[0])
        d_norm, d_gain = norm_first(d_normed)
        gain_grad_att = gain_grad_att + d_gain
        grad_rows.append((d_hidden[m] + d_norm).astype(BF))

    att_mine, att_theirs = exchange_grad(own_att)

    gate_grad = gate_sum * mixing * (1.0 - mixing)
    gate_padded = lax.dynamic_update_slice(
        jnp.zeros(gate_logit.shape, F32), gate_grad, (head_start,)
    )
    gain_grad = mlp_view(jnp.stack([gain_grad_att, gain_grad_mlp], axis=0)[None])
    gate_row = jnp.concatenate([gate_padded, jnp.zeros((128 - HEADS,), F32)])[None]
    small = small_sums(ff_owned, own_att, gain_grad, gate_row)
    small = sum_everywhere(small, z_count, att_theirs)
    arrays = [
        weight_qkv,
        moment_qkv,
        second_qkv,
        weight_out,
        moment_out,
        second_out,
        weight_mlp,
        moment_mlp,
        second_mlp,
        weight_down,
        moment_down,
        second_down,
        norm_gains,
        moment_gains,
        second_gains,
        gate_logit,
        moment_gate,
        second_gate,
    ]
    new = adam_all(small, x_place, arrays, (att_mine, att_theirs), ff_pairs)
    shape = (micro_count, 1, seg_count, own_len, D)
    return (
        jnp.stack(block_out, axis=0).reshape(shape),
        jnp.stack(grad_rows, axis=0).reshape(shape),
        new[-1],
        *new[:-1],
    )


def solution(mesh):
    seq_count, ctx_count = mesh.devices.shape
    inner = Mesh(
        mesh.devices.reshape(seq_count // 2, 2, ctx_count // 2, 2), ("z", "x", "y", "c")
    )
    seq, ctx = ("z", "x"), ("y", "c")
    rows = P(None, seq, None, ctx, None)
    wide = P(seq, None, ctx)
    flat = P(seq, ctx)
    weights = (wide,) * 3 + (flat,) * 3 + (wide,) * 3 + (flat,) * 3 + (P(),) * 6
    return jax.shard_map(
        on_device,
        mesh=inner,
        in_specs=(rows, P(None, seq, None, ctx), rows) + weights,
        out_specs=(rows, rows, P()) + weights,
        check_vma=False,
    )
```
